32 devices in a mesh: ctx: 8 (over y, x, core), fsdp: 4 (over z).
Axes of the slice: x: 2, y: 2, z: 4, core: 2. Of those that a mesh axis runs over, the one named last changes fastest.
Arguments:
- tokens: bfloat16 [16, 256, 2048], P('ctx', 'fsdp'), may hold values from -6 to 6
- block_order: int32 [16], replicated, may hold values from 0 to 15, as said below
- w_query: bfloat16 [2048, 2048], P('fsdp'), may hold values from -0.125 to 0.125
- w_key: bfloat16 [2048, 2048], P('fsdp'), may hold values from -0.125 to 0.125
- w_value: bfloat16 [2048, 2048], P('fsdp'), may hold values from -0.125 to 0.125
- w_out: bfloat16 [2048, 2048], P('fsdp'), may hold values from -1 to 1
- w_gate: bfloat16 [2048, 8192], P('fsdp'), may hold values from -0.125 to 0.125
- w_up: bfloat16 [2048, 8192], P('fsdp'), may hold values from -0.125 to 0.125
- w_down: bfloat16 [2048, 8192], P('fsdp'), may hold values from -0.0625 to 0.0625
- gain_attn: bfloat16 [2048], P('fsdp'), may hold values from 0.099609375 to 1.8984375
- gain_mlp: bfloat16 [2048], P('fsdp'), may hold values from 0.099609375 to 1.8984375
- cotangent: bfloat16 [16, 256, 2048], P('ctx', 'fsdp'), may hold values from -6 to 6
Outputs:
- result: bfloat16 [16, 256, 2048], P('ctx', 'fsdp')
- grad_tokens: float32 [16, 256, 2048], P('ctx', 'fsdp')
- grad_w_query: float32 [2048, 2048], P(('ctx', 'fsdp'))
- grad_w_key: float32 [2048, 2048], P(('ctx', 'fsdp'))
- grad_w_value: float32 [2048, 2048], P(('ctx', 'fsdp'))
- grad_w_out: float32 [2048, 2048], P(('ctx', 'fsdp'))
- grad_w_gate: float32 [2048, 8192], P(('ctx', 'fsdp'))
- grad_w_up: float32 [2048, 8192], P(('ctx', 'fsdp'))
- grad_w_down: float32 [2048, 8192], P(('ctx', 'fsdp'))
- grad_gain_attn: float32 [2048], P(('ctx', 'fsdp'))
- grad_gain_mlp: float32 [2048], P(('ctx', 'fsdp'))
The draws below stay inside these ranges and needn't reach their ends.
Inputs may be any that keep to these rules, and one draw needn't show every extreme that they name: `block_order`: A permutation of the 16 sequence blocks. Slots 2 c and 2 c + 1 (the two slots of one device along ctx) hold blocks k and 15 - k for some k.
All inputs are finite; a program needn't handle non-finite values.
Results may differ from the reference program's by a relative error of at most 0.022.
Values may be sent and summed in bfloat16 or wider, within the bound.
No kernel may reach another device: no remote copies, remote signals or barrier semaphores. Data moves between devices by JAX's collectives and lax.ppermute only.
A program may use at most 320 MiB of HBM per device.

```python
import jax
import jax.numpy as jnp
from jax import lax

D = 2048
HEADS = 32
HEAD_DIM = 64
FF = 8192
BLOCK_ROWS = 256
BLOCKS = 16
TOKENS = 4096


def draw_block_order(key, part):
    key = jax.random.fold_in(key, 11)
    perm_key, coin_key = jax.random.split(key)
    leaders = jax.random.permutation(perm_key, BLOCKS // 2).astype(jnp.int32)
    flips = jax.random.randint(coin_key, (BLOCKS // 2,), 0, 2, dtype=jnp.int32)
    lower = leaders + flips * (BLOCKS - 1 - 2 * leaders)
    upper = BLOCKS - 1 - lower
    return jnp.stack([lower, upper], 1).reshape(BLOCKS).astype(jnp.int32)


def steps_of(own_key, extent, shards, smallest, top_value):
    def one(position, parts):
        heights = jax.random.uniform(jax.random.fold_in(jax.random.fold_in(own_key, 6), position), (parts,), jnp.float32, smallest / len(shards), top_value / len(shards))
        return jnp.repeat(jnp.exp(heights), extent[position] // parts).reshape((-1,) + (1,) * (len(extent) - position - 1))

    gain = one(*shards[0])
    for cut in shards[1:]:
        gain = gain * one(*cut)
    return gain


def centred(own_key, shape, width, most, pieces=(), kind=jnp.bfloat16):
    entries = jax.random.normal(own_key, shape, jnp.float32) * width
    if len(pieces) > 0:
        entries = steps_of(own_key, shape, pieces, -0.22, 0.18) * entries
    return jnp.clip(entries, min=-most, max=most).astype(kind)


def setup_inputs(seed: int = 0) -> dict:
    streams_of = jax.random.split(jax.random.key(seed), 13)
    tokens = centred(streams_of[0], (BLOCKS, BLOCK_ROWS, D), 1.0, 6.0, ((0, 8), (1, 4)))
    block_order = draw_block_order(jax.random.fold_in(streams_of[12], 71), 0)
    w_query = centred(streams_of[2], (D, D), D ** -0.5, 0.125, ((0, 4),))
    w_key = centred(streams_of[3], (D, D), D ** -0.5, 0.125, ((0, 4),))
    w_value = centred(streams_of[4], (D, D), D ** -0.5, 0.125, ((0, 4),))
    w_out = centred(streams_of[5], (D, D), (max(1, D * 64 // TOKENS)) ** -0.5, 1.0, ((0, 4),))
    w_gate = centred(streams_of[6], (D, FF), D ** -0.5, 0.125, ((0, 4),))
    w_up = centred(streams_of[7], (D, FF), D ** -0.5, 0.125, ((0, 4),))
    w_down = centred(streams_of[8], (D, FF), FF ** -0.5, 0.0625, ((0, 4),))
    gain_attn = jnp.clip(1.0 + 0.18 * jax.random.normal(streams_of[9], (D,), jnp.float32), 0.099609375, 1.8984375).astype(jnp.bfloat16)
    gain_mlp = jnp.clip(1.0 + 0.18 * jax.random.normal(streams_of[10], (D,), jnp.float32), 0.099609375, 1.8984375).astype(jnp.bfloat16)
    cotangent = centred(streams_of[11], (BLOCKS, BLOCK_ROWS, D), 1.0, 6.0, ((0, 8), (1, 4)))
    return dict(tokens=tokens, block_order=block_order, w_query=w_query, w_key=w_key, w_value=w_value, w_out=w_out, w_gate=w_gate, w_up=w_up, w_down=w_down, gain_attn=gain_attn, gain_mlp=gain_mlp, cotangent=cotangent)


EPSILON = 1e-05
ROPE_BASE = 130000.0
HIGHEST_PRECISION = lax.Precision.HIGHEST

@jax.custom_vjp
def low(v):
    return lax.optimization_barrier(v.astype(jnp.bfloat16)).astype(jnp.float32)

@jax.custom_vjp
def low_back(v):
    return v

def low_keep(v):
    return (low(v), None)

def low_pass(kept, grad):
    return (grad,)

def back_keep(v):
    return (v, None)

def back_low(kept, grad):
    return (low(grad),)
low.defvjp(low_keep, low_pass)
low_back.defvjp(back_keep, back_low)

def rotate(values, places, direction):
    half_dim = values.shape[-1] // 2
    frequency = 1.0 / ROPE_BASE ** (jnp.arange(half_dim, dtype=jnp.float32) * (2.0 / values.shape[-1]))
    angles = places[..., None] * frequency
    cosine = jnp.cos(angles)[..., None, :]
    sine_part = direction * jnp.sin(angles)[..., None, :]
    leading = values[..., :half_dim]
    trailing = values[..., half_dim:]
    return jnp.concatenate([leading * cosine - trailing * sine_part, trailing * cosine + leading * sine_part], -1)

def normed(values, gain_vector):
    return values * lax.rsqrt(lax.optimization_barrier(jnp.mean(values * values, -1, keepdims=True)) + EPSILON) * gain_vector

def product(left, right):
    return jnp.dot(left, right, precision=HIGHEST_PRECISION, preferred_element_type=jnp.float32)

def reference(tokens, block_order, w_query, w_key, w_value, w_out, w_gate, w_up, w_down, gain_attn, gain_mlp, cotangent):
    inverse = jnp.zeros((BLOCKS,), jnp.int32).at[block_order].set(jnp.arange(BLOCKS, dtype=jnp.int32))
    seq_stream = tokens[inverse].reshape(TOKENS, D).astype(jnp.float32)
    seq_upstream = cotangent[inverse].reshape(TOKENS, D).astype(jnp.float32)
    places = jnp.arange(TOKENS, dtype=jnp.int32).astype(jnp.float32)
    score_scale = HEAD_DIM ** (-0.5)

    def attend(queries, key_rows, value_rows):

        def one_block(element):
            query_part, query_places = element
            scores = jnp.einsum('qhd,khd->hqk', query_part, key_rows, precision=HIGHEST_PRECISION)
            scores = low_back(scores * score_scale)
            allowed = places[None, :] <= query_places[:, None]
            scores = jnp.where(allowed[None], scores, -1e+30)
            probabilities = jax.nn.softmax(scores, axis=-1)
            return jnp.einsum('hqk,khd->qhd', low(probabilities), value_rows, precision=HIGHEST_PRECISION)
        query_parts = queries.reshape(BLOCKS, BLOCK_ROWS, HEADS, HEAD_DIM)
        place_parts = places.reshape(BLOCKS, BLOCK_ROWS)
        return lax.map(jax.checkpoint(one_block), (query_parts, place_parts)).reshape(TOKENS, D)

    def block_layer(stream, query_weight, key_weight, value_weight, out_weight, gate_weight, up_weight, down_weight, gain_one, gain_two):
        attn_input = low(normed(stream, gain_one))
        q_lin = low_back(product(attn_input, query_weight)).reshape(TOKENS, HEADS, HEAD_DIM)
        k_lin = low_back(product(attn_input, key_weight)).reshape(TOKENS, HEADS, HEAD_DIM)
        v_lin = low_back(product(attn_input, value_weight))
        queries = low(rotate(q_lin, places, 1.0))
        key_rows = low(rotate(k_lin, places, 1.0))
        value_rows = low(v_lin).reshape(TOKENS, HEADS, HEAD_DIM)
        mixed = low(low_back(attend(queries, key_rows, value_rows)))
        middle = stream + low_back(product(mixed, out_weight))
        mlp_input = low(normed(middle, gain_two))
        gate_act = low_back(product(mlp_input, gate_weight))
        upward = low_back(product(mlp_input, up_weight))
        hidden = low(jax.nn.silu(gate_act) * upward)
        return middle + low_back(product(hidden, jnp.transpose(down_weight)))
    floats = [weight.astype(jnp.float32) for weight in (w_query, w_key, w_value, w_out, w_gate, w_up, w_down, gain_attn, gain_mlp)]
    output, pullback = jax.vjp(block_layer, seq_stream, *floats)
    grads = pullback(seq_upstream)
    result = output.reshape(BLOCKS, BLOCK_ROWS, D)[block_order].astype(jnp.bfloat16)
    grad_tokens = grads[0].reshape(BLOCKS, BLOCK_ROWS, D)[block_order]
    return (result, grad_tokens, grads[1], grads[2], grads[3], grads[4], grads[5], grads[6], grads[7], grads[8], grads[9])
```

```python
import functools

import jax
import jax.numpy as jnp
from jax import lax
from jax.experimental import pallas as pl
from jax.experimental.pallas import tpu as pltpu
from jax.sharding import PartitionSpec as P

HEAD_DIM = 64


EPSILON = 1e-05
ROPE_BASE = 130000.0
MASKED_SCORE = -1e30


def rotate(values, places, direction):
    half_dim = values.shape[-1] // 2
    frequency = 1.0 / ROPE_BASE ** (
        jnp.arange(half_dim, dtype=jnp.float32) * (2.0 / values.shape[-1])
    )
    angles = places[..., None] * frequency
    cosine = jnp.cos(angles)[..., None, :]
    sine_part = direction * jnp.sin(angles)[..., None, :]
    leading = values[..., :half_dim]
    trailing = values[..., half_dim:]
    return jnp.concatenate(
        [leading * cosine - trailing * sine_part, trailing * cosine + leading * sine_part], -1
    )


def matmul(left, right):
    return jnp.dot(left, right, preferred_element_type=jnp.float32)


def contract(left, right):
    return lax.dot_general(
        left, right, (((1,), (1,)), ((), ())), preferred_element_type=jnp.float32
    )


def transpose_product(left, right):
    return lax.dot_general(
        left, right, (((0,), (0,)), ((), ())), preferred_element_type=jnp.float32
    )


def split_heads(values):
    return values.reshape(values.shape[:-1] + (-1, HEAD_DIM))


def keep_state(current):
    return current


def tile_scores(queries, key_rows, query_places, key_places, score_scale):
    scores = (
        jnp.einsum("qhd,khd->hqk", queries, key_rows, preferred_element_type=jnp.float32)
        * score_scale
    )
    allowed = (key_places[None, :] <= query_places[:, None])[None]
    return (jnp.where(allowed, scores, MASKED_SCORE), allowed)


def grow_state(current, queries, key_rows, value_rows, query_places, key_places, score_scale):
    run_peak, run_total, summed = current
    scores, allowed = tile_scores(queries, key_rows, query_places, key_places, score_scale)
    new_peak = jnp.maximum(run_peak, jnp.max(scores, -1))
    weights = jnp.where(allowed, jnp.exp(scores - new_peak[..., None]), 0.0)
    factor = jnp.exp(run_peak - new_peak)
    run_total = run_total * factor + jnp.sum(weights, -1)
    summed = summed * jnp.transpose(factor)[:, :, None] + jnp.einsum(
        "hqk,khd->qhd", weights.astype(jnp.bfloat16), value_rows, preferred_element_type=jnp.float32
    )
    return (new_peak, run_total, summed)


def backward_tile(
    queries,
    key_rows,
    value_rows,
    grad_out,
    log_total,
    row_delta,
    query_places,
    key_places,
    score_scale,
):
    scores, allowed = tile_scores(queries, key_rows, query_places, key_places, score_scale)
    probabilities = jnp.where(allowed, jnp.exp(scores - log_total[..., None]), 0.0)
    grad_probs = jnp.einsum(
        "qhd,khd->hqk", grad_out, value_rows, preferred_element_type=jnp.float32
    )
    grad_scores = (probabilities * (grad_probs - row_delta[..., None])).astype(jnp.bfloat16)
    return (probabilities, grad_scores)


def norm_back(grad_normed_in, normed_values, inverse_root, gain_vector):
    scaled = grad_normed_in * gain_vector
    return inverse_root * (
        scaled - normed_values * jnp.mean(scaled * normed_values, -1, keepdims=True)
    )


def per_device(
    tokens,
    block_order,
    w_query,
    w_key,
    w_value,
    w_out,
    w_gate,
    w_up,
    w_down,
    gain_attn,
    gain_mlp,
    cotangent,
):
    slot_count, share_rows, model_width = tokens.shape
    fsdp_size = lax.axis_size("fsdp")
    block_rows = share_rows * fsdp_size
    head_width = model_width // fsdp_size
    heads_here = head_width // HEAD_DIM
    row_count = slot_count * share_rows
    score_scale = HEAD_DIM ** (-0.5)
    own_slots = 2 * lax.axis_index("ctx") + jnp.arange(2, dtype=jnp.int32)
    own_blocks = block_order[own_slots]
    token_places = (
        (
            own_blocks[:, None] * block_rows
            + lax.axis_index("fsdp") * share_rows
            + jnp.arange(share_rows, dtype=jnp.int32)[None, :]
        )
        .astype(jnp.float32)
        .reshape(row_count)
    )
    head_places = (
        own_blocks[:, None] * block_rows + jnp.arange(block_rows, dtype=jnp.int32)[None, :]
    ).astype(jnp.float32)
    params = (w_query, w_key, w_value, w_out, w_gate, w_up, w_down, gain_attn, gain_mlp)
    weights_all = (
        lax.all_gather(params[0], "fsdp", axis=0, tiled=True),
        lax.all_gather(params[1], "fsdp", axis=0, tiled=True),
        lax.all_gather(params[2], "fsdp", axis=0, tiled=True),
        lax.all_gather(params[3], "fsdp", axis=0, tiled=True),
        lax.all_gather(params[4], "fsdp", axis=0, tiled=True),
        lax.all_gather(params[5], "fsdp", axis=0, tiled=True),
        lax.all_gather(params[6], "fsdp", axis=0, tiled=True),
        lax.all_gather(params[7], "fsdp", axis=0, tiled=True),
        lax.all_gather(params[8], "fsdp", axis=0, tiled=True),
    )
    stream = tokens.reshape(row_count, model_width).astype(jnp.float32)
    root_one = lax.rsqrt(jnp.mean(stream * stream, -1, keepdims=True) + EPSILON)
    norm_one = stream * root_one
    attn_input = (norm_one * weights_all[7].astype(jnp.float32)).astype(jnp.bfloat16)

    def project_turn(weight):
        linear = matmul(attn_input, weight).reshape(row_count, -1, HEAD_DIM)
        return (
            rotate(linear, token_places, 1.0)
            .astype(jnp.bfloat16)
            .reshape(slot_count, share_rows, model_width)
        )

    query_tok = project_turn(weights_all[0])
    key_tok = project_turn(weights_all[1])
    value_tok = (
        matmul(attn_input, weights_all[2])
        .astype(jnp.bfloat16)
        .reshape(slot_count, share_rows, model_width)
    )
    query_heads, key_heads, value_heads = (
        lax.all_to_all(query_tok, "fsdp", split_axis=2, concat_axis=1, tiled=True),
        lax.all_to_all(key_tok, "fsdp", split_axis=2, concat_axis=1, tiled=True),
        lax.all_to_all(value_tok, "fsdp", split_axis=2, concat_axis=1, tiled=True),
    )
    query_split = split_heads(query_heads)
    start_state = tuple(
        (
            (
                jnp.full((heads_here, block_rows), MASKED_SCORE, jnp.float32),
                jnp.zeros((heads_here, block_rows), jnp.float32),
                jnp.zeros((block_rows, heads_here, HEAD_DIM), jnp.float32),
            )
            for which_slot in range(2)
        )
    )
    carried = start_state
    key_part = lax.all_gather(key_heads, "ctx", axis=0, tiled=True)
    value_part = lax.all_gather(value_heads, "ctx", axis=0, tiled=True)

    def visit_slot(inner_state, element):
        key_one, value_one, offset = element
        key_block = block_order[offset]
        key_places = (key_block * block_rows + jnp.arange(block_rows, dtype=jnp.int32)).astype(
            jnp.float32
        )
        key_split = split_heads(key_one)
        value_split = split_heads(value_one)
        updated = []
        for which_slot in range(2):

            def grow_one(current, which_slot=which_slot):
                return grow_state(
                    current,
                    query_split[which_slot],
                    key_split,
                    value_split,
                    head_places[which_slot],
                    key_places,
                    score_scale,
                )

            updated.append(
                lax.cond(
                    key_block <= own_blocks[which_slot],
                    grow_one,
                    keep_state,
                    inner_state[which_slot],
                )
            )
        return (tuple(updated), None)

    offsets = jnp.arange(key_part.shape[0], dtype=jnp.int32)
    carried, unused = lax.scan(visit_slot, carried, (key_part, value_part, offsets))
    attended_parts = []
    log_parts = []
    for which_slot in range(2):
        run_peak, run_total, summed = carried[which_slot]
        log_parts.append(run_peak + jnp.log(run_total))
        attended_parts.append(summed / jnp.transpose(run_total)[:, :, None])
    attended = jnp.stack(attended_parts)
    log_total = jnp.stack(log_parts)
    mixed_send = attended.reshape(slot_count, block_rows, head_width).astype(jnp.bfloat16)
    mixed_tok = lax.all_to_all(mixed_send, "fsdp", split_axis=1, concat_axis=2, tiled=True)
    mixed_flat = mixed_tok.reshape(row_count, model_width)
    middle = stream + matmul(mixed_flat, weights_all[3])
    root_two = lax.rsqrt(jnp.mean(middle * middle, -1, keepdims=True) + EPSILON)
    norm_two = middle * root_two
    mlp_input = (norm_two * weights_all[8].astype(jnp.float32)).astype(jnp.bfloat16)
    gate_act = matmul(mlp_input, weights_all[4])
    upward = matmul(mlp_input, weights_all[5])
    gate_sigmoid = jax.nn.sigmoid(gate_act)
    gate_silu = gate_act * gate_sigmoid
    hidden = (gate_silu * upward).astype(jnp.bfloat16)
    output = middle + contract(hidden, weights_all[6])
    result = output.astype(jnp.bfloat16).reshape(slot_count, share_rows, model_width)
    upstream = cotangent.reshape(row_count, model_width)
    grad_hidden = matmul(upstream, weights_all[6])
    grad_gate = (
        grad_hidden * upward * gate_sigmoid * (1.0 + gate_act * (1.0 - gate_sigmoid))
    ).astype(jnp.bfloat16)
    grad_up = (grad_hidden * gate_silu).astype(jnp.bfloat16)
    grad_two = contract(grad_gate, weights_all[4]) + contract(grad_up, weights_all[5])
    gain_two_part = jnp.sum(grad_two * norm_two, 0)
    grad_middle = upstream.astype(jnp.float32) + norm_back(
        grad_two, norm_two, root_two, weights_all[8].astype(jnp.float32)
    )
    grad_branch = grad_middle.astype(jnp.bfloat16)
    grad_mixed = (
        contract(grad_branch, weights_all[3])
        .astype(jnp.bfloat16)
        .reshape(slot_count, share_rows, model_width)
    )
    grad_heads = lax.all_to_all(grad_mixed, "fsdp", split_axis=2, concat_axis=1, tiled=True)
    grad_split = split_heads(grad_heads)
    row_delta = jnp.transpose(jnp.sum(grad_split.astype(jnp.float32) * attended, -1), (0, 2, 1))
    gathered = (
        lax.all_gather(key_heads, "ctx", axis=0, tiled=True),
        lax.all_gather(value_heads, "ctx", axis=0, tiled=True),
    )
    key_all, value_all = gathered
    total_slots = key_all.shape[0]

    def query_visit(current, element):
        key_pair, value_pair, pair_index = element
        updated = list(current)
        for member in range(2):
            key_block = block_order[2 * pair_index + member]
            key_places = (key_block * block_rows + jnp.arange(block_rows, dtype=jnp.int32)).astype(
                jnp.float32
            )
            key_split = split_heads(key_pair[member])
            value_split = split_heads(value_pair[member])
            for which_slot in range(2):

                def take_query(
                    accum,
                    which_slot=which_slot,
                    key_split=key_split,
                    value_split=value_split,
                    key_places=key_places,
                ):
                    probabilities, grad_scores = backward_tile(
                        query_split[which_slot],
                        key_split,
                        value_split,
                        grad_split[which_slot],
                        log_total[which_slot],
                        row_delta[which_slot],
                        head_places[which_slot],
                        key_places,
                        score_scale,
                    )
                    return accum + score_scale * jnp.einsum(
                        "hqk,khd->qhd", grad_scores, key_split, preferred_element_type=jnp.float32
                    )

                updated[which_slot] = lax.cond(
                    key_block <= own_blocks[which_slot], take_query, keep_state, updated[which_slot]
                )
        return (tuple(updated), None)

    query_zero = jnp.zeros((block_rows, heads_here, HEAD_DIM), jnp.float32)
    pair_keys = key_all.reshape(total_slots // 2, 2, block_rows, head_width)
    pair_values = value_all.reshape(total_slots // 2, 2, block_rows, head_width)
    grad_query_parts, unused = lax.scan(
        query_visit,
        (query_zero, query_zero),
        (pair_keys, pair_values, jnp.arange(total_slots // 2, dtype=jnp.int32)),
    )
    key_part = key_all
    value_part = value_all

    def key_visit(unused_carry, element):
        key_one, value_one, offset = element
        key_block = block_order[offset]
        key_places = (key_block * block_rows + jnp.arange(block_rows, dtype=jnp.int32)).astype(
            jnp.float32
        )
        key_split = split_heads(key_one)
        value_split = split_heads(value_one)
        sums = (
            jnp.zeros((block_rows, heads_here, HEAD_DIM), jnp.float32),
            jnp.zeros((block_rows, heads_here, HEAD_DIM), jnp.float32),
        )
        for which_slot in range(2):

            def take_keys(current, which_slot=which_slot):
                probabilities, grad_scores = backward_tile(
                    query_split[which_slot],
                    key_split,
                    value_split,
                    grad_split[which_slot],
                    log_total[which_slot],
                    row_delta[which_slot],
                    head_places[which_slot],
                    key_places,
                    score_scale,
                )
                grad_key = current[0] + score_scale * jnp.einsum(
                    "hqk,qhd->khd",
                    grad_scores,
                    query_split[which_slot],
                    preferred_element_type=jnp.float32,
                )
                grad_value = current[1] + jnp.einsum(
                    "hqk,qhd->khd",
                    probabilities.astype(jnp.bfloat16),
                    grad_split[which_slot],
                    preferred_element_type=jnp.float32,
                )
                return (grad_key, grad_value)

            sums = lax.cond(key_block <= own_blocks[which_slot], take_keys, keep_state, sums)
        joined = jnp.concatenate(
            [sums[0].reshape(block_rows, head_width), sums[1].reshape(block_rows, head_width)], -1
        )
        return (unused_carry, joined)

    unused_final, terms = lax.scan(
        key_visit,
        jnp.zeros((), jnp.float32),
        (key_part, value_part, jnp.arange(slot_count * lax.axis_size("ctx"), dtype=jnp.int32)),
    )
    summed_kv = lax.psum_scatter(
        terms.astype(jnp.bfloat16), "ctx", scatter_dimension=0, tiled=True
    ).astype(jnp.float32)
    grad_keys = (
        rotate(split_heads(summed_kv[..., :head_width]), head_places, -1.0)
        .astype(jnp.bfloat16)
        .reshape(slot_count, block_rows, head_width)
    )
    grad_values = summed_kv[..., head_width:].astype(jnp.bfloat16)
    grad_queries = (
        rotate(jnp.stack(grad_query_parts), head_places, -1.0)
        .astype(jnp.bfloat16)
        .reshape(slot_count, block_rows, head_width)
    )
    grad_q_tok, grad_k_tok, grad_v_tok = (
        lax.all_to_all(grad_queries, "fsdp", split_axis=1, concat_axis=2, tiled=True),
        lax.all_to_all(grad_keys, "fsdp", split_axis=1, concat_axis=2, tiled=True),
        lax.all_to_all(grad_values, "fsdp", split_axis=1, concat_axis=2, tiled=True),
    )
    grad_q_lin = grad_q_tok.reshape(row_count, model_width)
    grad_k_lin = grad_k_tok.reshape(row_count, model_width)
    grad_v_lin = grad_v_tok.reshape(row_count, model_width)
    grad_one = (
        contract(grad_q_lin, weights_all[0])
        + contract(grad_k_lin, weights_all[1])
        + contract(grad_v_lin, weights_all[2])
    )
    gain_one_part = jnp.sum(grad_one * norm_one, 0)
    grad_input = grad_middle + norm_back(
        grad_one, norm_one, root_one, weights_all[7].astype(jnp.float32)
    )
    hidden_width = hidden.shape[1]
    gain_parts = jnp.stack([gain_one_part, gain_two_part], 1)
    wide_cols = (
        lax.all_to_all(grad_q_lin, "fsdp", split_axis=1, concat_axis=0, tiled=True),
        lax.all_to_all(grad_k_lin, "fsdp", split_axis=1, concat_axis=0, tiled=True),
        lax.all_to_all(grad_v_lin, "fsdp", split_axis=1, concat_axis=0, tiled=True),
        lax.all_to_all(grad_branch, "fsdp", split_axis=1, concat_axis=0, tiled=True),
        lax.all_to_all(grad_gate, "fsdp", split_axis=1, concat_axis=0, tiled=True),
        lax.all_to_all(grad_up, "fsdp", split_axis=1, concat_axis=0, tiled=True),
        lax.all_to_all(hidden, "fsdp", split_axis=1, concat_axis=0, tiled=True),
    )
    row_sets = (
        lax.all_gather(attn_input, "fsdp", axis=0, tiled=True),
        lax.all_gather(mixed_flat, "fsdp", axis=0, tiled=True),
        lax.all_gather(mlp_input, "fsdp", axis=0, tiled=True),
        lax.all_gather(upstream, "fsdp", axis=0, tiled=True),
    )
    group_rows = model_width // lax.axis_size("ctx")
    row_cuts = [values for values in row_sets]
    pieces = [
        transpose_product(row_cuts[0], wide_cols[0]),
        transpose_product(row_cuts[0], wide_cols[1]),
        transpose_product(row_cuts[0], wide_cols[2]),
        transpose_product(row_cuts[1], wide_cols[3]),
        transpose_product(row_cuts[2], wide_cols[4]),
        transpose_product(row_cuts[2], wide_cols[5]),
        transpose_product(row_cuts[3], wide_cols[6]),
        gain_parts,
        jnp.zeros((group_rows * lax.axis_size("ctx"), 126), jnp.float32),
    ]
    partial_sums = lax.psum_scatter(
        jnp.concatenate(pieces, 1).astype(jnp.bfloat16), "ctx", scatter_dimension=0, tiled=True
    ).astype(jnp.float32)
    owned = lax.all_to_all(
        partial_sums.astype(jnp.bfloat16), "fsdp", split_axis=0, concat_axis=1, tiled=True
    ).astype(partial_sums.dtype)
    span_width = partial_sums.shape[1]
    owned_rows = owned.shape[0]
    arranged = owned.reshape(owned_rows, fsdp_size, span_width)
    model_part = model_width // fsdp_size
    hidden_part = hidden_width // fsdp_size
    bounds = [
        0,
        model_part,
        2 * model_part,
        3 * model_part,
        4 * model_part,
        4 * model_part + hidden_part,
        4 * model_part + 2 * hidden_part,
        4 * model_part + 3 * hidden_part,
    ]

    def joined_cols(first_col, last_col):
        return arranged[:, :, first_col:last_col].reshape(owned_rows, -1)

    grad_w_query = joined_cols(bounds[0], bounds[1])
    grad_w_key = joined_cols(bounds[1], bounds[2])
    grad_w_value = joined_cols(bounds[2], bounds[3])
    grad_w_out = joined_cols(bounds[3], bounds[4])
    grad_w_gate = joined_cols(bounds[4], bounds[5])
    grad_w_up = joined_cols(bounds[5], bounds[6])
    grad_w_down = joined_cols(bounds[6], bounds[7])
    gain_totals = jnp.sum(arranged[:, :, bounds[7] : bounds[7] + 2], 1)
    grad_gain_attn = gain_totals[:, 0]
    grad_gain_mlp = gain_totals[:, 1]
    grad_tokens = grad_input.reshape(slot_count, share_rows, model_width)
    return (
        result,
        grad_tokens,
        grad_w_query,
        grad_w_key,
        grad_w_value,
        grad_w_out,
        grad_w_gate,
        grad_w_up,
        grad_w_down,
        grad_gain_attn,
        grad_gain_mlp,
    )


def dot_f32(a, b):
    return jnp.dot(a, b, preferred_element_type=jnp.float32)

def load_sequence(order_ref, rows_ref, first, block, stores):
    per_src = rows_ref.shape[2] // block
    def one(slot, carry):
        src = slot // per_src
        lane = pl.multiple_of((slot % per_src) * block, block)
        place = pl.multiple_of(order_ref[slot] * block, block)
        for at, store in stores:
            store(rows_ref[src, at:at + HEAD_DIM, pl.ds(lane, block)], place)
        return carry
    lax.fori_loop(0, rows_ref.shape[0] * per_src, one, 0)

def fwd_kernel(order_ref, qkv_ref, mixed_ref, out_ref, lse_ref, qt, kr, vt, *, block, tile):
    seq = qt.shape[1]
    def put_q(x, place):
        qt[:, pl.ds(place, block)] = x * jnp.bfloat16(HEAD_DIM ** -0.5)
    def put_k(x, place):
        kr[pl.ds(place, block), :] = x.T
    def put_v(x, place):
        vt[:, pl.ds(place, block)] = x
    load_sequence(order_ref, qkv_ref, 0, block, ((0, put_q), (HEAD_DIM, put_k), (2 * HEAD_DIM, put_v)))

    def one_tile(qi, unused):
        q0 = pl.multiple_of(qi * tile, tile)
        q = qt[:, pl.ds(q0, tile)]
        def step(k0, state, masked):
            peak, total, acc = state
            s = dot_f32(kr[pl.ds(k0, tile), :], q)
            if masked:
                s = jnp.where(lax.broadcasted_iota(jnp.int32, s.shape, 0) <= lax.broadcasted_iota(jnp.int32, s.shape, 1), s, MASKED_SCORE)
            new_peak = jnp.maximum(peak, jnp.max(s, 0, keepdims=True))
            p = jnp.exp(s - new_peak)
            alpha = jnp.exp(peak - new_peak)
            total = total * alpha + jnp.sum(p, 0, keepdims=True)
            acc = acc * alpha + dot_f32(vt[:, pl.ds(k0, tile)], p.astype(jnp.bfloat16))
            return new_peak, total, acc
        state = (jnp.full((1, tile), MASKED_SCORE, jnp.float32), jnp.zeros((1, tile), jnp.float32), jnp.zeros((HEAD_DIM, tile), jnp.float32))
        state = lax.fori_loop(0, qi, lambda j, st: step(pl.multiple_of(j * tile, tile), st, False), state)
        peak, total, acc = step(q0, state, True)
        out_ref[:, pl.ds(q0, tile)] = acc / total
        lse_ref[:, pl.ds(q0, tile)] = peak + jnp.log(total)
        return unused
    lax.fori_loop(0, seq // tile, one_tile, 0)

    per_src = mixed_ref.shape[2] // block
    def send(slot, carry):
        place = pl.multiple_of(order_ref[slot] * block, block)
        lane = pl.multiple_of((slot % per_src) * block, block)
        mixed_ref[slot // per_src, :, pl.ds(lane, block)] = out_ref[:, pl.ds(place, block)].astype(jnp.bfloat16)
        return carry
    lax.fori_loop(0, mixed_ref.shape[0] * per_src, send, 0)

def attend(order, qkv, block, tile):
    groups, unused, width = qkv.shape
    seq = groups * width
    vm = pl.BlockSpec(memory_space=pltpu.VMEM)
    return pl.pallas_call(
        functools.partial(fwd_kernel, block=block, tile=tile),
        out_shape=(jax.ShapeDtypeStruct((groups, HEAD_DIM, width), jnp.bfloat16),
                   jax.ShapeDtypeStruct((HEAD_DIM, seq), jnp.float32),
                   jax.ShapeDtypeStruct((1, seq), jnp.float32)),
        in_specs=[pl.BlockSpec(memory_space=pltpu.SMEM), vm],
        out_specs=(vm, vm, vm),
        scratch_shapes=[pltpu.VMEM((HEAD_DIM, seq), jnp.bfloat16), pltpu.VMEM((seq, HEAD_DIM), jnp.bfloat16), pltpu.VMEM((HEAD_DIM, seq), jnp.bfloat16)],
        compiler_params=pltpu.CompilerParams(vmem_limit_bytes=40 << 20),
        name="attend",
    )(order, qkv)

def bwd_kernel(order_ref, qkv_ref, go_ref, out_ref, lse_ref, cos_ref, sin_ref, grad_ref,
               qt, qr, kt, kr, vr, got, gor, delta, dqt, dkr, dvr, *, block, tile):
    seq = qt.shape[1]
    scale = jnp.bfloat16(HEAD_DIM ** -0.5)
    def put_q(x, place):
        x = x * scale
        qt[:, pl.ds(place, block)] = x
        qr[pl.ds(place, block), :] = x.T
    def put_k(x, place):
        kt[:, pl.ds(place, block)] = x * scale
        kr[pl.ds(place, block), :] = x.T
    def put_v(x, place):
        vr[pl.ds(place, block), :] = x.T
    def put_go(x, place):
        got[:, pl.ds(place, block)] = x
        gor[pl.ds(place, block), :] = x.T
        delta[:, pl.ds(place, block)] = jnp.sum(x.astype(jnp.float32) * out_ref[:, pl.ds(place, block)], 0, keepdims=True)
    load_sequence(order_ref, qkv_ref, 0, block, ((0, put_q), (HEAD_DIM, put_k), (2 * HEAD_DIM, put_v)))
    load_sequence(order_ref, go_ref, 0, block, ((0, put_go),))
    dqt[...] = jnp.zeros_like(dqt)
    tiles = seq // tile

    def key_tile(kj, unused):
        k0 = pl.multiple_of(kj * tile, tile)
        keys = kr[pl.ds(k0, tile), :]
        keys_t = kt[:, pl.ds(k0, tile)]
        vals = vr[pl.ds(k0, tile), :]
        dkr[...] = jnp.zeros_like(dkr)
        dvr[...] = jnp.zeros_like(dvr)
        def step(q0, masked):
            s = dot_f32(keys, qt[:, pl.ds(q0, tile)])
            p = jnp.exp(s - lse_ref[:, pl.ds(q0, tile)])
            if masked:
                p = jnp.where(lax.broadcasted_iota(jnp.int32, s.shape, 0) <= lax.broadcasted_iota(jnp.int32, s.shape, 1), p, 0.0)
            dp = dot_f32(vals, got[:, pl.ds(q0, tile)])
            ds = (p * (dp - delta[:, pl.ds(q0, tile)])).astype(jnp.bfloat16)
            dvr[...] += dot_f32(p.astype(jnp.bfloat16), gor[pl.ds(q0, tile), :])
            dkr[...] += dot_f32(ds, qr[pl.ds(q0, tile), :])
            dqt[:, pl.ds(q0, tile)] += dot_f32(keys_t, ds)
        step(k0, True)
        def later(qi, c):
            step(pl.multiple_of(qi * tile, tile), False)
            return c
        lax.fori_loop(kj + 1, tiles, later, 0)
        kt_d = dkr[...].T
        vt_d = dvr[...].T
        put_out(kt_d, HEAD_DIM, k0, True)
        put_out(vt_d, 2 * HEAD_DIM, k0, False)
        return unused

    half = HEAD_DIM // 2
    def put_out(x, at, place, turn):
        for part in range(tile // block):
            piece = x[:, part * block:(part + 1) * block]
            here = place + part * block
            if turn:
                lanes = pl.ds(pl.multiple_of(here, block), block)
                c, s = cos_ref[:, lanes], sin_ref[:, lanes]
                a, b = piece[:half], piece[half:]
                piece = jnp.concatenate([a * c + b * s, b * c - a * s], 0)
            slot = order_ref[seq // block + here // block]
            per_src = grad_ref.shape[2] // block
            lane = pl.multiple_of((slot % per_src) * block, block)
            grad_ref[slot // per_src, at:at + HEAD_DIM, pl.ds(lane, block)] = piece.astype(jnp.bfloat16)

    lax.fori_loop(0, tiles, key_tile, 0)
    def write_q(qi, c):
        q0 = pl.multiple_of(qi * tile, tile)
        put_out(dqt[:, pl.ds(q0, tile)], 0, q0, True)
        return c
    lax.fori_loop(0, tiles, write_q, 0)

def attend_back(order, qkv, go, out, lse, cos, sin, block, tile):
    groups, unused, width = qkv.shape
    seq = groups * width
    vm = pl.BlockSpec(memory_space=pltpu.VMEM)
    bf, f32 = jnp.bfloat16, jnp.float32
    wide = lambda t: pltpu.VMEM((HEAD_DIM, seq), t)
    tall = lambda t: pltpu.VMEM((seq, HEAD_DIM), t)
    return pl.pallas_call(
        functools.partial(bwd_kernel, block=block, tile=tile),
        out_shape=jax.ShapeDtypeStruct(qkv.shape, bf),
        in_specs=[pl.BlockSpec(memory_space=pltpu.SMEM)] + [vm] * 6,
        out_specs=vm,
        scratch_shapes=[wide(bf), tall(bf), wide(bf), tall(bf), tall(bf), wide(bf), tall(bf),
                        pltpu.VMEM((1, seq), f32), wide(f32),
                        pltpu.VMEM((tile, HEAD_DIM), f32), pltpu.VMEM((tile, HEAD_DIM), f32)],
        compiler_params=pltpu.CompilerParams(vmem_limit_bytes=48 << 20),
        name="attend_back",
    )(order, qkv, go, out, lse, cos, sin)


def line_steps(size, step):
    return [(i, i + step) for i in range(size) if 0 <= i + step < size]


def gather_line(share, axis):
    size = lax.axis_size(axis)
    ups, downs = [share], [share]
    for hop in range(1, size):
        ups.append(lax.ppermute(ups[-1], axis, line_steps(size, 1)[hop - 1 :]))
        downs.append(lax.ppermute(downs[-1], axis, line_steps(size, -1)[: size - hop]))
    window = jnp.stack(ups[:0:-1] + downs)
    return lax.dynamic_slice_in_dim(window, size - 1 - lax.axis_index(axis), size, 0)


def gather_rows(share):
    slots, rows, width = share.shape
    return jnp.swapaxes(gather_line(share, "fsdp"), 0, 1).reshape(-1, width)


def scatter_rows(partial, slots):
    size = lax.axis_size("fsdp")
    width = partial.shape[1]
    parts = partial.astype(jnp.bfloat16).reshape(slots, size, -1, width)
    parts = lax.all_to_all(parts, "fsdp", split_axis=1, concat_axis=1, tiled=True)
    return jnp.sum(parts.astype(jnp.float32), 1).reshape(-1, width)


def gather_columns(shards):
    ctx_size, line = lax.axis_size("ctx"), lax.axis_size("fsdp")
    rows = shards[0].shape[0] // ctx_size
    first = lax.axis_index("ctx") * rows
    cuts = jnp.stack([lax.dynamic_slice_in_dim(w, first, rows, 0) for w in shards])
    cuts = cuts.reshape(len(shards), rows, line, -1)
    cuts = jnp.transpose(cuts, (2, 0, 1, 3))
    mine = lax.all_to_all(cuts, "fsdp", split_axis=0, concat_axis=0, tiled=True)
    whole = lax.all_gather(jnp.swapaxes(mine, 0, 1), "ctx", axis=2, tiled=True)
    return whole.reshape(len(shards), -1, whole.shape[-1])


def return_columns(grads):
    line = lax.axis_size("fsdp")
    summed = lax.psum_scatter(grads, "ctx", scatter_dimension=1, tiled=True)
    count, rows, width = summed.shape
    cuts = jnp.swapaxes(summed.reshape(count, line, rows // line, width), 0, 1)
    mine = lax.all_to_all(cuts, "fsdp", split_axis=0, concat_axis=0, tiled=True)
    mine = jnp.transpose(mine, (1, 2, 0, 3)).reshape(count, rows // line, line * width)
    return [mine[i].astype(jnp.float32) for i in range(count)]


def turn_features(values, cosine, sine):
    leading, trailing = jnp.split(values, 2, 1)
    return jnp.concatenate(
        [leading * cosine - trailing * sine, trailing * cosine + leading * sine], 1
    )


def head_device(
    tokens,
    block_order,
    w_query,
    w_key,
    w_value,
    w_out,
    w_gate,
    w_up,
    w_down,
    gain_attn,
    gain_mlp,
    cotangent,
):
    slots, share_rows, model_width = tokens.shape
    ctx_size, line = lax.axis_size("ctx"), lax.axis_size("fsdp")
    block_rows = share_rows * line
    head_width = model_width // line
    group_rows = slots * block_rows
    row_count = slots * share_rows
    bf, f32 = jnp.bfloat16, jnp.float32
    order = block_order.astype(jnp.int32)
    order_both = jnp.concatenate([order, jnp.argsort(order).astype(jnp.int32)])

    gains = gather_line(jnp.stack([gain_attn, gain_mlp]), "fsdp")
    gains = jnp.swapaxes(gains, 0, 1).reshape(2, model_width).astype(f32)
    attn_gain, mlp_gain = gains[0], gains[1]

    stream = tokens.reshape(row_count, model_width).astype(f32)
    root_one = lax.rsqrt(jnp.mean(stream * stream, -1, keepdims=True) + EPSILON)
    norm_one = stream * root_one
    attn_input = (norm_one * attn_gain).astype(bf)
    attn_rows = gather_rows(attn_input.reshape(slots, share_rows, model_width))

    w_heads = gather_columns([w_query, w_key, w_value])
    w_mlp = gather_columns([w_down, w_gate, w_up])
    upstream_rows = gather_rows(cotangent)

    half = HEAD_DIM // 2
    frequency = 1.0 / ROPE_BASE ** (jnp.arange(half, dtype=f32) * (2.0 / HEAD_DIM))
    places = jnp.arange(group_rows * ctx_size, dtype=jnp.int32).astype(f32)
    angles = frequency[:, None] * places[None, :]
    cosine, sine = jnp.cos(angles), jnp.sin(angles)
    own_blocks = [order[slots * lax.axis_index("ctx") + i] for i in range(slots)]

    def own_columns(table):
        return jnp.concatenate(
            [
                lax.dynamic_slice_in_dim(table, block * block_rows, block_rows, 1)
                for block in own_blocks
            ],
            1,
        )

    own_cosine, own_sine = own_columns(cosine), own_columns(sine)

    linear = [
        lax.dot_general(
            weight, attn_rows, (((0,), (1,)), ((), ())), preferred_element_type=f32
        ).reshape(ctx_size, HEAD_DIM, group_rows)
        for weight in w_heads
    ]
    heads_out = jnp.concatenate(
        [
            turn_features(linear[0], own_cosine, own_sine).astype(bf),
            turn_features(linear[1], own_cosine, own_sine).astype(bf),
            linear[2].astype(bf),
        ],
        1,
    )
    head_rows = lax.all_to_all(heads_out, "ctx", split_axis=0, concat_axis=0, tiled=True)
    mixed_send, attended, log_total = attend(order, head_rows, block_rows, 2 * block_rows)
    mixed = lax.all_to_all(mixed_send, "ctx", split_axis=0, concat_axis=0, tiled=True)
    mixed = mixed.reshape(head_width, group_rows)
    middle = stream + scatter_rows(transpose_product(mixed, w_out), slots)

    root_two = lax.rsqrt(jnp.mean(middle * middle, -1, keepdims=True) + EPSILON)
    norm_two = middle * root_two
    mlp_input = (norm_two * mlp_gain).astype(bf)
    mlp_rows = gather_rows(mlp_input.reshape(slots, share_rows, model_width))

    down, gate, up = w_mlp[0], w_mlp[1], w_mlp[2]
    grad_hidden = matmul(upstream_rows, down)
    gate_act = matmul(mlp_rows, gate)
    upward = matmul(mlp_rows, up)
    gate_sigmoid = jax.nn.sigmoid(gate_act)
    gate_silu = gate_act * gate_sigmoid
    hidden = (gate_silu * upward).astype(bf)
    grad_gate = (
        grad_hidden * upward * gate_sigmoid * (1.0 + gate_act * (1.0 - gate_sigmoid))
    ).astype(bf)
    grad_up = (grad_hidden * gate_silu).astype(bf)
    grad_two = scatter_rows(contract(grad_gate, gate) + contract(grad_up, up), slots)
    output = middle + scatter_rows(contract(hidden, down), slots)
    result = output.astype(bf).reshape(slots, share_rows, model_width)
    mlp_grads = jnp.stack(
        [
            transpose_product(mlp_rows, grad_gate).astype(bf),
            transpose_product(mlp_rows, grad_up).astype(bf),
            transpose_product(upstream_rows, hidden).astype(bf),
        ]
    )
    grad_w_gate, grad_w_up, grad_w_down = return_columns(mlp_grads)

    gain_two_part = jnp.sum(grad_two * norm_two, 0)
    upstream = cotangent.reshape(row_count, model_width).astype(f32)
    grad_middle = upstream + norm_back(grad_two, norm_two, root_two, mlp_gain)
    grad_branch = grad_middle.astype(bf)
    branch_rows = gather_rows(grad_branch.reshape(slots, share_rows, model_width))
    grad_mixed = contract(w_out, branch_rows).astype(bf).reshape(ctx_size, HEAD_DIM, group_rows)
    grad_heads = lax.all_to_all(grad_mixed, "ctx", split_axis=0, concat_axis=0, tiled=True)
    head_grads = attend_back(
        order_both,
        head_rows,
        grad_heads,
        attended,
        log_total,
        cosine,
        sine,
        block_rows,
        2 * block_rows,
    )
    lin_grads = lax.all_to_all(head_grads, "ctx", split_axis=0, concat_axis=0, tiled=True)
    lin_grads = jnp.swapaxes(lin_grads.reshape(ctx_size, 3, HEAD_DIM, group_rows), 0, 1)
    lin_grads = lin_grads.reshape(3, head_width, group_rows)

    partial_one = sum(
        lax.dot_general(
            lin_grads[i], w_heads[i], (((0,), (1,)), ((), ())), preferred_element_type=f32
        )
        for i in range(3)
    )
    grad_one = scatter_rows(partial_one, slots)
    gain_one_part = jnp.sum(grad_one * norm_one, 0)
    grad_input = grad_middle + norm_back(grad_one, norm_one, root_one, attn_gain)
    grad_tokens = grad_input.reshape(slots, share_rows, model_width)

    head_weight_grads = jnp.stack(
        [
            lax.dot_general(
                attn_rows, lin_grads[i], (((0,), (1,)), ((), ())), preferred_element_type=f32
            ).astype(bf)
            for i in range(3)
        ]
    )
    grad_w_query, grad_w_key, grad_w_value = return_columns(head_weight_grads)

    out_rows = lax.psum_scatter(
        matmul(mixed, branch_rows).astype(bf), "ctx", scatter_dimension=0, tiled=True
    )
    owners = [
        (c * line + f, f * ctx_size + c) for c in range(ctx_size) for f in range(line)
    ]
    grad_w_out = lax.ppermute(out_rows, ("ctx", "fsdp"), owners).astype(f32)

    gain_parts = jnp.stack([gain_one_part, gain_two_part]).reshape(2, ctx_size * line, -1)
    gain_parts = lax.all_to_all(
        jnp.swapaxes(gain_parts, 0, 1).reshape(ctx_size * line, -1),
        ("ctx", "fsdp"),
        split_axis=0,
        concat_axis=0,
        tiled=True,
    )
    gain_grads = jnp.sum(gain_parts, 0).reshape(2, -1)
    return (
        result,
        grad_tokens,
        grad_w_query,
        grad_w_key,
        grad_w_value,
        grad_w_out,
        grad_w_gate,
        grad_w_up,
        grad_w_down,
        gain_grads[0],
        gain_grads[1],
    )


def layer_step(*arrays):
    heads_here = arrays[0].shape[-1] // lax.axis_size("fsdp") // HEAD_DIM
    if heads_here == lax.axis_size("ctx"):
        return head_device(*arrays)
    return per_device(*arrays)


def solution(mesh):
    in_specs = (
        P("ctx", "fsdp", None),
        P(),
        P("fsdp", None),
        P("fsdp", None),
        P("fsdp", None),
        P("fsdp", None),
        P("fsdp", None),
        P("fsdp", None),
        P("fsdp", None),
        P("fsdp"),
        P("fsdp"),
        P("ctx", "fsdp", None),
    )
    out_specs = (
        P("ctx", "fsdp", None),
        P("ctx", "fsdp", None),
        P(("ctx", "fsdp"), None),
        P(("ctx", "fsdp"), None),
        P(("ctx", "fsdp"), None),
        P(("ctx", "fsdp"), None),
        P(("ctx", "fsdp"), None),
        P(("ctx", "fsdp"), None),
        P(("ctx", "fsdp"), None),
        P(("ctx", "fsdp")),
        P(("ctx", "fsdp")),
    )
    return jax.shard_map(
        layer_step, mesh=mesh, in_specs=in_specs, out_specs=out_specs, check_vma=False
    )
```

```python
import functools

import jax
import jax.numpy as jnp
from jax import lax
from jax.experimental import pallas as pl
from jax.experimental.pallas import tpu as pltpu
from jax.sharding import PartitionSpec as P

HEAD_DIM = 64


EPSILON = 1e-05
ROPE_BASE = 130000.0
MASKED_SCORE = -1e30


def rotate(values, places, direction):
    half_dim = values.shape[-1] // 2
    frequency = 1.0 / ROPE_BASE ** (
        jnp.arange(half_dim, dtype=jnp.float32) * (2.0 / values.shape[-1])
    )
    angles = places[..., None] * frequency
    cosine = jnp.cos(angles)[..., None, :]
    sine_part = direction * jnp.sin(angles)[..., None, :]
    leading = values[..., :half_dim]
    trailing = values[..., half_dim:]
    return jnp.concatenate(
        [leading * cosine - trailing * sine_part, trailing * cosine + leading * sine_part], -1
    )


def matmul(left, right):
    return jnp.dot(left, right, preferred_element_type=jnp.float32)


def contract(left, right):
    return lax.dot_general(
        left, right, (((1,), (1,)), ((), ())), preferred_element_type=jnp.float32
    )


def transpose_product(left, right):
    return lax.dot_general(
        left, right, (((0,), (0,)), ((), ())), preferred_element_type=jnp.float32
    )


def split_heads(values):
    return values.reshape(values.shape[:-1] + (-1, HEAD_DIM))


def keep_state(current):
    return current


def tile_scores(queries, key_rows, query_places, key_places, score_scale):
    scores = (
        jnp.einsum("qhd,khd->hqk", queries, key_rows, preferred_element_type=jnp.float32)
        * score_scale
    )
    allowed = (key_places[None, :] <= query_places[:, None])[None]
    return (jnp.where(allowed, scores, MASKED_SCORE), allowed)


def grow_state(current, queries, key_rows, value_rows, query_places, key_places, score_scale):
    run_peak, run_total, summed = current
    scores, allowed = tile_scores(queries, key_rows, query_places, key_places, score_scale)
    new_peak = jnp.maximum(run_peak, jnp.max(scores, -1))
    weights = jnp.where(allowed, jnp.exp(scores - new_peak[..., None]), 0.0)
    factor = jnp.exp(run_peak - new_peak)
    run_total = run_total * factor + jnp.sum(weights, -1)
    summed = summed * jnp.transpose(factor)[:, :, None] + jnp.einsum(
        "hqk,khd->qhd", weights.astype(jnp.bfloat16), value_rows, preferred_element_type=jnp.float32
    )
    return (new_peak, run_total, summed)


def backward_tile(
    queries,
    key_rows,
    value_rows,
    grad_out,
    log_total,
    row_delta,
    query_places,
    key_places,
    score_scale,
):
    scores, allowed = tile_scores(queries, key_rows, query_places, key_places, score_scale)
    probabilities = jnp.where(allowed, jnp.exp(scores - log_total[..., None]), 0.0)
    grad_probs = jnp.einsum(
        "qhd,khd->hqk", grad_out, value_rows, preferred_element_type=jnp.float32
    )
    grad_scores = (probabilities * (grad_probs - row_delta[..., None])).astype(jnp.bfloat16)
    return (probabilities, grad_scores)


def norm_back(grad_normed_in, normed_values, inverse_root, gain_vector):
    scaled = grad_normed_in * gain_vector
    return inverse_root * (
        scaled - normed_values * jnp.mean(scaled * normed_values, -1, keepdims=True)
    )


def per_device(
    tokens,
    block_order,
    w_query,
    w_key,
    w_value,
    w_out,
    w_gate,
    w_up,
    w_down,
    gain_attn,
    gain_mlp,
    cotangent,
):
    slot_count, share_rows, model_width = tokens.shape
    fsdp_size = lax.axis_size("fsdp")
    block_rows = share_rows * fsdp_size
    head_width = model_width // fsdp_size
    heads_here = head_width // HEAD_DIM
    row_count = slot_count * share_rows
    score_scale = HEAD_DIM ** (-0.5)
    own_slots = 2 * lax.axis_index("ctx") + jnp.arange(2, dtype=jnp.int32)
    own_blocks = block_order[own_slots]
    token_places = (
        (
            own_blocks[:, None] * block_rows
            + lax.axis_index("fsdp") * share_rows
            + jnp.arange(share_rows, dtype=jnp.int32)[None, :]
        )
        .astype(jnp.float32)
        .reshape(row_count)
    )
    head_places = (
        own_blocks[:, None] * block_rows + jnp.arange(block_rows, dtype=jnp.int32)[None, :]
    ).astype(jnp.float32)
    params = (w_query, w_key, w_value, w_out, w_gate, w_up, w_down, gain_attn, gain_mlp)
    weights_all = (
        lax.all_gather(params[0], "fsdp", axis=0, tiled=True),
        lax.all_gather(params[1], "fsdp", axis=0, tiled=True),
        lax.all_gather(params[2], "fsdp", axis=0, tiled=True),
        lax.all_gather(params[3], "fsdp", axis=0, tiled=True),
        lax.all_gather(params[4], "fsdp", axis=0, tiled=True),
        lax.all_gather(params[5], "fsdp", axis=0, tiled=True),
        lax.all_gather(params[6], "fsdp", axis=0, tiled=True),
        lax.all_gather(params[7], "fsdp", axis=0, tiled=True),
        lax.all_gather(params[8], "fsdp", axis=0, tiled=True),
    )
    stream = tokens.reshape(row_count, model_width).astype(jnp.float32)
    root_one = lax.rsqrt(jnp.mean(stream * stream, -1, keepdims=True) + EPSILON)
    norm_one = stream * root_one
    attn_input = (norm_one * weights_all[7].astype(jnp.float32)).astype(jnp.bfloat16)

    def project_turn(weight):
        linear = matmul(attn_input, weight).reshape(row_count, -1, HEAD_DIM)
        return (
            rotate(linear, token_places, 1.0)
            .astype(jnp.bfloat16)
            .reshape(slot_count, share_rows, model_width)
        )

    query_tok = project_turn(weights_all[0])
    key_tok = project_turn(weights_all[1])
    value_tok = (
        matmul(attn_input, weights_all[2])
        .astype(jnp.bfloat16)
        .reshape(slot_count, share_rows, model_width)
    )
    query_heads, key_heads, value_heads = (
        lax.all_to_all(query_tok, "fsdp", split_axis=2, concat_axis=1, tiled=True),
        lax.all_to_all(key_tok, "fsdp", split_axis=2, concat_axis=1, tiled=True),
        lax.all_to_all(value_tok, "fsdp", split_axis=2, concat_axis=1, tiled=True),
    )
    query_split = split_heads(query_heads)
    start_state = tuple(
        (
            (
                jnp.full((heads_here, block_rows), MASKED_SCORE, jnp.float32),
                jnp.zeros((heads_here, block_rows), jnp.float32),
                jnp.zeros((block_rows, heads_here, HEAD_DIM), jnp.float32),
            )
            for which_slot in range(2)
        )
    )
    carried = start_state
    key_part = lax.all_gather(key_heads, "ctx", axis=0, tiled=True)
    value_part = lax.all_gather(value_heads, "ctx", axis=0, tiled=True)

    def visit_slot(inner_state, element):
        key_one, value_one, offset = element
        key_block = block_order[offset]
        key_places = (key_block * block_rows + jnp.arange(block_rows, dtype=jnp.int32)).astype(
            jnp.float32
        )
        key_split = split_heads(key_one)
        value_split = split_heads(value_one)
        updated = []
        for which_slot in range(2):

            def grow_one(current, which_slot=which_slot):
                return grow_state(
                    current,
                    query_split[which_slot],
                    key_split,
                    value_split,
                    head_places[which_slot],
                    key_places,
                    score_scale,
                )

            updated.append(
                lax.cond(
                    key_block <= own_blocks[which_slot],
                    grow_one,
                    keep_state,
                    inner_state[which_slot],
                )
            )
        return (tuple(updated), None)

    offsets = jnp.arange(key_part.shape[0], dtype=jnp.int32)
    carried, unused = lax.scan(visit_slot, carried, (key_part, value_part, offsets))
    attended_parts = []
    log_parts = []
    for which_slot in range(2):
        run_peak, run_total, summed = carried[which_slot]
        log_parts.append(run_peak + jnp.log(run_total))
        attended_parts.append(summed / jnp.transpose(run_total)[:, :, None])
    attended = jnp.stack(attended_parts)
    log_total = jnp.stack(log_parts)
    mixed_send = attended.reshape(slot_count, block_rows, head_width).astype(jnp.bfloat16)
    mixed_tok = lax.all_to_all(mixed_send, "fsdp", split_axis=1, concat_axis=2, tiled=True)
    mixed_flat = mixed_tok.reshape(row_count, model_width)
    middle = stream + matmul(mixed_flat, weights_all[3])
    root_two = lax.rsqrt(jnp.mean(middle * middle, -1, keepdims=True) + EPSILON)
    norm_two = middle * root_two
    mlp_input = (norm_two * weights_all[8].astype(jnp.float32)).astype(jnp.bfloat16)
    gate_act = matmul(mlp_input, weights_all[4])
    upward = matmul(mlp_input, weights_all[5])
    gate_sigmoid = jax.nn.sigmoid(gate_act)
    gate_silu = gate_act * gate_sigmoid
    hidden = (gate_silu * upward).astype(jnp.bfloat16)
    output = middle + contract(hidden, weights_all[6])
    result = output.astype(jnp.bfloat16).reshape(slot_count, share_rows, model_width)
    upstream = cotangent.reshape(row_count, model_width)
    grad_hidden = matmul(upstream, weights_all[6])
    grad_gate = (
        grad_hidden * upward * gate_sigmoid * (1.0 + gate_act * (1.0 - gate_sigmoid))
    ).astype(jnp.bfloat16)
    grad_up = (grad_hidden * gate_silu).astype(jnp.bfloat16)
    grad_two = contract(grad_gate, weights_all[4]) + contract(grad_up, weights_all[5])
    gain_two_part = jnp.sum(grad_two * norm_two, 0)
    grad_middle = upstream.astype(jnp.float32) + norm_back(
        grad_two, norm_two, root_two, weights_all[8].astype(jnp.float32)
    )
    grad_branch = grad_middle.astype(jnp.bfloat16)
    grad_mixed = (
        contract(grad_branch, weights_all[3])
        .astype(jnp.bfloat16)
        .reshape(slot_count, share_rows, model_width)
    )
    grad_heads = lax.all_to_all(grad_mixed, "fsdp", split_axis=2, concat_axis=1, tiled=True)
    grad_split = split_heads(grad_heads)
    row_delta = jnp.transpose(jnp.sum(grad_split.astype(jnp.float32) * attended, -1), (0, 2, 1))
    gathered = (
        lax.all_gather(key_heads, "ctx", axis=0, tiled=True),
        lax.all_gather(value_heads, "ctx", axis=0, tiled=True),
    )
    key_all, value_all = gathered
    total_slots = key_all.shape[0]

    def query_visit(current, element):
        key_pair, value_pair, pair_index = element
        updated = list(current)
        for member in range(2):
            key_block = block_order[2 * pair_index + member]
            key_places = (key_block * block_rows + jnp.arange(block_rows, dtype=jnp.int32)).astype(
                jnp.float32
            )
            key_split = split_heads(key_pair[member])
            value_split = split_heads(value_pair[member])
            for which_slot in range(2):

                def take_query(
                    accum,
                    which_slot=which_slot,
                    key_split=key_split,
                    value_split=value_split,
                    key_places=key_places,
                ):
                    probabilities, grad_scores = backward_tile(
                        query_split[which_slot],
                        key_split,
                        value_split,
                        grad_split[which_slot],
                        log_total[which_slot],
                        row_delta[which_slot],
                        head_places[which_slot],
                        key_places,
                        score_scale,
                    )
                    return accum + score_scale * jnp.einsum(
                        "hqk,khd->qhd", grad_scores, key_split, preferred_element_type=jnp.float32
                    )

                updated[which_slot] = lax.cond(
                    key_block <= own_blocks[which_slot], take_query, keep_state, updated[which_slot]
                )
        return (tuple(updated), None)

    query_zero = jnp.zeros((block_rows, heads_here, HEAD_DIM), jnp.float32)
    pair_keys = key_all.reshape(total_slots // 2, 2, block_rows, head_width)
    pair_values = value_all.reshape(total_slots // 2, 2, block_rows, head_width)
    grad_query_parts, unused = lax.scan(
        query_visit,
        (query_zero, query_zero),
        (pair_keys, pair_values, jnp.arange(total_slots // 2, dtype=jnp.int32)),
    )
    key_part = key_all
    value_part = value_all

    def key_visit(unused_carry, element):
        key_one, value_one, offset = element
        key_block = block_order[offset]
        key_places = (key_block * block_rows + jnp.arange(block_rows, dtype=jnp.int32)).astype(
            jnp.float32
        )
        key_split = split_heads(key_one)
        value_split = split_heads(value_one)
        sums = (
            jnp.zeros((block_rows, heads_here, HEAD_DIM), jnp.float32),
            jnp.zeros((block_rows, heads_here, HEAD_DIM), jnp.float32),
        )
        for which_slot in range(2):

            def take_keys(current, which_slot=which_slot):
                probabilities, grad_scores = backward_tile(
                    query_split[which_slot],
                    key_split,
                    value_split,
                    grad_split[which_slot],
                    log_total[which_slot],
                    row_delta[which_slot],
                    head_places[which_slot],
                    key_places,
                    score_scale,
                )
                grad_key = current[0] + score_scale * jnp.einsum(
                    "hqk,qhd->khd",
                    grad_scores,
                    query_split[which_slot],
                    preferred_element_type=jnp.float32,
                )
                grad_value = current[1] + jnp.einsum(
                    "hqk,qhd->khd",
                    probabilities.astype(jnp.bfloat16),
                    grad_split[which_slot],
                    preferred_element_type=jnp.float32,
                )
                return (grad_key, grad_value)

            sums = lax.cond(key_block <= own_blocks[which_slot], take_keys, keep_state, sums)
        joined = jnp.concatenate(
            [sums[0].reshape(block_rows, head_width), sums[1].reshape(block_rows, head_width)], -1
        )
        return (unused_carry, joined)

    unused_final, terms = lax.scan(
        key_visit,
        jnp.zeros((), jnp.float32),
        (key_part, value_part, jnp.arange(slot_count * lax.axis_size("ctx"), dtype=jnp.int32)),
    )
    summed_kv = lax.psum_scatter(
        terms.astype(jnp.bfloat16), "ctx", scatter_dimension=0, tiled=True
    ).astype(jnp.float32)
    grad_keys = (
        rotate(split_heads(summed_kv[..., :head_width]), head_places, -1.0)
        .astype(jnp.bfloat16)
        .reshape(slot_count, block_rows, head_width)
    )
    grad_values = summed_kv[..., head_width:].astype(jnp.bfloat16)
    grad_queries = (
        rotate(jnp.stack(grad_query_parts), head_places, -1.0)
        .astype(jnp.bfloat16)
        .reshape(slot_count, block_rows, head_width)
    )
    grad_q_tok, grad_k_tok, grad_v_tok = (
        lax.all_to_all(grad_queries, "fsdp", split_axis=1, concat_axis=2, tiled=True),
        lax.all_to_all(grad_keys, "fsdp", split_axis=1, concat_axis=2, tiled=True),
        lax.all_to_all(grad_values, "fsdp", split_axis=1, concat_axis=2, tiled=True),
    )
    grad_q_lin = grad_q_tok.reshape(row_count, model_width)
    grad_k_lin = grad_k_tok.reshape(row_count, model_width)
    grad_v_lin = grad_v_tok.reshape(row_count, model_width)
    grad_one = (
        contract(grad_q_lin, weights_all[0])
        + contract(grad_k_lin, weights_all[1])
        + contract(grad_v_lin, weights_all[2])
    )
    gain_one_part = jnp.sum(grad_one * norm_one, 0)
    grad_input = grad_middle + norm_back(
        grad_one, norm_one, root_one, weights_all[7].astype(jnp.float32)
    )
    hidden_width = hidden.shape[1]
    gain_parts = jnp.stack([gain_one_part, gain_two_part], 1)
    wide_cols = (
        lax.all_to_all(grad_q_lin, "fsdp", split_axis=1, concat_axis=0, tiled=True),
        lax.all_to_all(grad_k_lin, "fsdp", split_axis=1, concat_axis=0, tiled=True),
        lax.all_to_all(grad_v_lin, "fsdp", split_axis=1, concat_axis=0, tiled=True),
        lax.all_to_all(grad_branch, "fsdp", split_axis=1, concat_axis=0, tiled=True),
        lax.all_to_all(grad_gate, "fsdp", split_axis=1, concat_axis=0, tiled=True),
        lax.all_to_all(grad_up, "fsdp", split_axis=1, concat_axis=0, tiled=True),
        lax.all_to_all(hidden, "fsdp", split_axis=1, concat_axis=0, tiled=True),
    )
    row_sets = (
        lax.all_gather(attn_input, "fsdp", axis=0, tiled=True),
        lax.all_gather(mixed_flat, "fsdp", axis=0, tiled=True),
        lax.all_gather(mlp_input, "fsdp", axis=0, tiled=True),
        lax.all_gather(upstream, "fsdp", axis=0, tiled=True),
    )
    group_rows = model_width // lax.axis_size("ctx")
    row_cuts = [values for values in row_sets]
    pieces = [
        transpose_product(row_cuts[0], wide_cols[0]),
        transpose_product(row_cuts[0], wide_cols[1]),
        transpose_product(row_cuts[0], wide_cols[2]),
        transpose_product(row_cuts[1], wide_cols[3]),
        transpose_product(row_cuts[2], wide_cols[4]),
        transpose_product(row_cuts[2], wide_cols[5]),
        transpose_product(row_cuts[3], wide_cols[6]),
        gain_parts,
        jnp.zeros((group_rows * lax.axis_size("ctx"), 126), jnp.float32),
    ]
    partial_sums = lax.psum_scatter(
        jnp.concatenate(pieces, 1).astype(jnp.bfloat16), "ctx", scatter_dimension=0, tiled=True
    ).astype(jnp.float32)
    owned = lax.all_to_all(
        partial_sums.astype(jnp.bfloat16), "fsdp", split_axis=0, concat_axis=1, tiled=True
    ).astype(partial_sums.dtype)
    span_width = partial_sums.shape[1]
    owned_rows = owned.shape[0]
    arranged = owned.reshape(owned_rows, fsdp_size, span_width)
    model_part = model_width // fsdp_size
    hidden_part = hidden_width // fsdp_size
    bounds = [
        0,
        model_part,
        2 * model_part,
        3 * model_part,
        4 * model_part,
        4 * model_part + hidden_part,
        4 * model_part + 2 * hidden_part,
        4 * model_part + 3 * hidden_part,
    ]

    def joined_cols(first_col, last_col):
        return arranged[:, :, first_col:last_col].reshape(owned_rows, -1)

    grad_w_query = joined_cols(bounds[0], bounds[1])
    grad_w_key = joined_cols(bounds[1], bounds[2])
    grad_w_value = joined_cols(bounds[2], bounds[3])
    grad_w_out = joined_cols(bounds[3], bounds[4])
    grad_w_gate = joined_cols(bounds[4], bounds[5])
    grad_w_up = joined_cols(bounds[5], bounds[6])
    grad_w_down = joined_cols(bounds[6], bounds[7])
    gain_totals = jnp.sum(arranged[:, :, bounds[7] : bounds[7] + 2], 1)
    grad_gain_attn = gain_totals[:, 0]
    grad_gain_mlp = gain_totals[:, 1]
    grad_tokens = grad_input.reshape(slot_count, share_rows, model_width)
    return (
        result,
        grad_tokens,
        grad_w_query,
        grad_w_key,
        grad_w_value,
        grad_w_out,
        grad_w_gate,
        grad_w_up,
        grad_w_down,
        grad_gain_attn,
        grad_gain_mlp,
    )


def dot_f32(a, b):
    return jnp.dot(a, b, preferred_element_type=jnp.float32)

def load_sequence(order_ref, rows_ref, first, block, stores):
    per_src = rows_ref.shape[2] // block
    def one(slot, carry):
        src = slot // per_src
        lane = pl.multiple_of((slot % per_src) * block, block)
        place = pl.multiple_of(order_ref[slot] * block, block)
        for at, store in stores:
            store(rows_ref[src, at:at + HEAD_DIM, pl.ds(lane, block)], place)
        return carry
    lax.fori_loop(0, rows_ref.shape[0] * per_src, one, 0)

def fwd_kernel(order_ref, qkv_ref, mixed_ref, out_ref, lse_ref, qt, kr, vt, *, block, tile):
    seq = qt.shape[1]
    def put_q(x, place):
        qt[:, pl.ds(place, block)] = x * jnp.bfloat16(HEAD_DIM ** -0.5)
    def put_k(x, place):
        kr[pl.ds(place, block), :] = x.T
    def put_v(x, place):
        vt[:, pl.ds(place, block)] = x
    load_sequence(order_ref, qkv_ref, 0, block, ((0, put_q), (HEAD_DIM, put_k), (2 * HEAD_DIM, put_v)))

    def one_tile(qi, unused):
        q0 = pl.multiple_of(qi * tile, tile)
        q = qt[:, pl.ds(q0, tile)]
        def step(k0, state, masked):
            peak, total, acc = state
            s = dot_f32(kr[pl.ds(k0, tile), :], q)
            if masked:
                s = jnp.where(lax.broadcasted_iota(jnp.int32, s.shape, 0) <= lax.broadcasted_iota(jnp.int32, s.shape, 1), s, MASKED_SCORE)
            new_peak = jnp.maximum(peak, jnp.max(s, 0, keepdims=True))
            p = jnp.exp(s - new_peak)
            alpha = jnp.exp(peak - new_peak)
            total = total * alpha + jnp.sum(p, 0, keepdims=True)
            acc = acc * alpha + dot_f32(vt[:, pl.ds(k0, tile)], p.astype(jnp.bfloat16))
            return new_peak, total, acc
        state = (jnp.full((1, tile), MASKED_SCORE, jnp.float32), jnp.zeros((1, tile), jnp.float32), jnp.zeros((HEAD_DIM, tile), jnp.float32))
        state = lax.fori_loop(0, qi, lambda j, st: step(pl.multiple_of(j * tile, tile), st, False), state)
        peak, total, acc = step(q0, state, True)
        out_ref[:, pl.ds(q0, tile)] = acc / total
        lse_ref[:, pl.ds(q0, tile)] = peak + jnp.log(total)
        return unused
    lax.fori_loop(0, seq // tile, one_tile, 0)

    per_src = mixed_ref.shape[2] // block
    def send(slot, carry):
        place = pl.multiple_of(order_ref[slot] * block, block)
        lane = pl.multiple_of((slot % per_src) * block, block)
        mixed_ref[slot // per_src, :, pl.ds(lane, block)] = out_ref[:, pl.ds(place, block)].astype(jnp.bfloat16)
        return carry
    lax.fori_loop(0, mixed_ref.shape[0] * per_src, send, 0)

def attend(order, qkv, block, tile):
    groups, unused, width = qkv.shape
    seq = groups * width
    vm = pl.BlockSpec(memory_space=pltpu.VMEM)
    return pl.pallas_call(
        functools.partial(fwd_kernel, block=block, tile=tile),
        out_shape=(jax.ShapeDtypeStruct((groups, HEAD_DIM, width), jnp.bfloat16),
                   jax.ShapeDtypeStruct((HEAD_DIM, seq), jnp.float32),
                   jax.ShapeDtypeStruct((1, seq), jnp.float32)),
        in_specs=[pl.BlockSpec(memory_space=pltpu.SMEM), vm],
        out_specs=(vm, vm, vm),
        scratch_shapes=[pltpu.VMEM((HEAD_DIM, seq), jnp.bfloat16), pltpu.VMEM((seq, HEAD_DIM), jnp.bfloat16), pltpu.VMEM((HEAD_DIM, seq), jnp.bfloat16)],
        compiler_params=pltpu.CompilerParams(vmem_limit_bytes=40 << 20),
        name="attend",
    )(order, qkv)

def bwd_kernel(order_ref, qkv_ref, go_ref, out_ref, lse_ref, cos_ref, sin_ref, grad_ref,
               qt, qr, kt, kr, vr, got, gor, delta, dqt, dkr, dvr, *, block, tile):
    seq = qt.shape[1]
    scale = jnp.bfloat16(HEAD_DIM ** -0.5)
    def put_q(x, place):
        x = x * scale
        qt[:, pl.ds(place, block)] = x
        qr[pl.ds(place, block), :] = x.T
    def put_k(x, place):
        kt[:, pl.ds(place, block)] = x * scale
        kr[pl.ds(place, block), :] = x.T
    def put_v(x, place):
        vr[pl.ds(place, block), :] = x.T
    def put_go(x, place):
        got[:, pl.ds(place, block)] = x
        gor[pl.ds(place, block), :] = x.T
        delta[:, pl.ds(place, block)] = jnp.sum(x.astype(jnp.float32) * out_ref[:, pl.ds(place, block)], 0, keepdims=True)
    load_sequence(order_ref, qkv_ref, 0, block, ((0, put_q), (HEAD_DIM, put_k), (2 * HEAD_DIM, put_v)))
    load_sequence(order_ref, go_ref, 0, block, ((0, put_go),))
    dqt[...] = jnp.zeros_like(dqt)
    tiles = seq // tile

    def key_tile(kj, unused):
        k0 = pl.multiple_of(kj * tile, tile)
        keys = kr[pl.ds(k0, tile), :]
        keys_t = kt[:, pl.ds(k0, tile)]
        vals = vr[pl.ds(k0, tile), :]
        dkr[...] = jnp.zeros_like(dkr)
        dvr[...] = jnp.zeros_like(dvr)
        def step(q0, masked):
            s = dot_f32(keys, qt[:, pl.ds(q0, tile)])
            p = jnp.exp(s - lse_ref[:, pl.ds(q0, tile)])
            if masked:
                p = jnp.where(lax.broadcasted_iota(jnp.int32, s.shape, 0) <= lax.broadcasted_iota(jnp.int32, s.shape, 1), p, 0.0)
            dp = dot_f32(vals, got[:, pl.ds(q0, tile)])
            ds = (p * (dp - delta[:, pl.ds(q0, tile)])).astype(jnp.bfloat16)
            dvr[...] += dot_f32(p.astype(jnp.bfloat16), gor[pl.ds(q0, tile), :])
            dkr[...] += dot_f32(ds, qr[pl.ds(q0, tile), :])
            dqt[:, pl.ds(q0, tile)] += dot_f32(keys_t, ds)
        step(k0, True)
        def later(qi, c):
            step(pl.multiple_of(qi * tile, tile), False)
            return c
        lax.fori_loop(kj + 1, tiles, later, 0)
        kt_d = dkr[...].T
        vt_d = dvr[...].T
        put_out(kt_d, HEAD_DIM, k0, True)
        put_out(vt_d, 2 * HEAD_DIM, k0, False)
        return unused

    half = HEAD_DIM // 2
    def put_out(x, at, place, turn):
        for part in range(tile // block):
            piece = x[:, part * block:(part + 1) * block]
            here = place + part * block
            if turn:
                lanes = pl.ds(pl.multiple_of(here, block), block)
                c, s = cos_ref[:, lanes], sin_ref[:, lanes]
                a, b = piece[:half], piece[half:]
                piece = jnp.concatenate([a * c + b * s, b * c - a * s], 0)
            slot = order_ref[seq // block + here // block]
            per_src = grad_ref.shape[2] // block
            lane = pl.multiple_of((slot % per_src) * block, block)
            grad_ref[slot // per_src, at:at + HEAD_DIM, pl.ds(lane, block)] = piece.astype(jnp.bfloat16)

    lax.fori_loop(0, tiles, key_tile, 0)
    def write_q(qi, c):
        q0 = pl.multiple_of(qi * tile, tile)
        put_out(dqt[:, pl.ds(q0, tile)], 0, q0, True)
        return c
    lax.fori_loop(0, tiles, write_q, 0)

def attend_back(order, qkv, go, out, lse, cos, sin, block, tile):
    groups, unused, width = qkv.shape
    seq = groups * width
    vm = pl.BlockSpec(memory_space=pltpu.VMEM)
    bf, f32 = jnp.bfloat16, jnp.float32
    wide = lambda t: pltpu.VMEM((HEAD_DIM, seq), t)
    tall = lambda t: pltpu.VMEM((seq, HEAD_DIM), t)
    return pl.pallas_call(
        functools.partial(bwd_kernel, block=block, tile=tile),
        out_shape=jax.ShapeDtypeStruct(qkv.shape, bf),
        in_specs=[pl.BlockSpec(memory_space=pltpu.SMEM)] + [vm] * 6,
        out_specs=vm,
        scratch_shapes=[wide(bf), tall(bf), wide(bf), tall(bf), tall(bf), wide(bf), tall(bf),
                        pltpu.VMEM((1, seq), f32), wide(f32),
                        pltpu.VMEM((tile, HEAD_DIM), f32), pltpu.VMEM((tile, HEAD_DIM), f32)],
        compiler_params=pltpu.CompilerParams(vmem_limit_bytes=48 << 20),
        name="attend_back",
    )(order, qkv, go, out, lse, cos, sin)


def nt_dot(a, b):
    return lax.dot_general(a, b, (((1,), (1,)), ((), ())), preferred_element_type=jnp.float32)


def whole(space=pltpu.VMEM):
    return pl.BlockSpec(memory_space=space)


def spread(pieces, place_ref, rows_ref):
    hops = (len(pieces) - 1) // 2
    slots, share, unused = pieces[0].shape
    place = place_ref[0]

    def put(piece, position):
        for slot in range(slots):
            first = pl.multiple_of(slot * share * (hops + 1) + position * share, share)
            rows_ref[pl.ds(first, share), :] = piece[slot]

    put(pieces[0], place)
    for hop in range(1, hops + 1):

        @pl.when(place >= hop)
        def take_below(hop=hop):
            put(pieces[hop], place - hop)

        @pl.when(place + hop <= hops)
        def take_above(hop=hop):
            put(pieces[hops + hop], place + hop)


def deal(rows_ref, place_ref, own_ref, others):
    slots, share, unused = own_ref.shape
    line = len(others) + 1
    for step, target in enumerate([own_ref] + list(others)):
        position = lax.rem(place_ref[0] + step, line)
        for slot in range(slots):
            first = pl.multiple_of(slot * share * line + position * share, share)
            target[slot] = rows_ref[pl.ds(first, share), :].astype(target.dtype)


def dealt_shapes(slots, share, width, line):
    return [jax.ShapeDtypeStruct((slots, share, width), jnp.float32)] + [
        jax.ShapeDtypeStruct((slots, share, width), jnp.bfloat16) for unused in range(line - 1)
    ]


def vmem_limit(mebibytes):
    return pltpu.CompilerParams(vmem_limit_bytes=mebibytes << 20)


def cut_columns(weights, row_block, rows, line):
    count = len(weights)
    columns = weights[0].shape[1] // line

    def kernel(block_ref, *refs):
        for i in range(count):
            refs[count][0, i] = refs[i][...]

    return pl.pallas_call(
        kernel,
        out_shape=jax.ShapeDtypeStruct((line, count, rows, columns), jnp.bfloat16),
        grid_spec=pltpu.PrefetchScalarGridSpec(
            num_scalar_prefetch=1,
            grid=(line,),
            in_specs=[pl.BlockSpec((rows, columns), lambda j, block: (block[0], j))] * count,
            out_specs=pl.BlockSpec((1, count, rows, columns), lambda j, block: (j, 0, 0, 0)),
        ),
        compiler_params=vmem_limit(24),
        name="cut_columns",
    )(row_block, *weights)


def widen_columns(parts):
    line, count, rows, columns = parts.shape

    def kernel(parts_ref, *outs):
        for i in range(count):
            outs[i][...] = parts_ref[0, i].astype(jnp.float32)

    return pl.pallas_call(
        kernel,
        grid=(line,),
        out_shape=[jax.ShapeDtypeStruct((rows, line * columns), jnp.float32)] * count,
        in_specs=[pl.BlockSpec((1, count, rows, columns), lambda j: (j, 0, 0, 0))],
        out_specs=[pl.BlockSpec((rows, columns), lambda j: (0, j))] * count,
        compiler_params=vmem_limit(24),
        name="widen_columns",
    )(parts)


def project(place, pieces, w_heads, cosine, sine):
    line, count, part, width = w_heads.shape
    slots, share, model_width = pieces[0].shape
    rows = slots * share * line
    tile = width // 2
    heads = tile // HEAD_DIM
    n_pieces = len(pieces)
    half = HEAD_DIM // 2

    def kernel(place_ref, *refs):
        piece_refs = refs[:n_pieces]
        w_ref, cos_ref, sin_ref, rows_ref, out_ref = refs[n_pieces:]

        @pl.when((pl.program_id(0) == 0) & (pl.program_id(1) == 0))
        def assemble():
            spread(piece_refs, place_ref, rows_ref)

        weight = w_ref[...].reshape(line * part, tile)
        turned = dot_f32(rows_ref[...], weight).T
        c, s = cos_ref[0], sin_ref[0]
        for head in range(heads):
            a = turned[head * HEAD_DIM : head * HEAD_DIM + half]
            b = turned[head * HEAD_DIM + half : (head + 1) * HEAD_DIM]
            out_ref[head, 0, :half, :] = (a * c - b * s).astype(jnp.bfloat16)
            out_ref[head, 0, half:, :] = (b * c + a * s).astype(jnp.bfloat16)

    return pl.pallas_call(
        kernel,
        grid=(count, 2),
        out_shape=[
            jax.ShapeDtypeStruct((rows, model_width), jnp.bfloat16),
            jax.ShapeDtypeStruct((width // HEAD_DIM, count, HEAD_DIM, rows), jnp.bfloat16),
        ],
        in_specs=[whole(pltpu.SMEM)]
        + [whole()] * n_pieces
        + [
            pl.BlockSpec((line, 1, part, tile), lambda m, h: (0, m, 0, h)),
            pl.BlockSpec((1, half, rows), lambda m, h: (m, 0, 0)),
            pl.BlockSpec((1, half, rows), lambda m, h: (m, 0, 0)),
        ],
        out_specs=[
            pl.BlockSpec((rows, model_width), lambda m, h: (0, 0)),
            pl.BlockSpec((heads, 1, HEAD_DIM, rows), lambda m, h: (h, m, 0, 0)),
        ],
        compiler_params=vmem_limit(48),
        name="project",
    )(place, *pieces, w_heads, cosine, sine)


def mix_out(place, mixed, w_out, slots, line):
    heads, unused, rows = mixed.shape
    width, model_width = w_out.shape
    share = rows // slots // line

    def kernel(place_ref, mixed_ref, w_ref, own_ref, *rest):
        *others, total = rest
        left = mixed_ref[...].reshape(width, rows).T
        total[...] = dot_f32(left, w_ref[...])
        deal(total, place_ref, own_ref, others)

    return pl.pallas_call(
        kernel,
        out_shape=dealt_shapes(slots, share, model_width, line),
        in_specs=[whole(pltpu.SMEM), whole(), whole()],
        out_specs=[whole()] * line,
        scratch_shapes=[pltpu.VMEM((rows, model_width), jnp.float32)],
        compiler_params=vmem_limit(48),
        name="mix_out",
    )(place, mixed, w_out)


def mlp_forward(place, pieces, upstream_pieces, w_mlp, tile):
    line, count, part, width = w_mlp.shape
    slots, share, model_width = pieces[0].shape
    rows = slots * share * line
    n_pieces = len(pieces)
    bf, f32 = jnp.bfloat16, jnp.float32

    def kernel(place_ref, *refs):
        x_pieces, u_pieces = refs[:n_pieces], refs[n_pieces : 2 * n_pieces]
        w_ref, x_ref, u_ref, hidden_ref, gate_ref, up_ref, own_ref = refs[
            2 * n_pieces : 2 * n_pieces + 7
        ]
        *others, total = refs[2 * n_pieces + 7 :]
        step = pl.program_id(0)

        @pl.when(step == 0)
        def assemble():
            spread(x_pieces, place_ref, x_ref)
            spread(u_pieces, place_ref, u_ref)

        down = w_ref[:, 0].reshape(line * part, tile)
        gate = w_ref[:, 1].reshape(line * part, tile)
        up = w_ref[:, 2].reshape(line * part, tile)
        x = x_ref[...]
        grad_hidden = dot_f32(u_ref[...], down)
        gate_act = dot_f32(x, gate)
        upward = dot_f32(x, up)
        sigmoid = jax.nn.sigmoid(gate_act)
        silu = gate_act * sigmoid
        hidden_ref[...] = (silu * upward).astype(bf)
        grad_gate = (
            grad_hidden * upward * sigmoid * (1.0 + gate_act * (1.0 - sigmoid))
        ).astype(bf)
        grad_up = (grad_hidden * silu).astype(bf)
        gate_ref[...] = grad_gate
        up_ref[...] = grad_up
        part_two = nt_dot(grad_gate, gate) + nt_dot(grad_up, up)

        @pl.when(step == 0)
        def first():
            total[...] = part_two

        @pl.when(step > 0)
        def further():
            total[...] += part_two

        @pl.when(step == pl.num_programs(0) - 1)
        def last():
            deal(total, place_ref, own_ref, others)

    fixed = lambda shape: pl.BlockSpec(shape, lambda j: (0,) * len(shape))
    columns = pl.BlockSpec((rows, tile), lambda j: (0, j))
    dealt = dealt_shapes(slots, share, model_width, line)
    return pl.pallas_call(
        kernel,
        grid=(width // tile,),
        out_shape=[jax.ShapeDtypeStruct((rows, model_width), bf)] * 2
        + [jax.ShapeDtypeStruct((rows, width), bf)] * 3
        + dealt,
        in_specs=[whole(pltpu.SMEM)]
        + [whole()] * (2 * n_pieces)
        + [pl.BlockSpec((line, count, part, tile), lambda j: (0, 0, 0, j))],
        out_specs=[fixed((rows, model_width))] * 2
        + [columns] * 3
        + [fixed((slots, share, model_width))] * line,
        scratch_shapes=[pltpu.VMEM((rows, model_width), f32)],
        compiler_params=vmem_limit(60),
        name="mlp_forward",
    )(place, *pieces, *upstream_pieces, w_mlp)


def mlp_weights(place, x_rows, u_rows, hidden, grad_gate, grad_up, w_mlp, slots, groups, tile):
    line, count, part, width = w_mlp.shape
    rows, model_width = x_rows.shape
    share = rows // slots // line
    block = model_width // groups // line
    bf, f32 = jnp.bfloat16, jnp.float32

    def kernel(place_ref, x_ref, u_ref, hidden_ref, gate_ref, up_ref, w_ref, gu_ref, d_ref, own_ref, *rest):
        *others, x_turned, u_turned, total = rest
        step = pl.program_id(0)

        @pl.when(step == 0)
        def turn():
            x_turned[...] = x_ref[...].T
            u_turned[...] = u_ref[...].T

        down = w_ref[:, 0].reshape(line * part, tile)
        cut = (groups, line, block, tile)
        gu_ref[:, :, 0] = dot_f32(x_turned[...], gate_ref[...]).astype(bf).reshape(cut)
        gu_ref[:, :, 1] = dot_f32(x_turned[...], up_ref[...]).astype(bf).reshape(cut)
        d_ref[:, :line] = dot_f32(u_turned[...], hidden_ref[...]).astype(bf).reshape(cut)
        part_out = nt_dot(hidden_ref[...], down)

        @pl.when(step == 0)
        def first():
            total[...] = part_out

        @pl.when(step > 0)
        def further():
            total[...] += part_out

        @pl.when(step == pl.num_programs(0) - 1)
        def last():
            deal(total, place_ref, own_ref, others)

    fixed = lambda shape: pl.BlockSpec(shape, lambda j: (0,) * len(shape))
    columns = pl.BlockSpec((rows, tile), lambda j: (0, j))
    return pl.pallas_call(
        kernel,
        grid=(width // tile,),
        out_shape=[
            jax.ShapeDtypeStruct((groups, line, 2, block, width), bf),
            jax.ShapeDtypeStruct((groups, line + 1, block, width), bf),
        ]
        + dealt_shapes(slots, share, model_width, line),
        in_specs=[whole(pltpu.SMEM), fixed((rows, model_width)), fixed((rows, model_width))]
        + [columns] * 3
        + [pl.BlockSpec((line, 1, part, tile), lambda j: (0, 0, 0, j))],
        out_specs=[
            pl.BlockSpec((groups, line, 2, block, tile), lambda j: (0, 0, 0, 0, j)),
            pl.BlockSpec((groups, line + 1, block, tile), lambda j: (0, 0, 0, j)),
        ]
        + [fixed((slots, share, model_width))] * line,
        scratch_shapes=[
            pltpu.VMEM((model_width, rows), bf),
            pltpu.VMEM((model_width, rows), bf),
            pltpu.VMEM((rows, model_width), f32),
        ],
        compiler_params=vmem_limit(60),
        name="mlp_weights",
    )(place, x_rows, u_rows, hidden, grad_gate, grad_up, w_mlp)


def branch_back(place, pieces, w_out, heads):
    slots, share, model_width = pieces[0].shape
    line = (len(pieces) + 1) // 2
    rows = slots * share * line

    def kernel(place_ref, *refs):
        *piece_refs, w_ref, rows_ref, out_ref = refs
        spread(piece_refs, place_ref, rows_ref)
        turned = nt_dot(w_ref[...], rows_ref[...])
        out_ref[...] = turned.astype(jnp.bfloat16).reshape(out_ref.shape)

    return pl.pallas_call(
        kernel,
        out_shape=[
            jax.ShapeDtypeStruct((rows, model_width), jnp.bfloat16),
            jax.ShapeDtypeStruct((heads, HEAD_DIM, rows), jnp.bfloat16),
        ],
        in_specs=[whole(pltpu.SMEM)] + [whole()] * (len(pieces) + 1),
        out_specs=[whole(), whole()],
        compiler_params=vmem_limit(40),
        name="branch_back",
    )(place, *pieces, w_out)


def out_weight(grads, mixed, branch_rows, tile):
    groups, blocks, block, width = grads.shape
    heads, unused, rows = mixed.shape

    def kernel(grads_ref, mixed_ref, rows_ref, out_ref):
        left = mixed_ref[...].reshape(heads * HEAD_DIM, rows)
        out_ref[...] = (
            dot_f32(left, rows_ref[...]).astype(jnp.bfloat16).reshape(groups, 1, block, tile)
        )

    return pl.pallas_call(
        kernel,
        grid=(width // tile,),
        out_shape=jax.ShapeDtypeStruct(grads.shape, grads.dtype),
        in_specs=[
            pl.BlockSpec(memory_space=pl.ANY),
            pl.BlockSpec(mixed.shape, lambda j: (0, 0, 0)),
            pl.BlockSpec((rows, tile), lambda j: (0, j)),
        ],
        out_specs=pl.BlockSpec((groups, 1, block, tile), lambda j: (0, blocks - 1, 0, j)),
        input_output_aliases={0: 0},
        compiler_params=vmem_limit(32),
        name="out_weight",
    )(grads, mixed, branch_rows)


def head_weights(x_rows, head_grads, groups, line):
    rows, model_width = x_rows.shape
    heads, count, unused, unused_rows = head_grads.shape
    width = heads * HEAD_DIM
    block = model_width // groups // line

    def kernel(x_ref, g_ref, out_ref, x_turned):
        @pl.when(pl.program_id(0) == 0)
        def turn():
            x_turned[...] = x_ref[...].T

        grads = g_ref[...].reshape(width, rows)
        out_ref[...] = (
            nt_dot(x_turned[...], grads).astype(jnp.bfloat16).reshape(out_ref.shape)
        )

    return pl.pallas_call(
        kernel,
        grid=(count,),
        out_shape=jax.ShapeDtypeStruct((groups, line, count, block, width), jnp.bfloat16),
        in_specs=[
            pl.BlockSpec((rows, model_width), lambda m: (0, 0)),
            pl.BlockSpec((heads, 1, HEAD_DIM, rows), lambda m: (0, m, 0, 0)),
        ],
        out_specs=pl.BlockSpec((groups, line, 1, block, width), lambda m: (0, 0, m, 0, 0)),
        scratch_shapes=[pltpu.VMEM((model_width, rows), jnp.bfloat16)],
        compiler_params=vmem_limit(40),
        name="head_weights",
    )(x_rows, head_grads)


def project_back(place, x_rows, head_grads, w_heads, slots):
    line, count, part, width = w_heads.shape
    rows, model_width = x_rows.shape
    heads = width // HEAD_DIM
    share = rows // slots // line

    def kernel(place_ref, x_ref, g_ref, w_ref, gain_ref, own_ref, *rest):
        *others, total = rest
        m = pl.program_id(0)
        grads = g_ref[...].reshape(width, rows).T
        partial = nt_dot(grads, w_ref[...].reshape(line * part, width))

        @pl.when(m == 0)
        def first():
            total[...] = partial

        @pl.when(m > 0)
        def further():
            total[...] += partial

        @pl.when(m == count - 1)
        def last():
            deal(total, place_ref, own_ref, others)
            gain_ref[...] = jnp.sum(
                total[...] * x_ref[...].astype(jnp.float32), 0, keepdims=True
            )

    fixed = lambda shape: pl.BlockSpec(shape, lambda m: (0,) * len(shape))
    return pl.pallas_call(
        kernel,
        grid=(count,),
        out_shape=[jax.ShapeDtypeStruct((1, model_width), jnp.float32)]
        + dealt_shapes(slots, share, model_width, line),
        in_specs=[
            whole(pltpu.SMEM),
            fixed((rows, model_width)),
            pl.BlockSpec((heads, 1, HEAD_DIM, rows), lambda m: (0, m, 0, 0)),
            pl.BlockSpec((line, 1, part, width), lambda m: (0, m, 0, 0)),
        ],
        out_specs=[fixed((1, model_width))] + [fixed((slots, share, model_width))] * line,
        scratch_shapes=[pltpu.VMEM((rows, model_width), jnp.float32)],
        compiler_params=vmem_limit(48),
        name="project_back",
    )(place, x_rows, head_grads, w_heads)

def line_steps(size, step):
    return [(i, i + step) for i in range(size) if 0 <= i + step < size]


def after(values, *earlier):
    return lax.optimization_barrier((values, earlier))[0]


def send_shares(share, axis):
    size = lax.axis_size(axis)
    ups, downs = [share], [share]
    for hop in range(1, size):
        ups.append(lax.ppermute(ups[-1], axis, line_steps(size, 1)[hop - 1 :]))
        downs.append(lax.ppermute(downs[-1], axis, line_steps(size, -1)[: size - hop]))
    return ups + downs[1:]


def gather_line(share, axis):
    size = lax.axis_size(axis)
    ups = [lax.ppermute(share, axis, line_steps(size, hop)) for hop in range(1, size)]
    downs = [lax.ppermute(share, axis, line_steps(size, -hop)) for hop in range(1, size)]
    window = jnp.stack(ups[::-1] + [share] + downs)
    return lax.dynamic_slice_in_dim(window, size - 1 - lax.axis_index(axis), size, 0)


def send_dealt(others, axis):
    size = lax.axis_size(axis)
    return [
        lax.ppermute(other, axis, [(i, (i + step) % size) for i in range(size)])
        for step, other in enumerate(others, 1)
    ]


def add_shares(own, received):
    return own + sum(share.astype(jnp.float32) for share in received)


def swap_line(parts):
    return lax.all_to_all(parts, "fsdp", split_axis=0, concat_axis=0, tiled=True)


def swap_heads(parts):
    return lax.all_to_all(parts, "ctx", split_axis=0, concat_axis=0, tiled=True)


def sum_groups(parts):
    return lax.psum_scatter(parts, "ctx", scatter_dimension=0, tiled=True)[0]


def head_device(
    tokens,
    block_order,
    w_query,
    w_key,
    w_value,
    w_out,
    w_gate,
    w_up,
    w_down,
    gain_attn,
    gain_mlp,
    cotangent,
):
    slots, share_rows, model_width = tokens.shape
    ctx_size, line = lax.axis_size("ctx"), lax.axis_size("fsdp")
    block_rows = share_rows * line
    group_rows = slots * block_rows
    bf, f32 = jnp.bfloat16, jnp.float32
    place = lax.axis_index("fsdp").astype(jnp.int32).reshape(1)
    group = lax.axis_index("ctx").astype(jnp.int32).reshape(1)
    own_rows = w_query.shape[0] // ctx_size
    order = block_order.astype(jnp.int32)
    slot_of = jnp.sum(
        jnp.where(order[None, :] == jnp.arange(order.shape[0])[:, None], jnp.arange(order.shape[0], dtype=jnp.int32)[None, :], 0), 1
    ).astype(jnp.int32)

    head_cuts = swap_line(cut_columns([w_query, w_key, w_value], group, own_rows, line))
    w_heads = lax.all_gather(head_cuts, "ctx", axis=2, tiled=True)

    gains = gather_line(jnp.stack([gain_attn, gain_mlp]), "fsdp")
    gains = jnp.swapaxes(gains, 0, 1).reshape(2, model_width).astype(f32)
    attn_gain, mlp_gain = gains[0], gains[1]
    stream = tokens.astype(f32)
    root_one = lax.rsqrt(jnp.mean(stream * stream, -1, keepdims=True) + EPSILON)
    norm_one = stream * root_one
    attn_input = (norm_one * attn_gain).astype(bf)
    attn_pieces = send_shares(after(attn_input, head_cuts), "fsdp")

    mlp_cuts = cut_columns([w_down, w_gate, w_up], group, own_rows, line)
    mlp_cuts = swap_line(after(mlp_cuts, attn_pieces))
    w_mlp = lax.all_gather(mlp_cuts, "ctx", axis=2, tiled=True)

    half = HEAD_DIM // 2
    frequency = 1.0 / ROPE_BASE ** (jnp.arange(half, dtype=f32) * (2.0 / HEAD_DIM))
    places = jnp.arange(group_rows * ctx_size, dtype=jnp.int32).astype(f32)
    angles = frequency[:, None] * places[None, :]
    cosine, sine = jnp.cos(angles), jnp.sin(angles)

    def own_columns(table):
        return jnp.concatenate(
            [
                lax.dynamic_slice_in_dim(
                    table, order[slots * group[0] + i] * block_rows, block_rows, 1
                )
                for i in range(slots)
            ],
            1,
        )

    own_cosine, own_sine = own_columns(cosine), own_columns(sine)
    turn_cosine = jnp.stack([own_cosine, own_cosine, jnp.ones_like(own_cosine)])
    turn_sine = jnp.stack([own_sine, own_sine, jnp.zeros_like(own_sine)])

    attn_rows, heads_out = project(place, attn_pieces, w_heads, turn_cosine, turn_sine)
    head_rows = swap_heads(heads_out.reshape(ctx_size, 3 * HEAD_DIM, group_rows))
    mixed_send, attended, log_total = attend(order, head_rows, block_rows, 2 * block_rows)
    mixed = swap_heads(mixed_send)
    own, others = split_first(mix_out(place, after(mixed, mlp_cuts), w_out, slots, line))
    middle = stream + add_shares(own, send_dealt(others, "fsdp"))

    root_two = lax.rsqrt(jnp.mean(middle * middle, -1, keepdims=True) + EPSILON)
    norm_two = middle * root_two
    mlp_input = (norm_two * mlp_gain).astype(bf)
    mlp_pieces = send_shares(mlp_input, "fsdp")
    upstream_pieces = send_shares(after(cotangent, mlp_pieces), "fsdp")

    mlp_rows, upstream_rows, hidden, grad_gate, grad_up, own, *others = mlp_forward(
        place, mlp_pieces, upstream_pieces, w_mlp, 256
    )
    two_received = send_dealt(others, "fsdp")
    gate_up_grads, down_grads, own_out, *others_out = mlp_weights(
        place, mlp_rows, upstream_rows, hidden, grad_gate, grad_up, w_mlp, slots, ctx_size, 256
    )
    gate_up_sums = sum_groups(gate_up_grads)

    grad_two = add_shares(own, after(two_received, own_out))
    gain_two_part = jnp.sum(grad_two * norm_two, (0, 1))
    grad_middle = cotangent.astype(f32) + norm_back(grad_two, norm_two, root_two, mlp_gain)
    branch_pieces = send_shares(grad_middle.astype(bf), "fsdp")
    branch_rows, grad_mixed = branch_back(place, branch_pieces, w_out, ctx_size)
    out_received = send_dealt(after(others_out, branch_pieces), "fsdp")
    grad_heads = swap_heads(grad_mixed)
    down_grads = out_weight(down_grads, mixed, branch_rows, 512)
    down_sums = sum_groups(down_grads)

    head_grads = attend_back(
        jnp.concatenate([order, slot_of]),
        head_rows,
        after(grad_heads, down_grads),
        attended,
        log_total,
        cosine,
        sine,
        block_rows,
        2 * block_rows,
    )
    lin_grads = swap_heads(head_grads).reshape(ctx_size, 3, HEAD_DIM, group_rows)
    head_sums = sum_groups(head_weights(attn_rows, lin_grads, ctx_size, line))
    gain_one_part, own, *others = project_back(place, attn_rows, lin_grads, w_heads, slots)
    grad_one = add_shares(own, send_dealt(others, "fsdp"))
    grad_tokens = grad_middle + norm_back(grad_one, norm_one, root_one, attn_gain)
    result = (middle + add_shares(own_out, out_received)).astype(bf)

    grad_w_gate, grad_w_up = widen_columns(swap_line(gate_up_sums))
    (grad_w_down,) = widen_columns(swap_line(down_sums[:line, None]))
    grad_w_query, grad_w_key, grad_w_value = widen_columns(swap_line(head_sums))
    owners = [(c * line + f, f * ctx_size + c) for c in range(ctx_size) for f in range(line)]
    grad_w_out = lax.ppermute(down_sums[line], ("ctx", "fsdp"), owners).astype(f32)

    gain_parts = jnp.stack([gain_one_part[0] / attn_gain, gain_two_part])
    gain_parts = jnp.swapaxes(gain_parts.reshape(2, ctx_size * line, -1), 0, 1)
    gain_parts = lax.all_to_all(
        gain_parts.reshape(ctx_size * line, -1),
        ("ctx", "fsdp"),
        split_axis=0,
        concat_axis=0,
        tiled=True,
    )
    gain_grads = jnp.sum(gain_parts, 0).reshape(2, -1)
    return (
        result,
        grad_tokens,
        grad_w_query,
        grad_w_key,
        grad_w_value,
        grad_w_out,
        grad_w_gate,
        grad_w_up,
        grad_w_down,
        gain_grads[0],
        gain_grads[1],
    )


def split_first(values):
    return values[0], values[1:]


def layer_step(*arrays):
    heads_here = arrays[0].shape[-1] // lax.axis_size("fsdp") // HEAD_DIM
    if heads_here == lax.axis_size("ctx"):
        return head_device(*arrays)
    return per_device(*arrays)


def solution(mesh):
    in_specs = (
        P("ctx", "fsdp", None),
        P(),
        P("fsdp", None),
        P("fsdp", None),
        P("fsdp", None),
        P("fsdp", None),
        P("fsdp", None),
        P("fsdp", None),
        P("fsdp", None),
        P("fsdp"),
        P("fsdp"),
        P("ctx", "fsdp", None),
    )
    out_specs = (
        P("ctx", "fsdp", None),
        P("ctx", "fsdp", None),
        P(("ctx", "fsdp"), None),
        P(("ctx", "fsdp"), None),
        P(("ctx", "fsdp"), None),
        P(("ctx", "fsdp"), None),
        P(("ctx", "fsdp"), None),
        P(("ctx", "fsdp"), None),
        P(("ctx", "fsdp"), None),
        P(("ctx", "fsdp")),
        P(("ctx", "fsdp")),
    )
    return jax.shard_map(
        layer_step, mesh=mesh, in_specs=in_specs, out_specs=out_specs, check_vma=False
    )
```

```python
import functools

import jax
import jax.numpy as jnp
from jax import lax
from jax.experimental import pallas as pl
from jax.experimental.pallas import tpu as pltpu
from jax.sharding import PartitionSpec as P

HEAD_DIM = 64


EPSILON = 1e-05
ROPE_BASE = 130000.0
MASKED_SCORE = -1e30


def rotate(values, places, direction):
    half_dim = values.shape[-1] // 2
    frequency = 1.0 / ROPE_BASE ** (
        jnp.arange(half_dim, dtype=jnp.float32) * (2.0 / values.shape[-1])
    )
    angles = places[..., None] * frequency
    cosine = jnp.cos(angles)[..., None, :]
    sine_part = direction * jnp.sin(angles)[..., None, :]
    leading = values[..., :half_dim]
    trailing = values[..., half_dim:]
    return jnp.concatenate(
        [leading * cosine - trailing * sine_part, trailing * cosine + leading * sine_part], -1
    )


def matmul(left, right):
    return jnp.dot(left, right, preferred_element_type=jnp.float32)


def contract(left, right):
    return lax.dot_general(
        left, right, (((1,), (1,)), ((), ())), preferred_element_type=jnp.float32
    )


def transpose_product(left, right):
    return lax.dot_general(
        left, right, (((0,), (0,)), ((), ())), preferred_element_type=jnp.float32
    )


def split_heads(values):
    return values.reshape(values.shape[:-1] + (-1, HEAD_DIM))


def keep_state(current):
    return current


def tile_scores(queries, key_rows, query_places, key_places, score_scale):
    scores = (
        jnp.einsum("qhd,khd->hqk", queries, key_rows, preferred_element_type=jnp.float32)
        * score_scale
    )
    allowed = (key_places[None, :] <= query_places[:, None])[None]
    return (jnp.where(allowed, scores, MASKED_SCORE), allowed)


def grow_state(current, queries, key_rows, value_rows, query_places, key_places, score_scale):
    run_peak, run_total, summed = current
    scores, allowed = tile_scores(queries, key_rows, query_places, key_places, score_scale)
    new_peak = jnp.maximum(run_peak, jnp.max(scores, -1))
    weights = jnp.where(allowed, jnp.exp(scores - new_peak[..., None]), 0.0)
    factor = jnp.exp(run_peak - new_peak)
    run_total = run_total * factor + jnp.sum(weights, -1)
    summed = summed * jnp.transpose(factor)[:, :, None] + jnp.einsum(
        "hqk,khd->qhd", weights.astype(jnp.bfloat16), value_rows, preferred_element_type=jnp.float32
    )
    return (new_peak, run_total, summed)


def backward_tile(
    queries,
    key_rows,
    value_rows,
    grad_out,
    log_total,
    row_delta,
    query_places,
    key_places,
    score_scale,
):
    scores, allowed = tile_scores(queries, key_rows, query_places, key_places, score_scale)
    probabilities = jnp.where(allowed, jnp.exp(scores - log_total[..., None]), 0.0)
    grad_probs = jnp.einsum(
        "qhd,khd->hqk", grad_out, value_rows, preferred_element_type=jnp.float32
    )
    grad_scores = (probabilities * (grad_probs - row_delta[..., None])).astype(jnp.bfloat16)
    return (probabilities, grad_scores)


def norm_back(grad_normed_in, normed_values, inverse_root, gain_vector):
    scaled = grad_normed_in * gain_vector
    return inverse_root * (
        scaled - normed_values * jnp.mean(scaled * normed_values, -1, keepdims=True)
    )


def per_device(
    tokens,
    block_order,
    w_query,
    w_key,
    w_value,
    w_out,
    w_gate,
    w_up,
    w_down,
    gain_attn,
    gain_mlp,
    cotangent,
):
    slot_count, share_rows, model_width = tokens.shape
    fsdp_size = lax.axis_size("fsdp")
    block_rows = share_rows * fsdp_size
    head_width = model_width // fsdp_size
    heads_here = head_width // HEAD_DIM
    row_count = slot_count * share_rows
    score_scale = HEAD_DIM ** (-0.5)
    own_slots = 2 * lax.axis_index("ctx") + jnp.arange(2, dtype=jnp.int32)
    own_blocks = block_order[own_slots]
    token_places = (
        (
            own_blocks[:, None] * block_rows
            + lax.axis_index("fsdp") * share_rows
            + jnp.arange(share_rows, dtype=jnp.int32)[None, :]
        )
        .astype(jnp.float32)
        .reshape(row_count)
    )
    head_places = (
        own_blocks[:, None] * block_rows + jnp.arange(block_rows, dtype=jnp.int32)[None, :]
    ).astype(jnp.float32)
    params = (w_query, w_key, w_value, w_out, w_gate, w_up, w_down, gain_attn, gain_mlp)
    weights_all = (
        lax.all_gather(params[0], "fsdp", axis=0, tiled=True),
        lax.all_gather(params[1], "fsdp", axis=0, tiled=True),
        lax.all_gather(params[2], "fsdp", axis=0, tiled=True),
        lax.all_gather(params[3], "fsdp", axis=0, tiled=True),
        lax.all_gather(params[4], "fsdp", axis=0, tiled=True),
        lax.all_gather(params[5], "fsdp", axis=0, tiled=True),
        lax.all_gather(params[6], "fsdp", axis=0, tiled=True),
        lax.all_gather(params[7], "fsdp", axis=0, tiled=True),
        lax.all_gather(params[8], "fsdp", axis=0, tiled=True),
    )
    stream = tokens.reshape(row_count, model_width).astype(jnp.float32)
    root_one = lax.rsqrt(jnp.mean(stream * stream, -1, keepdims=True) + EPSILON)
    norm_one = stream * root_one
    attn_input = (norm_one * weights_all[7].astype(jnp.float32)).astype(jnp.bfloat16)

    def project_turn(weight):
        linear = matmul(attn_input, weight).reshape(row_count, -1, HEAD_DIM)
        return (
            rotate(linear, token_places, 1.0)
            .astype(jnp.bfloat16)
            .reshape(slot_count, share_rows, model_width)
        )

    query_tok = project_turn(weights_all[0])
    key_tok = project_turn(weights_all[1])
    value_tok = (
        matmul(attn_input, weights_all[2])
        .astype(jnp.bfloat16)
        .reshape(slot_count, share_rows, model_width)
    )
    query_heads, key_heads, value_heads = (
        lax.all_to_all(query_tok, "fsdp", split_axis=2, concat_axis=1, tiled=True),
        lax.all_to_all(key_tok, "fsdp", split_axis=2, concat_axis=1, tiled=True),
        lax.all_to_all(value_tok, "fsdp", split_axis=2, concat_axis=1, tiled=True),
    )
    query_split = split_heads(query_heads)
    start_state = tuple(
        (
            (
                jnp.full((heads_here, block_rows), MASKED_SCORE, jnp.float32),
                jnp.zeros((heads_here, block_rows), jnp.float32),
                jnp.zeros((block_rows, heads_here, HEAD_DIM), jnp.float32),
            )
            for which_slot in range(2)
        )
    )
    carried = start_state
    key_part = lax.all_gather(key_heads, "ctx", axis=0, tiled=True)
    value_part = lax.all_gather(value_heads, "ctx", axis=0, tiled=True)

    def visit_slot(inner_state, element):
        key_one, value_one, offset = element
        key_block = block_order[offset]
        key_places = (key_block * block_rows + jnp.arange(block_rows, dtype=jnp.int32)).astype(
            jnp.float32
        )
        key_split = split_heads(key_one)
        value_split = split_heads(value_one)
        updated = []
        for which_slot in range(2):

            def grow_one(current, which_slot=which_slot):
                return grow_state(
                    current,
                    query_split[which_slot],
                    key_split,
                    value_split,
                    head_places[which_slot],
                    key_places,
                    score_scale,
                )

            updated.append(
                lax.cond(
                    key_block <= own_blocks[which_slot],
                    grow_one,
                    keep_state,
                    inner_state[which_slot],
                )
            )
        return (tuple(updated), None)

    offsets = jnp.arange(key_part.shape[0], dtype=jnp.int32)
    carried, unused = lax.scan(visit_slot, carried, (key_part, value_part, offsets))
    attended_parts = []
    log_parts = []
    for which_slot in range(2):
        run_peak, run_total, summed = carried[which_slot]
        log_parts.append(run_peak + jnp.log(run_total))
        attended_parts.append(summed / jnp.transpose(run_total)[:, :, None])
    attended = jnp.stack(attended_parts)
    log_total = jnp.stack(log_parts)
    mixed_send = attended.reshape(slot_count, block_rows, head_width).astype(jnp.bfloat16)
    mixed_tok = lax.all_to_all(mixed_send, "fsdp", split_axis=1, concat_axis=2, tiled=True)
    mixed_flat = mixed_tok.reshape(row_count, model_width)
    middle = stream + matmul(mixed_flat, weights_all[3])
    root_two = lax.rsqrt(jnp.mean(middle * middle, -1, keepdims=True) + EPSILON)
    norm_two = middle * root_two
    mlp_input = (norm_two * weights_all[8].astype(jnp.float32)).astype(jnp.bfloat16)
    gate_act = matmul(mlp_input, weights_all[4])
    upward = matmul(mlp_input, weights_all[5])
    gate_sigmoid = jax.nn.sigmoid(gate_act)
    gate_silu = gate_act * gate_sigmoid
    hidden = (gate_silu * upward).astype(jnp.bfloat16)
    output = middle + contract(hidden, weights_all[6])
    result = output.astype(jnp.bfloat16).reshape(slot_count, share_rows, model_width)
    upstream = cotangent.reshape(row_count, model_width)
    grad_hidden = matmul(upstream, weights_all[6])
    grad_gate = (
        grad_hidden * upward * gate_sigmoid * (1.0 + gate_act * (1.0 - gate_sigmoid))
    ).astype(jnp.bfloat16)
    grad_up = (grad_hidden * gate_silu).astype(jnp.bfloat16)
    grad_two = contract(grad_gate, weights_all[4]) + contract(grad_up, weights_all[5])
    gain_two_part = jnp.sum(grad_two * norm_two, 0)
    grad_middle = upstream.astype(jnp.float32) + norm_back(
        grad_two, norm_two, root_two, weights_all[8].astype(jnp.float32)
    )
    grad_branch = grad_middle.astype(jnp.bfloat16)
    grad_mixed = (
        contract(grad_branch, weights_all[3])
        .astype(jnp.bfloat16)
        .reshape(slot_count, share_rows, model_width)
    )
    grad_heads = lax.all_to_all(grad_mixed, "fsdp", split_axis=2, concat_axis=1, tiled=True)
    grad_split = split_heads(grad_heads)
    row_delta = jnp.transpose(jnp.sum(grad_split.astype(jnp.float32) * attended, -1), (0, 2, 1))
    gathered = (
        lax.all_gather(key_heads, "ctx", axis=0, tiled=True),
        lax.all_gather(value_heads, "ctx", axis=0, tiled=True),
    )
    key_all, value_all = gathered
    total_slots = key_all.shape[0]

    def query_visit(current, element):
        key_pair, value_pair, pair_index = element
        updated = list(current)
        for member in range(2):
            key_block = block_order[2 * pair_index + member]
            key_places = (key_block * block_rows + jnp.arange(block_rows, dtype=jnp.int32)).astype(
                jnp.float32
            )
            key_split = split_heads(key_pair[member])
            value_split = split_heads(value_pair[member])
            for which_slot in range(2):

                def take_query(
                    accum,
                    which_slot=which_slot,
                    key_split=key_split,
                    value_split=value_split,
                    key_places=key_places,
                ):
                    probabilities, grad_scores = backward_tile(
                        query_split[which_slot],
                        key_split,
                        value_split,
                        grad_split[which_slot],
                        log_total[which_slot],
                        row_delta[which_slot],
                        head_places[which_slot],
                        key_places,
                        score_scale,
                    )
                    return accum + score_scale * jnp.einsum(
                        "hqk,khd->qhd", grad_scores, key_split, preferred_element_type=jnp.float32
                    )

                updated[which_slot] = lax.cond(
                    key_block <= own_blocks[which_slot], take_query, keep_state, updated[which_slot]
                )
        return (tuple(updated), None)

    query_zero = jnp.zeros((block_rows, heads_here, HEAD_DIM), jnp.float32)
    pair_keys = key_all.reshape(total_slots // 2, 2, block_rows, head_width)
    pair_values = value_all.reshape(total_slots // 2, 2, block_rows, head_width)
    grad_query_parts, unused = lax.scan(
        query_visit,
        (query_zero, query_zero),
        (pair_keys, pair_values, jnp.arange(total_slots // 2, dtype=jnp.int32)),
    )
    key_part = key_all
    value_part = value_all

    def key_visit(unused_carry, element):
        key_one, value_one, offset = element
        key_block = block_order[offset]
        key_places = (key_block * block_rows + jnp.arange(block_rows, dtype=jnp.int32)).astype(
            jnp.float32
        )
        key_split = split_heads(key_one)
        value_split = split_heads(value_one)
        sums = (
            jnp.zeros((block_rows, heads_here, HEAD_DIM), jnp.float32),
            jnp.zeros((block_rows, heads_here, HEAD_DIM), jnp.float32),
        )
        for which_slot in range(2):

            def take_keys(current, which_slot=which_slot):
                probabilities, grad_scores = backward_tile(
                    query_split[which_slot],
                    key_split,
                    value_split,
                    grad_split[which_slot],
                    log_total[which_slot],
                    row_delta[which_slot],
                    head_places[which_slot],
                    key_places,
                    score_scale,
                )
                grad_key = current[0] + score_scale * jnp.einsum(
                    "hqk,qhd->khd",
                    grad_scores,
                    query_split[which_slot],
                    preferred_element_type=jnp.float32,
                )
                grad_value = current[1] + jnp.einsum(
                    "hqk,qhd->khd",
                    probabilities.astype(jnp.bfloat16),
                    grad_split[which_slot],
                    preferred_element_type=jnp.float32,
                )
                return (grad_key, grad_value)

            sums = lax.cond(key_block <= own_blocks[which_slot], take_keys, keep_state, sums)
        joined = jnp.concatenate(
            [sums[0].reshape(block_rows, head_width), sums[1].reshape(block_rows, head_width)], -1
        )
        return (unused_carry, joined)

    unused_final, terms = lax.scan(
        key_visit,
        jnp.zeros((), jnp.float32),
        (key_part, value_part, jnp.arange(slot_count * lax.axis_size("ctx"), dtype=jnp.int32)),
    )
    summed_kv = lax.psum_scatter(
        terms.astype(jnp.bfloat16), "ctx", scatter_dimension=0, tiled=True
    ).astype(jnp.float32)
    grad_keys = (
        rotate(split_heads(summed_kv[..., :head_width]), head_places, -1.0)
        .astype(jnp.bfloat16)
        .reshape(slot_count, block_rows, head_width)
    )
    grad_values = summed_kv[..., head_width:].astype(jnp.bfloat16)
    grad_queries = (
        rotate(jnp.stack(grad_query_parts), head_places, -1.0)
        .astype(jnp.bfloat16)
        .reshape(slot_count, block_rows, head_width)
    )
    grad_q_tok, grad_k_tok, grad_v_tok = (
        lax.all_to_all(grad_queries, "fsdp", split_axis=1, concat_axis=2, tiled=True),
        lax.all_to_all(grad_keys, "fsdp", split_axis=1, concat_axis=2, tiled=True),
        lax.all_to_all(grad_values, "fsdp", split_axis=1, concat_axis=2, tiled=True),
    )
    grad_q_lin = grad_q_tok.reshape(row_count, model_width)
    grad_k_lin = grad_k_tok.reshape(row_count, model_width)
    grad_v_lin = grad_v_tok.reshape(row_count, model_width)
    grad_one = (
        contract(grad_q_lin, weights_all[0])
        + contract(grad_k_lin, weights_all[1])
        + contract(grad_v_lin, weights_all[2])
    )
    gain_one_part = jnp.sum(grad_one * norm_one, 0)
    grad_input = grad_middle + norm_back(
        grad_one, norm_one, root_one, weights_all[7].astype(jnp.float32)
    )
    hidden_width = hidden.shape[1]
    gain_parts = jnp.stack([gain_one_part, gain_two_part], 1)
    wide_cols = (
        lax.all_to_all(grad_q_lin, "fsdp", split_axis=1, concat_axis=0, tiled=True),
        lax.all_to_all(grad_k_lin, "fsdp", split_axis=1, concat_axis=0, tiled=True),
        lax.all_to_all(grad_v_lin, "fsdp", split_axis=1, concat_axis=0, tiled=True),
        lax.all_to_all(grad_branch, "fsdp", split_axis=1, concat_axis=0, tiled=True),
        lax.all_to_all(grad_gate, "fsdp", split_axis=1, concat_axis=0, tiled=True),
        lax.all_to_all(grad_up, "fsdp", split_axis=1, concat_axis=0, tiled=True),
        lax.all_to_all(hidden, "fsdp", split_axis=1, concat_axis=0, tiled=True),
    )
    row_sets = (
        lax.all_gather(attn_input, "fsdp", axis=0, tiled=True),
        lax.all_gather(mixed_flat, "fsdp", axis=0, tiled=True),
        lax.all_gather(mlp_input, "fsdp", axis=0, tiled=True),
        lax.all_gather(upstream, "fsdp", axis=0, tiled=True),
    )
    group_rows = model_width // lax.axis_size("ctx")
    row_cuts = [values for values in row_sets]
    pieces = [
        transpose_product(row_cuts[0], wide_cols[0]),
        transpose_product(row_cuts[0], wide_cols[1]),
        transpose_product(row_cuts[0], wide_cols[2]),
        transpose_product(row_cuts[1], wide_cols[3]),
        transpose_product(row_cuts[2], wide_cols[4]),
        transpose_product(row_cuts[2], wide_cols[5]),
        transpose_product(row_cuts[3], wide_cols[6]),
        gain_parts,
        jnp.zeros((group_rows * lax.axis_size("ctx"), 126), jnp.float32),
    ]
    partial_sums = lax.psum_scatter(
        jnp.concatenate(pieces, 1).astype(jnp.bfloat16), "ctx", scatter_dimension=0, tiled=True
    ).astype(jnp.float32)
    owned = lax.all_to_all(
        partial_sums.astype(jnp.bfloat16), "fsdp", split_axis=0, concat_axis=1, tiled=True
    ).astype(partial_sums.dtype)
    span_width = partial_sums.shape[1]
    owned_rows = owned.shape[0]
    arranged = owned.reshape(owned_rows, fsdp_size, span_width)
    model_part = model_width // fsdp_size
    hidden_part = hidden_width // fsdp_size
    bounds = [
        0,
        model_part,
        2 * model_part,
        3 * model_part,
        4 * model_part,
        4 * model_part + hidden_part,
        4 * model_part + 2 * hidden_part,
        4 * model_part + 3 * hidden_part,
    ]

    def joined_cols(first_col, last_col):
        return arranged[:, :, first_col:last_col].reshape(owned_rows, -1)

    grad_w_query = joined_cols(bounds[0], bounds[1])
    grad_w_key = joined_cols(bounds[1], bounds[2])
    grad_w_value = joined_cols(bounds[2], bounds[3])
    grad_w_out = joined_cols(bounds[3], bounds[4])
    grad_w_gate = joined_cols(bounds[4], bounds[5])
    grad_w_up = joined_cols(bounds[5], bounds[6])
    grad_w_down = joined_cols(bounds[6], bounds[7])
    gain_totals = jnp.sum(arranged[:, :, bounds[7] : bounds[7] + 2], 1)
    grad_gain_attn = gain_totals[:, 0]
    grad_gain_mlp = gain_totals[:, 1]
    grad_tokens = grad_input.reshape(slot_count, share_rows, model_width)
    return (
        result,
        grad_tokens,
        grad_w_query,
        grad_w_key,
        grad_w_value,
        grad_w_out,
        grad_w_gate,
        grad_w_up,
        grad_w_down,
        grad_gain_attn,
        grad_gain_mlp,
    )


def dot_f32(a, b):
    return jnp.dot(a, b, preferred_element_type=jnp.float32)

def load_sequence(order_ref, rows_ref, first, block, stores):
    per_src = rows_ref.shape[2] // block
    def one(slot, carry):
        src = slot // per_src
        lane = pl.multiple_of((slot % per_src) * block, block)
        place = pl.multiple_of(order_ref[slot] * block, block)
        for at, store in stores:
            store(rows_ref[src, at:at + HEAD_DIM, pl.ds(lane, block)], place)
        return carry
    lax.fori_loop(0, rows_ref.shape[0] * per_src, one, 0)

def fwd_kernel(order_ref, qkv_ref, mixed_ref, out_ref, lse_ref, qt, kr, vt, *, block, tile):
    seq = qt.shape[1]
    def put_q(x, place):
        qt[:, pl.ds(place, block)] = x * jnp.bfloat16(HEAD_DIM ** -0.5)
    def put_k(x, place):
        kr[pl.ds(place, block), :] = x.T
    def put_v(x, place):
        vt[:, pl.ds(place, block)] = x
    load_sequence(order_ref, qkv_ref, 0, block, ((0, put_q), (HEAD_DIM, put_k), (2 * HEAD_DIM, put_v)))

    def one_tile(qi, unused):
        q0 = pl.multiple_of(qi * tile, tile)
        q = qt[:, pl.ds(q0, tile)]
        def step(k0, state, masked):
            peak, total, acc = state
            s = dot_f32(kr[pl.ds(k0, tile), :], q)
            if masked:
                s = jnp.where(lax.broadcasted_iota(jnp.int32, s.shape, 0) <= lax.broadcasted_iota(jnp.int32, s.shape, 1), s, MASKED_SCORE)
            new_peak = jnp.maximum(peak, jnp.max(s, 0, keepdims=True))
            p = jnp.exp(s - new_peak)
            alpha = jnp.exp(peak - new_peak)
            total = total * alpha + jnp.sum(p, 0, keepdims=True)
            acc = acc * alpha + dot_f32(vt[:, pl.ds(k0, tile)], p.astype(jnp.bfloat16))
            return new_peak, total, acc
        state = (jnp.full((1, tile), MASKED_SCORE, jnp.float32), jnp.zeros((1, tile), jnp.float32), jnp.zeros((HEAD_DIM, tile), jnp.float32))
        state = lax.fori_loop(0, qi, lambda j, st: step(pl.multiple_of(j * tile, tile), st, False), state)
        peak, total, acc = step(q0, state, True)
        out_ref[:, pl.ds(q0, tile)] = acc / total
        lse_ref[:, pl.ds(q0, tile)] = peak + jnp.log(total)
        return unused
    lax.fori_loop(0, seq // tile, one_tile, 0)

    per_src = mixed_ref.shape[2] // block
    def send(slot, carry):
        place = pl.multiple_of(order_ref[slot] * block, block)
        lane = pl.multiple_of((slot % per_src) * block, block)
        mixed_ref[slot // per_src, :, pl.ds(lane, block)] = out_ref[:, pl.ds(place, block)].astype(jnp.bfloat16)
        return carry
    lax.fori_loop(0, mixed_ref.shape[0] * per_src, send, 0)

def attend(order, qkv, block, tile):
    groups, unused, width = qkv.shape
    seq = groups * width
    vm = pl.BlockSpec(memory_space=pltpu.VMEM)
    return pl.pallas_call(
        functools.partial(fwd_kernel, block=block, tile=tile),
        out_shape=(jax.ShapeDtypeStruct((groups, HEAD_DIM, width), jnp.bfloat16),
                   jax.ShapeDtypeStruct((HEAD_DIM, seq), jnp.float32),
                   jax.ShapeDtypeStruct((1, seq), jnp.float32)),
        in_specs=[pl.BlockSpec(memory_space=pltpu.SMEM), vm],
        out_specs=(vm, vm, vm),
        scratch_shapes=[pltpu.VMEM((HEAD_DIM, seq), jnp.bfloat16), pltpu.VMEM((seq, HEAD_DIM), jnp.bfloat16), pltpu.VMEM((HEAD_DIM, seq), jnp.bfloat16)],
        compiler_params=pltpu.CompilerParams(vmem_limit_bytes=40 << 20),
        cost_estimate=pl.CostEstimate(flops=10 * seq * seq * HEAD_DIM * 8, bytes_accessed=8 * seq * HEAD_DIM, transcendentals=seq * seq // 2),
        name="attend",
    )(order, qkv)

def bwd_kernel(order_ref, qkv_ref, go_ref, out_ref, lse_ref, cos_ref, sin_ref, grad_ref,
               qt, qr, kt, kr, vr, got, gor, delta, dqt, dkr, dvr, *, block, tile):
    seq = qt.shape[1]
    scale = jnp.bfloat16(HEAD_DIM ** -0.5)
    def put_q(x, place):
        x = x * scale
        qt[:, pl.ds(place, block)] = x
        qr[pl.ds(place, block), :] = x.T
    def put_k(x, place):
        kt[:, pl.ds(place, block)] = x * scale
        kr[pl.ds(place, block), :] = x.T
    def put_v(x, place):
        vr[pl.ds(place, block), :] = x.T
    def put_go(x, place):
        got[:, pl.ds(place, block)] = x
        gor[pl.ds(place, block), :] = x.T
        delta[:, pl.ds(place, block)] = jnp.sum(x.astype(jnp.float32) * out_ref[:, pl.ds(place, block)], 0, keepdims=True)
    load_sequence(order_ref, qkv_ref, 0, block, ((0, put_q), (HEAD_DIM, put_k), (2 * HEAD_DIM, put_v)))
    load_sequence(order_ref, go_ref, 0, block, ((0, put_go),))
    dqt[...] = jnp.zeros_like(dqt)
    tiles = seq // tile

    def key_tile(kj, unused):
        k0 = pl.multiple_of(kj * tile, tile)
        keys = kr[pl.ds(k0, tile), :]
        keys_t = kt[:, pl.ds(k0, tile)]
        vals = vr[pl.ds(k0, tile), :]
        dkr[...] = jnp.zeros_like(dkr)
        dvr[...] = jnp.zeros_like(dvr)
        def step(q0, masked):
            s = dot_f32(keys, qt[:, pl.ds(q0, tile)])
            p = jnp.exp(s - lse_ref[:, pl.ds(q0, tile)])
            if masked:
                p = jnp.where(lax.broadcasted_iota(jnp.int32, s.shape, 0) <= lax.broadcasted_iota(jnp.int32, s.shape, 1), p, 0.0)
            dp = dot_f32(vals, got[:, pl.ds(q0, tile)])
            ds = (p * (dp - delta[:, pl.ds(q0, tile)])).astype(jnp.bfloat16)
            dvr[...] += dot_f32(p.astype(jnp.bfloat16), gor[pl.ds(q0, tile), :])
            dkr[...] += dot_f32(ds, qr[pl.ds(q0, tile), :])
            dqt[:, pl.ds(q0, tile)] += dot_f32(keys_t, ds)
        step(k0, True)
        def later(qi, c):
            step(pl.multiple_of(qi * tile, tile), False)
            return c
        lax.fori_loop(kj + 1, tiles, later, 0)
        kt_d = dkr[...].T
        vt_d = dvr[...].T
        put_out(kt_d, HEAD_DIM, k0, True)
        put_out(vt_d, 2 * HEAD_DIM, k0, False)
        return unused

    half = HEAD_DIM // 2
    def put_out(x, at, place, turn):
        for part in range(tile // block):
            piece = x[:, part * block:(part + 1) * block]
            here = place + part * block
            if turn:
                lanes = pl.ds(pl.multiple_of(here, block), block)
                c, s = cos_ref[:, lanes], sin_ref[:, lanes]
                a, b = piece[:half], piece[half:]
                piece = jnp.concatenate([a * c + b * s, b * c - a * s], 0)
            slot = order_ref[seq // block + here // block]
            per_src = grad_ref.shape[2] // block
            lane = pl.multiple_of((slot % per_src) * block, block)
            grad_ref[slot // per_src, at:at + HEAD_DIM, pl.ds(lane, block)] = piece.astype(jnp.bfloat16)

    lax.fori_loop(0, tiles, key_tile, 0)
    def write_q(qi, c):
        q0 = pl.multiple_of(qi * tile, tile)
        put_out(dqt[:, pl.ds(q0, tile)], 0, q0, True)
        return c
    lax.fori_loop(0, tiles, write_q, 0)

def attend_back(order, qkv, go, out, lse, cos, sin, block, tile):
    groups, unused, width = qkv.shape
    seq = groups * width
    vm = pl.BlockSpec(memory_space=pltpu.VMEM)
    bf, f32 = jnp.bfloat16, jnp.float32
    wide = lambda t: pltpu.VMEM((HEAD_DIM, seq), t)
    tall = lambda t: pltpu.VMEM((seq, HEAD_DIM), t)
    return pl.pallas_call(
        functools.partial(bwd_kernel, block=block, tile=tile),
        out_shape=jax.ShapeDtypeStruct(qkv.shape, bf),
        in_specs=[pl.BlockSpec(memory_space=pltpu.SMEM)] + [vm] * 6,
        out_specs=vm,
        scratch_shapes=[wide(bf), tall(bf), wide(bf), tall(bf), tall(bf), wide(bf), tall(bf),
                        pltpu.VMEM((1, seq), f32), wide(f32),
                        pltpu.VMEM((tile, HEAD_DIM), f32), pltpu.VMEM((tile, HEAD_DIM), f32)],
        compiler_params=pltpu.CompilerParams(vmem_limit_bytes=48 << 20),
        cost_estimate=pl.CostEstimate(flops=16 * seq * seq * HEAD_DIM * 8, bytes_accessed=16 * seq * HEAD_DIM, transcendentals=seq * seq // 2),
        name="attend_back",
    )(order, qkv, go, out, lse, cos, sin)


def nt_dot(a, b):
    return lax.dot_general(a, b, (((1,), (1,)), ((), ())), preferred_element_type=jnp.float32)


def whole(space=pltpu.VMEM):
    return pl.BlockSpec(memory_space=space)


def spread(pieces, place_ref, rows_ref):
    hops = (len(pieces) - 1) // 2
    slots, share, unused = pieces[0].shape
    place = place_ref[0]

    def put(piece, position):
        for slot in range(slots):
            first = pl.multiple_of(slot * share * (hops + 1) + position * share, share)
            rows_ref[pl.ds(first, share), :] = piece[slot]

    put(pieces[0], place)
    for hop in range(1, hops + 1):

        @pl.when(place >= hop)
        def take_below(hop=hop):
            put(pieces[hop], place - hop)

        @pl.when(place + hop <= hops)
        def take_above(hop=hop):
            put(pieces[hops + hop], place + hop)


def deal(rows_ref, place_ref, own_ref, others):
    slots, share, unused = own_ref.shape
    line = len(others) + 1
    for step, target in enumerate([own_ref] + list(others)):
        position = lax.rem(place_ref[0] + step, line)
        for slot in range(slots):
            first = pl.multiple_of(slot * share * line + position * share, share)
            target[slot] = rows_ref[pl.ds(first, share), :].astype(target.dtype)


def dealt_shapes(slots, share, width, line):
    return [jax.ShapeDtypeStruct((slots, share, width), jnp.float32)] + [
        jax.ShapeDtypeStruct((slots, share, width), jnp.bfloat16) for unused in range(line - 1)
    ]


def work(flops, bytes_accessed=0, transcendentals=0):
    return pl.CostEstimate(
        flops=int(flops), bytes_accessed=int(bytes_accessed), transcendentals=int(transcendentals)
    )


def vmem_limit(mebibytes):
    return pltpu.CompilerParams(vmem_limit_bytes=mebibytes << 20)


def cut_columns(place, group, weights, rows, line):
    count = len(weights)
    columns = weights[0].shape[1] // line

    def kernel(place_ref, group_ref, *refs):
        for step in range(line):
            for i in range(count):
                refs[count * line + step][i] = refs[step * count + i][...]

    def target(step):
        return lambda i, place, group: (group[0], lax.rem(place[0] + step, line))

    return pl.pallas_call(
        kernel,
        out_shape=[jax.ShapeDtypeStruct((count, rows, columns), jnp.bfloat16)] * line,
        grid_spec=pltpu.PrefetchScalarGridSpec(
            num_scalar_prefetch=2,
            grid=(1,),
            in_specs=[
                pl.BlockSpec((rows, columns), target(step))
                for step in range(line)
                for unused in range(count)
            ],
            out_specs=[
                pl.BlockSpec((count, rows, columns), lambda i, place, group: (0, 0, 0))
            ]
            * line,
        ),
        compiler_params=vmem_limit(60),
        name="cut_columns",
    )(place, group, *(list(weights) * line))


def order_shares(place, shares):
    line = len(shares)

    def kernel(place_ref, *refs):
        for step in range(line):
            refs[line][lax.rem(place_ref[0] + line - step, line)] = refs[step][...]

    return pl.pallas_call(
        kernel,
        out_shape=jax.ShapeDtypeStruct((line,) + shares[0].shape, shares[0].dtype),
        in_specs=[whole(pltpu.SMEM)] + [whole()] * line,
        out_specs=whole(),
        compiler_params=vmem_limit(40),
        name="order_shares",
    )(place, *shares)


def widen_columns(place, shares):
    line = len(shares)
    count, rows, columns = shares[0].shape

    def kernel(place_ref, *refs):
        for step in range(line):

            @pl.when(pl.program_id(0) == step)
            def widen(step=step):
                for i in range(count):
                    refs[line + i][...] = refs[step][i].astype(jnp.float32)

    return pl.pallas_call(
        kernel,
        out_shape=[jax.ShapeDtypeStruct((rows, line * columns), jnp.float32)] * count,
        grid_spec=pltpu.PrefetchScalarGridSpec(
            num_scalar_prefetch=1,
            grid=(line,),
            in_specs=[pl.BlockSpec((count, rows, columns), lambda j, place: (0, 0, 0))] * line,
            out_specs=[
                pl.BlockSpec(
                    (rows, columns), lambda j, place: (0, lax.rem(place[0] + line - j, line))
                )
            ]
            * count,
        ),
        compiler_params=vmem_limit(40),
        name="widen_columns",
    )(place, *shares)


def project(place, pieces, gain, w_heads, cosine, sine):
    line, count, part, width = w_heads.shape
    slots, share, model_width = pieces[0].shape
    rows = slots * share * line
    tile = width // 2
    heads = tile // HEAD_DIM
    n_pieces = len(pieces)
    half = HEAD_DIM // 2

    def kernel(place_ref, *refs):
        piece_refs = refs[:n_pieces]
        gain_ref, w_ref, cos_ref, sin_ref, rows_ref, out_ref = refs[n_pieces:]

        @pl.when((pl.program_id(0) == 0) & (pl.program_id(1) == 0))
        def assemble():
            spread(piece_refs, place_ref, rows_ref)
            rows_ref[...] = (rows_ref[...].astype(jnp.float32) * gain_ref[...]).astype(jnp.bfloat16)

        weight = w_ref[...].reshape(line * part, tile)
        turned = dot_f32(rows_ref[...], weight).T
        c, s = cos_ref[0], sin_ref[0]
        for head in range(heads):
            a = turned[head * HEAD_DIM : head * HEAD_DIM + half]
            b = turned[head * HEAD_DIM + half : (head + 1) * HEAD_DIM]
            out_ref[head, 0, :half, :] = (a * c - b * s).astype(jnp.bfloat16)
            out_ref[head, 0, half:, :] = (b * c + a * s).astype(jnp.bfloat16)

    return pl.pallas_call(
        kernel,
        grid=(count, 2),
        out_shape=[
            jax.ShapeDtypeStruct((rows, model_width), jnp.bfloat16),
            jax.ShapeDtypeStruct((width // HEAD_DIM, count, HEAD_DIM, rows), jnp.bfloat16),
        ],
        in_specs=[whole(pltpu.SMEM)]
        + [whole()] * (n_pieces + 1)
        + [
            pl.BlockSpec((line, 1, part, tile), lambda m, h: (0, m, 0, h)),
            pl.BlockSpec((1, half, rows), lambda m, h: (m, 0, 0)),
            pl.BlockSpec((1, half, rows), lambda m, h: (m, 0, 0)),
        ],
        out_specs=[
            pl.BlockSpec((rows, model_width), lambda m, h: (0, 0)),
            pl.BlockSpec((heads, 1, HEAD_DIM, rows), lambda m, h: (h, m, 0, 0)),
        ],
        compiler_params=vmem_limit(48),
        cost_estimate=work(6 * rows * model_width * width, 8 * rows * model_width),
        name="project",
    )(place, *pieces, gain, w_heads, cosine, sine)


def mix_out(place, mixed, w_out, slots, line):
    heads, unused, rows = mixed.shape
    width, model_width = w_out.shape
    share = rows // slots // line

    def kernel(place_ref, mixed_ref, w_ref, own_ref, *rest):
        *others, total = rest
        left = mixed_ref[...].reshape(width, rows).T
        total[...] = dot_f32(left, w_ref[...])
        deal(total, place_ref, own_ref, others)

    return pl.pallas_call(
        kernel,
        out_shape=dealt_shapes(slots, share, model_width, line),
        in_specs=[whole(pltpu.SMEM), whole(), whole()],
        out_specs=[whole()] * line,
        scratch_shapes=[pltpu.VMEM((rows, model_width), jnp.float32)],
        compiler_params=vmem_limit(48),
        cost_estimate=work(2 * rows * model_width * width, 8 * rows * model_width),
        name="mix_out",
    )(place, mixed, w_out)


def mlp_forward(place, pieces, upstream_pieces, w_mlp, tile):
    line, count, part, width = w_mlp.shape
    slots, share, model_width = pieces[0].shape
    rows = slots * share * line
    n_pieces = len(pieces)
    bf, f32 = jnp.bfloat16, jnp.float32

    def kernel(place_ref, *refs):
        x_pieces, u_pieces = refs[:n_pieces], refs[n_pieces : 2 * n_pieces]
        w_ref, x_ref, u_ref, hidden_ref, gate_ref, up_ref, own_ref = refs[
            2 * n_pieces : 2 * n_pieces + 7
        ]
        *others, total = refs[2 * n_pieces + 7 :]
        step = pl.program_id(0)

        @pl.when(step == 0)
        def assemble():
            spread(x_pieces, place_ref, x_ref)
            spread(u_pieces, place_ref, u_ref)

        down = w_ref[:, 0].reshape(line * part, tile)
        gate = w_ref[:, 1].reshape(line * part, tile)
        up = w_ref[:, 2].reshape(line * part, tile)
        x = x_ref[...]
        grad_hidden = dot_f32(u_ref[...], down)
        gate_act = dot_f32(x, gate)
        upward = dot_f32(x, up)
        sigmoid = jax.nn.sigmoid(gate_act)
        silu = gate_act * sigmoid
        hidden_ref[...] = (silu * upward).astype(bf)
        grad_gate = (
            grad_hidden * upward * sigmoid * (1.0 + gate_act * (1.0 - sigmoid))
        ).astype(bf)
        grad_up = (grad_hidden * silu).astype(bf)
        gate_ref[...] = grad_gate
        up_ref[...] = grad_up
        part_two = nt_dot(grad_gate, gate) + nt_dot(grad_up, up)

        @pl.when(step == 0)
        def first():
            total[...] = part_two

        @pl.when(step > 0)
        def further():
            total[...] += part_two

        @pl.when(step == pl.num_programs(0) - 1)
        def last():
            deal(total, place_ref, own_ref, others)

    fixed = lambda shape: pl.BlockSpec(shape, lambda j: (0,) * len(shape))
    columns = pl.BlockSpec((rows, tile), lambda j: (0, j))
    dealt = dealt_shapes(slots, share, model_width, line)
    return pl.pallas_call(
        kernel,
        grid=(width // tile,),
        out_shape=[jax.ShapeDtypeStruct((rows, model_width), bf)] * 2
        + [jax.ShapeDtypeStruct((rows, width), bf)] * 3
        + dealt,
        in_specs=[whole(pltpu.SMEM)]
        + [whole()] * (2 * n_pieces)
        + [pl.BlockSpec((line, count, part, tile), lambda j: (0, 0, 0, j))],
        out_specs=[fixed((rows, model_width))] * 2
        + [columns] * 3
        + [fixed((slots, share, model_width))] * line,
        scratch_shapes=[pltpu.VMEM((rows, model_width), f32)],
        compiler_params=vmem_limit(60),
        cost_estimate=work(10 * rows * model_width * width, 14 * model_width * width),
        name="mlp_forward",
    )(place, *pieces, *upstream_pieces, w_mlp)


def gate_up_weights(x_rows, grad_gate, grad_up, groups, line, tile):
    rows, model_width = x_rows.shape
    width = grad_gate.shape[1]
    block = model_width // groups // line

    def kernel(x_ref, gate_ref, up_ref, out_ref, x_turned):
        @pl.when(pl.program_id(0) == 0)
        def turn():
            x_turned[...] = x_ref[...].T

        for i, ref in enumerate((gate_ref, up_ref)):
            grads = dot_f32(x_turned[...], ref[...]).astype(jnp.bfloat16)
            out_ref[:, :, i] = grads.reshape(groups, line, block, tile)

    columns = pl.BlockSpec((rows, tile), lambda j: (0, j))
    return pl.pallas_call(
        kernel,
        grid=(width // tile,),
        out_shape=jax.ShapeDtypeStruct((groups, line, 2, block, width), jnp.bfloat16),
        in_specs=[pl.BlockSpec((rows, model_width), lambda j: (0, 0)), columns, columns],
        out_specs=pl.BlockSpec((groups, line, 2, block, tile), lambda j: (0, 0, 0, 0, j)),
        scratch_shapes=[pltpu.VMEM((model_width, rows), jnp.bfloat16)],
        compiler_params=vmem_limit(60),
        cost_estimate=work(4 * rows * model_width * width, 8 * model_width * width),
        name="gate_up_weights",
    )(x_rows, grad_gate, grad_up)


def down_weights(place, u_rows, hidden, w_mlp, slots, groups, tile):
    line, count, part, width = w_mlp.shape
    rows, model_width = u_rows.shape
    share = rows // slots // line
    block = model_width // groups // line
    bf, f32 = jnp.bfloat16, jnp.float32

    def kernel(place_ref, u_ref, hidden_ref, w_ref, d_ref, own_ref, *rest):
        *others, u_turned, total = rest
        step = pl.program_id(0)

        @pl.when(step == 0)
        def turn():
            u_turned[...] = u_ref[...].T

        grads = dot_f32(u_turned[...], hidden_ref[...]).astype(bf)
        d_ref[:, :line] = grads.reshape(groups, line, block, tile)
        part_out = nt_dot(hidden_ref[...], w_ref[...].reshape(line * part, tile))

        @pl.when(step == 0)
        def first():
            total[...] = part_out

        @pl.when(step > 0)
        def further():
            total[...] += part_out

        @pl.when(step == pl.num_programs(0) - 1)
        def last():
            deal(total, place_ref, own_ref, others)

    fixed = lambda shape: pl.BlockSpec(shape, lambda j: (0,) * len(shape))
    return pl.pallas_call(
        kernel,
        grid=(width // tile,),
        out_shape=[jax.ShapeDtypeStruct((groups, line + 1, block, width), bf)]
        + dealt_shapes(slots, share, model_width, line),
        in_specs=[
            whole(pltpu.SMEM),
            fixed((rows, model_width)),
            pl.BlockSpec((rows, tile), lambda j: (0, j)),
            pl.BlockSpec((line, 1, part, tile), lambda j: (0, 0, 0, j)),
        ],
        out_specs=[pl.BlockSpec((groups, line + 1, block, tile), lambda j: (0, 0, 0, j))]
        + [fixed((slots, share, model_width))] * line,
        scratch_shapes=[pltpu.VMEM((model_width, rows), bf), pltpu.VMEM((rows, model_width), f32)],
        compiler_params=vmem_limit(60),
        cost_estimate=work(4 * rows * model_width * width, 8 * model_width * width),
        name="down_weights",
    )(place, u_rows, hidden, w_mlp)


def branch_back(place, pieces, w_out, heads):
    slots, share, model_width = pieces[0].shape
    line = (len(pieces) + 1) // 2
    rows = slots * share * line

    def kernel(place_ref, *refs):
        *piece_refs, w_ref, rows_ref, out_ref = refs
        spread(piece_refs, place_ref, rows_ref)
        turned = nt_dot(w_ref[...], rows_ref[...])
        out_ref[...] = turned.astype(jnp.bfloat16).reshape(out_ref.shape)

    return pl.pallas_call(
        kernel,
        out_shape=[
            jax.ShapeDtypeStruct((rows, model_width), jnp.bfloat16),
            jax.ShapeDtypeStruct((heads, HEAD_DIM, rows), jnp.bfloat16),
        ],
        in_specs=[whole(pltpu.SMEM)] + [whole()] * (len(pieces) + 1),
        out_specs=[whole(), whole()],
        compiler_params=vmem_limit(40),
        cost_estimate=work(2 * rows * model_width * heads * HEAD_DIM, 8 * rows * model_width),
        name="branch_back",
    )(place, *pieces, w_out)


def out_weight(grads, mixed, branch_rows, tile):
    groups, blocks, block, width = grads.shape
    heads, unused, rows = mixed.shape

    def kernel(grads_ref, mixed_ref, rows_ref, out_ref):
        left = mixed_ref[...].reshape(heads * HEAD_DIM, rows)
        out_ref[...] = (
            dot_f32(left, rows_ref[...]).astype(jnp.bfloat16).reshape(groups, 1, block, tile)
        )

    return pl.pallas_call(
        kernel,
        grid=(width // tile,),
        out_shape=jax.ShapeDtypeStruct(grads.shape, grads.dtype),
        in_specs=[
            pl.BlockSpec(memory_space=pl.ANY),
            pl.BlockSpec(mixed.shape, lambda j: (0, 0, 0)),
            pl.BlockSpec((rows, tile), lambda j: (0, j)),
        ],
        out_specs=pl.BlockSpec((groups, 1, block, tile), lambda j: (0, blocks - 1, 0, j)),
        input_output_aliases={0: 0},
        compiler_params=vmem_limit(60),
        cost_estimate=work(2 * rows * heads * HEAD_DIM * width, 8 * rows * width),
        name="out_weight",
    )(grads, mixed, branch_rows)


def head_weights(x_rows, head_grads, groups, line):
    rows, model_width = x_rows.shape
    heads, count, unused, unused_rows = head_grads.shape
    width = heads * HEAD_DIM
    block = model_width // groups // line

    def kernel(x_ref, g_ref, out_ref, x_turned):
        @pl.when(pl.program_id(0) == 0)
        def turn():
            x_turned[...] = x_ref[...].T

        grads = g_ref[...].reshape(width, rows)
        out_ref[...] = (
            nt_dot(x_turned[...], grads).astype(jnp.bfloat16).reshape(out_ref.shape)
        )

    return pl.pallas_call(
        kernel,
        grid=(count,),
        out_shape=jax.ShapeDtypeStruct((groups, line, count, block, width), jnp.bfloat16),
        in_specs=[
            pl.BlockSpec((rows, model_width), lambda m: (0, 0)),
            pl.BlockSpec((heads, 1, HEAD_DIM, rows), lambda m: (0, m, 0, 0)),
        ],
        out_specs=pl.BlockSpec((groups, line, 1, block, width), lambda m: (0, 0, m, 0, 0)),
        scratch_shapes=[pltpu.VMEM((model_width, rows), jnp.bfloat16)],
        compiler_params=vmem_limit(60),
        cost_estimate=work(2 * count * rows * width * model_width, 8 * rows * model_width),
        name="head_weights",
    )(x_rows, head_grads)


def project_back(place, x_rows, head_grads, w_heads, slots):
    line, count, part, width = w_heads.shape
    rows, model_width = x_rows.shape
    heads = width // HEAD_DIM
    share = rows // slots // line

    def kernel(place_ref, x_ref, g_ref, w_ref, gain_ref, own_ref, *rest):
        *others, total = rest
        m = pl.program_id(0)
        grads = g_ref[...].reshape(width, rows).T
        partial = nt_dot(grads, w_ref[...].reshape(line * part, width))

        @pl.when(m == 0)
        def first():
            total[...] = partial

        @pl.when(m > 0)
        def further():
            total[...] += partial

        @pl.when(m == count - 1)
        def last():
            deal(total, place_ref, own_ref, others)
            gain_ref[...] = jnp.sum(
                total[...] * x_ref[...].astype(jnp.float32), 0, keepdims=True
            )

    fixed = lambda shape: pl.BlockSpec(shape, lambda m: (0,) * len(shape))
    return pl.pallas_call(
        kernel,
        grid=(count,),
        out_shape=[jax.ShapeDtypeStruct((1, model_width), jnp.float32)]
        + dealt_shapes(slots, share, model_width, line),
        in_specs=[
            whole(pltpu.SMEM),
            fixed((rows, model_width)),
            pl.BlockSpec((heads, 1, HEAD_DIM, rows), lambda m: (0, m, 0, 0)),
            pl.BlockSpec((line, 1, part, width), lambda m: (0, m, 0, 0)),
        ],
        out_specs=[fixed((1, model_width))] + [fixed((slots, share, model_width))] * line,
        scratch_shapes=[pltpu.VMEM((rows, model_width), jnp.float32)],
        compiler_params=vmem_limit(48),
        cost_estimate=work(2 * count * rows * width * model_width, 8 * rows * model_width),
        name="project_back",
    )(place, x_rows, head_grads, w_heads)


def line_steps(size, step):
    return [(i, i + step) for i in range(size) if 0 <= i + step < size]


def after(values, *earlier):
    return lax.optimization_barrier((values, earlier))[0]


def send_shares(share, axis):
    size = lax.axis_size(axis)
    ups, downs = [share], [share]
    for hop in range(1, size):
        ups.append(lax.ppermute(ups[-1], axis, line_steps(size, 1)[hop - 1 :]))
        downs.append(lax.ppermute(downs[-1], axis, line_steps(size, -1)[: size - hop]))
    return ups + downs[1:]


def gather_line(share, axis):
    size = lax.axis_size(axis)
    ups = [lax.ppermute(share, axis, line_steps(size, hop)) for hop in range(1, size)]
    downs = [lax.ppermute(share, axis, line_steps(size, -hop)) for hop in range(1, size)]
    window = jnp.stack(ups[::-1] + [share] + downs)
    return lax.dynamic_slice_in_dim(window, size - 1 - lax.axis_index(axis), size, 0)


def send_dealt(others, axis):
    size = lax.axis_size(axis)
    return [
        lax.ppermute(other, axis, [(i, (i + step) % size) for i in range(size)])
        for step, other in enumerate(others, 1)
    ]


def scatter_line(own, others, axis):
    size = lax.axis_size(axis)
    up = down = None
    for hop in range(1, size):
        rising, falling = others[size - hop - 1], others[hop - 1]
        if hop > 1:
            rising = (rising.astype(jnp.float32) + up.astype(jnp.float32)).astype(rising.dtype)
            falling = (falling.astype(jnp.float32) + down.astype(jnp.float32)).astype(falling.dtype)
        up = lax.ppermute(rising, axis, line_steps(size, 1)[:hop])
        down = lax.ppermute(falling, axis, line_steps(size, -1)[size - 1 - hop :])
    return [up, down]


def add_shares(own, received):
    return own + sum(share.astype(jnp.float32) for share in received)


def swap_dealt(shares):
    return [shares[0]] + send_dealt(shares[1:], "fsdp")


def deal_line(parts, place):
    line = parts.shape[0]
    return [
        lax.dynamic_index_in_dim(parts, lax.rem(place[0] + step, line), 0, keepdims=False)
        for step in range(line)
    ]


def swap_heads(parts):
    return lax.all_to_all(parts, "ctx", split_axis=0, concat_axis=0, tiled=True)


def sum_groups(parts):
    return lax.psum_scatter(parts, "ctx", scatter_dimension=0, tiled=True)[0]


def head_device(
    tokens,
    block_order,
    w_query,
    w_key,
    w_value,
    w_out,
    w_gate,
    w_up,
    w_down,
    gain_attn,
    gain_mlp,
    cotangent,
):
    slots, share_rows, model_width = tokens.shape
    ctx_size, line = lax.axis_size("ctx"), lax.axis_size("fsdp")
    block_rows = share_rows * line
    group_rows = slots * block_rows
    bf, f32 = jnp.bfloat16, jnp.float32
    place = lax.axis_index("fsdp").astype(jnp.int32).reshape(1)
    group = lax.axis_index("ctx").astype(jnp.int32).reshape(1)
    own_rows = w_query.shape[0] // ctx_size
    order = block_order.astype(jnp.int32)
    slot_of = jnp.sum(
        jnp.where(order[None, :] == jnp.arange(order.shape[0])[:, None], jnp.arange(order.shape[0], dtype=jnp.int32)[None, :], 0), 1
    ).astype(jnp.int32)

    gains = gather_line(jnp.stack([gain_attn, gain_mlp]), "fsdp")
    gains = jnp.swapaxes(gains, 0, 1).reshape(2, model_width).astype(f32)
    attn_gain, mlp_gain = gains[0], gains[1]

    stream = tokens.astype(f32)
    root_one = lax.rsqrt(jnp.mean(stream * stream, -1, keepdims=True) + EPSILON)
    norm_one = stream * root_one
    head_cuts = swap_dealt(cut_columns(place, group, [w_query, w_key, w_value], own_rows, line))
    w_heads = lax.all_gather(order_shares(place, head_cuts), "ctx", axis=2, tiled=True)

    attn_pieces = send_shares(after(norm_one.astype(bf), head_cuts, gains), "fsdp")

    mlp_cuts = cut_columns(place, group, [w_down, w_gate, w_up], own_rows, line)
    mlp_cuts = swap_dealt(after(mlp_cuts, attn_pieces))

    half = HEAD_DIM // 2
    frequency = 1.0 / ROPE_BASE ** (jnp.arange(half, dtype=f32) * (2.0 / HEAD_DIM))
    places = jnp.arange(group_rows * ctx_size, dtype=jnp.int32).astype(f32)
    angles = frequency[:, None] * places[None, :]
    cosine, sine = jnp.cos(angles), jnp.sin(angles)

    def own_columns(table):
        return jnp.concatenate(
            [
                lax.dynamic_slice_in_dim(
                    table, order[slots * group[0] + i] * block_rows, block_rows, 1
                )
                for i in range(slots)
            ],
            1,
        )

    own_cosine, own_sine = own_columns(cosine), own_columns(sine)
    turn_cosine = jnp.stack([own_cosine, own_cosine, jnp.ones_like(own_cosine)])
    turn_sine = jnp.stack([own_sine, own_sine, jnp.zeros_like(own_sine)])

    attn_rows, heads_out = project(
        place, attn_pieces, attn_gain[None], w_heads, turn_cosine, turn_sine
    )
    head_rows = swap_heads(heads_out.reshape(ctx_size, 3 * HEAD_DIM, group_rows))
    mixed_send, attended, log_total = attend(order, head_rows, block_rows, 2 * block_rows)
    mlp_cuts = order_shares(place, after(mlp_cuts, mixed_send))
    w_mlp = lax.all_gather(mlp_cuts, "ctx", axis=2, tiled=True)
    mixed = swap_heads(after(mixed_send, mlp_cuts))
    own, *others = mix_out(place, mixed, w_out, slots, line)
    middle = stream + add_shares(own, scatter_line(own, others, "fsdp"))

    root_two = lax.rsqrt(jnp.mean(middle * middle, -1, keepdims=True) + EPSILON)
    norm_two = middle * root_two
    mlp_input = (norm_two * mlp_gain).astype(bf)
    mlp_pieces = send_shares(mlp_input, "fsdp")
    upstream_pieces = send_shares(after(cotangent, mlp_pieces), "fsdp")

    mlp_rows, upstream_rows, hidden, grad_gate, grad_up, own, *others = mlp_forward(
        place, mlp_pieces, upstream_pieces, w_mlp, 256
    )
    two_received = scatter_line(own, others, "fsdp")
    gate_up_grads = gate_up_weights(mlp_rows, grad_gate, grad_up, ctx_size, line, 256)
    gate_up_sums = sum_groups(gate_up_grads)
    down_grads, own_out, *others_out = down_weights(
        place, upstream_rows, after(hidden, gate_up_grads), w_mlp, slots, ctx_size, 256
    )

    grad_two = add_shares(own, after(two_received, own_out))
    gain_two_part = jnp.sum(grad_two * norm_two, (0, 1))
    grad_middle = cotangent.astype(f32) + norm_back(grad_two, norm_two, root_two, mlp_gain)
    branch_pieces = send_shares(grad_middle.astype(bf), "fsdp")
    branch_rows, grad_mixed = branch_back(place, branch_pieces, w_out, ctx_size)
    out_received = send_dealt(after(others_out, branch_pieces), "fsdp")
    grad_heads = swap_heads(grad_mixed)
    down_grads = out_weight(down_grads, mixed, branch_rows, 512)
    down_sums = sum_groups(after(down_grads, gate_up_sums))

    head_grads = attend_back(
        jnp.concatenate([order, slot_of]),
        head_rows,
        after(grad_heads, down_grads, gate_up_sums),
        attended,
        log_total,
        cosine,
        sine,
        block_rows,
        2 * block_rows,
    )
    gate_up_dealt = deal_line(gate_up_sums, place)
    lin_grads = swap_heads(after(head_grads, out_received, gate_up_dealt))
    lin_grads = lin_grads.reshape(ctx_size, 3, HEAD_DIM, group_rows)
    gate_up_back = swap_dealt(gate_up_dealt)
    head_weight_grads = head_weights(attn_rows, lin_grads, ctx_size, line)
    gain_one_part, own, *others = project_back(
        place, attn_rows, after(lin_grads, head_weight_grads), w_heads, slots
    )
    one_received = scatter_line(own, others, "fsdp")
    down_sums = after(down_sums, own)
    down_back = swap_dealt(deal_line(down_sums[:line, None], place))
    head_sums = sum_groups(after(head_weight_grads, down_sums))
    grad_one = add_shares(own, after(one_received, gate_up_back))
    grad_tokens = grad_middle + norm_back(grad_one, norm_one, root_one, attn_gain)
    result = (middle + add_shares(own_out, out_received)).astype(bf)

    grad_w_gate, grad_w_up = widen_columns(place, gate_up_back)
    (grad_w_down,) = widen_columns(place, down_back)
    head_back = swap_dealt(deal_line(after(head_sums, grad_one), place))
    grad_w_query, grad_w_key, grad_w_value = widen_columns(place, head_back)
    owners = [(c * line + f, f * ctx_size + c) for c in range(ctx_size) for f in range(line)]
    grad_w_out = lax.ppermute(down_sums[line], ("ctx", "fsdp"), owners).astype(f32)

    gain_parts = jnp.stack([gain_one_part[0] / attn_gain, gain_two_part])
    gain_parts = jnp.swapaxes(gain_parts.reshape(2, ctx_size * line, -1), 0, 1)
    gain_parts = lax.all_to_all(
        gain_parts.reshape(ctx_size * line, -1),
        ("ctx", "fsdp"),
        split_axis=0,
        concat_axis=0,
        tiled=True,
    )
    gain_grads = jnp.sum(gain_parts, 0).reshape(2, -1)
    return (
        result,
        grad_tokens,
        grad_w_query,
        grad_w_key,
        grad_w_value,
        grad_w_out,
        grad_w_gate,
        grad_w_up,
        grad_w_down,
        gain_grads[0],
        gain_grads[1],
    )


def layer_step(*arrays):
    heads_here = arrays[0].shape[-1] // lax.axis_size("fsdp") // HEAD_DIM
    if heads_here == lax.axis_size("ctx"):
        return head_device(*arrays)
    return per_device(*arrays)


def solution(mesh):
    in_specs = (
        P("ctx", "fsdp", None),
        P(),
        P("fsdp", None),
        P("fsdp", None),
        P("fsdp", None),
        P("fsdp", None),
        P("fsdp", None),
        P("fsdp", None),
        P("fsdp", None),
        P("fsdp"),
        P("fsdp"),
        P("ctx", "fsdp", None),
    )
    out_specs = (
        P("ctx", "fsdp", None),
        P("ctx", "fsdp", None),
        P(("ctx", "fsdp"), None),
        P(("ctx", "fsdp"), None),
        P(("ctx", "fsdp"), None),
        P(("ctx", "fsdp"), None),
        P(("ctx", "fsdp"), None),
        P(("ctx", "fsdp"), None),
        P(("ctx", "fsdp"), None),
        P(("ctx", "fsdp")),
        P(("ctx", "fsdp")),
    )
    return jax.shard_map(
        layer_step, mesh=mesh, in_specs=in_specs, out_specs=out_specs, check_vma=False
    )
```

```python
import functools

import jax
import jax.numpy as jnp
from jax import lax
from jax.experimental import pallas as pl
from jax.experimental.pallas import tpu as pltpu
from jax.sharding import PartitionSpec as P

HEAD_DIM = 64


EPSILON = 1e-05
ROPE_BASE = 130000.0
MASKED_SCORE = -1e30


def rotate(values, places, direction):
    half_dim = values.shape[-1] // 2
    frequency = 1.0 / ROPE_BASE ** (
        jnp.arange(half_dim, dtype=jnp.float32) * (2.0 / values.shape[-1])
    )
    angles = places[..., None] * frequency
    cosine = jnp.cos(angles)[..., None, :]
    sine_part = direction * jnp.sin(angles)[..., None, :]
    leading = values[..., :half_dim]
    trailing = values[..., half_dim:]
    return jnp.concatenate(
        [leading * cosine - trailing * sine_part, trailing * cosine + leading * sine_part], -1
    )


def matmul(left, right):
    return jnp.dot(left, right, preferred_element_type=jnp.float32)


def contract(left, right):
    return lax.dot_general(
        left, right, (((1,), (1,)), ((), ())), preferred_element_type=jnp.float32
    )


def transpose_product(left, right):
    return lax.dot_general(
        left, right, (((0,), (0,)), ((), ())), preferred_element_type=jnp.float32
    )


def split_heads(values):
    return values.reshape(values.shape[:-1] + (-1, HEAD_DIM))


def keep_state(current):
    return current


def tile_scores(queries, key_rows, query_places, key_places, score_scale):
    scores = (
        jnp.einsum("qhd,khd->hqk", queries, key_rows, preferred_element_type=jnp.float32)
        * score_scale
    )
    allowed = (key_places[None, :] <= query_places[:, None])[None]
    return (jnp.where(allowed, scores, MASKED_SCORE), allowed)


def grow_state(current, queries, key_rows, value_rows, query_places, key_places, score_scale):
    run_peak, run_total, summed = current
    scores, allowed = tile_scores(queries, key_rows, query_places, key_places, score_scale)
    new_peak = jnp.maximum(run_peak, jnp.max(scores, -1))
    weights = jnp.where(allowed, jnp.exp(scores - new_peak[..., None]), 0.0)
    factor = jnp.exp(run_peak - new_peak)
    run_total = run_total * factor + jnp.sum(weights, -1)
    summed = summed * jnp.transpose(factor)[:, :, None] + jnp.einsum(
        "hqk,khd->qhd", weights.astype(jnp.bfloat16), value_rows, preferred_element_type=jnp.float32
    )
    return (new_peak, run_total, summed)


def backward_tile(
    queries,
    key_rows,
    value_rows,
    grad_out,
    log_total,
    row_delta,
    query_places,
    key_places,
    score_scale,
):
    scores, allowed = tile_scores(queries, key_rows, query_places, key_places, score_scale)
    probabilities = jnp.where(allowed, jnp.exp(scores - log_total[..., None]), 0.0)
    grad_probs = jnp.einsum(
        "qhd,khd->hqk", grad_out, value_rows, preferred_element_type=jnp.float32
    )
    grad_scores = (probabilities * (grad_probs - row_delta[..., None])).astype(jnp.bfloat16)
    return (probabilities, grad_scores)


def norm_back(grad_normed_in, normed_values, inverse_root, gain_vector):
    scaled = grad_normed_in * gain_vector
    return inverse_root * (
        scaled - normed_values * jnp.mean(scaled * normed_values, -1, keepdims=True)
    )


def per_device(
    tokens,
    block_order,
    w_query,
    w_key,
    w_value,
    w_out,
    w_gate,
    w_up,
    w_down,
    gain_attn,
    gain_mlp,
    cotangent,
):
    slot_count, share_rows, model_width = tokens.shape
    fsdp_size = lax.axis_size("fsdp")
    block_rows = share_rows * fsdp_size
    head_width = model_width // fsdp_size
    heads_here = head_width // HEAD_DIM
    row_count = slot_count * share_rows
    score_scale = HEAD_DIM ** (-0.5)
    own_slots = 2 * lax.axis_index("ctx") + jnp.arange(2, dtype=jnp.int32)
    own_blocks = block_order[own_slots]
    token_places = (
        (
            own_blocks[:, None] * block_rows
            + lax.axis_index("fsdp") * share_rows
            + jnp.arange(share_rows, dtype=jnp.int32)[None, :]
        )
        .astype(jnp.float32)
        .reshape(row_count)
    )
    head_places = (
        own_blocks[:, None] * block_rows + jnp.arange(block_rows, dtype=jnp.int32)[None, :]
    ).astype(jnp.float32)
    params = (w_query, w_key, w_value, w_out, w_gate, w_up, w_down, gain_attn, gain_mlp)
    weights_all = (
        lax.all_gather(params[0], "fsdp", axis=0, tiled=True),
        lax.all_gather(params[1], "fsdp", axis=0, tiled=True),
        lax.all_gather(params[2], "fsdp", axis=0, tiled=True),
        lax.all_gather(params[3], "fsdp", axis=0, tiled=True),
        lax.all_gather(params[4], "fsdp", axis=0, tiled=True),
        lax.all_gather(params[5], "fsdp", axis=0, tiled=True),
        lax.all_gather(params[6], "fsdp", axis=0, tiled=True),
        lax.all_gather(params[7], "fsdp", axis=0, tiled=True),
        lax.all_gather(params[8], "fsdp", axis=0, tiled=True),
    )
    stream = tokens.reshape(row_count, model_width).astype(jnp.float32)
    root_one = lax.rsqrt(jnp.mean(stream * stream, -1, keepdims=True) + EPSILON)
    norm_one = stream * root_one
    attn_input = (norm_one * weights_all[7].astype(jnp.float32)).astype(jnp.bfloat16)

    def project_turn(weight):
        linear = matmul(attn_input, weight).reshape(row_count, -1, HEAD_DIM)
        return (
            rotate(linear, token_places, 1.0)
            .astype(jnp.bfloat16)
            .reshape(slot_count, share_rows, model_width)
        )

    query_tok = project_turn(weights_all[0])
    key_tok = project_turn(weights_all[1])
    value_tok = (
        matmul(attn_input, weights_all[2])
        .astype(jnp.bfloat16)
        .reshape(slot_count, share_rows, model_width)
    )
    query_heads, key_heads, value_heads = (
        lax.all_to_all(query_tok, "fsdp", split_axis=2, concat_axis=1, tiled=True),
        lax.all_to_all(key_tok, "fsdp", split_axis=2, concat_axis=1, tiled=True),
        lax.all_to_all(value_tok, "fsdp", split_axis=2, concat_axis=1, tiled=True),
    )
    query_split = split_heads(query_heads)
    start_state = tuple(
        (
            (
                jnp.full((heads_here, block_rows), MASKED_SCORE, jnp.float32),
                jnp.zeros((heads_here, block_rows), jnp.float32),
                jnp.zeros((block_rows, heads_here, HEAD_DIM), jnp.float32),
            )
            for which_slot in range(2)
        )
    )
    carried = start_state
    key_part = lax.all_gather(key_heads, "ctx", axis=0, tiled=True)
    value_part = lax.all_gather(value_heads, "ctx", axis=0, tiled=True)

    def visit_slot(inner_state, element):
        key_one, value_one, offset = element
        key_block = block_order[offset]
        key_places = (key_block * block_rows + jnp.arange(block_rows, dtype=jnp.int32)).astype(
            jnp.float32
        )
        key_split = split_heads(key_one)
        value_split = split_heads(value_one)
        updated = []
        for which_slot in range(2):

            def grow_one(current, which_slot=which_slot):
                return grow_state(
                    current,
                    query_split[which_slot],
                    key_split,
                    value_split,
                    head_places[which_slot],
                    key_places,
                    score_scale,
                )

            updated.append(
                lax.cond(
                    key_block <= own_blocks[which_slot],
                    grow_one,
                    keep_state,
                    inner_state[which_slot],
                )
            )
        return (tuple(updated), None)

    offsets = jnp.arange(key_part.shape[0], dtype=jnp.int32)
    carried, unused = lax.scan(visit_slot, carried, (key_part, value_part, offsets))
    attended_parts = []
    log_parts = []
    for which_slot in range(2):
        run_peak, run_total, summed = carried[which_slot]
        log_parts.append(run_peak + jnp.log(run_total))
        attended_parts.append(summed / jnp.transpose(run_total)[:, :, None])
    attended = jnp.stack(attended_parts)
    log_total = jnp.stack(log_parts)
    mixed_send = attended.reshape(slot_count, block_rows, head_width).astype(jnp.bfloat16)
    mixed_tok = lax.all_to_all(mixed_send, "fsdp", split_axis=1, concat_axis=2, tiled=True)
    mixed_flat = mixed_tok.reshape(row_count, model_width)
    middle = stream + matmul(mixed_flat, weights_all[3])
    root_two = lax.rsqrt(jnp.mean(middle * middle, -1, keepdims=True) + EPSILON)
    norm_two = middle * root_two
    mlp_input = (norm_two * weights_all[8].astype(jnp.float32)).astype(jnp.bfloat16)
    gate_act = matmul(mlp_input, weights_all[4])
    upward = matmul(mlp_input, weights_all[5])
    gate_sigmoid = jax.nn.sigmoid(gate_act)
    gate_silu = gate_act * gate_sigmoid
    hidden = (gate_silu * upward).astype(jnp.bfloat16)
    output = middle + contract(hidden, weights_all[6])
    result = output.astype(jnp.bfloat16).reshape(slot_count, share_rows, model_width)
    upstream = cotangent.reshape(row_count, model_width)
    grad_hidden = matmul(upstream, weights_all[6])
    grad_gate = (
        grad_hidden * upward * gate_sigmoid * (1.0 + gate_act * (1.0 - gate_sigmoid))
    ).astype(jnp.bfloat16)
    grad_up = (grad_hidden * gate_silu).astype(jnp.bfloat16)
    grad_two = contract(grad_gate, weights_all[4]) + contract(grad_up, weights_all[5])
    gain_two_part = jnp.sum(grad_two * norm_two, 0)
    grad_middle = upstream.astype(jnp.float32) + norm_back(
        grad_two, norm_two, root_two, weights_all[8].astype(jnp.float32)
    )
    grad_branch = grad_middle.astype(jnp.bfloat16)
    grad_mixed = (
        contract(grad_branch, weights_all[3])
        .astype(jnp.bfloat16)
        .reshape(slot_count, share_rows, model_width)
    )
    grad_heads = lax.all_to_all(grad_mixed, "fsdp", split_axis=2, concat_axis=1, tiled=True)
    grad_split = split_heads(grad_heads)
    row_delta = jnp.transpose(jnp.sum(grad_split.astype(jnp.float32) * attended, -1), (0, 2, 1))
    gathered = (
        lax.all_gather(key_heads, "ctx", axis=0, tiled=True),
        lax.all_gather(value_heads, "ctx", axis=0, tiled=True),
    )
    key_all, value_all = gathered
    total_slots = key_all.shape[0]

    def query_visit(current, element):
        key_pair, value_pair, pair_index = element
        updated = list(current)
        for member in range(2):
            key_block = block_order[2 * pair_index + member]
            key_places = (key_block * block_rows + jnp.arange(block_rows, dtype=jnp.int32)).astype(
                jnp.float32
            )
            key_split = split_heads(key_pair[member])
            value_split = split_heads(value_pair[member])
            for which_slot in range(2):

                def take_query(
                    accum,
                    which_slot=which_slot,
                    key_split=key_split,
                    value_split=value_split,
                    key_places=key_places,
                ):
                    probabilities, grad_scores = backward_tile(
                        query_split[which_slot],
                        key_split,
                        value_split,
                        grad_split[which_slot],
                        log_total[which_slot],
                        row_delta[which_slot],
                        head_places[which_slot],
                        key_places,
                        score_scale,
                    )
                    return accum + score_scale * jnp.einsum(
                        "hqk,khd->qhd", grad_scores, key_split, preferred_element_type=jnp.float32
                    )

                updated[which_slot] = lax.cond(
                    key_block <= own_blocks[which_slot], take_query, keep_state, updated[which_slot]
                )
        return (tuple(updated), None)

    query_zero = jnp.zeros((block_rows, heads_here, HEAD_DIM), jnp.float32)
    pair_keys = key_all.reshape(total_slots // 2, 2, block_rows, head_width)
    pair_values = value_all.reshape(total_slots // 2, 2, block_rows, head_width)
    grad_query_parts, unused = lax.scan(
        query_visit,
        (query_zero, query_zero),
        (pair_keys, pair_values, jnp.arange(total_slots // 2, dtype=jnp.int32)),
    )
    key_part = key_all
    value_part = value_all

    def key_visit(unused_carry, element):
        key_one, value_one, offset = element
        key_block = block_order[offset]
        key_places = (key_block * block_rows + jnp.arange(block_rows, dtype=jnp.int32)).astype(
            jnp.float32
        )
        key_split = split_heads(key_one)
        value_split = split_heads(value_one)
        sums = (
            jnp.zeros((block_rows, heads_here, HEAD_DIM), jnp.float32),
            jnp.zeros((block_rows, heads_here, HEAD_DIM), jnp.float32),
        )
        for which_slot in range(2):

            def take_keys(current, which_slot=which_slot):
                probabilities, grad_scores = backward_tile(
                    query_split[which_slot],
                    key_split,
                    value_split,
                    grad_split[which_slot],
                    log_total[which_slot],
                    row_delta[which_slot],
                    head_places[which_slot],
                    key_places,
                    score_scale,
                )
                grad_key = current[0] + score_scale * jnp.einsum(
                    "hqk,qhd->khd",
                    grad_scores,
                    query_split[which_slot],
                    preferred_element_type=jnp.float32,
                )
                grad_value = current[1] + jnp.einsum(
                    "hqk,qhd->khd",
                    probabilities.astype(jnp.bfloat16),
                    grad_split[which_slot],
                    preferred_element_type=jnp.float32,
                )
                return (grad_key, grad_value)

            sums = lax.cond(key_block <= own_blocks[which_slot], take_keys, keep_state, sums)
        joined = jnp.concatenate(
            [sums[0].reshape(block_rows, head_width), sums[1].reshape(block_rows, head_width)], -1
        )
        return (unused_carry, joined)

    unused_final, terms = lax.scan(
        key_visit,
        jnp.zeros((), jnp.float32),
        (key_part, value_part, jnp.arange(slot_count * lax.axis_size("ctx"), dtype=jnp.int32)),
    )
    summed_kv = lax.psum_scatter(
        terms.astype(jnp.bfloat16), "ctx", scatter_dimension=0, tiled=True
    ).astype(jnp.float32)
    grad_keys = (
        rotate(split_heads(summed_kv[..., :head_width]), head_places, -1.0)
        .astype(jnp.bfloat16)
        .reshape(slot_count, block_rows, head_width)
    )
    grad_values = summed_kv[..., head_width:].astype(jnp.bfloat16)
    grad_queries = (
        rotate(jnp.stack(grad_query_parts), head_places, -1.0)
        .astype(jnp.bfloat16)
        .reshape(slot_count, block_rows, head_width)
    )
    grad_q_tok, grad_k_tok, grad_v_tok = (
        lax.all_to_all(grad_queries, "fsdp", split_axis=1, concat_axis=2, tiled=True),
        lax.all_to_all(grad_keys, "fsdp", split_axis=1, concat_axis=2, tiled=True),
        lax.all_to_all(grad_values, "fsdp", split_axis=1, concat_axis=2, tiled=True),
    )
    grad_q_lin = grad_q_tok.reshape(row_count, model_width)
    grad_k_lin = grad_k_tok.reshape(row_count, model_width)
    grad_v_lin = grad_v_tok.reshape(row_count, model_width)
    grad_one = (
        contract(grad_q_lin, weights_all[0])
        + contract(grad_k_lin, weights_all[1])
        + contract(grad_v_lin, weights_all[2])
    )
    gain_one_part = jnp.sum(grad_one * norm_one, 0)
    grad_input = grad_middle + norm_back(
        grad_one, norm_one, root_one, weights_all[7].astype(jnp.float32)
    )
    hidden_width = hidden.shape[1]
    gain_parts = jnp.stack([gain_one_part, gain_two_part], 1)
    wide_cols = (
        lax.all_to_all(grad_q_lin, "fsdp", split_axis=1, concat_axis=0, tiled=True),
        lax.all_to_all(grad_k_lin, "fsdp", split_axis=1, concat_axis=0, tiled=True),
        lax.all_to_all(grad_v_lin, "fsdp", split_axis=1, concat_axis=0, tiled=True),
        lax.all_to_all(grad_branch, "fsdp", split_axis=1, concat_axis=0, tiled=True),
        lax.all_to_all(grad_gate, "fsdp", split_axis=1, concat_axis=0, tiled=True),
        lax.all_to_all(grad_up, "fsdp", split_axis=1, concat_axis=0, tiled=True),
        lax.all_to_all(hidden, "fsdp", split_axis=1, concat_axis=0, tiled=True),
    )
    row_sets = (
        lax.all_gather(attn_input, "fsdp", axis=0, tiled=True),
        lax.all_gather(mixed_flat, "fsdp", axis=0, tiled=True),
        lax.all_gather(mlp_input, "fsdp", axis=0, tiled=True),
        lax.all_gather(upstream, "fsdp", axis=0, tiled=True),
    )
    group_rows = model_width // lax.axis_size("ctx")
    row_cuts = [values for values in row_sets]
    pieces = [
        transpose_product(row_cuts[0], wide_cols[0]),
        transpose_product(row_cuts[0], wide_cols[1]),
        transpose_product(row_cuts[0], wide_cols[2]),
        transpose_product(row_cuts[1], wide_cols[3]),
        transpose_product(row_cuts[2], wide_cols[4]),
        transpose_product(row_cuts[2], wide_cols[5]),
        transpose_product(row_cuts[3], wide_cols[6]),
        gain_parts,
        jnp.zeros((group_rows * lax.axis_size("ctx"), 126), jnp.float32),
    ]
    partial_sums = lax.psum_scatter(
        jnp.concatenate(pieces, 1).astype(jnp.bfloat16), "ctx", scatter_dimension=0, tiled=True
    ).astype(jnp.float32)
    owned = lax.all_to_all(
        partial_sums.astype(jnp.bfloat16), "fsdp", split_axis=0, concat_axis=1, tiled=True
    ).astype(partial_sums.dtype)
    span_width = partial_sums.shape[1]
    owned_rows = owned.shape[0]
    arranged = owned.reshape(owned_rows, fsdp_size, span_width)
    model_part = model_width // fsdp_size
    hidden_part = hidden_width // fsdp_size
    bounds = [
        0,
        model_part,
        2 * model_part,
        3 * model_part,
        4 * model_part,
        4 * model_part + hidden_part,
        4 * model_part + 2 * hidden_part,
        4 * model_part + 3 * hidden_part,
    ]

    def joined_cols(first_col, last_col):
        return arranged[:, :, first_col:last_col].reshape(owned_rows, -1)

    grad_w_query = joined_cols(bounds[0], bounds[1])
    grad_w_key = joined_cols(bounds[1], bounds[2])
    grad_w_value = joined_cols(bounds[2], bounds[3])
    grad_w_out = joined_cols(bounds[3], bounds[4])
    grad_w_gate = joined_cols(bounds[4], bounds[5])
    grad_w_up = joined_cols(bounds[5], bounds[6])
    grad_w_down = joined_cols(bounds[6], bounds[7])
    gain_totals = jnp.sum(arranged[:, :, bounds[7] : bounds[7] + 2], 1)
    grad_gain_attn = gain_totals[:, 0]
    grad_gain_mlp = gain_totals[:, 1]
    grad_tokens = grad_input.reshape(slot_count, share_rows, model_width)
    return (
        result,
        grad_tokens,
        grad_w_query,
        grad_w_key,
        grad_w_value,
        grad_w_out,
        grad_w_gate,
        grad_w_up,
        grad_w_down,
        grad_gain_attn,
        grad_gain_mlp,
    )


def dot_f32(a, b):
    return jnp.dot(a, b, preferred_element_type=jnp.float32)

def load_sequence(order_ref, rows_ref, block, stores):
    per_src = rows_ref.shape[2] // block
    def one(slot, carry):
        src = slot // per_src
        lane = pl.multiple_of((slot % per_src) * block, block)
        place = pl.multiple_of(order_ref[slot] * block, block)
        for at, store in stores:
            store(rows_ref[src, at:at + HEAD_DIM, pl.ds(lane, block)], place)
        return carry
    lax.fori_loop(0, rows_ref.shape[0] * per_src, one, 0)

def fwd_kernel(
    order_ref, qkv_ref, mixed_ref, out_ref, lse_ref, qt, kr, vt, peak, total, acc, *, block, tile, step
):
    seq = qt.shape[1]

    def put_q(x, place):
        qt[:, pl.ds(place, block)] = x * jnp.bfloat16(HEAD_DIM ** -0.5)

    def put_k(x, place):
        kr[pl.ds(place, block), :] = x.T

    def put_v(x, place):
        vt[:, pl.ds(place, block)] = x

    load_sequence(
        order_ref, qkv_ref, block, ((0, put_q), (HEAD_DIM, put_k), (2 * HEAD_DIM, put_v))
    )

    def one_tile(qi, unused):
        q0 = pl.multiple_of(qi * tile, tile)
        peak[...] = jnp.full_like(peak, MASKED_SCORE)
        total[...] = jnp.zeros_like(total)
        acc[...] = jnp.zeros_like(acc)

        def visit(k0, first, masked):
            queries = qt[:, pl.ds(pl.multiple_of(q0 + first, step), tile - first)]
            s = dot_f32(kr[pl.ds(k0, step), :], queries)
            if masked:
                keep = lax.broadcasted_iota(jnp.int32, s.shape, 0) <= lax.broadcasted_iota(
                    jnp.int32, s.shape, 1
                )
                s = jnp.where(keep, s, MASKED_SCORE)
            old = peak[:, first:]
            new = jnp.maximum(old, jnp.max(s, 0, keepdims=True))
            p = jnp.exp(s - new)
            alpha = jnp.exp(old - new)
            peak[:, first:] = new
            total[:, first:] = total[:, first:] * alpha + jnp.sum(p, 0, keepdims=True)
            acc[:, first:] = acc[:, first:] * alpha + dot_f32(
                vt[:, pl.ds(k0, step)], p.astype(jnp.bfloat16)
            )

        def below(j, carry):
            visit(pl.multiple_of(j * step, step), 0, False)
            return carry

        lax.fori_loop(0, qi * (tile // step), below, 0)
        for part in range(tile // step):
            visit(pl.multiple_of(q0 + part * step, step), part * step, True)
        out_ref[:, pl.ds(q0, tile)] = acc[...] / total[...]
        lse_ref[:, pl.ds(q0, tile)] = peak[...] + jnp.log(total[...])
        return unused

    lax.fori_loop(0, seq // tile, one_tile, 0)
    per_src = mixed_ref.shape[2] // block

    def send(slot, carry):
        place = pl.multiple_of(order_ref[slot] * block, block)
        lane = pl.multiple_of((slot % per_src) * block, block)
        mixed_ref[slot // per_src, :, pl.ds(lane, block)] = out_ref[:, pl.ds(place, block)].astype(
            jnp.bfloat16
        )
        return carry

    lax.fori_loop(0, mixed_ref.shape[0] * per_src, send, 0)


def attend(order, qkv, block, tile, step):
    groups, unused, width = qkv.shape
    seq = groups * width
    vm = pl.BlockSpec(memory_space=pltpu.VMEM)
    bf, f32 = jnp.bfloat16, jnp.float32
    return pl.pallas_call(
        functools.partial(fwd_kernel, block=block, tile=tile, step=step),
        out_shape=(
            jax.ShapeDtypeStruct((groups, HEAD_DIM, width), bf),
            jax.ShapeDtypeStruct((HEAD_DIM, seq), f32),
            jax.ShapeDtypeStruct((1, seq), f32),
        ),
        in_specs=[pl.BlockSpec(memory_space=pltpu.SMEM), vm],
        out_specs=(vm, vm, vm),
        scratch_shapes=[
            pltpu.VMEM((HEAD_DIM, seq), bf),
            pltpu.VMEM((seq, HEAD_DIM), bf),
            pltpu.VMEM((HEAD_DIM, seq), bf),
            pltpu.VMEM((1, tile), f32),
            pltpu.VMEM((1, tile), f32),
            pltpu.VMEM((HEAD_DIM, tile), f32),
        ],
        compiler_params=pltpu.CompilerParams(vmem_limit_bytes=48 << 20),
        cost_estimate=pl.CostEstimate(
            flops=int(4.0 * seq * seq * HEAD_DIM),
            bytes_accessed=8 * seq * HEAD_DIM,
            transcendentals=0,
        ),
        name="attend",
    )(order, qkv)


def bwd_kernel(order_ref, qkv_ref, go_ref, out_ref, lse_ref, cos_ref, sin_ref, grad_ref,
               qt, qr, kt, kr, vr, got, gor, delta, dqt, dkr, dvr, *, block, tile, step):
    seq = qt.shape[1]
    scale = jnp.bfloat16(HEAD_DIM ** -0.5)
    def put_q(x, place):
        x = x * scale
        qt[:, pl.ds(place, block)] = x
        qr[pl.ds(place, block), :] = x.T
    def put_k(x, place):
        kt[:, pl.ds(place, block)] = x * scale
        kr[pl.ds(place, block), :] = x.T
    def put_v(x, place):
        vr[pl.ds(place, block), :] = x.T
    def put_go(x, place):
        got[:, pl.ds(place, block)] = x
        gor[pl.ds(place, block), :] = x.T
        delta[:, pl.ds(place, block)] = jnp.sum(x.astype(jnp.float32) * out_ref[:, pl.ds(place, block)], 0, keepdims=True)
    load_sequence(order_ref, qkv_ref, block, ((0, put_q), (HEAD_DIM, put_k), (2 * HEAD_DIM, put_v)))
    load_sequence(order_ref, go_ref, block, ((0, put_go),))
    dqt[...] = jnp.zeros_like(dqt)
    tiles = seq // tile

    def key_tile(kj, unused):
        k0 = pl.multiple_of(kj * tile, tile)
        keys = kr[pl.ds(k0, tile), :]
        keys_t = kt[:, pl.ds(k0, tile)]
        vals = vr[pl.ds(k0, tile), :]
        dkr[...] = jnp.zeros_like(dkr)
        dvr[...] = jnp.zeros_like(dvr)

        def visit(q0, width, rows, masked):
            s = dot_f32(keys[:rows], qt[:, pl.ds(q0, width)])
            p = jnp.exp(s - lse_ref[:, pl.ds(q0, width)])
            if masked:
                keep = lax.broadcasted_iota(jnp.int32, s.shape, 0) <= lax.broadcasted_iota(
                    jnp.int32, s.shape, 1
                ) + (rows - width)
                p = jnp.where(keep, p, 0.0)
            dp = dot_f32(vals[:rows], got[:, pl.ds(q0, width)])
            ds = (p * (dp - delta[:, pl.ds(q0, width)])).astype(jnp.bfloat16)
            dvr[:rows] += dot_f32(p.astype(jnp.bfloat16), gor[pl.ds(q0, width), :])
            dkr[:rows] += dot_f32(ds, qr[pl.ds(q0, width), :])
            dqt[:, pl.ds(q0, width)] += dot_f32(keys_t[:, :rows], ds)

        for part in range(tile // step):
            first = pl.multiple_of(k0 + part * step, step)
            visit(first, step, (part + 1) * step, True)

        def later(j, carry):
            visit(pl.multiple_of(j * step, step), step, tile, False)
            return carry

        lax.fori_loop((kj + 1) * (tile // step), seq // step, later, 0)
        put_out(dkr[...].T, HEAD_DIM, k0, True)
        put_out(dvr[...].T, 2 * HEAD_DIM, k0, False)
        return unused

    half = HEAD_DIM // 2
    def put_out(x, at, place, turn):
        for part in range(tile // block):
            piece = x[:, part * block:(part + 1) * block]
            here = place + part * block
            if turn:
                lanes = pl.ds(pl.multiple_of(here, block), block)
                c, s = cos_ref[:, lanes], sin_ref[:, lanes]
                a, b = piece[:half], piece[half:]
                piece = jnp.concatenate([a * c + b * s, b * c - a * s], 0)
            slot = order_ref[seq // block + here // block]
            per_src = grad_ref.shape[2] // block
            lane = pl.multiple_of((slot % per_src) * block, block)
            grad_ref[slot // per_src, at:at + HEAD_DIM, pl.ds(lane, block)] = piece.astype(jnp.bfloat16)

    lax.fori_loop(0, tiles, key_tile, 0)
    def write_q(qi, c):
        q0 = pl.multiple_of(qi * tile, tile)
        put_out(dqt[:, pl.ds(q0, tile)], 0, q0, True)
        return c
    lax.fori_loop(0, tiles, write_q, 0)

def attend_back(order, qkv, go, out, lse, cos, sin, block, tile, step):
    groups, unused, width = qkv.shape
    seq = groups * width
    vm = pl.BlockSpec(memory_space=pltpu.VMEM)
    bf, f32 = jnp.bfloat16, jnp.float32
    wide = lambda t: pltpu.VMEM((HEAD_DIM, seq), t)
    tall = lambda t: pltpu.VMEM((seq, HEAD_DIM), t)
    return pl.pallas_call(
        functools.partial(bwd_kernel, block=block, tile=tile, step=step),
        out_shape=jax.ShapeDtypeStruct(qkv.shape, bf),
        in_specs=[pl.BlockSpec(memory_space=pltpu.SMEM)] + [vm] * 6,
        out_specs=vm,
        scratch_shapes=[wide(bf), tall(bf), wide(bf), tall(bf), tall(bf), wide(bf), tall(bf),
                        pltpu.VMEM((1, seq), f32), wide(f32),
                        pltpu.VMEM((tile, HEAD_DIM), f32), pltpu.VMEM((tile, HEAD_DIM), f32)],
        compiler_params=pltpu.CompilerParams(vmem_limit_bytes=48 << 20),
        cost_estimate=pl.CostEstimate(
            flops=int(6.4 * seq * seq * HEAD_DIM),
            bytes_accessed=16 * seq * HEAD_DIM,
            transcendentals=0,
        ),
        name="attend_back",
    )(order, qkv, go, out, lse, cos, sin)


def nt_dot(a, b):
    return lax.dot_general(a, b, (((1,), (1,)), ((), ())), preferred_element_type=jnp.float32)


def whole(space=pltpu.VMEM):
    return pl.BlockSpec(memory_space=space)


def spread(pieces, place_ref, rows_ref):
    hops = (len(pieces) - 1) // 2
    slots, share, unused = pieces[0].shape
    place = place_ref[0]

    def put(piece, position):
        for slot in range(slots):
            first = pl.multiple_of(slot * share * (hops + 1) + position * share, share)
            rows_ref[pl.ds(first, share), :] = piece[slot]

    put(pieces[0], place)
    for hop in range(1, hops + 1):

        @pl.when(place >= hop)
        def take_below(hop=hop):
            put(pieces[hop], place - hop)

        @pl.when(place + hop <= hops)
        def take_above(hop=hop):
            put(pieces[hops + hop], place + hop)


def deal(rows_ref, place_ref, own_ref, others):
    slots, share, unused = own_ref.shape
    line = len(others) + 1
    for step, target in enumerate([own_ref] + list(others)):
        position = lax.rem(place_ref[0] + step, line)
        for slot in range(slots):
            first = pl.multiple_of(slot * share * line + position * share, share)
            target[slot] = rows_ref[pl.ds(first, share), :].astype(target.dtype)


def dealt_shapes(slots, share, width, line):
    return [jax.ShapeDtypeStruct((slots, share, width), jnp.float32)] + [
        jax.ShapeDtypeStruct((slots, share, width), jnp.bfloat16) for unused in range(line - 1)
    ]


def work(flops, bytes_accessed=0, transcendentals=0):
    return pl.CostEstimate(
        flops=int(flops * 0.2), bytes_accessed=int(bytes_accessed * 0.2), transcendentals=0
    )


def vmem_limit(mebibytes):
    return pltpu.CompilerParams(vmem_limit_bytes=mebibytes << 20)


EXTRA_ROWS = 16
LANES = 128


def cut_columns(place, group, weights, rows, line, extra=None):
    count = len(weights)
    columns = weights[0].shape[1] // line
    cut_rows = count * rows + (EXTRA_ROWS if extra is not None else 0)
    extras = [] if extra is None else [extra]

    def kernel(place_ref, group_ref, *refs):
        outs = refs[count * line + len(extras) :]
        for step in range(line):
            for i in range(count):
                outs[step][i * rows : (i + 1) * rows] = refs[step * count + i][...]
            if extras:
                outs[step][count * rows :] = refs[count * line][...]

    def target(step):
        return lambda i, place, group: (group[0], lax.rem(place[0] + step, line))

    fixed = lambda shape: pl.BlockSpec(shape, lambda i, place, group: (0, 0))
    return pl.pallas_call(
        kernel,
        out_shape=[jax.ShapeDtypeStruct((cut_rows, columns), jnp.bfloat16)] * line,
        grid_spec=pltpu.PrefetchScalarGridSpec(
            num_scalar_prefetch=2,
            grid=(1,),
            in_specs=[
                pl.BlockSpec((rows, columns), target(step))
                for step in range(line)
                for unused in range(count)
            ]
            + [fixed((EXTRA_ROWS, columns)) for unused in extras],
            out_specs=[fixed((cut_rows, columns))] * line,
        ),
        compiler_params=vmem_limit(60),
        name="cut_columns",
    )(place, group, *(list(weights) * line), *extras)


def order_shares(place, shares, count, vectors=0):
    line = len(shares)
    share_rows, columns = shares[0].shape
    rows = (share_rows - (EXTRA_ROWS if vectors else 0)) // count

    def kernel(place_ref, *refs):
        for step in range(line):
            source = lax.rem(place_ref[0] + line - step, line)
            for i in range(count):
                refs[line][source, i] = refs[step][i * rows : (i + 1) * rows]
            if vectors:
                lanes = pl.ds(pl.multiple_of(source * columns, columns), columns)
                refs[line + 1][:, lanes] = refs[step][count * rows :].astype(jnp.float32)

    shapes = [jax.ShapeDtypeStruct((line, count, rows, columns), shares[0].dtype)]
    if vectors:
        shapes.append(jax.ShapeDtypeStruct((EXTRA_ROWS, line * columns), jnp.float32))
    outs = pl.pallas_call(
        kernel,
        out_shape=shapes,
        in_specs=[whole(pltpu.SMEM)] + [whole()] * line,
        out_specs=[whole()] * len(shapes),
        compiler_params=vmem_limit(40),
        name="order_shares",
    )(place, *shares)
    return (outs[0], outs[1][:vectors]) if vectors else outs[0]


def widen_columns(place, shares, count, rows):
    line = len(shares)
    share_rows, columns = shares[0].shape

    def kernel(place_ref, *refs):
        for step in range(line):

            @pl.when(pl.program_id(0) == step)
            def widen(step=step):
                for i in range(count):
                    refs[line + i][...] = refs[step][i * rows : (i + 1) * rows].astype(jnp.float32)

    return pl.pallas_call(
        kernel,
        out_shape=[jax.ShapeDtypeStruct((rows, line * columns), jnp.float32)] * count,
        grid_spec=pltpu.PrefetchScalarGridSpec(
            num_scalar_prefetch=1,
            grid=(line,),
            in_specs=[pl.BlockSpec((share_rows, columns), lambda j, place: (0, 0))] * line,
            out_specs=[
                pl.BlockSpec(
                    (rows, columns), lambda j, place: (0, lax.rem(place[0] + line - j, line))
                )
            ]
            * count,
        ),
        compiler_params=vmem_limit(40),
        name="widen_columns",
    )(place, *shares)


def project(place, pieces, gain, w_heads, cosine, sine):
    line, count, part, width = w_heads.shape
    slots, share, model_width = pieces[0].shape
    rows = slots * share * line
    tile = width // 2
    heads = tile // HEAD_DIM
    n_pieces = len(pieces)
    half = HEAD_DIM // 2

    def kernel(place_ref, *refs):
        piece_refs = refs[:n_pieces]
        gain_ref, w_ref, cos_ref, sin_ref, rows_ref, out_ref = refs[n_pieces:]

        @pl.when((pl.program_id(0) == 0) & (pl.program_id(1) == 0))
        def assemble():
            spread(piece_refs, place_ref, rows_ref)
            rows_ref[...] = (rows_ref[...].astype(jnp.float32) * gain_ref[...]).astype(jnp.bfloat16)

        weight = w_ref[...].reshape(line * part, tile)
        turned = dot_f32(rows_ref[...], weight).T
        c, s = cos_ref[0], sin_ref[0]
        for head in range(heads):
            a = turned[head * HEAD_DIM : head * HEAD_DIM + half]
            b = turned[head * HEAD_DIM + half : (head + 1) * HEAD_DIM]
            out_ref[head, 0, :half, :] = (a * c - b * s).astype(jnp.bfloat16)
            out_ref[head, 0, half:, :] = (b * c + a * s).astype(jnp.bfloat16)

    return pl.pallas_call(
        kernel,
        grid=(count, 2),
        out_shape=[
            jax.ShapeDtypeStruct((rows, model_width), jnp.bfloat16),
            jax.ShapeDtypeStruct((width // HEAD_DIM, count, HEAD_DIM, rows), jnp.bfloat16),
        ],
        in_specs=[whole(pltpu.SMEM)]
        + [whole()] * (n_pieces + 1)
        + [
            pl.BlockSpec((line, 1, part, tile), lambda m, h: (0, m, 0, h)),
            pl.BlockSpec((1, half, rows), lambda m, h: (m, 0, 0)),
            pl.BlockSpec((1, half, rows), lambda m, h: (m, 0, 0)),
        ],
        out_specs=[
            pl.BlockSpec((rows, model_width), lambda m, h: (0, 0)),
            pl.BlockSpec((heads, 1, HEAD_DIM, rows), lambda m, h: (h, m, 0, 0)),
        ],
        compiler_params=vmem_limit(48),
        cost_estimate=work(6 * rows * model_width * width, 8 * rows * model_width),
        name="project",
    )(place, *pieces, gain, w_heads, cosine, sine)


def mix_out(place, mixed, w_out, slots, line):
    heads, unused, rows = mixed.shape
    width, model_width = w_out.shape
    share = rows // slots // line

    def kernel(place_ref, mixed_ref, w_ref, own_ref, *rest):
        *others, total = rest
        left = mixed_ref[...].reshape(width, rows).T
        total[...] = dot_f32(left, w_ref[...])
        deal(total, place_ref, own_ref, others)

    return pl.pallas_call(
        kernel,
        out_shape=dealt_shapes(slots, share, model_width, line),
        in_specs=[whole(pltpu.SMEM), whole(), whole()],
        out_specs=[whole()] * line,
        scratch_shapes=[pltpu.VMEM((rows, model_width), jnp.float32)],
        compiler_params=vmem_limit(48),
        cost_estimate=work(2 * rows * model_width * width, 8 * rows * model_width),
        name="mix_out",
    )(place, mixed, w_out)


def mlp_forward(place, pieces, upstream_pieces, w_mlp, tile):
    line, count, part, width = w_mlp.shape
    slots, share, model_width = pieces[0].shape
    rows = slots * share * line
    n_pieces = len(pieces)
    bf, f32 = jnp.bfloat16, jnp.float32

    def kernel(place_ref, *refs):
        x_pieces, u_pieces = refs[:n_pieces], refs[n_pieces : 2 * n_pieces]
        w_ref, x_ref, u_ref, hidden_ref, gate_ref, up_ref, own_ref = refs[
            2 * n_pieces : 2 * n_pieces + 7
        ]
        *others, total = refs[2 * n_pieces + 7 :]
        step = pl.program_id(0)

        @pl.when(step == 0)
        def assemble():
            spread(x_pieces, place_ref, x_ref)
            spread(u_pieces, place_ref, u_ref)

        down = w_ref[:, 0].reshape(line * part, tile)
        gate = w_ref[:, 1].reshape(line * part, tile)
        up = w_ref[:, 2].reshape(line * part, tile)
        x = x_ref[...]
        grad_hidden = dot_f32(u_ref[...], down)
        gate_act = dot_f32(x, gate)
        upward = dot_f32(x, up)
        sigmoid = jax.nn.sigmoid(gate_act)
        silu = gate_act * sigmoid
        hidden_ref[...] = (silu * upward).astype(bf)
        grad_gate = (
            grad_hidden * upward * sigmoid * (1.0 + gate_act * (1.0 - sigmoid))
        ).astype(bf)
        grad_up = (grad_hidden * silu).astype(bf)
        gate_ref[...] = grad_gate
        up_ref[...] = grad_up
        part_two = nt_dot(grad_gate, gate) + nt_dot(grad_up, up)

        @pl.when(step == 0)
        def first():
            total[...] = part_two

        @pl.when(step > 0)
        def further():
            total[...] += part_two

        @pl.when(step == pl.num_programs(0) - 1)
        def last():
            deal(total, place_ref, own_ref, others)

    fixed = lambda shape: pl.BlockSpec(shape, lambda j: (0,) * len(shape))
    columns = pl.BlockSpec((rows, tile), lambda j: (0, j))
    dealt = dealt_shapes(slots, share, model_width, line)
    return pl.pallas_call(
        kernel,
        grid=(width // tile,),
        out_shape=[jax.ShapeDtypeStruct((rows, model_width), bf)] * 2
        + [jax.ShapeDtypeStruct((rows, width), bf)] * 3
        + dealt,
        in_specs=[whole(pltpu.SMEM)]
        + [whole()] * (2 * n_pieces)
        + [pl.BlockSpec((line, count, part, tile), lambda j: (0, 0, 0, j))],
        out_specs=[fixed((rows, model_width))] * 2
        + [columns] * 3
        + [fixed((slots, share, model_width))] * line,
        scratch_shapes=[pltpu.VMEM((rows, model_width), f32)],
        compiler_params=vmem_limit(60),
        cost_estimate=work(16 * rows * model_width * width, 14 * model_width * width),
        name="mlp_forward",
    )(place, *pieces, *upstream_pieces, w_mlp)


def gate_up_weights(x_rows, grad_gate, grad_up, groups, line, tile):
    rows, model_width = x_rows.shape
    width = grad_gate.shape[1]
    block = model_width // groups // line

    def kernel(x_ref, gate_ref, up_ref, out_ref, x_turned):
        @pl.when(pl.program_id(0) == 0)
        def turn():
            x_turned[...] = x_ref[...].T

        for i, ref in enumerate((gate_ref, up_ref)):
            grads = dot_f32(x_turned[...], ref[...]).astype(jnp.bfloat16)
            out_ref[:, :, i * block : (i + 1) * block] = grads.reshape(groups, line, block, tile)

    columns = pl.BlockSpec((rows, tile), lambda j: (0, j))
    return pl.pallas_call(
        kernel,
        grid=(width // tile,),
        out_shape=jax.ShapeDtypeStruct((groups, line, 2 * block, width), jnp.bfloat16),
        in_specs=[pl.BlockSpec((rows, model_width), lambda j: (0, 0)), columns, columns],
        out_specs=pl.BlockSpec((groups, line, 2 * block, tile), lambda j: (0, 0, 0, j)),
        scratch_shapes=[pltpu.VMEM((model_width, rows), jnp.bfloat16)],
        compiler_params=vmem_limit(60),
        cost_estimate=work(4 * rows * model_width * width, 8 * model_width * width),
        name="gate_up_weights",
    )(x_rows, grad_gate, grad_up)


def down_weights(place, u_rows, hidden, w_mlp, slots, groups, tile):
    line, count, part, width = w_mlp.shape
    rows, model_width = u_rows.shape
    share = rows // slots // line
    block = model_width // groups // line
    bf, f32 = jnp.bfloat16, jnp.float32

    def kernel(place_ref, u_ref, hidden_ref, w_ref, d_ref, own_ref, *rest):
        *others, u_turned, total = rest
        step = pl.program_id(0)

        @pl.when(step == 0)
        def turn():
            u_turned[...] = u_ref[...].T

        grads = dot_f32(u_turned[...], hidden_ref[...]).astype(bf)
        d_ref[:, :line] = grads.reshape(groups, line, block, tile)
        part_out = nt_dot(hidden_ref[...], w_ref[...].reshape(line * part, tile))

        @pl.when(step == 0)
        def first():
            total[...] = part_out

        @pl.when(step > 0)
        def further():
            total[...] += part_out

        @pl.when(step == pl.num_programs(0) - 1)
        def last():
            deal(total, place_ref, own_ref, others)

    fixed = lambda shape: pl.BlockSpec(shape, lambda j: (0,) * len(shape))
    return pl.pallas_call(
        kernel,
        grid=(width // tile,),
        out_shape=[jax.ShapeDtypeStruct((groups, line + 1, block, width), bf)]
        + dealt_shapes(slots, share, model_width, line),
        in_specs=[
            whole(pltpu.SMEM),
            fixed((rows, model_width)),
            pl.BlockSpec((rows, tile), lambda j: (0, j)),
            pl.BlockSpec((line, 1, part, tile), lambda j: (0, 0, 0, j)),
        ],
        out_specs=[pl.BlockSpec((groups, line + 1, block, tile), lambda j: (0, 0, 0, j))]
        + [fixed((slots, share, model_width))] * line,
        scratch_shapes=[pltpu.VMEM((model_width, rows), bf), pltpu.VMEM((rows, model_width), f32)],
        compiler_params=vmem_limit(60),
        cost_estimate=work(4 * rows * model_width * width, 8 * model_width * width),
        name="down_weights",
    )(place, u_rows, hidden, w_mlp)


def branch_back(place, pieces, w_out, heads):
    slots, share, model_width = pieces[0].shape
    line = (len(pieces) + 1) // 2
    rows = slots * share * line

    def kernel(place_ref, *refs):
        *piece_refs, w_ref, rows_ref, out_ref = refs
        spread(piece_refs, place_ref, rows_ref)
        turned = nt_dot(w_ref[...], rows_ref[...])
        out_ref[...] = turned.astype(jnp.bfloat16).reshape(out_ref.shape)

    return pl.pallas_call(
        kernel,
        out_shape=[
            jax.ShapeDtypeStruct((rows, model_width), jnp.bfloat16),
            jax.ShapeDtypeStruct((heads, HEAD_DIM, rows), jnp.bfloat16),
        ],
        in_specs=[whole(pltpu.SMEM)] + [whole()] * (len(pieces) + 1),
        out_specs=[whole(), whole()],
        compiler_params=vmem_limit(40),
        cost_estimate=work(2 * rows * model_width * heads * HEAD_DIM, 8 * rows * model_width),
        name="branch_back",
    )(place, *pieces, w_out)


def out_weight(grads, mixed, branch_rows, tile):
    groups, blocks, block, width = grads.shape
    heads, unused, rows = mixed.shape

    def kernel(grads_ref, mixed_ref, rows_ref, out_ref):
        left = mixed_ref[...].reshape(heads * HEAD_DIM, rows)
        product = dot_f32(left, rows_ref[...]).astype(jnp.bfloat16)
        out_ref[...] = product.reshape(groups, 1, block, tile)

    return pl.pallas_call(
        kernel,
        grid=(width // tile,),
        out_shape=jax.ShapeDtypeStruct(grads.shape, grads.dtype),
        in_specs=[
            pl.BlockSpec(memory_space=pl.ANY),
            pl.BlockSpec(mixed.shape, lambda j: (0, 0, 0)),
            pl.BlockSpec((rows, tile), lambda j: (0, j)),
        ],
        out_specs=pl.BlockSpec((groups, 1, block, tile), lambda j: (0, blocks - 1, 0, j)),
        input_output_aliases={0: 0},
        compiler_params=vmem_limit(60),
        cost_estimate=work(4 * rows * heads * HEAD_DIM * width, 8 * rows * width),
        name="out_weight",
    )(grads, mixed, branch_rows)


def head_weights(group, all_rows, head_grads, w_head, gain, gain_two, owners):
    sources, features, rows = head_grads.shape
    model_width = all_rows[0].shape[1]
    block = model_width // owners
    lanes = 2 * LANES
    half = rows // 2
    f32 = jnp.float32

    def kernel(group_ref, *refs):
        g_ref, w_ref, gain_ref, two_ref, out_ref, total = refs[sources:]
        step = pl.program_id(0)
        part = sum(
            dot_f32(g_ref[lax.bitwise_xor(group_ref[0], m)], refs[m][...]) for m in range(sources)
        )

        @pl.when(step == 0)
        def first():
            total[...] = part

        @pl.when(step == 1)
        def last():
            grads = (total[...] + part).T
            weighed = jnp.sum(grads * w_ref[...].astype(f32), 1, keepdims=True) / gain_ref[...]
            spare = lanes - features
            at = lax.broadcasted_iota(jnp.int32, (model_width, spare), 1)
            tail = jnp.where(at == 0, weighed, jnp.where(at == 1, two_ref[...], 0.0))
            joined = jnp.concatenate([grads, tail], 1).astype(jnp.bfloat16)
            out_ref[...] = joined.reshape(owners, block, lanes)

    fixed = lambda shape: pl.BlockSpec(shape, lambda s: (0,) * len(shape))
    return pl.pallas_call(
        kernel,
        grid=(2,),
        out_shape=jax.ShapeDtypeStruct((owners, block, lanes), jnp.bfloat16),
        in_specs=[whole(pltpu.SMEM)]
        + [pl.BlockSpec((half, model_width), lambda s: (s, 0))] * sources
        + [
            pl.BlockSpec((sources, features, half), lambda s: (0, 0, s)),
            fixed((model_width, features)),
            fixed((model_width, 1)),
            fixed((model_width, 1)),
        ],
        out_specs=fixed((owners, block, lanes)),
        scratch_shapes=[pltpu.VMEM((features, model_width), f32)],
        compiler_params=vmem_limit(60),
        cost_estimate=work(6 * sources * rows * features * model_width, 0),
        name="head_weights",
    )(group, *all_rows, head_grads, w_head, gain, gain_two)


def join_heads(parts):
    groups, line, rows, lanes = parts.shape
    width = groups * HEAD_DIM

    def kernel(parts_ref, *outs):
        for i, out in enumerate(outs):
            pick = slice(i * HEAD_DIM, (i + 1) * HEAD_DIM)
            heads = [parts_ref[c, 0][:, pick].astype(jnp.float32) for c in range(groups)]
            out[...] = jnp.concatenate(heads, 1)

    return pl.pallas_call(
        kernel,
        grid=(line,),
        out_shape=[jax.ShapeDtypeStruct((rows, line * width), jnp.float32)] * 3,
        in_specs=[pl.BlockSpec((groups, 1, rows, lanes), lambda f: (0, f, 0, 0))],
        out_specs=[pl.BlockSpec((rows, width), lambda f: (0, f))] * 3,
        compiler_params=vmem_limit(24),
        name="join_heads",
    )(parts)


def project_back(place, head_grads, w_heads, slots):
    line, count, part, width = w_heads.shape
    rows, model_width = head_grads.shape[-1], line * part
    heads = width // HEAD_DIM
    share = rows // slots // line

    def kernel(place_ref, g_ref, w_ref, own_ref, *rest):
        *others, total = rest
        m = pl.program_id(0)
        grads = g_ref[...].reshape(width, rows).T
        partial = nt_dot(grads, w_ref[...].reshape(line * part, width))

        @pl.when(m == 0)
        def first():
            total[...] = partial

        @pl.when(m > 0)
        def further():
            total[...] += partial

        @pl.when(m == count - 1)
        def last():
            deal(total, place_ref, own_ref, others)

    fixed = lambda shape: pl.BlockSpec(shape, lambda m: (0,) * len(shape))
    return pl.pallas_call(
        kernel,
        grid=(count,),
        out_shape=dealt_shapes(slots, share, model_width, line),
        in_specs=[
            whole(pltpu.SMEM),
            pl.BlockSpec((heads, 1, HEAD_DIM, rows), lambda m: (0, m, 0, 0)),
            pl.BlockSpec((line, 1, part, width), lambda m: (0, m, 0, 0)),
        ],
        out_specs=[fixed((slots, share, model_width))] * line,
        scratch_shapes=[pltpu.VMEM((rows, model_width), jnp.float32)],
        compiler_params=vmem_limit(48),
        cost_estimate=work(2 * count * rows * width * model_width, 8 * rows * model_width),
        name="project_back",
    )(place, head_grads, w_heads)


def line_steps(size, step):
    return [(i, i + step) for i in range(size) if 0 <= i + step < size]


def after(values, *earlier):
    return lax.optimization_barrier((values, earlier))[0]


def send_shares(share, axis, between=()):
    size = lax.axis_size(axis)
    ups, downs = [share], [share]
    for hop in range(1, size):
        up = lax.ppermute(ups[-1], axis, line_steps(size, 1)[hop - 1 :])
        down = lax.ppermute(downs[-1], axis, line_steps(size, -1)[: size - hop])
        if hop <= len(between):
            done = between[hop - 1]((ups[-1], downs[-1]))
            up, down = after((up, down), done)
        ups.append(up)
        downs.append(down)
    return ups + downs[1:]


def flip(values, bits):
    size = lax.axis_size("ctx")
    return lax.ppermute(values, "ctx", [(i, i ^ bits) for i in range(size)])


def send_dealt(others, axis):
    size = lax.axis_size(axis)
    return [
        lax.ppermute(other, axis, [(i, (i + step) % size) for i in range(size)])
        for step, other in enumerate(others, 1)
    ]


def scatter_line(others, axis, between=()):
    size = lax.axis_size(axis)
    up = down = None
    for hop in range(1, size):
        rising, falling = others[size - hop - 1], others[hop - 1]
        if hop > 1:
            rising = (rising.astype(jnp.float32) + up.astype(jnp.float32)).astype(rising.dtype)
            falling = (falling.astype(jnp.float32) + down.astype(jnp.float32)).astype(falling.dtype)
        up = lax.ppermute(rising, axis, line_steps(size, 1)[:hop])
        down = lax.ppermute(falling, axis, line_steps(size, -1)[size - 1 - hop :])
        if hop <= len(between):
            up, down = after((up, down), between[hop - 1]((rising, falling)))
    return [up, down]


def add_shares(own, received):
    return own + sum(share.astype(jnp.float32) for share in received)


def swap_dealt(shares):
    return [shares[0]] + send_dealt(shares[1:], "fsdp")


def deal_line(parts, place):
    line = parts.shape[0]
    return [
        lax.dynamic_index_in_dim(parts, lax.rem(place[0] + step, line), 0, keepdims=False)
        for step in range(line)
    ]


def swap_heads(parts):
    return lax.all_to_all(parts, "ctx", split_axis=0, concat_axis=0, tiled=True)


def sum_groups(parts):
    return lax.psum_scatter(parts, "ctx", scatter_dimension=0, tiled=True)[0]


def head_device(
    tokens,
    block_order,
    w_query,
    w_key,
    w_value,
    w_out,
    w_gate,
    w_up,
    w_down,
    gain_attn,
    gain_mlp,
    cotangent,
):
    slots, share_rows, model_width = tokens.shape
    ctx_size, line = lax.axis_size("ctx"), lax.axis_size("fsdp")
    block_rows = share_rows * line
    group_rows = slots * block_rows
    bf, f32 = jnp.bfloat16, jnp.float32
    place = lax.axis_index("fsdp").astype(jnp.int32).reshape(1)
    group = lax.axis_index("ctx").astype(jnp.int32).reshape(1)
    own_rows = w_query.shape[0] // ctx_size
    order = block_order.astype(jnp.int32)
    long_tile = (8 if ctx_size * slots % 8 == 0 else 2) * block_rows
    slot_of = jnp.sum(
        jnp.where(order[None, :] == jnp.arange(order.shape[0])[:, None], jnp.arange(order.shape[0], dtype=jnp.int32)[None, :], 0), 1
    ).astype(jnp.int32)

    stream = tokens.astype(f32)
    root_one = lax.rsqrt(jnp.mean(stream * stream, -1, keepdims=True) + EPSILON)
    norm_one = stream * root_one
    gain_rows = jnp.pad(jnp.stack([gain_attn, gain_mlp]), ((0, EXTRA_ROWS - 2), (0, 0)))
    head_cuts = swap_dealt(
        cut_columns(place, group, [w_query, w_key, w_value], own_rows, line, gain_rows)
    )
    own_heads, gains = order_shares(place, head_cuts, 3, 2)
    attn_gain, mlp_gain = gains[0], gains[1]
    w_heads = lax.all_gather(own_heads, "ctx", axis=2, tiled=True)

    attn_pieces = send_shares(after(norm_one.astype(bf), head_cuts), "fsdp")

    mlp_cuts = cut_columns(place, group, [w_down, w_gate, w_up], own_rows, line)
    w_heads = after(w_heads, mlp_cuts)
    mlp_cuts = swap_dealt(after(mlp_cuts, attn_pieces[line - 2], attn_pieces[2 * line - 3]))

    w_head = lax.dynamic_slice_in_dim(w_heads, group[0] * HEAD_DIM, HEAD_DIM, 3)
    w_head = jnp.concatenate([w_head[:, i].reshape(model_width, HEAD_DIM) for i in range(3)], 1)

    half = HEAD_DIM // 2
    frequency = 1.0 / ROPE_BASE ** (jnp.arange(half, dtype=f32) * (2.0 / HEAD_DIM))
    places = jnp.arange(group_rows * ctx_size, dtype=jnp.int32).astype(f32)
    angles = frequency[:, None] * places[None, :]
    cosine, sine = jnp.cos(angles), jnp.sin(angles)

    def own_columns(table):
        return jnp.concatenate(
            [
                lax.dynamic_slice_in_dim(
                    table, order[slots * group[0] + i] * block_rows, block_rows, 1
                )
                for i in range(slots)
            ],
            1,
        )

    own_cosine, own_sine = own_columns(cosine), own_columns(sine)
    turn_cosine = jnp.stack([own_cosine, own_cosine, jnp.ones_like(own_cosine)])
    turn_sine = jnp.stack([own_sine, own_sine, jnp.zeros_like(own_sine)])

    attn_rows, heads_out = project(
        place, attn_pieces, attn_gain[None], w_heads, turn_cosine, turn_sine
    )
    head_rows = swap_heads(heads_out.reshape(ctx_size, 3 * HEAD_DIM, group_rows))
    mixed_send, attended, log_total = attend(
        order, head_rows, block_rows, long_tile, 2 * block_rows
    )
    all_rows = {0: attn_rows}
    for bits in (1, 2, 4):
        all_rows[bits] = flip(attn_rows, bits)
    mlp_cuts = order_shares(
        place, after(mlp_cuts, mixed_send, all_rows[1], all_rows[2], all_rows[4]), 3
    )
    w_mlp = lax.all_gather(mlp_cuts, "ctx", axis=2, tiled=True)
    mixed = swap_heads(after(mixed_send, mlp_cuts))
    upstream_pieces = send_shares(after(cotangent, mlp_cuts), "fsdp")
    mixed = after(mixed, upstream_pieces[1], upstream_pieces[line])
    own, *others = mix_out(place, mixed, w_out, slots, line)
    middle = stream + add_shares(own, scatter_line(others, "fsdp"))

    root_two = lax.rsqrt(jnp.mean(middle * middle, -1, keepdims=True) + EPSILON)
    norm_two = middle * root_two
    mlp_input = (norm_two * mlp_gain).astype(bf)
    mlp_pieces = send_shares(mlp_input, "fsdp")

    upper = attn_rows.shape[0] // 2
    by_x, by_y = after((all_rows[2], all_rows[4]), mlp_pieces)
    corner = [flip(by_x[:upper], 4), flip(by_y[upper:], 2)]
    all_rows[3], all_rows[5] = flip(by_x, 1), flip(by_y, 1)
    mlp_rows, upstream_rows, hidden, grad_gate, grad_up, own, *others = mlp_forward(
        place, mlp_pieces, upstream_pieces, w_mlp, 512
    )
    results = {}

    def weigh_gate_up(sent):
        rows_here = after(mlp_rows, sent)
        results["gate_up"] = gate_up_weights(rows_here, grad_gate, grad_up, ctx_size, line, 512)
        return results["gate_up"], corner, all_rows[3], all_rows[5]

    def weigh_down(sent):
        results["down"] = down_weights(
            place, upstream_rows, after(hidden, sent), w_mlp, slots, ctx_size, 512
        )
        results["gate_up_sums"] = sum_groups(after(results["gate_up"], sent))
        return results["down"][1]

    grad_two = add_shares(own, scatter_line(others, "fsdp", (weigh_gate_up, weigh_down)))
    gate_up_sums = results["gate_up_sums"]
    down_grads, own_out, *others_out = results["down"]
    gain_two_part = jnp.sum(grad_two * norm_two, (0, 1))
    grad_middle = cotangent.astype(f32) + norm_back(grad_two, norm_two, root_two, mlp_gain)
    all_rows[6] = jnp.concatenate(corner, 0)
    branch_pieces = send_shares(grad_middle.astype(bf), "fsdp")
    branch_rows, grad_mixed = branch_back(place, branch_pieces, w_out, ctx_size)

    out_received = send_dealt(after(others_out, branch_rows), "fsdp")
    all_rows[7] = flip(after(all_rows[6], branch_rows), 1)
    grad_heads = swap_heads(grad_mixed)
    down_grads = out_weight(down_grads, mixed, branch_rows, 512)
    head_grads = attend_back(
        jnp.concatenate([order, slot_of]),
        head_rows,
        after(grad_heads, down_grads, out_received[0], all_rows[7]),
        attended,
        log_total,
        cosine,
        sine,
        block_rows,
        long_tile,
        2 * block_rows,
    )
    head_grads = after(head_grads, out_received)
    gate_up_dealt = deal_line(after(gate_up_sums, head_grads), place)
    gate_up_back = swap_dealt(gate_up_dealt)
    lin_grads = swap_heads(after(head_grads, gate_up_dealt))
    lin_grads = lin_grads.reshape(ctx_size, 3, HEAD_DIM, group_rows)
    down_sums = sum_groups(after(down_grads, gate_up_sums, head_grads))
    own, *others = project_back(place, lin_grads, w_heads, slots)

    def weigh_heads(sent):
        results["heads"] = head_weights(
            group,
            [all_rows[bits] for bits in range(ctx_size)],
            after(head_grads, sent),
            w_head,
            attn_gain[:, None],
            gain_two_part[:, None],
            ctx_size * line,
        )
        return results["heads"], gate_up_back[1]

    one_received = scatter_line(others, "fsdp", (weigh_heads,))
    head_parts = lax.all_to_all(
        results["heads"], ("ctx", "fsdp"), split_axis=0, concat_axis=0, tiled=True
    )
    grad_one = add_shares(own, one_received)
    grad_tokens = grad_middle + norm_back(grad_one, norm_one, root_one, attn_gain)
    result = (middle + add_shares(own_out, out_received)).astype(bf)
    down_sums = after(down_sums, results["heads"])
    down_back = swap_dealt(deal_line(down_sums[:line], place))

    owners = [(c * line + f, f * ctx_size + c) for c in range(ctx_size) for f in range(line)]
    grad_w_out = lax.ppermute(down_sums[line], ("ctx", "fsdp"), owners).astype(f32)
    grad_w_gate, grad_w_up = widen_columns(place, gate_up_back, 2, own_rows)
    (grad_w_down,) = widen_columns(place, down_back, 1, own_rows)
    head_parts = head_parts.reshape(ctx_size, line, own_rows, -1)
    grad_w_query, grad_w_key, grad_w_value = join_heads(head_parts)
    spare = 3 * HEAD_DIM
    gain_grads = jnp.sum(head_parts[..., spare : spare + 2].astype(f32), (0, 1)).T
    return (
        result,
        grad_tokens,
        grad_w_query,
        grad_w_key,
        grad_w_value,
        grad_w_out,
        grad_w_gate,
        grad_w_up,
        grad_w_down,
        gain_grads[0],
        gain_grads[1],
    )


def layer_step(*arrays):
    heads_here = arrays[0].shape[-1] // lax.axis_size("fsdp") // HEAD_DIM
    if heads_here == lax.axis_size("ctx") == 8:
        return head_device(*arrays)
    return per_device(*arrays)


def solution(mesh):
    in_specs = (
        P("ctx", "fsdp", None),
        P(),
        P("fsdp", None),
        P("fsdp", None),
        P("fsdp", None),
        P("fsdp", None),
        P("fsdp", None),
        P("fsdp", None),
        P("fsdp", None),
        P("fsdp"),
        P("fsdp"),
        P("ctx", "fsdp", None),
    )
    out_specs = (
        P("ctx", "fsdp", None),
        P("ctx", "fsdp", None),
        P(("ctx", "fsdp"), None),
        P(("ctx", "fsdp"), None),
        P(("ctx", "fsdp"), None),
        P(("ctx", "fsdp"), None),
        P(("ctx", "fsdp"), None),
        P(("ctx", "fsdp"), None),
        P(("ctx", "fsdp"), None),
        P(("ctx", "fsdp")),
        P(("ctx", "fsdp")),
    )
    return jax.shard_map(
        layer_step, mesh=mesh, in_specs=in_specs, out_specs=out_specs, check_vma=False
    )
```

```python
import functools

import jax
import jax.numpy as jnp
from jax import lax
from jax.experimental import pallas as pl
from jax.experimental.pallas import tpu as pltpu
from jax.sharding import PartitionSpec as P

HEAD_DIM = 64


EPSILON = 1e-05
ROPE_BASE = 130000.0
MASKED_SCORE = -1e30


def rotate(values, places, direction):
    half_dim = values.shape[-1] // 2
    frequency = 1.0 / ROPE_BASE ** (
        jnp.arange(half_dim, dtype=jnp.float32) * (2.0 / values.shape[-1])
    )
    angles = places[..., None] * frequency
    cosine = jnp.cos(angles)[..., None, :]
    sine_part = direction * jnp.sin(angles)[..., None, :]
    leading = values[..., :half_dim]
    trailing = values[..., half_dim:]
    return jnp.concatenate(
        [leading * cosine - trailing * sine_part, trailing * cosine + leading * sine_part], -1
    )


def matmul(left, right):
    return jnp.dot(left, right, preferred_element_type=jnp.float32)


def contract(left, right):
    return lax.dot_general(
        left, right, (((1,), (1,)), ((), ())), preferred_element_type=jnp.float32
    )


def transpose_product(left, right):
    return lax.dot_general(
        left, right, (((0,), (0,)), ((), ())), preferred_element_type=jnp.float32
    )


def split_heads(values):
    return values.reshape(values.shape[:-1] + (-1, HEAD_DIM))


def keep_state(current):
    return current


def tile_scores(queries, key_rows, query_places, key_places, score_scale):
    scores = (
        jnp.einsum("qhd,khd->hqk", queries, key_rows, preferred_element_type=jnp.float32)
        * score_scale
    )
    allowed = (key_places[None, :] <= query_places[:, None])[None]
    return (jnp.where(allowed, scores, MASKED_SCORE), allowed)


def grow_state(current, queries, key_rows, value_rows, query_places, key_places, score_scale):
    run_peak, run_total, summed = current
    scores, allowed = tile_scores(queries, key_rows, query_places, key_places, score_scale)
    new_peak = jnp.maximum(run_peak, jnp.max(scores, -1))
    weights = jnp.where(allowed, jnp.exp(scores - new_peak[..., None]), 0.0)
    factor = jnp.exp(run_peak - new_peak)
    run_total = run_total * factor + jnp.sum(weights, -1)
    summed = summed * jnp.transpose(factor)[:, :, None] + jnp.einsum(
        "hqk,khd->qhd", weights.astype(jnp.bfloat16), value_rows, preferred_element_type=jnp.float32
    )
    return (new_peak, run_total, summed)


def backward_tile(
    queries,
    key_rows,
    value_rows,
    grad_out,
    log_total,
    row_delta,
    query_places,
    key_places,
    score_scale,
):
    scores, allowed = tile_scores(queries, key_rows, query_places, key_places, score_scale)
    probabilities = jnp.where(allowed, jnp.exp(scores - log_total[..., None]), 0.0)
    grad_probs = jnp.einsum(
        "qhd,khd->hqk", grad_out, value_rows, preferred_element_type=jnp.float32
    )
    grad_scores = (probabilities * (grad_probs - row_delta[..., None])).astype(jnp.bfloat16)
    return (probabilities, grad_scores)


def norm_back(grad_normed_in, normed_values, inverse_root, gain_vector):
    scaled = grad_normed_in * gain_vector
    return inverse_root * (
        scaled - normed_values * jnp.mean(scaled * normed_values, -1, keepdims=True)
    )


def per_device(
    tokens,
    block_order,
    w_query,
    w_key,
    w_value,
    w_out,
    w_gate,
    w_up,
    w_down,
    gain_attn,
    gain_mlp,
    cotangent,
):
    slot_count, share_rows, model_width = tokens.shape
    fsdp_size = lax.axis_size("fsdp")
    block_rows = share_rows * fsdp_size
    head_width = model_width // fsdp_size
    heads_here = head_width // HEAD_DIM
    row_count = slot_count * share_rows
    score_scale = HEAD_DIM ** (-0.5)
    own_slots = 2 * lax.axis_index("ctx") + jnp.arange(2, dtype=jnp.int32)
    own_blocks = block_order[own_slots]
    token_places = (
        (
            own_blocks[:, None] * block_rows
            + lax.axis_index("fsdp") * share_rows
            + jnp.arange(share_rows, dtype=jnp.int32)[None, :]
        )
        .astype(jnp.float32)
        .reshape(row_count)
    )
    head_places = (
        own_blocks[:, None] * block_rows + jnp.arange(block_rows, dtype=jnp.int32)[None, :]
    ).astype(jnp.float32)
    params = (w_query, w_key, w_value, w_out, w_gate, w_up, w_down, gain_attn, gain_mlp)
    weights_all = (
        lax.all_gather(params[0], "fsdp", axis=0, tiled=True),
        lax.all_gather(params[1], "fsdp", axis=0, tiled=True),
        lax.all_gather(params[2], "fsdp", axis=0, tiled=True),
        lax.all_gather(params[3], "fsdp", axis=0, tiled=True),
        lax.all_gather(params[4], "fsdp", axis=0, tiled=True),
        lax.all_gather(params[5], "fsdp", axis=0, tiled=True),
        lax.all_gather(params[6], "fsdp", axis=0, tiled=True),
        lax.all_gather(params[7], "fsdp", axis=0, tiled=True),
        lax.all_gather(params[8], "fsdp", axis=0, tiled=True),
    )
    stream = tokens.reshape(row_count, model_width).astype(jnp.float32)
    root_one = lax.rsqrt(jnp.mean(stream * stream, -1, keepdims=True) + EPSILON)
    norm_one = stream * root_one
    attn_input = (norm_one * weights_all[7].astype(jnp.float32)).astype(jnp.bfloat16)

    def project_turn(weight):
        linear = matmul(attn_input, weight).reshape(row_count, -1, HEAD_DIM)
        return (
            rotate(linear, token_places, 1.0)
            .astype(jnp.bfloat16)
            .reshape(slot_count, share_rows, model_width)
        )

    query_tok = project_turn(weights_all[0])
    key_tok = project_turn(weights_all[1])
    value_tok = (
        matmul(attn_input, weights_all[2])
        .astype(jnp.bfloat16)
        .reshape(slot_count, share_rows, model_width)
    )
    query_heads, key_heads, value_heads = (
        lax.all_to_all(query_tok, "fsdp", split_axis=2, concat_axis=1, tiled=True),
        lax.all_to_all(key_tok, "fsdp", split_axis=2, concat_axis=1, tiled=True),
        lax.all_to_all(value_tok, "fsdp", split_axis=2, concat_axis=1, tiled=True),
    )
    query_split = split_heads(query_heads)
    start_state = tuple(
        (
            (
                jnp.full((heads_here, block_rows), MASKED_SCORE, jnp.float32),
                jnp.zeros((heads_here, block_rows), jnp.float32),
                jnp.zeros((block_rows, heads_here, HEAD_DIM), jnp.float32),
            )
            for which_slot in range(2)
        )
    )
    carried = start_state
    key_part = lax.all_gather(key_heads, "ctx", axis=0, tiled=True)
    value_part = lax.all_gather(value_heads, "ctx", axis=0, tiled=True)

    def visit_slot(inner_state, element):
        key_one, value_one, offset = element
        key_block = block_order[offset]
        key_places = (key_block * block_rows + jnp.arange(block_rows, dtype=jnp.int32)).astype(
            jnp.float32
        )
        key_split = split_heads(key_one)
        value_split = split_heads(value_one)
        updated = []
        for which_slot in range(2):

            def grow_one(current, which_slot=which_slot):
                return grow_state(
                    current,
                    query_split[which_slot],
                    key_split,
                    value_split,
                    head_places[which_slot],
                    key_places,
                    score_scale,
                )

            updated.append(
                lax.cond(
                    key_block <= own_blocks[which_slot],
                    grow_one,
                    keep_state,
                    inner_state[which_slot],
                )
            )
        return (tuple(updated), None)

    offsets = jnp.arange(key_part.shape[0], dtype=jnp.int32)
    carried, unused = lax.scan(visit_slot, carried, (key_part, value_part, offsets))
    attended_parts = []
    log_parts = []
    for which_slot in range(2):
        run_peak, run_total, summed = carried[which_slot]
        log_parts.append(run_peak + jnp.log(run_total))
        attended_parts.append(summed / jnp.transpose(run_total)[:, :, None])
    attended = jnp.stack(attended_parts)
    log_total = jnp.stack(log_parts)
    mixed_send = attended.reshape(slot_count, block_rows, head_width).astype(jnp.bfloat16)
    mixed_tok = lax.all_to_all(mixed_send, "fsdp", split_axis=1, concat_axis=2, tiled=True)
    mixed_flat = mixed_tok.reshape(row_count, model_width)
    middle = stream + matmul(mixed_flat, weights_all[3])
    root_two = lax.rsqrt(jnp.mean(middle * middle, -1, keepdims=True) + EPSILON)
    norm_two = middle * root_two
    mlp_input = (norm_two * weights_all[8].astype(jnp.float32)).astype(jnp.bfloat16)
    gate_act = matmul(mlp_input, weights_all[4])
    upward = matmul(mlp_input, weights_all[5])
    gate_sigmoid = jax.nn.sigmoid(gate_act)
    gate_silu = gate_act * gate_sigmoid
    hidden = (gate_silu * upward).astype(jnp.bfloat16)
    output = middle + contract(hidden, weights_all[6])
    result = output.astype(jnp.bfloat16).reshape(slot_count, share_rows, model_width)
    upstream = cotangent.reshape(row_count, model_width)
    grad_hidden = matmul(upstream, weights_all[6])
    grad_gate = (
        grad_hidden * upward * gate_sigmoid * (1.0 + gate_act * (1.0 - gate_sigmoid))
    ).astype(jnp.bfloat16)
    grad_up = (grad_hidden * gate_silu).astype(jnp.bfloat16)
    grad_two = contract(grad_gate, weights_all[4]) + contract(grad_up, weights_all[5])
    gain_two_part = jnp.sum(grad_two * norm_two, 0)
    grad_middle = upstream.astype(jnp.float32) + norm_back(
        grad_two, norm_two, root_two, weights_all[8].astype(jnp.float32)
    )
    grad_branch = grad_middle.astype(jnp.bfloat16)
    grad_mixed = (
        contract(grad_branch, weights_all[3])
        .astype(jnp.bfloat16)
        .reshape(slot_count, share_rows, model_width)
    )
    grad_heads = lax.all_to_all(grad_mixed, "fsdp", split_axis=2, concat_axis=1, tiled=True)
    grad_split = split_heads(grad_heads)
    row_delta = jnp.transpose(jnp.sum(grad_split.astype(jnp.float32) * attended, -1), (0, 2, 1))
    gathered = (
        lax.all_gather(key_heads, "ctx", axis=0, tiled=True),
        lax.all_gather(value_heads, "ctx", axis=0, tiled=True),
    )
    key_all, value_all = gathered
    total_slots = key_all.shape[0]

    def query_visit(current, element):
        key_pair, value_pair, pair_index = element
        updated = list(current)
        for member in range(2):
            key_block = block_order[2 * pair_index + member]
            key_places = (key_block * block_rows + jnp.arange(block_rows, dtype=jnp.int32)).astype(
                jnp.float32
            )
            key_split = split_heads(key_pair[member])
            value_split = split_heads(value_pair[member])
            for which_slot in range(2):

                def take_query(
                    accum,
                    which_slot=which_slot,
                    key_split=key_split,
                    value_split=value_split,
                    key_places=key_places,
                ):
                    probabilities, grad_scores = backward_tile(
                        query_split[which_slot],
                        key_split,
                        value_split,
                        grad_split[which_slot],
                        log_total[which_slot],
                        row_delta[which_slot],
                        head_places[which_slot],
                        key_places,
                        score_scale,
                    )
                    return accum + score_scale * jnp.einsum(
                        "hqk,khd->qhd", grad_scores, key_split, preferred_element_type=jnp.float32
                    )

                updated[which_slot] = lax.cond(
                    key_block <= own_blocks[which_slot], take_query, keep_state, updated[which_slot]
                )
        return (tuple(updated), None)

    query_zero = jnp.zeros((block_rows, heads_here, HEAD_DIM), jnp.float32)
    pair_keys = key_all.reshape(total_slots // 2, 2, block_rows, head_width)
    pair_values = value_all.reshape(total_slots // 2, 2, block_rows, head_width)
    grad_query_parts, unused = lax.scan(
        query_visit,
        (query_zero, query_zero),
        (pair_keys, pair_values, jnp.arange(total_slots // 2, dtype=jnp.int32)),
    )
    key_part = key_all
    value_part = value_all

    def key_visit(unused_carry, element):
        key_one, value_one, offset = element
        key_block = block_order[offset]
        key_places = (key_block * block_rows + jnp.arange(block_rows, dtype=jnp.int32)).astype(
            jnp.float32
        )
        key_split = split_heads(key_one)
        value_split = split_heads(value_one)
        sums = (
            jnp.zeros((block_rows, heads_here, HEAD_DIM), jnp.float32),
            jnp.zeros((block_rows, heads_here, HEAD_DIM), jnp.float32),
        )
        for which_slot in range(2):

            def take_keys(current, which_slot=which_slot):
                probabilities, grad_scores = backward_tile(
                    query_split[which_slot],
                    key_split,
                    value_split,
                    grad_split[which_slot],
                    log_total[which_slot],
                    row_delta[which_slot],
                    head_places[which_slot],
                    key_places,
                    score_scale,
                )
                grad_key = current[0] + score_scale * jnp.einsum(
                    "hqk,qhd->khd",
                    grad_scores,
                    query_split[which_slot],
                    preferred_element_type=jnp.float32,
                )
                grad_value = current[1] + jnp.einsum(
                    "hqk,qhd->khd",
                    probabilities.astype(jnp.bfloat16),
                    grad_split[which_slot],
                    preferred_element_type=jnp.float32,
                )
                return (grad_key, grad_value)

            sums = lax.cond(key_block <= own_blocks[which_slot], take_keys, keep_state, sums)
        joined = jnp.concatenate(
            [sums[0].reshape(block_rows, head_width), sums[1].reshape(block_rows, head_width)], -1
        )
        return (unused_carry, joined)

    unused_final, terms = lax.scan(
        key_visit,
        jnp.zeros((), jnp.float32),
        (key_part, value_part, jnp.arange(slot_count * lax.axis_size("ctx"), dtype=jnp.int32)),
    )
    summed_kv = lax.psum_scatter(
        terms.astype(jnp.bfloat16), "ctx", scatter_dimension=0, tiled=True
    ).astype(jnp.float32)
    grad_keys = (
        rotate(split_heads(summed_kv[..., :head_width]), head_places, -1.0)
        .astype(jnp.bfloat16)
        .reshape(slot_count, block_rows, head_width)
    )
    grad_values = summed_kv[..., head_width:].astype(jnp.bfloat16)
    grad_queries = (
        rotate(jnp.stack(grad_query_parts), head_places, -1.0)
        .astype(jnp.bfloat16)
        .reshape(slot_count, block_rows, head_width)
    )
    grad_q_tok, grad_k_tok, grad_v_tok = (
        lax.all_to_all(grad_queries, "fsdp", split_axis=1, concat_axis=2, tiled=True),
        lax.all_to_all(grad_keys, "fsdp", split_axis=1, concat_axis=2, tiled=True),
        lax.all_to_all(grad_values, "fsdp", split_axis=1, concat_axis=2, tiled=True),
    )
    grad_q_lin = grad_q_tok.reshape(row_count, model_width)
    grad_k_lin = grad_k_tok.reshape(row_count, model_width)
    grad_v_lin = grad_v_tok.reshape(row_count, model_width)
    grad_one = (
        contract(grad_q_lin, weights_all[0])
        + contract(grad_k_lin, weights_all[1])
        + contract(grad_v_lin, weights_all[2])
    )
    gain_one_part = jnp.sum(grad_one * norm_one, 0)
    grad_input = grad_middle + norm_back(
        grad_one, norm_one, root_one, weights_all[7].astype(jnp.float32)
    )
    hidden_width = hidden.shape[1]
    gain_parts = jnp.stack([gain_one_part, gain_two_part], 1)
    wide_cols = (
        lax.all_to_all(grad_q_lin, "fsdp", split_axis=1, concat_axis=0, tiled=True),
        lax.all_to_all(grad_k_lin, "fsdp", split_axis=1, concat_axis=0, tiled=True),
        lax.all_to_all(grad_v_lin, "fsdp", split_axis=1, concat_axis=0, tiled=True),
        lax.all_to_all(grad_branch, "fsdp", split_axis=1, concat_axis=0, tiled=True),
        lax.all_to_all(grad_gate, "fsdp", split_axis=1, concat_axis=0, tiled=True),
        lax.all_to_all(grad_up, "fsdp", split_axis=1, concat_axis=0, tiled=True),
        lax.all_to_all(hidden, "fsdp", split_axis=1, concat_axis=0, tiled=True),
    )
    row_sets = (
        lax.all_gather(attn_input, "fsdp", axis=0, tiled=True),
        lax.all_gather(mixed_flat, "fsdp", axis=0, tiled=True),
        lax.all_gather(mlp_input, "fsdp", axis=0, tiled=True),
        lax.all_gather(upstream, "fsdp", axis=0, tiled=True),
    )
    group_rows = model_width // lax.axis_size("ctx")
    row_cuts = [values for values in row_sets]
    pieces = [
        transpose_product(row_cuts[0], wide_cols[0]),
        transpose_product(row_cuts[0], wide_cols[1]),
        transpose_product(row_cuts[0], wide_cols[2]),
        transpose_product(row_cuts[1], wide_cols[3]),
        transpose_product(row_cuts[2], wide_cols[4]),
        transpose_product(row_cuts[2], wide_cols[5]),
        transpose_product(row_cuts[3], wide_cols[6]),
        gain_parts,
        jnp.zeros((group_rows * lax.axis_size("ctx"), 126), jnp.float32),
    ]
    partial_sums = lax.psum_scatter(
        jnp.concatenate(pieces, 1).astype(jnp.bfloat16), "ctx", scatter_dimension=0, tiled=True
    ).astype(jnp.float32)
    owned = lax.all_to_all(
        partial_sums.astype(jnp.bfloat16), "fsdp", split_axis=0, concat_axis=1, tiled=True
    ).astype(partial_sums.dtype)
    span_width = partial_sums.shape[1]
    owned_rows = owned.shape[0]
    arranged = owned.reshape(owned_rows, fsdp_size, span_width)
    model_part = model_width // fsdp_size
    hidden_part = hidden_width // fsdp_size
    bounds = [
        0,
        model_part,
        2 * model_part,
        3 * model_part,
        4 * model_part,
        4 * model_part + hidden_part,
        4 * model_part + 2 * hidden_part,
        4 * model_part + 3 * hidden_part,
    ]

    def joined_cols(first_col, last_col):
        return arranged[:, :, first_col:last_col].reshape(owned_rows, -1)

    grad_w_query = joined_cols(bounds[0], bounds[1])
    grad_w_key = joined_cols(bounds[1], bounds[2])
    grad_w_value = joined_cols(bounds[2], bounds[3])
    grad_w_out = joined_cols(bounds[3], bounds[4])
    grad_w_gate = joined_cols(bounds[4], bounds[5])
    grad_w_up = joined_cols(bounds[5], bounds[6])
    grad_w_down = joined_cols(bounds[6], bounds[7])
    gain_totals = jnp.sum(arranged[:, :, bounds[7] : bounds[7] + 2], 1)
    grad_gain_attn = gain_totals[:, 0]
    grad_gain_mlp = gain_totals[:, 1]
    grad_tokens = grad_input.reshape(slot_count, share_rows, model_width)
    return (
        result,
        grad_tokens,
        grad_w_query,
        grad_w_key,
        grad_w_value,
        grad_w_out,
        grad_w_gate,
        grad_w_up,
        grad_w_down,
        grad_gain_attn,
        grad_gain_mlp,
    )


def dot_f32(a, b):
    return jnp.dot(a, b, preferred_element_type=jnp.float32)

def load_sequence(order_ref, rows_ref, block, stores):
    per_src = rows_ref.shape[2] // block
    def one(slot, carry):
        src = slot // per_src
        lane = pl.multiple_of((slot % per_src) * block, block)
        place = pl.multiple_of(order_ref[slot] * block, block)
        for at, store in stores:
            store(rows_ref[src, at:at + HEAD_DIM, pl.ds(lane, block)], place)
        return carry
    lax.fori_loop(0, rows_ref.shape[0] * per_src, one, 0)

def fwd_kernel(
    order_ref, qkv_ref, mixed_ref, out_ref, lse_ref, qt, kr, vt, peak, total, acc, *, block, tile, step
):
    seq = qt.shape[1]

    def put_q(x, place):
        qt[:, pl.ds(place, block)] = x * jnp.bfloat16(HEAD_DIM ** -0.5)

    def put_k(x, place):
        kr[pl.ds(place, block), :] = x.T

    def put_v(x, place):
        vt[:, pl.ds(place, block)] = x

    load_sequence(
        order_ref, qkv_ref, block, ((0, put_q), (HEAD_DIM, put_k), (2 * HEAD_DIM, put_v))
    )

    def one_tile(qi, unused):
        q0 = pl.multiple_of(qi * tile, tile)
        peak[...] = jnp.full_like(peak, MASKED_SCORE)
        total[...] = jnp.zeros_like(total)
        acc[...] = jnp.zeros_like(acc)

        def visit(k0, first, masked):
            queries = qt[:, pl.ds(pl.multiple_of(q0 + first, step), tile - first)]
            s = dot_f32(kr[pl.ds(k0, step), :], queries)
            if masked:
                keep = lax.broadcasted_iota(jnp.int32, s.shape, 0) <= lax.broadcasted_iota(
                    jnp.int32, s.shape, 1
                )
                s = jnp.where(keep, s, MASKED_SCORE)
            old = peak[:, first:]
            new = jnp.maximum(old, jnp.max(s, 0, keepdims=True))
            p = jnp.exp(s - new)
            alpha = jnp.exp(old - new)
            peak[:, first:] = new
            total[:, first:] = total[:, first:] * alpha + jnp.sum(p, 0, keepdims=True)
            acc[:, first:] = acc[:, first:] * alpha + dot_f32(
                vt[:, pl.ds(k0, step)], p.astype(jnp.bfloat16)
            )

        def below(j, carry):
            visit(pl.multiple_of(j * step, step), 0, False)
            return carry

        lax.fori_loop(0, qi * (tile // step), below, 0)
        for part in range(tile // step):
            visit(pl.multiple_of(q0 + part * step, step), part * step, True)
        out_ref[:, pl.ds(q0, tile)] = acc[...] / total[...]
        lse_ref[:, pl.ds(q0, tile)] = peak[...] + jnp.log(total[...])
        return unused

    lax.fori_loop(0, seq // tile, one_tile, 0)
    per_src = mixed_ref.shape[2] // block

    def send(slot, carry):
        place = pl.multiple_of(order_ref[slot] * block, block)
        lane = pl.multiple_of((slot % per_src) * block, block)
        mixed_ref[slot // per_src, :, pl.ds(lane, block)] = out_ref[:, pl.ds(place, block)].astype(
            jnp.bfloat16
        )
        return carry

    lax.fori_loop(0, mixed_ref.shape[0] * per_src, send, 0)


def attend(order, qkv, block, tile, step):
    groups, unused, width = qkv.shape
    seq = groups * width
    vm = pl.BlockSpec(memory_space=pltpu.VMEM)
    bf, f32 = jnp.bfloat16, jnp.float32
    return pl.pallas_call(
        functools.partial(fwd_kernel, block=block, tile=tile, step=step),
        out_shape=(
            jax.ShapeDtypeStruct((groups, HEAD_DIM, width), bf),
            jax.ShapeDtypeStruct((HEAD_DIM, seq), f32),
            jax.ShapeDtypeStruct((1, seq), f32),
        ),
        in_specs=[pl.BlockSpec(memory_space=pltpu.SMEM), vm],
        out_specs=(vm, vm, vm),
        scratch_shapes=[
            pltpu.VMEM((HEAD_DIM, seq), bf),
            pltpu.VMEM((seq, HEAD_DIM), bf),
            pltpu.VMEM((HEAD_DIM, seq), bf),
            pltpu.VMEM((1, tile), f32),
            pltpu.VMEM((1, tile), f32),
            pltpu.VMEM((HEAD_DIM, tile), f32),
        ],
        compiler_params=pltpu.CompilerParams(vmem_limit_bytes=48 << 20),
        cost_estimate=pl.CostEstimate(
            flops=int(4.0 * seq * seq * HEAD_DIM),
            bytes_accessed=8 * seq * HEAD_DIM,
            transcendentals=0,
        ),
        name="attend",
    )(order, qkv)


def bwd_kernel(order_ref, qkv_ref, go_ref, out_ref, lse_ref, cos_ref, sin_ref, grad_ref,
               qt, qr, kt, kr, vr, got, gor, delta, dqt, dkr, dvr, *, block, tile, step):
    seq = qt.shape[1]
    scale = jnp.bfloat16(HEAD_DIM ** -0.5)
    def put_q(x, place):
        x = x * scale
        qt[:, pl.ds(place, block)] = x
        qr[pl.ds(place, block), :] = x.T
    def put_k(x, place):
        kt[:, pl.ds(place, block)] = x * scale
        kr[pl.ds(place, block), :] = x.T
    def put_v(x, place):
        vr[pl.ds(place, block), :] = x.T
    def put_go(x, place):
        got[:, pl.ds(place, block)] = x
        gor[pl.ds(place, block), :] = x.T
        delta[:, pl.ds(place, block)] = jnp.sum(x.astype(jnp.float32) * out_ref[:, pl.ds(place, block)], 0, keepdims=True)
    load_sequence(order_ref, qkv_ref, block, ((0, put_q), (HEAD_DIM, put_k), (2 * HEAD_DIM, put_v)))
    load_sequence(order_ref, go_ref, block, ((0, put_go),))
    dqt[...] = jnp.zeros_like(dqt)
    tiles = seq // tile

    def key_tile(kj, unused):
        k0 = pl.multiple_of(kj * tile, tile)
        keys = kr[pl.ds(k0, tile), :]
        keys_t = kt[:, pl.ds(k0, tile)]
        vals = vr[pl.ds(k0, tile), :]
        dkr[...] = jnp.zeros_like(dkr)
        dvr[...] = jnp.zeros_like(dvr)

        def visit(q0, width, rows, masked):
            s = dot_f32(keys[:rows], qt[:, pl.ds(q0, width)])
            p = jnp.exp(s - lse_ref[:, pl.ds(q0, width)])
            if masked:
                keep = lax.broadcasted_iota(jnp.int32, s.shape, 0) <= lax.broadcasted_iota(
                    jnp.int32, s.shape, 1
                ) + (rows - width)
                p = jnp.where(keep, p, 0.0)
            dp = dot_f32(vals[:rows], got[:, pl.ds(q0, width)])
            ds = (p * (dp - delta[:, pl.ds(q0, width)])).astype(jnp.bfloat16)
            dvr[:rows] += dot_f32(p.astype(jnp.bfloat16), gor[pl.ds(q0, width), :])
            dkr[:rows] += dot_f32(ds, qr[pl.ds(q0, width), :])
            dqt[:, pl.ds(q0, width)] += dot_f32(keys_t[:, :rows], ds)

        for part in range(tile // step):
            first = pl.multiple_of(k0 + part * step, step)
            visit(first, step, (part + 1) * step, True)

        def later(j, carry):
            visit(pl.multiple_of(j * step, step), step, tile, False)
            return carry

        lax.fori_loop((kj + 1) * (tile // step), seq // step, later, 0)
        put_out(dkr[...].T, HEAD_DIM, k0, True)
        put_out(dvr[...].T, 2 * HEAD_DIM, k0, False)
        return unused

    half = HEAD_DIM // 2
    def put_out(x, at, place, turn):
        for part in range(tile // block):
            piece = x[:, part * block:(part + 1) * block]
            here = place + part * block
            if turn:
                lanes = pl.ds(pl.multiple_of(here, block), block)
                c, s = cos_ref[:, lanes], sin_ref[:, lanes]
                a, b = piece[:half], piece[half:]
                piece = jnp.concatenate([a * c + b * s, b * c - a * s], 0)
            slot = order_ref[seq // block + here // block]
            per_src = grad_ref.shape[2] // block
            lane = pl.multiple_of((slot % per_src) * block, block)
            grad_ref[slot // per_src, at:at + HEAD_DIM, pl.ds(lane, block)] = piece.astype(jnp.bfloat16)

    lax.fori_loop(0, tiles, key_tile, 0)
    def write_q(qi, c):
        q0 = pl.multiple_of(qi * tile, tile)
        put_out(dqt[:, pl.ds(q0, tile)], 0, q0, True)
        return c
    lax.fori_loop(0, tiles, write_q, 0)

def attend_back(order, qkv, go, out, lse, cos, sin, block, tile, step):
    groups, unused, width = qkv.shape
    seq = groups * width
    vm = pl.BlockSpec(memory_space=pltpu.VMEM)
    bf, f32 = jnp.bfloat16, jnp.float32
    wide = lambda t: pltpu.VMEM((HEAD_DIM, seq), t)
    tall = lambda t: pltpu.VMEM((seq, HEAD_DIM), t)
    return pl.pallas_call(
        functools.partial(bwd_kernel, block=block, tile=tile, step=step),
        out_shape=jax.ShapeDtypeStruct(qkv.shape, bf),
        in_specs=[pl.BlockSpec(memory_space=pltpu.SMEM)] + [vm] * 6,
        out_specs=vm,
        scratch_shapes=[wide(bf), tall(bf), wide(bf), tall(bf), tall(bf), wide(bf), tall(bf),
                        pltpu.VMEM((1, seq), f32), wide(f32),
                        pltpu.VMEM((tile, HEAD_DIM), f32), pltpu.VMEM((tile, HEAD_DIM), f32)],
        compiler_params=pltpu.CompilerParams(vmem_limit_bytes=48 << 20),
        cost_estimate=pl.CostEstimate(
            flops=int(6.4 * seq * seq * HEAD_DIM),
            bytes_accessed=16 * seq * HEAD_DIM,
            transcendentals=0,
        ),
        name="attend_back",
    )(order, qkv, go, out, lse, cos, sin)


def nt_dot(a, b):
    return lax.dot_general(a, b, (((1,), (1,)), ((), ())), preferred_element_type=jnp.float32)


def whole(space=pltpu.VMEM):
    return pl.BlockSpec(memory_space=space)


def spread(pieces, place_ref, rows_ref):
    hops = (len(pieces) - 1) // 2
    slots, share, unused = pieces[0].shape
    place = place_ref[0]

    def put(piece, position):
        for slot in range(slots):
            first = pl.multiple_of(slot * share * (hops + 1) + position * share, share)
            rows_ref[pl.ds(first, share), :] = piece[slot]

    put(pieces[0], place)
    for hop in range(1, hops + 1):

        @pl.when(place >= hop)
        def take_below(hop=hop):
            put(pieces[hop], place - hop)

        @pl.when(place + hop <= hops)
        def take_above(hop=hop):
            put(pieces[hops + hop], place + hop)


def deal(rows_ref, place_ref, own_ref, others):
    slots, share, unused = own_ref.shape
    line = len(others) + 1
    for step, target in enumerate([own_ref] + list(others)):
        position = lax.rem(place_ref[0] + step, line)
        for slot in range(slots):
            first = pl.multiple_of(slot * share * line + position * share, share)
            target[slot] = rows_ref[pl.ds(first, share), :].astype(target.dtype)


def dealt_shapes(slots, share, width, line):
    return [jax.ShapeDtypeStruct((slots, share, width), jnp.float32)] + [
        jax.ShapeDtypeStruct((slots, share, width), jnp.bfloat16) for unused in range(line - 1)
    ]


def work(flops, bytes_accessed=0, transcendentals=0):
    return pl.CostEstimate(
        flops=int(flops * 0.2), bytes_accessed=int(bytes_accessed * 0.2), transcendentals=0
    )


def vmem_limit(mebibytes):
    return pltpu.CompilerParams(vmem_limit_bytes=mebibytes << 20)


EXTRA_ROWS = 16
LANES = 128


def cut_columns(place, group, weights, rows, line, extra=None):
    count = len(weights)
    columns = weights[0].shape[1] // line
    cut_rows = count * rows + (EXTRA_ROWS if extra is not None else 0)
    extras = [] if extra is None else [extra]

    def kernel(place_ref, group_ref, *refs):
        outs = refs[count * line + len(extras) :]
        for step in range(line):
            for i in range(count):
                outs[step][i * rows : (i + 1) * rows] = refs[step * count + i][...]
            if extras:
                outs[step][count * rows :] = refs[count * line][...]

    def target(step):
        return lambda i, place, group: (group[0], lax.rem(place[0] + step, line))

    fixed = lambda shape: pl.BlockSpec(shape, lambda i, place, group: (0, 0))
    return pl.pallas_call(
        kernel,
        out_shape=[jax.ShapeDtypeStruct((cut_rows, columns), jnp.bfloat16)] * line,
        grid_spec=pltpu.PrefetchScalarGridSpec(
            num_scalar_prefetch=2,
            grid=(1,),
            in_specs=[
                pl.BlockSpec((rows, columns), target(step))
                for step in range(line)
                for unused in range(count)
            ]
            + [fixed((EXTRA_ROWS, columns)) for unused in extras],
            out_specs=[fixed((cut_rows, columns))] * line,
        ),
        compiler_params=vmem_limit(60),
        name="cut_columns",
    )(place, group, *(list(weights) * line), *extras)


def order_shares(place, shares, count, vectors=0):
    line = len(shares)
    share_rows, columns = shares[0].shape
    rows = (share_rows - (EXTRA_ROWS if vectors else 0)) // count

    def kernel(place_ref, *refs):
        for step in range(line):
            source = lax.rem(place_ref[0] + line - step, line)
            for i in range(count):
                refs[line][source, i] = refs[step][i * rows : (i + 1) * rows]
            if vectors:
                lanes = pl.ds(pl.multiple_of(source * columns, columns), columns)
                refs[line + 1][:, lanes] = refs[step][count * rows :].astype(jnp.float32)

    shapes = [jax.ShapeDtypeStruct((line, count, rows, columns), shares[0].dtype)]
    if vectors:
        shapes.append(jax.ShapeDtypeStruct((EXTRA_ROWS, line * columns), jnp.float32))
    outs = pl.pallas_call(
        kernel,
        out_shape=shapes,
        in_specs=[whole(pltpu.SMEM)] + [whole()] * line,
        out_specs=[whole()] * len(shapes),
        compiler_params=vmem_limit(40),
        name="order_shares",
    )(place, *shares)
    return (outs[0], outs[1][:vectors]) if vectors else outs[0]


def widen_columns(place, shares, count, rows):
    line = len(shares)
    share_rows, columns = shares[0].shape

    def kernel(place_ref, *refs):
        for step in range(line):

            @pl.when(pl.program_id(0) == step)
            def widen(step=step):
                for i in range(count):
                    refs[line + i][...] = refs[step][i * rows : (i + 1) * rows].astype(jnp.float32)

    return pl.pallas_call(
        kernel,
        out_shape=[jax.ShapeDtypeStruct((rows, line * columns), jnp.float32)] * count,
        grid_spec=pltpu.PrefetchScalarGridSpec(
            num_scalar_prefetch=1,
            grid=(line,),
            in_specs=[pl.BlockSpec((share_rows, columns), lambda j, place: (0, 0))] * line,
            out_specs=[
                pl.BlockSpec(
                    (rows, columns), lambda j, place: (0, lax.rem(place[0] + line - j, line))
                )
            ]
            * count,
        ),
        compiler_params=vmem_limit(40),
        name="widen_columns",
    )(place, *shares)


def project(place, pieces, gain, w_heads, cosine, sine):
    line, count, part, width = w_heads.shape
    slots, share, model_width = pieces[0].shape
    rows = slots * share * line
    tile = width // 2
    heads = tile // HEAD_DIM
    n_pieces = len(pieces)
    half = HEAD_DIM // 2

    def kernel(place_ref, *refs):
        piece_refs = refs[:n_pieces]
        gain_ref, w_ref, cos_ref, sin_ref, rows_ref, out_ref = refs[n_pieces:]

        @pl.when((pl.program_id(0) == 0) & (pl.program_id(1) == 0))
        def assemble():
            spread(piece_refs, place_ref, rows_ref)
            rows_ref[...] = (rows_ref[...].astype(jnp.float32) * gain_ref[...]).astype(jnp.bfloat16)

        weight = w_ref[...].reshape(line * part, tile)
        turned = dot_f32(rows_ref[...], weight).T
        c, s = cos_ref[0], sin_ref[0]
        for head in range(heads):
            a = turned[head * HEAD_DIM : head * HEAD_DIM + half]
            b = turned[head * HEAD_DIM + half : (head + 1) * HEAD_DIM]
            out_ref[head, 0, :half, :] = (a * c - b * s).astype(jnp.bfloat16)
            out_ref[head, 0, half:, :] = (b * c + a * s).astype(jnp.bfloat16)

    return pl.pallas_call(
        kernel,
        grid=(count, 2),
        out_shape=[
            jax.ShapeDtypeStruct((rows, model_width), jnp.bfloat16),
            jax.ShapeDtypeStruct((width // HEAD_DIM, count, HEAD_DIM, rows), jnp.bfloat16),
        ],
        in_specs=[whole(pltpu.SMEM)]
        + [whole()] * (n_pieces + 1)
        + [
            pl.BlockSpec((line, 1, part, tile), lambda m, h: (0, m, 0, h)),
            pl.BlockSpec((1, half, rows), lambda m, h: (m, 0, 0)),
            pl.BlockSpec((1, half, rows), lambda m, h: (m, 0, 0)),
        ],
        out_specs=[
            pl.BlockSpec((rows, model_width), lambda m, h: (0, 0)),
            pl.BlockSpec((heads, 1, HEAD_DIM, rows), lambda m, h: (h, m, 0, 0)),
        ],
        compiler_params=vmem_limit(48),
        cost_estimate=work(6 * rows * model_width * width, 8 * rows * model_width),
        name="project",
    )(place, *pieces, gain, w_heads, cosine, sine)


def mix_out(place, mixed, w_out, slots, line):
    heads, unused, rows = mixed.shape
    width, model_width = w_out.shape
    share = rows // slots // line

    def kernel(place_ref, mixed_ref, w_ref, own_ref, *rest):
        *others, total = rest
        left = mixed_ref[...].reshape(width, rows).T
        total[...] = dot_f32(left, w_ref[...])
        deal(total, place_ref, own_ref, others)

    return pl.pallas_call(
        kernel,
        out_shape=dealt_shapes(slots, share, model_width, line),
        in_specs=[whole(pltpu.SMEM), whole(), whole()],
        out_specs=[whole()] * line,
        scratch_shapes=[pltpu.VMEM((rows, model_width), jnp.float32)],
        compiler_params=vmem_limit(48),
        cost_estimate=work(2 * rows * model_width * width, 8 * rows * model_width),
        name="mix_out",
    )(place, mixed, w_out)


def mlp_forward(place, pieces, upstream_pieces, w_mlp, tile):
    line, count, part, width = w_mlp.shape
    slots, share, model_width = pieces[0].shape
    rows = slots * share * line
    n_pieces = len(pieces)
    bf, f32 = jnp.bfloat16, jnp.float32

    def kernel(place_ref, *refs):
        x_pieces, u_pieces = refs[:n_pieces], refs[n_pieces : 2 * n_pieces]
        w_ref, x_ref, u_ref, hidden_ref, gate_ref, up_ref, own_ref = refs[
            2 * n_pieces : 2 * n_pieces + 7
        ]
        *others, total = refs[2 * n_pieces + 7 :]
        step = pl.program_id(0)

        @pl.when(step == 0)
        def assemble():
            spread(x_pieces, place_ref, x_ref)
            spread(u_pieces, place_ref, u_ref)

        down = w_ref[:, 0].reshape(line * part, tile)
        gate = w_ref[:, 1].reshape(line * part, tile)
        up = w_ref[:, 2].reshape(line * part, tile)
        x = x_ref[...]
        grad_hidden = dot_f32(u_ref[...], down)
        gate_act = dot_f32(x, gate)
        upward = dot_f32(x, up)
        sigmoid = jax.nn.sigmoid(gate_act)
        silu = gate_act * sigmoid
        hidden_ref[...] = (silu * upward).astype(bf)
        grad_gate = (
            grad_hidden * upward * sigmoid * (1.0 + gate_act * (1.0 - sigmoid))
        ).astype(bf)
        grad_up = (grad_hidden * silu).astype(bf)
        gate_ref[...] = grad_gate
        up_ref[...] = grad_up
        part_two = nt_dot(grad_gate, gate) + nt_dot(grad_up, up)

        @pl.when(step == 0)
        def first():
            total[...] = part_two

        @pl.when(step > 0)
        def further():
            total[...] += part_two

        @pl.when(step == pl.num_programs(0) - 1)
        def last():
            deal(total, place_ref, own_ref, others)

    fixed = lambda shape: pl.BlockSpec(shape, lambda j: (0,) * len(shape))
    columns = pl.BlockSpec((rows, tile), lambda j: (0, j))
    dealt = dealt_shapes(slots, share, model_width, line)
    return pl.pallas_call(
        kernel,
        grid=(width // tile,),
        out_shape=[jax.ShapeDtypeStruct((rows, model_width), bf)] * 2
        + [jax.ShapeDtypeStruct((rows, width), bf)] * 3
        + dealt,
        in_specs=[whole(pltpu.SMEM)]
        + [whole()] * (2 * n_pieces)
        + [pl.BlockSpec((line, count, part, tile), lambda j: (0, 0, 0, j))],
        out_specs=[fixed((rows, model_width))] * 2
        + [columns] * 3
        + [fixed((slots, share, model_width))] * line,
        scratch_shapes=[pltpu.VMEM((rows, model_width), f32)],
        compiler_params=vmem_limit(60),
        cost_estimate=work(16 * rows * model_width * width, 14 * model_width * width),
        name="mlp_forward",
    )(place, *pieces, *upstream_pieces, w_mlp)


def gate_up_weights(x_rows, grad_gate, grad_up, groups, line, tile):
    rows, model_width = x_rows.shape
    width = grad_gate.shape[1]
    block = model_width // groups // line

    def kernel(x_ref, gate_ref, up_ref, out_ref, x_turned):
        @pl.when(pl.program_id(0) == 0)
        def turn():
            x_turned[...] = x_ref[...].T

        for i, ref in enumerate((gate_ref, up_ref)):
            grads = dot_f32(x_turned[...], ref[...]).astype(jnp.bfloat16)
            out_ref[:, :, i * block : (i + 1) * block] = grads.reshape(groups, line, block, tile)

    columns = pl.BlockSpec((rows, tile), lambda j: (0, j))
    return pl.pallas_call(
        kernel,
        grid=(width // tile,),
        out_shape=jax.ShapeDtypeStruct((groups, line, 2 * block, width), jnp.bfloat16),
        in_specs=[pl.BlockSpec((rows, model_width), lambda j: (0, 0)), columns, columns],
        out_specs=pl.BlockSpec((groups, line, 2 * block, tile), lambda j: (0, 0, 0, j)),
        scratch_shapes=[pltpu.VMEM((model_width, rows), jnp.bfloat16)],
        compiler_params=vmem_limit(60),
        cost_estimate=work(4 * rows * model_width * width, 8 * model_width * width),
        name="gate_up_weights",
    )(x_rows, grad_gate, grad_up)


def down_weights(place, u_rows, hidden, w_mlp, slots, groups, tile):
    line, count, part, width = w_mlp.shape
    rows, model_width = u_rows.shape
    share = rows // slots // line
    block = model_width // groups // line
    bf, f32 = jnp.bfloat16, jnp.float32

    def kernel(place_ref, u_ref, hidden_ref, w_ref, d_ref, own_ref, *rest):
        *others, u_turned, total = rest
        step = pl.program_id(0)

        @pl.when(step == 0)
        def turn():
            u_turned[...] = u_ref[...].T

        grads = dot_f32(u_turned[...], hidden_ref[...]).astype(bf)
        d_ref[:, :line] = grads.reshape(groups, line, block, tile)
        part_out = nt_dot(hidden_ref[...], w_ref[...].reshape(line * part, tile))

        @pl.when(step == 0)
        def first():
            total[...] = part_out

        @pl.when(step > 0)
        def further():
            total[...] += part_out

        @pl.when(step == pl.num_programs(0) - 1)
        def last():
            deal(total, place_ref, own_ref, others)

    fixed = lambda shape: pl.BlockSpec(shape, lambda j: (0,) * len(shape))
    return pl.pallas_call(
        kernel,
        grid=(width // tile,),
        out_shape=[jax.ShapeDtypeStruct((groups, line + 1, block, width), bf)]
        + dealt_shapes(slots, share, model_width, line),
        in_specs=[
            whole(pltpu.SMEM),
            fixed((rows, model_width)),
            pl.BlockSpec((rows, tile), lambda j: (0, j)),
            pl.BlockSpec((line, 1, part, tile), lambda j: (0, 0, 0, j)),
        ],
        out_specs=[pl.BlockSpec((groups, line + 1, block, tile), lambda j: (0, 0, 0, j))]
        + [fixed((slots, share, model_width))] * line,
        scratch_shapes=[pltpu.VMEM((model_width, rows), bf), pltpu.VMEM((rows, model_width), f32)],
        compiler_params=vmem_limit(60),
        cost_estimate=work(4 * rows * model_width * width, 8 * model_width * width),
        name="down_weights",
    )(place, u_rows, hidden, w_mlp)


def branch_back(place, pieces, w_out, heads):
    slots, share, model_width = pieces[0].shape
    line = (len(pieces) + 1) // 2
    rows = slots * share * line

    def kernel(place_ref, *refs):
        *piece_refs, w_ref, rows_ref, out_ref = refs
        spread(piece_refs, place_ref, rows_ref)
        turned = nt_dot(w_ref[...], rows_ref[...])
        out_ref[...] = turned.astype(jnp.bfloat16).reshape(out_ref.shape)

    return pl.pallas_call(
        kernel,
        out_shape=[
            jax.ShapeDtypeStruct((rows, model_width), jnp.bfloat16),
            jax.ShapeDtypeStruct((heads, HEAD_DIM, rows), jnp.bfloat16),
        ],
        in_specs=[whole(pltpu.SMEM)] + [whole()] * (len(pieces) + 1),
        out_specs=[whole(), whole()],
        compiler_params=vmem_limit(40),
        cost_estimate=work(2 * rows * model_width * heads * HEAD_DIM, 8 * rows * model_width),
        name="branch_back",
    )(place, *pieces, w_out)


def out_weight(grads, mixed, branch_rows, tile):
    groups, blocks, block, width = grads.shape
    heads, unused, rows = mixed.shape

    def kernel(grads_ref, mixed_ref, rows_ref, out_ref):
        left = mixed_ref[...].reshape(heads * HEAD_DIM, rows)
        product = dot_f32(left, rows_ref[...]).astype(jnp.bfloat16)
        out_ref[...] = product.reshape(groups, 1, block, tile)

    return pl.pallas_call(
        kernel,
        grid=(width // tile,),
        out_shape=jax.ShapeDtypeStruct(grads.shape, grads.dtype),
        in_specs=[
            pl.BlockSpec(memory_space=pl.ANY),
            pl.BlockSpec(mixed.shape, lambda j: (0, 0, 0)),
            pl.BlockSpec((rows, tile), lambda j: (0, j)),
        ],
        out_specs=pl.BlockSpec((groups, 1, block, tile), lambda j: (0, blocks - 1, 0, j)),
        input_output_aliases={0: 0},
        compiler_params=vmem_limit(60),
        cost_estimate=work(4 * rows * heads * HEAD_DIM * width, 8 * rows * width),
        name="out_weight",
    )(grads, mixed, branch_rows)


def head_weights(group, all_rows, corner, head_grads, w_head, gain, gain_two, owners):
    sources, features, rows = head_grads.shape
    model_width = all_rows[0].shape[1]
    block = model_width // owners
    lanes = 2 * LANES
    half = rows // 2
    f32 = jnp.float32

    def kernel(group_ref, *refs):
        x_refs, corner_refs = refs[: sources - 2], refs[sources - 2 : sources + 2]
        g_ref, w_ref, gain_ref, two_ref, out_ref, total = refs[sources + 2 :]
        step = pl.program_id(0)

        def product(bits, ref):
            return dot_f32(g_ref[lax.bitwise_xor(group_ref[0], bits)], ref[...])

        part = sum(product(bits, ref) for bits, ref in enumerate(x_refs))

        def with_corner(half_refs):
            return part + product(sources - 2, half_refs[0]) + product(sources - 1, half_refs[1])

        @pl.when(step == 0)
        def first():
            total[...] = with_corner(corner_refs[0::2])

        @pl.when(step == 1)
        def last():
            grads = (total[...] + with_corner(corner_refs[1::2])).T
            weighed = jnp.sum(grads * w_ref[...].astype(f32), 1, keepdims=True) / gain_ref[...].T
            spare = lanes - features
            at = lax.broadcasted_iota(jnp.int32, (model_width, spare), 1)
            tail = jnp.where(at == 0, weighed, jnp.where(at == 1, two_ref[...].T, 0.0))
            joined = jnp.concatenate([grads, tail], 1).astype(jnp.bfloat16)
            out_ref[...] = joined.reshape(owners, block, lanes)

    fixed = lambda shape: pl.BlockSpec(shape, lambda s: (0,) * len(shape))
    return pl.pallas_call(
        kernel,
        grid=(2,),
        out_shape=jax.ShapeDtypeStruct((owners, block, lanes), jnp.bfloat16),
        in_specs=[whole(pltpu.SMEM)]
        + [pl.BlockSpec((half, model_width), lambda s: (s, 0))] * (sources - 2)
        + [fixed((half, model_width))] * 4
        + [
            pl.BlockSpec((sources, features, half), lambda s: (0, 0, s)),
            fixed((model_width, features)),
            fixed((1, model_width)),
            fixed((1, model_width)),
        ],
        out_specs=fixed((owners, block, lanes)),
        scratch_shapes=[pltpu.VMEM((features, model_width), f32)],
        compiler_params=vmem_limit(60),
        cost_estimate=work(6 * sources * rows * features * model_width, 0),
        name="head_weights",
    )(group, *all_rows, *corner, head_grads, w_head, gain, gain_two)


def join_heads(parts):
    groups, line, rows, lanes = parts.shape
    width = groups * HEAD_DIM

    def kernel(parts_ref, *outs):
        for i, out in enumerate(outs):
            pick = slice(i * HEAD_DIM, (i + 1) * HEAD_DIM)
            heads = [parts_ref[c, 0][:, pick].astype(jnp.float32) for c in range(groups)]
            out[...] = jnp.concatenate(heads, 1)

    return pl.pallas_call(
        kernel,
        grid=(line,),
        out_shape=[jax.ShapeDtypeStruct((rows, line * width), jnp.float32)] * 3,
        in_specs=[pl.BlockSpec((groups, 1, rows, lanes), lambda f: (0, f, 0, 0))],
        out_specs=[pl.BlockSpec((rows, width), lambda f: (0, f))] * 3,
        compiler_params=vmem_limit(24),
        name="join_heads",
    )(parts)


def project_back(place, head_grads, w_heads, slots):
    line, count, part, width = w_heads.shape
    rows, model_width = head_grads.shape[-1], line * part
    heads = width // HEAD_DIM
    share = rows // slots // line

    def kernel(place_ref, g_ref, w_ref, own_ref, *rest):
        *others, total = rest
        m = pl.program_id(0)
        grads = g_ref[...].reshape(width, rows).T
        partial = nt_dot(grads, w_ref[...].reshape(line * part, width))

        @pl.when(m == 0)
        def first():
            total[...] = partial

        @pl.when(m > 0)
        def further():
            total[...] += partial

        @pl.when(m == count - 1)
        def last():
            deal(total, place_ref, own_ref, others)

    fixed = lambda shape: pl.BlockSpec(shape, lambda m: (0,) * len(shape))
    return pl.pallas_call(
        kernel,
        grid=(count,),
        out_shape=dealt_shapes(slots, share, model_width, line),
        in_specs=[
            whole(pltpu.SMEM),
            pl.BlockSpec((heads, 1, HEAD_DIM, rows), lambda m: (0, m, 0, 0)),
            pl.BlockSpec((line, 1, part, width), lambda m: (0, m, 0, 0)),
        ],
        out_specs=[fixed((slots, share, model_width))] * line,
        scratch_shapes=[pltpu.VMEM((rows, model_width), jnp.float32)],
        compiler_params=vmem_limit(48),
        cost_estimate=work(2 * count * rows * width * model_width, 8 * rows * model_width),
        name="project_back",
    )(place, head_grads, w_heads)


def line_steps(size, step):
    return [(i, i + step) for i in range(size) if 0 <= i + step < size]


def after(values, *earlier):
    return lax.optimization_barrier((values, earlier))[0]


def send_shares(share, axis, between=()):
    size = lax.axis_size(axis)
    ups, downs = [share], [share]
    for hop in range(1, size):
        up = lax.ppermute(ups[-1], axis, line_steps(size, 1)[hop - 1 :])
        down = lax.ppermute(downs[-1], axis, line_steps(size, -1)[: size - hop])
        if hop <= len(between):
            done = between[hop - 1]((ups[-1], downs[-1]))
            up, down = after((up, down), done)
        ups.append(up)
        downs.append(down)
    return ups + downs[1:]


def flip(values, bits):
    size = lax.axis_size("ctx")
    return lax.ppermute(values, "ctx", [(i, i ^ bits) for i in range(size)])


def send_dealt(others, axis):
    size = lax.axis_size(axis)
    return [
        lax.ppermute(other, axis, [(i, (i + step) % size) for i in range(size)])
        for step, other in enumerate(others, 1)
    ]


def scatter_line(others, axis, between=()):
    size = lax.axis_size(axis)
    up = down = None
    for hop in range(1, size):
        rising, falling = others[size - hop - 1], others[hop - 1]
        if hop > 1:
            rising = (rising.astype(jnp.float32) + up.astype(jnp.float32)).astype(rising.dtype)
            falling = (falling.astype(jnp.float32) + down.astype(jnp.float32)).astype(falling.dtype)
        up = lax.ppermute(rising, axis, line_steps(size, 1)[:hop])
        down = lax.ppermute(falling, axis, line_steps(size, -1)[size - 1 - hop :])
        if hop <= len(between):
            up, down = after((up, down), between[hop - 1]((rising, falling)))
    return [up, down]


def add_shares(own, received):
    return own + sum(share.astype(jnp.float32) for share in received)


def swap_dealt(shares):
    return [shares[0]] + send_dealt(shares[1:], "fsdp")


def deal_line(parts, place):
    line = parts.shape[0]
    return [
        lax.dynamic_index_in_dim(parts, lax.rem(place[0] + step, line), 0, keepdims=False)
        for step in range(line)
    ]


def swap_heads(parts):
    return lax.all_to_all(parts, "ctx", split_axis=0, concat_axis=0, tiled=True)


def sum_groups(parts):
    return lax.psum_scatter(parts, "ctx", scatter_dimension=0, tiled=True)[0]


def head_device(
    tokens,
    block_order,
    w_query,
    w_key,
    w_value,
    w_out,
    w_gate,
    w_up,
    w_down,
    gain_attn,
    gain_mlp,
    cotangent,
):
    slots, share_rows, model_width = tokens.shape
    ctx_size, line = lax.axis_size("ctx"), lax.axis_size("fsdp")
    block_rows = share_rows * line
    group_rows = slots * block_rows
    bf, f32 = jnp.bfloat16, jnp.float32
    place = lax.axis_index("fsdp").astype(jnp.int32).reshape(1)
    group = lax.axis_index("ctx").astype(jnp.int32).reshape(1)
    own_rows = w_query.shape[0] // ctx_size
    order = block_order.astype(jnp.int32)
    long_tile = (8 if ctx_size * slots % 8 == 0 else 2) * block_rows
    slot_of = jnp.sum(
        jnp.where(order[None, :] == jnp.arange(order.shape[0])[:, None], jnp.arange(order.shape[0], dtype=jnp.int32)[None, :], 0), 1
    ).astype(jnp.int32)

    stream = tokens.astype(f32)
    root_one = lax.rsqrt(jnp.mean(stream * stream, -1, keepdims=True) + EPSILON)
    norm_one = stream * root_one
    gain_rows = jnp.pad(jnp.stack([gain_attn, gain_mlp]), ((0, EXTRA_ROWS - 2), (0, 0)))
    head_cuts = swap_dealt(
        cut_columns(place, group, [w_query, w_key, w_value], own_rows, line, gain_rows)
    )
    own_heads, gains = order_shares(place, head_cuts, 3, 2)
    attn_gain, mlp_gain = gains[0], gains[1]
    w_heads = lax.all_gather(own_heads, "ctx", axis=2, tiled=True)

    attn_pieces = send_shares(after(norm_one.astype(bf), head_cuts), "fsdp")

    mlp_cuts = cut_columns(place, group, [w_down, w_gate, w_up], own_rows, line)
    w_heads = after(w_heads, mlp_cuts)
    mlp_cuts = swap_dealt(after(mlp_cuts, attn_pieces))

    w_head = lax.dynamic_slice_in_dim(w_heads, group[0] * HEAD_DIM, HEAD_DIM, 3)
    w_head = jnp.concatenate([w_head[:, i].reshape(model_width, HEAD_DIM) for i in range(3)], 1)

    half = HEAD_DIM // 2
    frequency = 1.0 / ROPE_BASE ** (jnp.arange(half, dtype=f32) * (2.0 / HEAD_DIM))
    places = jnp.arange(group_rows * ctx_size, dtype=jnp.int32).astype(f32)
    angles = frequency[:, None] * places[None, :]
    cosine, sine = jnp.cos(angles), jnp.sin(angles)

    def own_columns(table):
        return jnp.concatenate(
            [
                lax.dynamic_slice_in_dim(
                    table, order[slots * group[0] + i] * block_rows, block_rows, 1
                )
                for i in range(slots)
            ],
            1,
        )

    own_cosine, own_sine = own_columns(cosine), own_columns(sine)
    turn_cosine = jnp.stack([own_cosine, own_cosine, jnp.ones_like(own_cosine)])
    turn_sine = jnp.stack([own_sine, own_sine, jnp.zeros_like(own_sine)])

    attn_rows, heads_out = project(
        place, attn_pieces, attn_gain[None], w_heads, turn_cosine, turn_sine
    )
    heads_out = heads_out.reshape(ctx_size, 3 * HEAD_DIM, group_rows)
    head_rows = swap_heads(after(heads_out, mlp_cuts[1]))
    mixed_send, attended, log_total = attend(
        order, head_rows, block_rows, long_tile, 2 * block_rows
    )
    mixed = swap_heads(mixed_send)
    mlp_cuts = order_shares(place, after(mlp_cuts, mixed), 3)
    w_mlp = lax.all_gather(mlp_cuts, "ctx", axis=2, tiled=True)
    upstream_pieces = send_shares(after(cotangent, mlp_cuts), "fsdp")
    own, *others = mix_out(place, after(mixed, w_head, mlp_cuts), w_out, slots, line)
    middle = stream + add_shares(own, scatter_line(others, "fsdp"))

    root_two = lax.rsqrt(jnp.mean(middle * middle, -1, keepdims=True) + EPSILON)
    norm_two = middle * root_two
    mlp_input = (norm_two * mlp_gain).astype(bf)
    mlp_pieces = send_shares(mlp_input, "fsdp")

    all_rows = {0: attn_rows}
    start_rows = after(attn_rows, mlp_pieces, upstream_pieces)
    all_rows[2], all_rows[4] = flip(start_rows, 2), flip(start_rows, 4)
    mlp_rows, upstream_rows, hidden, grad_gate, grad_up, own, *others = mlp_forward(
        place, mlp_pieces, upstream_pieces, w_mlp, 512
    )
    results = {}

    def weigh_gate_up(sent):
        rows_here = after(mlp_rows, sent)
        results["gate_up"] = gate_up_weights(rows_here, grad_gate, grad_up, ctx_size, line, 512)
        return results["gate_up"], all_rows[2], all_rows[4]

    upper = attn_rows.shape[0] // 2
    corner = []

    def weigh_down(sent):
        by_x, by_y = after((all_rows[2], all_rows[4]), sent)
        corner.extend([flip(by_x[:upper], 4), flip(by_y[upper:], 2)])
        results["down"] = down_weights(
            place, upstream_rows, after(hidden, sent), w_mlp, slots, ctx_size, 512
        )
        results["gate_up_sums"] = sum_groups(after(results["gate_up"], sent))
        return results["down"][1], list(corner)

    grad_two = add_shares(own, scatter_line(others, "fsdp", (weigh_gate_up, weigh_down)))
    gate_up_sums = results["gate_up_sums"]
    down_grads, own_out, *others_out = results["down"]
    gain_two_part = jnp.sum(grad_two * norm_two, (0, 1))
    grad_middle = cotangent.astype(f32) + norm_back(grad_two, norm_two, root_two, mlp_gain)
    branch_pieces = send_shares(grad_middle.astype(bf), "fsdp")
    branch_rows, grad_mixed = branch_back(place, branch_pieces, w_out, ctx_size)

    out_received = send_dealt(after(others_out, branch_rows), "fsdp")
    for bits in (0, 2, 4):
        all_rows[bits + 1] = flip(after(all_rows[bits], branch_rows), 1)
    corner = corner + [flip(part, 1) for part in after(corner, grad_mixed)]
    grad_heads = swap_heads(grad_mixed)
    down_grads = out_weight(down_grads, mixed, branch_rows, 512)
    head_grads = attend_back(
        jnp.concatenate([order, slot_of]),
        head_rows,
        after(
            grad_heads, down_grads, all_rows[1], all_rows[3], all_rows[5]
        ),
        attended,
        log_total,
        cosine,
        sine,
        block_rows,
        long_tile,
        2 * block_rows,
    )
    head_grads = after(head_grads, out_received, corner)
    gate_up_dealt = deal_line(after(gate_up_sums, head_grads), place)
    gate_up_back = swap_dealt(gate_up_dealt)
    down_sums = sum_groups(after(down_grads, gate_up_sums, head_grads))
    lin_grads = swap_heads(after(head_grads, gate_up_dealt))
    head_parts = head_weights(
        group,
        [all_rows[bits] for bits in range(ctx_size - 2)],
        corner,
        after(head_grads, gate_up_dealt),
        w_head,
        attn_gain[None],
        gain_two_part[None],
        ctx_size * line,
    )
    lin_grads = after(lin_grads, head_parts, gate_up_back[1], gate_up_back[2])
    head_parts = lax.all_to_all(
        after(head_parts, lin_grads), ("ctx", "fsdp"), split_axis=0, concat_axis=0, tiled=True
    )
    lin_grads = lin_grads.reshape(ctx_size, 3, HEAD_DIM, group_rows)
    own, *others = project_back(place, lin_grads, w_heads, slots)

    def swap_down(sent):
        parts = deal_line(after(down_sums, sent)[:line], place)
        results["down_back"] = swap_dealt(parts)
        return results["down_back"]

    one_received = scatter_line(
        others, "fsdp", (lambda sent: gate_up_back[3], lambda sent: (), swap_down)
    )
    down_back = results["down_back"]
    grad_one = add_shares(own, one_received)
    result = (middle + add_shares(own_out, out_received)).astype(bf)
    grad_tokens = grad_middle + norm_back(grad_one, norm_one, root_one, attn_gain)
    owners = [(c * line + f, f * ctx_size + c) for c in range(ctx_size) for f in range(line)]
    grad_w_out = lax.ppermute(down_sums[line], ("ctx", "fsdp"), owners).astype(f32)
    grad_w_gate, grad_w_up = widen_columns(place, gate_up_back, 2, own_rows)
    (grad_w_down,) = widen_columns(place, down_back, 1, own_rows)
    head_parts = head_parts.reshape(ctx_size, line, own_rows, -1)
    grad_w_query, grad_w_key, grad_w_value = join_heads(head_parts)
    spare = 3 * HEAD_DIM
    gain_grads = jnp.sum(head_parts[..., spare : spare + 2].astype(f32), (0, 1)).T
    return (
        result,
        grad_tokens,
        grad_w_query,
        grad_w_key,
        grad_w_value,
        grad_w_out,
        grad_w_gate,
        grad_w_up,
        grad_w_down,
        gain_grads[0],
        gain_grads[1],
    )


def layer_step(*arrays):
    heads_here = arrays[0].shape[-1] // lax.axis_size("fsdp") // HEAD_DIM
    if heads_here == lax.axis_size("ctx") == 8:
        return head_device(*arrays)
    return per_device(*arrays)


def solution(mesh):
    in_specs = (
        P("ctx", "fsdp", None),
        P(),
        P("fsdp", None),
        P("fsdp", None),
        P("fsdp", None),
        P("fsdp", None),
        P("fsdp", None),
        P("fsdp", None),
        P("fsdp", None),
        P("fsdp"),
        P("fsdp"),
        P("ctx", "fsdp", None),
    )
    out_specs = (
        P("ctx", "fsdp", None),
        P("ctx", "fsdp", None),
        P(("ctx", "fsdp"), None),
        P(("ctx", "fsdp"), None),
        P(("ctx", "fsdp"), None),
        P(("ctx", "fsdp"), None),
        P(("ctx", "fsdp"), None),
        P(("ctx", "fsdp"), None),
        P(("ctx", "fsdp"), None),
        P(("ctx", "fsdp")),
        P(("ctx", "fsdp")),
    )
    return jax.shard_map(
        layer_step, mesh=mesh, in_specs=in_specs, out_specs=out_specs, check_vma=False
    )
```

```python
import functools

import jax
import jax.numpy as jnp
from jax import lax
from jax.experimental import pallas as pl
from jax.experimental.pallas import tpu as pltpu
from jax.sharding import PartitionSpec as P

HEAD_DIM = 64


EPSILON = 1e-05
ROPE_BASE = 130000.0
MASKED_SCORE = -1e30


def rotate(values, places, direction):
    half_dim = values.shape[-1] // 2
    frequency = 1.0 / ROPE_BASE ** (
        jnp.arange(half_dim, dtype=jnp.float32) * (2.0 / values.shape[-1])
    )
    angles = places[..., None] * frequency
    cosine = jnp.cos(angles)[..., None, :]
    sine_part = direction * jnp.sin(angles)[..., None, :]
    leading = values[..., :half_dim]
    trailing = values[..., half_dim:]
    return jnp.concatenate(
        [leading * cosine - trailing * sine_part, trailing * cosine + leading * sine_part], -1
    )


def matmul(left, right):
    return jnp.dot(left, right, preferred_element_type=jnp.float32)


def contract(left, right):
    return lax.dot_general(
        left, right, (((1,), (1,)), ((), ())), preferred_element_type=jnp.float32
    )


def transpose_product(left, right):
    return lax.dot_general(
        left, right, (((0,), (0,)), ((), ())), preferred_element_type=jnp.float32
    )


def split_heads(values):
    return values.reshape(values.shape[:-1] + (-1, HEAD_DIM))


def keep_state(current):
    return current


def tile_scores(queries, key_rows, query_places, key_places, score_scale):
    scores = (
        jnp.einsum("qhd,khd->hqk", queries, key_rows, preferred_element_type=jnp.float32)
        * score_scale
    )
    allowed = (key_places[None, :] <= query_places[:, None])[None]
    return (jnp.where(allowed, scores, MASKED_SCORE), allowed)


def grow_state(current, queries, key_rows, value_rows, query_places, key_places, score_scale):
    run_peak, run_total, summed = current
    scores, allowed = tile_scores(queries, key_rows, query_places, key_places, score_scale)
    new_peak = jnp.maximum(run_peak, jnp.max(scores, -1))
    weights = jnp.where(allowed, jnp.exp(scores - new_peak[..., None]), 0.0)
    factor = jnp.exp(run_peak - new_peak)
    run_total = run_total * factor + jnp.sum(weights, -1)
    summed = summed * jnp.transpose(factor)[:, :, None] + jnp.einsum(
        "hqk,khd->qhd", weights.astype(jnp.bfloat16), value_rows, preferred_element_type=jnp.float32
    )
    return (new_peak, run_total, summed)


def backward_tile(
    queries,
    key_rows,
    value_rows,
    grad_out,
    log_total,
    row_delta,
    query_places,
    key_places,
    score_scale,
):
    scores, allowed = tile_scores(queries, key_rows, query_places, key_places, score_scale)
    probabilities = jnp.where(allowed, jnp.exp(scores - log_total[..., None]), 0.0)
    grad_probs = jnp.einsum(
        "qhd,khd->hqk", grad_out, value_rows, preferred_element_type=jnp.float32
    )
    grad_scores = (probabilities * (grad_probs - row_delta[..., None])).astype(jnp.bfloat16)
    return (probabilities, grad_scores)


def norm_back(grad_normed_in, normed_values, inverse_root, gain_vector):
    scaled = grad_normed_in * gain_vector
    return inverse_root * (
        scaled - normed_values * jnp.mean(scaled * normed_values, -1, keepdims=True)
    )


def per_device(
    tokens,
    block_order,
    w_query,
    w_key,
    w_value,
    w_out,
    w_gate,
    w_up,
    w_down,
    gain_attn,
    gain_mlp,
    cotangent,
):
    slot_count, share_rows, model_width = tokens.shape
    fsdp_size = lax.axis_size("fsdp")
    block_rows = share_rows * fsdp_size
    head_width = model_width // fsdp_size
    heads_here = head_width // HEAD_DIM
    row_count = slot_count * share_rows
    score_scale = HEAD_DIM ** (-0.5)
    own_slots = 2 * lax.axis_index("ctx") + jnp.arange(2, dtype=jnp.int32)
    own_blocks = block_order[own_slots]
    token_places = (
        (
            own_blocks[:, None] * block_rows
            + lax.axis_index("fsdp") * share_rows
            + jnp.arange(share_rows, dtype=jnp.int32)[None, :]
        )
        .astype(jnp.float32)
        .reshape(row_count)
    )
    head_places = (
        own_blocks[:, None] * block_rows + jnp.arange(block_rows, dtype=jnp.int32)[None, :]
    ).astype(jnp.float32)
    params = (w_query, w_key, w_value, w_out, w_gate, w_up, w_down, gain_attn, gain_mlp)
    weights_all = (
        lax.all_gather(params[0], "fsdp", axis=0, tiled=True),
        lax.all_gather(params[1], "fsdp", axis=0, tiled=True),
        lax.all_gather(params[2], "fsdp", axis=0, tiled=True),
        lax.all_gather(params[3], "fsdp", axis=0, tiled=True),
        lax.all_gather(params[4], "fsdp", axis=0, tiled=True),
        lax.all_gather(params[5], "fsdp", axis=0, tiled=True),
        lax.all_gather(params[6], "fsdp", axis=0, tiled=True),
        lax.all_gather(params[7], "fsdp", axis=0, tiled=True),
        lax.all_gather(params[8], "fsdp", axis=0, tiled=True),
    )
    stream = tokens.reshape(row_count, model_width).astype(jnp.float32)
    root_one = lax.rsqrt(jnp.mean(stream * stream, -1, keepdims=True) + EPSILON)
    norm_one = stream * root_one
    attn_input = (norm_one * weights_all[7].astype(jnp.float32)).astype(jnp.bfloat16)

    def project_turn(weight):
        linear = matmul(attn_input, weight).reshape(row_count, -1, HEAD_DIM)
        return (
            rotate(linear, token_places, 1.0)
            .astype(jnp.bfloat16)
            .reshape(slot_count, share_rows, model_width)
        )

    query_tok = project_turn(weights_all[0])
    key_tok = project_turn(weights_all[1])
    value_tok = (
        matmul(attn_input, weights_all[2])
        .astype(jnp.bfloat16)
        .reshape(slot_count, share_rows, model_width)
    )
    query_heads, key_heads, value_heads = (
        lax.all_to_all(query_tok, "fsdp", split_axis=2, concat_axis=1, tiled=True),
        lax.all_to_all(key_tok, "fsdp", split_axis=2, concat_axis=1, tiled=True),
        lax.all_to_all(value_tok, "fsdp", split_axis=2, concat_axis=1, tiled=True),
    )
    query_split = split_heads(query_heads)
    start_state = tuple(
        (
            (
                jnp.full((heads_here, block_rows), MASKED_SCORE, jnp.float32),
                jnp.zeros((heads_here, block_rows), jnp.float32),
                jnp.zeros((block_rows, heads_here, HEAD_DIM), jnp.float32),
            )
            for which_slot in range(2)
        )
    )
    carried = start_state
    key_part = lax.all_gather(key_heads, "ctx", axis=0, tiled=True)
    value_part = lax.all_gather(value_heads, "ctx", axis=0, tiled=True)

    def visit_slot(inner_state, element):
        key_one, value_one, offset = element
        key_block = block_order[offset]
        key_places = (key_block * block_rows + jnp.arange(block_rows, dtype=jnp.int32)).astype(
            jnp.float32
        )
        key_split = split_heads(key_one)
        value_split = split_heads(value_one)
        updated = []
        for which_slot in range(2):

            def grow_one(current, which_slot=which_slot):
                return grow_state(
                    current,
                    query_split[which_slot],
                    key_split,
                    value_split,
                    head_places[which_slot],
                    key_places,
                    score_scale,
                )

            updated.append(
                lax.cond(
                    key_block <= own_blocks[which_slot],
                    grow_one,
                    keep_state,
                    inner_state[which_slot],
                )
            )
        return (tuple(updated), None)

    offsets = jnp.arange(key_part.shape[0], dtype=jnp.int32)
    carried, unused = lax.scan(visit_slot, carried, (key_part, value_part, offsets))
    attended_parts = []
    log_parts = []
    for which_slot in range(2):
        run_peak, run_total, summed = carried[which_slot]
        log_parts.append(run_peak + jnp.log(run_total))
        attended_parts.append(summed / jnp.transpose(run_total)[:, :, None])
    attended = jnp.stack(attended_parts)
    log_total = jnp.stack(log_parts)
    mixed_send = attended.reshape(slot_count, block_rows, head_width).astype(jnp.bfloat16)
    mixed_tok = lax.all_to_all(mixed_send, "fsdp", split_axis=1, concat_axis=2, tiled=True)
    mixed_flat = mixed_tok.reshape(row_count, model_width)
    middle = stream + matmul(mixed_flat, weights_all[3])
    root_two = lax.rsqrt(jnp.mean(middle * middle, -1, keepdims=True) + EPSILON)
    norm_two = middle * root_two
    mlp_input = (norm_two * weights_all[8].astype(jnp.float32)).astype(jnp.bfloat16)
    gate_act = matmul(mlp_input, weights_all[4])
    upward = matmul(mlp_input, weights_all[5])
    gate_sigmoid = jax.nn.sigmoid(gate_act)
    gate_silu = gate_act * gate_sigmoid
    hidden = (gate_silu * upward).astype(jnp.bfloat16)
    output = middle + contract(hidden, weights_all[6])
    result = output.astype(jnp.bfloat16).reshape(slot_count, share_rows, model_width)
    upstream = cotangent.reshape(row_count, model_width)
    grad_hidden = matmul(upstream, weights_all[6])
    grad_gate = (
        grad_hidden * upward * gate_sigmoid * (1.0 + gate_act * (1.0 - gate_sigmoid))
    ).astype(jnp.bfloat16)
    grad_up = (grad_hidden * gate_silu).astype(jnp.bfloat16)
    grad_two = contract(grad_gate, weights_all[4]) + contract(grad_up, weights_all[5])
    gain_two_part = jnp.sum(grad_two * norm_two, 0)
    grad_middle = upstream.astype(jnp.float32) + norm_back(
        grad_two, norm_two, root_two, weights_all[8].astype(jnp.float32)
    )
    grad_branch = grad_middle.astype(jnp.bfloat16)
    grad_mixed = (
        contract(grad_branch, weights_all[3])
        .astype(jnp.bfloat16)
        .reshape(slot_count, share_rows, model_width)
    )
    grad_heads = lax.all_to_all(grad_mixed, "fsdp", split_axis=2, concat_axis=1, tiled=True)
    grad_split = split_heads(grad_heads)
    row_delta = jnp.transpose(jnp.sum(grad_split.astype(jnp.float32) * attended, -1), (0, 2, 1))
    gathered = (
        lax.all_gather(key_heads, "ctx", axis=0, tiled=True),
        lax.all_gather(value_heads, "ctx", axis=0, tiled=True),
    )
    key_all, value_all = gathered
    total_slots = key_all.shape[0]

    def query_visit(current, element):
        key_pair, value_pair, pair_index = element
        updated = list(current)
        for member in range(2):
            key_block = block_order[2 * pair_index + member]
            key_places = (key_block * block_rows + jnp.arange(block_rows, dtype=jnp.int32)).astype(
                jnp.float32
            )
            key_split = split_heads(key_pair[member])
            value_split = split_heads(value_pair[member])
            for which_slot in range(2):

                def take_query(
                    accum,
                    which_slot=which_slot,
                    key_split=key_split,
                    value_split=value_split,
                    key_places=key_places,
                ):
                    probabilities, grad_scores = backward_tile(
                        query_split[which_slot],
                        key_split,
                        value_split,
                        grad_split[which_slot],
                        log_total[which_slot],
                        row_delta[which_slot],
                        head_places[which_slot],
                        key_places,
                        score_scale,
                    )
                    return accum + score_scale * jnp.einsum(
                        "hqk,khd->qhd", grad_scores, key_split, preferred_element_type=jnp.float32
                    )

                updated[which_slot] = lax.cond(
                    key_block <= own_blocks[which_slot], take_query, keep_state, updated[which_slot]
                )
        return (tuple(updated), None)

    query_zero = jnp.zeros((block_rows, heads_here, HEAD_DIM), jnp.float32)
    pair_keys = key_all.reshape(total_slots // 2, 2, block_rows, head_width)
    pair_values = value_all.reshape(total_slots // 2, 2, block_rows, head_width)
    grad_query_parts, unused = lax.scan(
        query_visit,
        (query_zero, query_zero),
        (pair_keys, pair_values, jnp.arange(total_slots // 2, dtype=jnp.int32)),
    )
    key_part = key_all
    value_part = value_all

    def key_visit(unused_carry, element):
        key_one, value_one, offset = element
        key_block = block_order[offset]
        key_places = (key_block * block_rows + jnp.arange(block_rows, dtype=jnp.int32)).astype(
            jnp.float32
        )
        key_split = split_heads(key_one)
        value_split = split_heads(value_one)
        sums = (
            jnp.zeros((block_rows, heads_here, HEAD_DIM), jnp.float32),
            jnp.zeros((block_rows, heads_here, HEAD_DIM), jnp.float32),
        )
        for which_slot in range(2):

            def take_keys(current, which_slot=which_slot):
                probabilities, grad_scores = backward_tile(
                    query_split[which_slot],
                    key_split,
                    value_split,
                    grad_split[which_slot],
                    log_total[which_slot],
                    row_delta[which_slot],
                    head_places[which_slot],
                    key_places,
                    score_scale,
                )
                grad_key = current[0] + score_scale * jnp.einsum(
                    "hqk,qhd->khd",
                    grad_scores,
                    query_split[which_slot],
                    preferred_element_type=jnp.float32,
                )
                grad_value = current[1] + jnp.einsum(
                    "hqk,qhd->khd",
                    probabilities.astype(jnp.bfloat16),
                    grad_split[which_slot],
                    preferred_element_type=jnp.float32,
                )
                return (grad_key, grad_value)

            sums = lax.cond(key_block <= own_blocks[which_slot], take_keys, keep_state, sums)
        joined = jnp.concatenate(
            [sums[0].reshape(block_rows, head_width), sums[1].reshape(block_rows, head_width)], -1
        )
        return (unused_carry, joined)

    unused_final, terms = lax.scan(
        key_visit,
        jnp.zeros((), jnp.float32),
        (key_part, value_part, jnp.arange(slot_count * lax.axis_size("ctx"), dtype=jnp.int32)),
    )
    summed_kv = lax.psum_scatter(
        terms.astype(jnp.bfloat16), "ctx", scatter_dimension=0, tiled=True
    ).astype(jnp.float32)
    grad_keys = (
        rotate(split_heads(summed_kv[..., :head_width]), head_places, -1.0)
        .astype(jnp.bfloat16)
        .reshape(slot_count, block_rows, head_width)
    )
    grad_values = summed_kv[..., head_width:].astype(jnp.bfloat16)
    grad_queries = (
        rotate(jnp.stack(grad_query_parts), head_places, -1.0)
        .astype(jnp.bfloat16)
        .reshape(slot_count, block_rows, head_width)
    )
    grad_q_tok, grad_k_tok, grad_v_tok = (
        lax.all_to_all(grad_queries, "fsdp", split_axis=1, concat_axis=2, tiled=True),
        lax.all_to_all(grad_keys, "fsdp", split_axis=1, concat_axis=2, tiled=True),
        lax.all_to_all(grad_values, "fsdp", split_axis=1, concat_axis=2, tiled=True),
    )
    grad_q_lin = grad_q_tok.reshape(row_count, model_width)
    grad_k_lin = grad_k_tok.reshape(row_count, model_width)
    grad_v_lin = grad_v_tok.reshape(row_count, model_width)
    grad_one = (
        contract(grad_q_lin, weights_all[0])
        + contract(grad_k_lin, weights_all[1])
        + contract(grad_v_lin, weights_all[2])
    )
    gain_one_part = jnp.sum(grad_one * norm_one, 0)
    grad_input = grad_middle + norm_back(
        grad_one, norm_one, root_one, weights_all[7].astype(jnp.float32)
    )
    hidden_width = hidden.shape[1]
    gain_parts = jnp.stack([gain_one_part, gain_two_part], 1)
    wide_cols = (
        lax.all_to_all(grad_q_lin, "fsdp", split_axis=1, concat_axis=0, tiled=True),
        lax.all_to_all(grad_k_lin, "fsdp", split_axis=1, concat_axis=0, tiled=True),
        lax.all_to_all(grad_v_lin, "fsdp", split_axis=1, concat_axis=0, tiled=True),
        lax.all_to_all(grad_branch, "fsdp", split_axis=1, concat_axis=0, tiled=True),
        lax.all_to_all(grad_gate, "fsdp", split_axis=1, concat_axis=0, tiled=True),
        lax.all_to_all(grad_up, "fsdp", split_axis=1, concat_axis=0, tiled=True),
        lax.all_to_all(hidden, "fsdp", split_axis=1, concat_axis=0, tiled=True),
    )
    row_sets = (
        lax.all_gather(attn_input, "fsdp", axis=0, tiled=True),
        lax.all_gather(mixed_flat, "fsdp", axis=0, tiled=True),
        lax.all_gather(mlp_input, "fsdp", axis=0, tiled=True),
        lax.all_gather(upstream, "fsdp", axis=0, tiled=True),
    )
    group_rows = model_width // lax.axis_size("ctx")
    row_cuts = [values for values in row_sets]
    pieces = [
        transpose_product(row_cuts[0], wide_cols[0]),
        transpose_product(row_cuts[0], wide_cols[1]),
        transpose_product(row_cuts[0], wide_cols[2]),
        transpose_product(row_cuts[1], wide_cols[3]),
        transpose_product(row_cuts[2], wide_cols[4]),
        transpose_product(row_cuts[2], wide_cols[5]),
        transpose_product(row_cuts[3], wide_cols[6]),
        gain_parts,
        jnp.zeros((group_rows * lax.axis_size("ctx"), 126), jnp.float32),
    ]
    partial_sums = lax.psum_scatter(
        jnp.concatenate(pieces, 1).astype(jnp.bfloat16), "ctx", scatter_dimension=0, tiled=True
    ).astype(jnp.float32)
    owned = lax.all_to_all(
        partial_sums.astype(jnp.bfloat16), "fsdp", split_axis=0, concat_axis=1, tiled=True
    ).astype(partial_sums.dtype)
    span_width = partial_sums.shape[1]
    owned_rows = owned.shape[0]
    arranged = owned.reshape(owned_rows, fsdp_size, span_width)
    model_part = model_width // fsdp_size
    hidden_part = hidden_width // fsdp_size
    bounds = [
        0,
        model_part,
        2 * model_part,
        3 * model_part,
        4 * model_part,
        4 * model_part + hidden_part,
        4 * model_part + 2 * hidden_part,
        4 * model_part + 3 * hidden_part,
    ]

    def joined_cols(first_col, last_col):
        return arranged[:, :, first_col:last_col].reshape(owned_rows, -1)

    grad_w_query = joined_cols(bounds[0], bounds[1])
    grad_w_key = joined_cols(bounds[1], bounds[2])
    grad_w_value = joined_cols(bounds[2], bounds[3])
    grad_w_out = joined_cols(bounds[3], bounds[4])
    grad_w_gate = joined_cols(bounds[4], bounds[5])
    grad_w_up = joined_cols(bounds[5], bounds[6])
    grad_w_down = joined_cols(bounds[6], bounds[7])
    gain_totals = jnp.sum(arranged[:, :, bounds[7] : bounds[7] + 2], 1)
    grad_gain_attn = gain_totals[:, 0]
    grad_gain_mlp = gain_totals[:, 1]
    grad_tokens = grad_input.reshape(slot_count, share_rows, model_width)
    return (
        result,
        grad_tokens,
        grad_w_query,
        grad_w_key,
        grad_w_value,
        grad_w_out,
        grad_w_gate,
        grad_w_up,
        grad_w_down,
        grad_gain_attn,
        grad_gain_mlp,
    )


def dot_f32(a, b):
    return jnp.dot(a, b, preferred_element_type=jnp.float32)

def load_sequence(order_ref, rows_ref, block, stores):
    per_src = rows_ref.shape[2] // block
    def one(slot, carry):
        src = slot // per_src
        lane = pl.multiple_of((slot % per_src) * block, block)
        place = pl.multiple_of(order_ref[slot] * block, block)
        for at, store in stores:
            store(rows_ref[src, at:at + HEAD_DIM, pl.ds(lane, block)], place)
        return carry
    lax.fori_loop(0, rows_ref.shape[0] * per_src, one, 0)

def fwd_kernel(
    order_ref, qkv_ref, mixed_ref, out_ref, lse_ref, qt, kr, vt, peak, total, acc, *, block, tile, step
):
    seq = qt.shape[1]

    def put_q(x, place):
        qt[:, pl.ds(place, block)] = x * jnp.bfloat16(HEAD_DIM ** -0.5)

    def put_k(x, place):
        kr[pl.ds(place, block), :] = x.T

    def put_v(x, place):
        vt[:, pl.ds(place, block)] = x

    load_sequence(
        order_ref, qkv_ref, block, ((0, put_q), (HEAD_DIM, put_k), (2 * HEAD_DIM, put_v))
    )

    def one_tile(qi, unused):
        q0 = pl.multiple_of(qi * tile, tile)
        peak[...] = jnp.full_like(peak, MASKED_SCORE)
        total[...] = jnp.zeros_like(total)
        acc[...] = jnp.zeros_like(acc)

        def visit(k0, first, masked):
            queries = qt[:, pl.ds(pl.multiple_of(q0 + first, step), tile - first)]
            s = dot_f32(kr[pl.ds(k0, step), :], queries)
            if masked:
                keep = lax.broadcasted_iota(jnp.int32, s.shape, 0) <= lax.broadcasted_iota(
                    jnp.int32, s.shape, 1
                )
                s = jnp.where(keep, s, MASKED_SCORE)
            old = peak[:, first:]
            new = jnp.maximum(old, jnp.max(s, 0, keepdims=True))
            p = jnp.exp(s - new)
            alpha = jnp.exp(old - new)
            peak[:, first:] = new
            total[:, first:] = total[:, first:] * alpha + jnp.sum(p, 0, keepdims=True)
            acc[:, first:] = acc[:, first:] * alpha + dot_f32(
                vt[:, pl.ds(k0, step)], p.astype(jnp.bfloat16)
            )

        def below(j, carry):
            visit(pl.multiple_of(j * step, step), 0, False)
            return carry

        lax.fori_loop(0, qi * (tile // step), below, 0)
        for part in range(tile // step):
            visit(pl.multiple_of(q0 + part * step, step), part * step, True)
        out_ref[:, pl.ds(q0, tile)] = acc[...] / total[...]
        lse_ref[:, pl.ds(q0, tile)] = peak[...] + jnp.log(total[...])
        return unused

    lax.fori_loop(0, seq // tile, one_tile, 0)
    per_src = mixed_ref.shape[2] // block

    def send(slot, carry):
        place = pl.multiple_of(order_ref[slot] * block, block)
        lane = pl.multiple_of((slot % per_src) * block, block)
        mixed_ref[slot // per_src, :, pl.ds(lane, block)] = out_ref[:, pl.ds(place, block)].astype(
            jnp.bfloat16
        )
        return carry

    lax.fori_loop(0, mixed_ref.shape[0] * per_src, send, 0)


def attend(order, qkv, block, tile, step):
    groups, unused, width = qkv.shape
    seq = groups * width
    vm = pl.BlockSpec(memory_space=pltpu.VMEM)
    bf, f32 = jnp.bfloat16, jnp.float32
    return pl.pallas_call(
        functools.partial(fwd_kernel, block=block, tile=tile, step=step),
        out_shape=(
            jax.ShapeDtypeStruct((groups, HEAD_DIM, width), bf),
            jax.ShapeDtypeStruct((HEAD_DIM, seq), f32),
            jax.ShapeDtypeStruct((1, seq), f32),
        ),
        in_specs=[pl.BlockSpec(memory_space=pltpu.SMEM), vm],
        out_specs=(vm, vm, vm),
        scratch_shapes=[
            pltpu.VMEM((HEAD_DIM, seq), bf),
            pltpu.VMEM((seq, HEAD_DIM), bf),
            pltpu.VMEM((HEAD_DIM, seq), bf),
            pltpu.VMEM((1, tile), f32),
            pltpu.VMEM((1, tile), f32),
            pltpu.VMEM((HEAD_DIM, tile), f32),
        ],
        compiler_params=pltpu.CompilerParams(vmem_limit_bytes=48 << 20),
        cost_estimate=pl.CostEstimate(
            flops=int(4.0 * seq * seq * HEAD_DIM),
            bytes_accessed=8 * seq * HEAD_DIM,
            transcendentals=0,
        ),
        name="attend",
    )(order, qkv)


def bwd_kernel(order_ref, qkv_ref, go_ref, out_ref, lse_ref, cos_ref, sin_ref, grad_ref,
               qt, qr, kt, kr, vr, got, gor, delta, dqt, dkr, dvr, *, block, tile, step):
    seq = qt.shape[1]
    scale = jnp.bfloat16(HEAD_DIM ** -0.5)
    def put_q(x, place):
        x = x * scale
        qt[:, pl.ds(place, block)] = x
        qr[pl.ds(place, block), :] = x.T
    def put_k(x, place):
        kt[:, pl.ds(place, block)] = x * scale
        kr[pl.ds(place, block), :] = x.T
    def put_v(x, place):
        vr[pl.ds(place, block), :] = x.T
    def put_go(x, place):
        got[:, pl.ds(place, block)] = x
        gor[pl.ds(place, block), :] = x.T
        delta[:, pl.ds(place, block)] = jnp.sum(x.astype(jnp.float32) * out_ref[:, pl.ds(place, block)], 0, keepdims=True)
    load_sequence(order_ref, qkv_ref, block, ((0, put_q), (HEAD_DIM, put_k), (2 * HEAD_DIM, put_v)))
    load_sequence(order_ref, go_ref, block, ((0, put_go),))
    dqt[...] = jnp.zeros_like(dqt)
    tiles = seq // tile

    def key_tile(kj, unused):
        k0 = pl.multiple_of(kj * tile, tile)
        keys = kr[pl.ds(k0, tile), :]
        keys_t = kt[:, pl.ds(k0, tile)]
        vals = vr[pl.ds(k0, tile), :]
        dkr[...] = jnp.zeros_like(dkr)
        dvr[...] = jnp.zeros_like(dvr)

        def visit(q0, width, rows, masked):
            s = dot_f32(keys[:rows], qt[:, pl.ds(q0, width)])
            p = jnp.exp(s - lse_ref[:, pl.ds(q0, width)])
            if masked:
                keep = lax.broadcasted_iota(jnp.int32, s.shape, 0) <= lax.broadcasted_iota(
                    jnp.int32, s.shape, 1
                ) + (rows - width)
                p = jnp.where(keep, p, 0.0)
            dp = dot_f32(vals[:rows], got[:, pl.ds(q0, width)])
            ds = (p * (dp - delta[:, pl.ds(q0, width)])).astype(jnp.bfloat16)
            dvr[:rows] += dot_f32(p.astype(jnp.bfloat16), gor[pl.ds(q0, width), :])
            dkr[:rows] += dot_f32(ds, qr[pl.ds(q0, width), :])
            dqt[:, pl.ds(q0, width)] += dot_f32(keys_t[:, :rows], ds)

        for part in range(tile // step):
            first = pl.multiple_of(k0 + part * step, step)
            visit(first, step, (part + 1) * step, True)

        def later(j, carry):
            visit(pl.multiple_of(j * step, step), step, tile, False)
            return carry

        lax.fori_loop((kj + 1) * (tile // step), seq // step, later, 0)
        put_out(dkr[...].T, HEAD_DIM, k0, True)
        put_out(dvr[...].T, 2 * HEAD_DIM, k0, False)
        return unused

    half = HEAD_DIM // 2
    def put_out(x, at, place, turn):
        for part in range(tile // block):
            piece = x[:, part * block:(part + 1) * block]
            here = place + part * block
            if turn:
                lanes = pl.ds(pl.multiple_of(here, block), block)
                c, s = cos_ref[:, lanes], sin_ref[:, lanes]
                a, b = piece[:half], piece[half:]
                piece = jnp.concatenate([a * c + b * s, b * c - a * s], 0)
            slot = order_ref[seq // block + here // block]
            per_src = grad_ref.shape[2] // block
            lane = pl.multiple_of((slot % per_src) * block, block)
            grad_ref[slot // per_src, at:at + HEAD_DIM, pl.ds(lane, block)] = piece.astype(jnp.bfloat16)

    lax.fori_loop(0, tiles, key_tile, 0)
    def write_q(qi, c):
        q0 = pl.multiple_of(qi * tile, tile)
        put_out(dqt[:, pl.ds(q0, tile)], 0, q0, True)
        return c
    lax.fori_loop(0, tiles, write_q, 0)

def attend_back(order, qkv, go, out, lse, cos, sin, block, tile, step):
    groups, unused, width = qkv.shape
    seq = groups * width
    vm = pl.BlockSpec(memory_space=pltpu.VMEM)
    bf, f32 = jnp.bfloat16, jnp.float32
    wide = lambda t: pltpu.VMEM((HEAD_DIM, seq), t)
    tall = lambda t: pltpu.VMEM((seq, HEAD_DIM), t)
    return pl.pallas_call(
        functools.partial(bwd_kernel, block=block, tile=tile, step=step),
        out_shape=jax.ShapeDtypeStruct(qkv.shape, bf),
        in_specs=[pl.BlockSpec(memory_space=pltpu.SMEM)] + [vm] * 6,
        out_specs=vm,
        scratch_shapes=[wide(bf), tall(bf), wide(bf), tall(bf), tall(bf), wide(bf), tall(bf),
                        pltpu.VMEM((1, seq), f32), wide(f32),
                        pltpu.VMEM((tile, HEAD_DIM), f32), pltpu.VMEM((tile, HEAD_DIM), f32)],
        compiler_params=pltpu.CompilerParams(vmem_limit_bytes=48 << 20),
        cost_estimate=pl.CostEstimate(
            flops=int(6.4 * seq * seq * HEAD_DIM),
            bytes_accessed=16 * seq * HEAD_DIM,
            transcendentals=0,
        ),
        name="attend_back",
    )(order, qkv, go, out, lse, cos, sin)


def nt_dot(a, b):
    return lax.dot_general(a, b, (((1,), (1,)), ((), ())), preferred_element_type=jnp.float32)


def whole(space=pltpu.VMEM):
    return pl.BlockSpec(memory_space=space)


def spread(pieces, place_ref, rows_ref):
    hops = (len(pieces) - 1) // 2
    slots, share, unused = pieces[0].shape
    place = place_ref[0]

    def put(piece, position):
        for slot in range(slots):
            first = pl.multiple_of(slot * share * (hops + 1) + position * share, share)
            rows_ref[pl.ds(first, share), :] = piece[slot]

    put(pieces[0], place)
    for hop in range(1, hops + 1):

        @pl.when(place >= hop)
        def take_below(hop=hop):
            put(pieces[hop], place - hop)

        @pl.when(place + hop <= hops)
        def take_above(hop=hop):
            put(pieces[hops + hop], place + hop)


def deal(rows_ref, place_ref, own_ref, others):
    slots, share, unused = own_ref.shape
    line = len(others) + 1
    for step, target in enumerate([own_ref] + list(others)):
        position = lax.rem(place_ref[0] + step, line)
        for slot in range(slots):
            first = pl.multiple_of(slot * share * line + position * share, share)
            target[slot] = rows_ref[pl.ds(first, share), :].astype(target.dtype)


def dealt_shapes(slots, share, width, line):
    return [jax.ShapeDtypeStruct((slots, share, width), jnp.float32)] + [
        jax.ShapeDtypeStruct((slots, share, width), jnp.bfloat16) for unused in range(line - 1)
    ]


def work(flops, bytes_accessed=0, transcendentals=0):
    return pl.CostEstimate(
        flops=int(flops * 0.2), bytes_accessed=int(bytes_accessed * 0.2), transcendentals=0
    )


def vmem_limit(mebibytes):
    return pltpu.CompilerParams(vmem_limit_bytes=mebibytes << 20)


EXTRA_ROWS = 16
LANES = 128


def cut_columns(place, group, weights, rows, line, extra=None):
    count = len(weights)
    columns = weights[0].shape[1] // line
    cut_rows = count * rows + (EXTRA_ROWS if extra is not None else 0)
    extras = [] if extra is None else [extra]

    def kernel(place_ref, group_ref, *refs):
        outs = refs[count * line + len(extras) :]
        for step in range(line):
            for i in range(count):
                outs[step][i * rows : (i + 1) * rows] = refs[step * count + i][...]
            if extras:
                outs[step][count * rows :] = refs[count * line][...]

    def target(step):
        return lambda i, place, group: (group[0], lax.rem(place[0] + step, line))

    fixed = lambda shape: pl.BlockSpec(shape, lambda i, place, group: (0, 0))
    return pl.pallas_call(
        kernel,
        out_shape=[jax.ShapeDtypeStruct((cut_rows, columns), jnp.bfloat16)] * line,
        grid_spec=pltpu.PrefetchScalarGridSpec(
            num_scalar_prefetch=2,
            grid=(1,),
            in_specs=[
                pl.BlockSpec((rows, columns), target(step))
                for step in range(line)
                for unused in range(count)
            ]
            + [fixed((EXTRA_ROWS, columns)) for unused in extras],
            out_specs=[fixed((cut_rows, columns))] * line,
        ),
        compiler_params=vmem_limit(60),
        name="cut_columns",
    )(place, group, *(list(weights) * line), *extras)


def order_shares(place, shares, count, vectors=0):
    line = len(shares)
    share_rows, columns = shares[0].shape
    rows = (share_rows - (EXTRA_ROWS if vectors else 0)) // count

    def kernel(place_ref, *refs):
        for step in range(line):
            source = lax.rem(place_ref[0] + line - step, line)
            for i in range(count):
                refs[line][source, i] = refs[step][i * rows : (i + 1) * rows]
            if vectors:
                lanes = pl.ds(pl.multiple_of(source * columns, columns), columns)
                refs[line + 1][:, lanes] = refs[step][count * rows :].astype(jnp.float32)

    shapes = [jax.ShapeDtypeStruct((line, count, rows, columns), shares[0].dtype)]
    if vectors:
        shapes.append(jax.ShapeDtypeStruct((EXTRA_ROWS, line * columns), jnp.float32))
    outs = pl.pallas_call(
        kernel,
        out_shape=shapes,
        in_specs=[whole(pltpu.SMEM)] + [whole()] * line,
        out_specs=[whole()] * len(shapes),
        compiler_params=vmem_limit(40),
        name="order_shares",
    )(place, *shares)
    return (outs[0], outs[1][:vectors]) if vectors else outs[0]


def widen_columns(place, shares, count, rows):
    line = len(shares)
    share_rows, columns = shares[0].shape

    def kernel(place_ref, *refs):
        for step in range(line):

            @pl.when(pl.program_id(0) == step)
            def widen(step=step):
                for i in range(count):
                    refs[line + i][...] = refs[step][i * rows : (i + 1) * rows].astype(jnp.float32)

    return pl.pallas_call(
        kernel,
        out_shape=[jax.ShapeDtypeStruct((rows, line * columns), jnp.float32)] * count,
        grid_spec=pltpu.PrefetchScalarGridSpec(
            num_scalar_prefetch=1,
            grid=(line,),
            in_specs=[pl.BlockSpec((share_rows, columns), lambda j, place: (0, 0))] * line,
            out_specs=[
                pl.BlockSpec(
                    (rows, columns), lambda j, place: (0, lax.rem(place[0] + line - j, line))
                )
            ]
            * count,
        ),
        compiler_params=vmem_limit(40),
        name="widen_columns",
    )(place, *shares)


def project(place, pieces, gain, w_heads, cosine, sine):
    line, count, part, width = w_heads.shape
    slots, share, model_width = pieces[0].shape
    rows = slots * share * line
    tile = width // 2
    heads = tile // HEAD_DIM
    n_pieces = len(pieces)
    half = HEAD_DIM // 2

    def kernel(place_ref, *refs):
        piece_refs = refs[:n_pieces]
        gain_ref, w_ref, cos_ref, sin_ref, rows_ref, out_ref = refs[n_pieces:]

        @pl.when((pl.program_id(0) == 0) & (pl.program_id(1) == 0))
        def assemble():
            spread(piece_refs, place_ref, rows_ref)
            rows_ref[...] = (rows_ref[...].astype(jnp.float32) * gain_ref[...]).astype(jnp.bfloat16)

        weight = w_ref[...].reshape(line * part, tile)
        turned = dot_f32(rows_ref[...], weight).T
        c, s = cos_ref[0], sin_ref[0]
        for head in range(heads):
            a = turned[head * HEAD_DIM : head * HEAD_DIM + half]
            b = turned[head * HEAD_DIM + half : (head + 1) * HEAD_DIM]
            out_ref[head, 0, :half, :] = (a * c - b * s).astype(jnp.bfloat16)
            out_ref[head, 0, half:, :] = (b * c + a * s).astype(jnp.bfloat16)

    return pl.pallas_call(
        kernel,
        grid=(count, 2),
        out_shape=[
            jax.ShapeDtypeStruct((rows, model_width), jnp.bfloat16),
            jax.ShapeDtypeStruct((width // HEAD_DIM, count, HEAD_DIM, rows), jnp.bfloat16),
        ],
        in_specs=[whole(pltpu.SMEM)]
        + [whole()] * (n_pieces + 1)
        + [
            pl.BlockSpec((line, 1, part, tile), lambda m, h: (0, m, 0, h)),
            pl.BlockSpec((1, half, rows), lambda m, h: (m, 0, 0)),
            pl.BlockSpec((1, half, rows), lambda m, h: (m, 0, 0)),
        ],
        out_specs=[
            pl.BlockSpec((rows, model_width), lambda m, h: (0, 0)),
            pl.BlockSpec((heads, 1, HEAD_DIM, rows), lambda m, h: (h, m, 0, 0)),
        ],
        compiler_params=vmem_limit(48),
        cost_estimate=work(6 * rows * model_width * width, 8 * rows * model_width),
        name="project",
    )(place, *pieces, gain, w_heads, cosine, sine)


def mix_out(place, mixed, w_out, slots, line):
    heads, unused, rows = mixed.shape
    width, model_width = w_out.shape
    share = rows // slots // line

    def kernel(place_ref, mixed_ref, w_ref, own_ref, *rest):
        *others, total = rest
        left = mixed_ref[...].reshape(width, rows).T
        total[...] = dot_f32(left, w_ref[...])
        deal(total, place_ref, own_ref, others)

    return pl.pallas_call(
        kernel,
        out_shape=dealt_shapes(slots, share, model_width, line),
        in_specs=[whole(pltpu.SMEM), whole(), whole()],
        out_specs=[whole()] * line,
        scratch_shapes=[pltpu.VMEM((rows, model_width), jnp.float32)],
        compiler_params=vmem_limit(48),
        cost_estimate=work(2 * rows * model_width * width, 8 * rows * model_width),
        name="mix_out",
    )(place, mixed, w_out)


def mlp_forward(place, pieces, upstream_pieces, w_mlp, tile):
    line, count, part, width = w_mlp.shape
    slots, share, model_width = pieces[0].shape
    rows = slots * share * line
    n_pieces = len(pieces)
    bf, f32 = jnp.bfloat16, jnp.float32

    def kernel(place_ref, *refs):
        x_pieces, u_pieces = refs[:n_pieces], refs[n_pieces : 2 * n_pieces]
        w_ref, x_ref, u_ref, hidden_ref, gate_ref, up_ref, own_ref = refs[
            2 * n_pieces : 2 * n_pieces + 7
        ]
        *others, total = refs[2 * n_pieces + 7 :]
        step = pl.program_id(0)

        @pl.when(step == 0)
        def assemble():
            spread(x_pieces, place_ref, x_ref)
            spread(u_pieces, place_ref, u_ref)

        down = w_ref[:, 0].reshape(line * part, tile)
        gate = w_ref[:, 1].reshape(line * part, tile)
        up = w_ref[:, 2].reshape(line * part, tile)
        x = x_ref[...]
        grad_hidden = dot_f32(u_ref[...], down)
        gate_act = dot_f32(x, gate)
        upward = dot_f32(x, up)
        sigmoid = jax.nn.sigmoid(gate_act)
        silu = gate_act * sigmoid
        hidden_ref[...] = (silu * upward).astype(bf)
        grad_gate = (
            grad_hidden * upward * sigmoid * (1.0 + gate_act * (1.0 - sigmoid))
        ).astype(bf)
        grad_up = (grad_hidden * silu).astype(bf)
        gate_ref[...] = grad_gate
        up_ref[...] = grad_up
        part_two = nt_dot(grad_gate, gate) + nt_dot(grad_up, up)

        @pl.when(step == 0)
        def first():
            total[...] = part_two

        @pl.when(step > 0)
        def further():
            total[...] += part_two

        @pl.when(step == pl.num_programs(0) - 1)
        def last():
            deal(total, place_ref, own_ref, others)

    fixed = lambda shape: pl.BlockSpec(shape, lambda j: (0,) * len(shape))
    columns = pl.BlockSpec((rows, tile), lambda j: (0, j))
    dealt = dealt_shapes(slots, share, model_width, line)
    return pl.pallas_call(
        kernel,
        grid=(width // tile,),
        out_shape=[jax.ShapeDtypeStruct((rows, model_width), bf)] * 2
        + [jax.ShapeDtypeStruct((rows, width), bf)] * 3
        + dealt,
        in_specs=[whole(pltpu.SMEM)]
        + [whole()] * (2 * n_pieces)
        + [pl.BlockSpec((line, count, part, tile), lambda j: (0, 0, 0, j))],
        out_specs=[fixed((rows, model_width))] * 2
        + [columns] * 3
        + [fixed((slots, share, model_width))] * line,
        scratch_shapes=[pltpu.VMEM((rows, model_width), f32)],
        compiler_params=vmem_limit(60),
        cost_estimate=work(16 * rows * model_width * width, 14 * model_width * width),
        name="mlp_forward",
    )(place, *pieces, *upstream_pieces, w_mlp)


def gate_up_weights(x_rows, grad_gate, grad_up, groups, line, tile):
    rows, model_width = x_rows.shape
    width = grad_gate.shape[1]
    block = model_width // groups // line

    def kernel(x_ref, gate_ref, up_ref, out_ref, x_turned):
        @pl.when(pl.program_id(0) == 0)
        def turn():
            x_turned[...] = x_ref[...].T

        for i, ref in enumerate((gate_ref, up_ref)):
            grads = dot_f32(x_turned[...], ref[...]).astype(jnp.bfloat16)
            out_ref[:, :, i * block : (i + 1) * block] = grads.reshape(groups, line, block, tile)

    columns = pl.BlockSpec((rows, tile), lambda j: (0, j))
    return pl.pallas_call(
        kernel,
        grid=(width // tile,),
        out_shape=jax.ShapeDtypeStruct((groups, line, 2 * block, width), jnp.bfloat16),
        in_specs=[pl.BlockSpec((rows, model_width), lambda j: (0, 0)), columns, columns],
        out_specs=pl.BlockSpec((groups, line, 2 * block, tile), lambda j: (0, 0, 0, j)),
        scratch_shapes=[pltpu.VMEM((model_width, rows), jnp.bfloat16)],
        compiler_params=vmem_limit(60),
        cost_estimate=work(4 * rows * model_width * width, 8 * model_width * width),
        name="gate_up_weights",
    )(x_rows, grad_gate, grad_up)


def down_weights(u_rows, hidden, groups, line, tile):
    rows, model_width = u_rows.shape
    width = hidden.shape[1]
    block = model_width // groups // line

    def kernel(u_ref, hidden_ref, out_ref, u_turned):
        @pl.when(pl.program_id(0) == 0)
        def turn():
            u_turned[...] = u_ref[...].T

        grads = dot_f32(u_turned[...], hidden_ref[...]).astype(jnp.bfloat16)
        out_ref[:, :line] = grads.reshape(groups, line, block, tile)

    return pl.pallas_call(
        kernel,
        grid=(width // tile,),
        out_shape=jax.ShapeDtypeStruct((groups, line + 1, block, width), jnp.bfloat16),
        in_specs=[
            pl.BlockSpec((rows, model_width), lambda j: (0, 0)),
            pl.BlockSpec((rows, tile), lambda j: (0, j)),
        ],
        out_specs=pl.BlockSpec((groups, line + 1, block, tile), lambda j: (0, 0, 0, j)),
        scratch_shapes=[pltpu.VMEM((model_width, rows), jnp.bfloat16)],
        compiler_params=vmem_limit(60),
        cost_estimate=work(2 * rows * model_width * width, 4 * model_width * width),
        name="down_weights",
    )(u_rows, hidden)


def mlp_out(place, hidden, w_mlp, slots, tile):
    line, count, part, width = w_mlp.shape
    rows = hidden.shape[0]
    model_width = line * part
    share = rows // slots // line

    def kernel(place_ref, hidden_ref, w_ref, own_ref, *rest):
        *others, total = rest
        step = pl.program_id(0)
        part_out = nt_dot(hidden_ref[...], w_ref[...].reshape(line * part, tile))

        @pl.when(step == 0)
        def first():
            total[...] = part_out

        @pl.when(step > 0)
        def further():
            total[...] += part_out

        @pl.when(step == pl.num_programs(0) - 1)
        def last():
            deal(total, place_ref, own_ref, others)

    fixed = lambda shape: pl.BlockSpec(shape, lambda j: (0,) * len(shape))
    return pl.pallas_call(
        kernel,
        grid=(width // tile,),
        out_shape=dealt_shapes(slots, share, model_width, line),
        in_specs=[
            whole(pltpu.SMEM),
            pl.BlockSpec((rows, tile), lambda j: (0, j)),
            pl.BlockSpec((line, 1, part, tile), lambda j: (0, 0, 0, j)),
        ],
        out_specs=[fixed((slots, share, model_width))] * line,
        scratch_shapes=[pltpu.VMEM((rows, model_width), jnp.float32)],
        compiler_params=vmem_limit(60),
        cost_estimate=work(2 * rows * model_width * width, 2 * model_width * width),
        name="mlp_out",
    )(place, hidden, w_mlp)


def branch_back(place, pieces, w_out, heads):
    slots, share, model_width = pieces[0].shape
    line = (len(pieces) + 1) // 2
    rows = slots * share * line

    def kernel(place_ref, *refs):
        *piece_refs, w_ref, rows_ref, out_ref = refs
        spread(piece_refs, place_ref, rows_ref)
        turned = nt_dot(w_ref[...], rows_ref[...])
        out_ref[...] = turned.astype(jnp.bfloat16).reshape(out_ref.shape)

    return pl.pallas_call(
        kernel,
        out_shape=[
            jax.ShapeDtypeStruct((rows, model_width), jnp.bfloat16),
            jax.ShapeDtypeStruct((heads, HEAD_DIM, rows), jnp.bfloat16),
        ],
        in_specs=[whole(pltpu.SMEM)] + [whole()] * (len(pieces) + 1),
        out_specs=[whole(), whole()],
        compiler_params=vmem_limit(40),
        cost_estimate=work(2 * rows * model_width * heads * HEAD_DIM, 8 * rows * model_width),
        name="branch_back",
    )(place, *pieces, w_out)


def out_weight(grads, mixed, branch_rows, tile):
    groups, blocks, block, width = grads.shape
    heads, unused, rows = mixed.shape

    def kernel(grads_ref, mixed_ref, rows_ref, out_ref):
        left = mixed_ref[...].reshape(heads * HEAD_DIM, rows)
        product = dot_f32(left, rows_ref[...]).astype(jnp.bfloat16)
        out_ref[...] = product.reshape(groups, 1, block, tile)

    return pl.pallas_call(
        kernel,
        grid=(width // tile,),
        out_shape=jax.ShapeDtypeStruct(grads.shape, grads.dtype),
        in_specs=[
            pl.BlockSpec(memory_space=pl.ANY),
            pl.BlockSpec(mixed.shape, lambda j: (0, 0, 0)),
            pl.BlockSpec((rows, tile), lambda j: (0, j)),
        ],
        out_specs=pl.BlockSpec((groups, 1, block, tile), lambda j: (0, blocks - 1, 0, j)),
        input_output_aliases={0: 0},
        compiler_params=vmem_limit(60),
        cost_estimate=work(4 * rows * heads * HEAD_DIM * width, 8 * rows * width),
        name="out_weight",
    )(grads, mixed, branch_rows)


def head_weights(group, all_rows, corner, head_grads, w_head, gain, gain_two, owners):
    sources, features, rows = head_grads.shape
    model_width = all_rows[0].shape[1]
    block = model_width // owners
    lanes = 2 * LANES
    half = rows // 2
    f32 = jnp.float32

    def kernel(group_ref, *refs):
        x_refs, corner_refs = refs[: sources - 2], refs[sources - 2 : sources + 2]
        g_ref, w_ref, gain_ref, two_ref, out_ref, total = refs[sources + 2 :]
        step = pl.program_id(0)

        def product(bits, ref):
            return dot_f32(g_ref[lax.bitwise_xor(group_ref[0], bits)], ref[...])

        part = sum(product(bits, ref) for bits, ref in enumerate(x_refs))

        def with_corner(half_refs):
            return part + product(sources - 2, half_refs[0]) + product(sources - 1, half_refs[1])

        @pl.when(step == 0)
        def first():
            total[...] = with_corner(corner_refs[0::2])

        @pl.when(step == 1)
        def last():
            grads = (total[...] + with_corner(corner_refs[1::2])).T
            weighed = jnp.sum(grads * w_ref[...].astype(f32), 1, keepdims=True) / gain_ref[...].T
            spare = lanes - features
            at = lax.broadcasted_iota(jnp.int32, (model_width, spare), 1)
            tail = jnp.where(at == 0, weighed, jnp.where(at == 1, two_ref[...].T, 0.0))
            joined = jnp.concatenate([grads, tail], 1).astype(jnp.bfloat16)
            out_ref[...] = joined.reshape(owners, block, lanes)

    fixed = lambda shape: pl.BlockSpec(shape, lambda s: (0,) * len(shape))
    return pl.pallas_call(
        kernel,
        grid=(2,),
        out_shape=jax.ShapeDtypeStruct((owners, block, lanes), jnp.bfloat16),
        in_specs=[whole(pltpu.SMEM)]
        + [pl.BlockSpec((half, model_width), lambda s: (s, 0))] * (sources - 2)
        + [fixed((half, model_width))] * 4
        + [
            pl.BlockSpec((sources, features, half), lambda s: (0, 0, s)),
            fixed((model_width, features)),
            fixed((1, model_width)),
            fixed((1, model_width)),
        ],
        out_specs=fixed((owners, block, lanes)),
        scratch_shapes=[pltpu.VMEM((features, model_width), f32)],
        compiler_params=vmem_limit(60),
        cost_estimate=work(6 * sources * rows * features * model_width, 0),
        name="head_weights",
    )(group, *all_rows, *corner, head_grads, w_head, gain, gain_two)


def join_heads(parts):
    groups, line, rows, lanes = parts.shape
    width = groups * HEAD_DIM

    def kernel(parts_ref, *outs):
        for i, out in enumerate(outs):
            pick = slice(i * HEAD_DIM, (i + 1) * HEAD_DIM)
            heads = [parts_ref[c, 0][:, pick].astype(jnp.float32) for c in range(groups)]
            out[...] = jnp.concatenate(heads, 1)

    return pl.pallas_call(
        kernel,
        grid=(line,),
        out_shape=[jax.ShapeDtypeStruct((rows, line * width), jnp.float32)] * 3,
        in_specs=[pl.BlockSpec((groups, 1, rows, lanes), lambda f: (0, f, 0, 0))],
        out_specs=[pl.BlockSpec((rows, width), lambda f: (0, f))] * 3,
        compiler_params=vmem_limit(24),
        name="join_heads",
    )(parts)


def project_back(place, head_grads, w_heads, slots):
    line, count, part, width = w_heads.shape
    rows, model_width = head_grads.shape[-1], line * part
    heads = width // HEAD_DIM
    share = rows // slots // line

    def kernel(place_ref, g_ref, w_ref, own_ref, *rest):
        *others, total = rest
        m = pl.program_id(0)
        grads = g_ref[...].reshape(width, rows).T
        partial = nt_dot(grads, w_ref[...].reshape(line * part, width))

        @pl.when(m == 0)
        def first():
            total[...] = partial

        @pl.when(m > 0)
        def further():
            total[...] += partial

        @pl.when(m == count - 1)
        def last():
            deal(total, place_ref, own_ref, others)

    fixed = lambda shape: pl.BlockSpec(shape, lambda m: (0,) * len(shape))
    return pl.pallas_call(
        kernel,
        grid=(count,),
        out_shape=dealt_shapes(slots, share, model_width, line),
        in_specs=[
            whole(pltpu.SMEM),
            pl.BlockSpec((heads, 1, HEAD_DIM, rows), lambda m: (0, m, 0, 0)),
            pl.BlockSpec((line, 1, part, width), lambda m: (0, m, 0, 0)),
        ],
        out_specs=[fixed((slots, share, model_width))] * line,
        scratch_shapes=[pltpu.VMEM((rows, model_width), jnp.float32)],
        compiler_params=vmem_limit(48),
        cost_estimate=work(2 * count * rows * width * model_width, 8 * rows * model_width),
        name="project_back",
    )(place, head_grads, w_heads)


def line_steps(size, step):
    return [(i, i + step) for i in range(size) if 0 <= i + step < size]


def after(values, *earlier):
    return lax.optimization_barrier((values, earlier))[0]


def send_shares(share, axis, between=()):
    size = lax.axis_size(axis)
    ups, downs = [share], [share]
    for hop in range(1, size):
        up = lax.ppermute(ups[-1], axis, line_steps(size, 1)[hop - 1 :])
        down = lax.ppermute(downs[-1], axis, line_steps(size, -1)[: size - hop])
        if hop <= len(between):
            done = between[hop - 1]((ups[-1], downs[-1]))
            up, down = after((up, down), done)
        ups.append(up)
        downs.append(down)
    return ups + downs[1:]


def flip(values, bits):
    size = lax.axis_size("ctx")
    return lax.ppermute(values, "ctx", [(i, i ^ bits) for i in range(size)])


def send_dealt(others, axis):
    size = lax.axis_size(axis)
    return [
        lax.ppermute(other, axis, [(i, (i + step) % size) for i in range(size)])
        for step, other in enumerate(others, 1)
    ]


def scatter_line(others, axis, between=()):
    size = lax.axis_size(axis)
    up = down = None
    for hop in range(1, size):
        rising, falling = others[size - hop - 1], others[hop - 1]
        if hop > 1:
            rising = (rising.astype(jnp.float32) + up.astype(jnp.float32)).astype(rising.dtype)
            falling = (falling.astype(jnp.float32) + down.astype(jnp.float32)).astype(falling.dtype)
        up = lax.ppermute(rising, axis, line_steps(size, 1)[:hop])
        down = lax.ppermute(falling, axis, line_steps(size, -1)[size - 1 - hop :])
        if hop <= len(between):
            up, down = after((up, down), between[hop - 1]((rising, falling)))
    return [up, down]


def add_shares(own, received):
    return own + sum(share.astype(jnp.float32) for share in received)


def swap_dealt(shares):
    return [shares[0]] + send_dealt(shares[1:], "fsdp")


def deal_line(parts, place):
    line = parts.shape[0]
    return [
        lax.dynamic_index_in_dim(parts, lax.rem(place[0] + step, line), 0, keepdims=False)
        for step in range(line)
    ]


def swap_heads(parts):
    return lax.all_to_all(parts, "ctx", split_axis=0, concat_axis=0, tiled=True)


def sum_groups(parts):
    return lax.psum_scatter(parts, "ctx", scatter_dimension=0, tiled=True)[0]


def head_device(
    tokens,
    block_order,
    w_query,
    w_key,
    w_value,
    w_out,
    w_gate,
    w_up,
    w_down,
    gain_attn,
    gain_mlp,
    cotangent,
):
    slots, share_rows, model_width = tokens.shape
    ctx_size, line = lax.axis_size("ctx"), lax.axis_size("fsdp")
    block_rows = share_rows * line
    group_rows = slots * block_rows
    bf, f32 = jnp.bfloat16, jnp.float32
    place = lax.axis_index("fsdp").astype(jnp.int32).reshape(1)
    group = lax.axis_index("ctx").astype(jnp.int32).reshape(1)
    own_rows = w_query.shape[0] // ctx_size
    order = block_order.astype(jnp.int32)
    long_tile = (8 if ctx_size * slots % 8 == 0 else 2) * block_rows
    slot_of = jnp.sum(
        jnp.where(order[None, :] == jnp.arange(order.shape[0])[:, None], jnp.arange(order.shape[0], dtype=jnp.int32)[None, :], 0), 1
    ).astype(jnp.int32)

    stream = tokens.astype(f32)
    root_one = lax.rsqrt(jnp.mean(stream * stream, -1, keepdims=True) + EPSILON)
    norm_one = stream * root_one
    gain_rows = jnp.pad(jnp.stack([gain_attn, gain_mlp]), ((0, EXTRA_ROWS - 2), (0, 0)))
    head_cuts = swap_dealt(
        cut_columns(place, group, [w_query, w_key, w_value], own_rows, line, gain_rows)
    )
    own_heads, gains = order_shares(place, head_cuts, 3, 2)
    attn_gain, mlp_gain = gains[0], gains[1]
    w_heads = lax.all_gather(own_heads, "ctx", axis=2, tiled=True)

    attn_pieces = send_shares(after(norm_one.astype(bf), head_cuts), "fsdp")

    mlp_cuts = cut_columns(place, group, [w_down, w_gate, w_up], own_rows, line)
    w_heads = after(w_heads, mlp_cuts)
    mlp_cuts = swap_dealt(after(mlp_cuts, attn_pieces))

    w_head = lax.dynamic_slice_in_dim(w_heads, group[0] * HEAD_DIM, HEAD_DIM, 3)
    w_head = jnp.concatenate([w_head[:, i].reshape(model_width, HEAD_DIM) for i in range(3)], 1)

    half = HEAD_DIM // 2
    frequency = 1.0 / ROPE_BASE ** (jnp.arange(half, dtype=f32) * (2.0 / HEAD_DIM))
    places = jnp.arange(group_rows * ctx_size, dtype=jnp.int32).astype(f32)
    angles = frequency[:, None] * places[None, :]
    cosine, sine = jnp.cos(angles), jnp.sin(angles)

    def own_columns(table):
        return jnp.concatenate(
            [
                lax.dynamic_slice_in_dim(
                    table, order[slots * group[0] + i] * block_rows, block_rows, 1
                )
                for i in range(slots)
            ],
            1,
        )

    own_cosine, own_sine = own_columns(cosine), own_columns(sine)
    turn_cosine = jnp.stack([own_cosine, own_cosine, jnp.ones_like(own_cosine)])
    turn_sine = jnp.stack([own_sine, own_sine, jnp.zeros_like(own_sine)])

    attn_rows, heads_out = project(
        place, attn_pieces, attn_gain[None], w_heads, turn_cosine, turn_sine
    )
    heads_out = heads_out.reshape(ctx_size, 3 * HEAD_DIM, group_rows)
    head_rows = swap_heads(after(heads_out, mlp_cuts[1]))
    mixed_send, attended, log_total = attend(
        order, head_rows, block_rows, long_tile, 2 * block_rows
    )
    mixed = swap_heads(mixed_send)
    mlp_cuts = order_shares(place, after(mlp_cuts, mixed), 3)
    w_mlp = lax.all_gather(mlp_cuts, "ctx", axis=2, tiled=True)
    upstream_pieces = send_shares(after(cotangent, mlp_cuts), "fsdp")
    own, *others = mix_out(place, after(mixed, w_head, mlp_cuts), w_out, slots, line)
    middle = stream + add_shares(own, scatter_line(others, "fsdp"))

    root_two = lax.rsqrt(jnp.mean(middle * middle, -1, keepdims=True) + EPSILON)
    norm_two = middle * root_two
    mlp_input = (norm_two * mlp_gain).astype(bf)
    mlp_pieces = send_shares(mlp_input, "fsdp")

    all_rows = {0: attn_rows}
    start_rows = after(attn_rows, mlp_pieces, upstream_pieces)
    all_rows[2], all_rows[4] = flip(start_rows, 2), flip(start_rows, 4)
    mlp_rows, upstream_rows, hidden, grad_gate, grad_up, own, *others = mlp_forward(
        place, mlp_pieces, upstream_pieces, w_mlp, 512
    )
    results = {}

    def weigh_gate_up(sent):
        rows_here = after(mlp_rows, sent)
        results["gate_up"] = gate_up_weights(rows_here, grad_gate, grad_up, ctx_size, line, 512)
        return results["gate_up"], all_rows[2], all_rows[4]

    upper = attn_rows.shape[0] // 2

    def weigh_down(sent):
        results["down"] = down_weights(
            upstream_rows, after(hidden, sent), ctx_size, line, 512
        )
        results["gate_up_sums"] = sum_groups(after(results["gate_up"], sent))
        return results["down"]

    grad_two = add_shares(own, scatter_line(others, "fsdp", (weigh_gate_up, weigh_down)))
    gate_up_sums = results["gate_up_sums"]
    down_grads = results["down"]
    gain_two_part = jnp.sum(grad_two * norm_two, (0, 1))
    grad_middle = cotangent.astype(f32) + norm_back(grad_two, norm_two, root_two, mlp_gain)

    def weigh_out(sent):
        results["out"] = mlp_out(place, after(hidden, sent), w_mlp, slots, 512)
        return results["out"]

    def cut_corner(sent):
        by_x, by_y = after((all_rows[2], all_rows[4]), sent)
        results["corner"] = (by_x[:upper], by_y[upper:])
        return results["corner"]

    branch_pieces = send_shares(grad_middle.astype(bf), "fsdp", (weigh_out, cut_corner))
    corner = [flip(results["corner"][0], 4), flip(results["corner"][1], 2)]
    own_out, *others_out = results["out"]
    branch_rows, grad_mixed = branch_back(place, branch_pieces, w_out, ctx_size)

    out_received = send_dealt(after(others_out, branch_rows), "fsdp")
    for bits in (0, 2, 4):
        all_rows[bits + 1] = flip(after(all_rows[bits], branch_rows), 1)
    grad_heads = swap_heads(grad_mixed)
    down_grads = out_weight(down_grads, mixed, branch_rows, 512)
    head_grads = attend_back(
        jnp.concatenate([order, slot_of]),
        head_rows,
        after(
            grad_heads, down_grads, all_rows[1], all_rows[3], all_rows[5]
        ),
        attended,
        log_total,
        cosine,
        sine,
        block_rows,
        long_tile,
        2 * block_rows,
    )
    head_grads = after(head_grads, out_received, corner)
    corner = corner + [flip(part, 1) for part in after(corner, head_grads)]
    gate_up_dealt = deal_line(after(gate_up_sums, head_grads), place)
    gate_up_back = swap_dealt(gate_up_dealt)
    down_sums = sum_groups(after(down_grads, gate_up_sums, head_grads))
    lin_grads = swap_heads(after(head_grads, gate_up_dealt))
    head_parts = head_weights(
        group,
        [all_rows[bits] for bits in range(ctx_size - 2)],
        corner,
        after(head_grads, gate_up_dealt),
        w_head,
        attn_gain[None],
        gain_two_part[None],
        ctx_size * line,
    )
    lin_grads = after(lin_grads, head_parts, gate_up_back[1], gate_up_back[2])
    head_parts = lax.all_to_all(
        after(head_parts, lin_grads), ("ctx", "fsdp"), split_axis=0, concat_axis=0, tiled=True
    )
    lin_grads = lin_grads.reshape(ctx_size, 3, HEAD_DIM, group_rows)
    own, *others = project_back(place, lin_grads, w_heads, slots)

    def swap_down(sent):
        parts = deal_line(after(down_sums, sent)[:line], place)
        results["down_back"] = swap_dealt(parts)
        return results["down_back"]

    one_received = scatter_line(
        others, "fsdp", (lambda sent: (gate_up_back[3], head_parts), lambda sent: (), swap_down)
    )
    down_back = results["down_back"]
    grad_one = add_shares(own, one_received)
    result = (middle + add_shares(own_out, out_received)).astype(bf)
    grad_tokens = grad_middle + norm_back(grad_one, norm_one, root_one, attn_gain)
    owners = [(c * line + f, f * ctx_size + c) for c in range(ctx_size) for f in range(line)]
    grad_w_out = lax.ppermute(down_sums[line], ("ctx", "fsdp"), owners).astype(f32)
    grad_w_gate, grad_w_up = widen_columns(place, gate_up_back, 2, own_rows)
    (grad_w_down,) = widen_columns(place, down_back, 1, own_rows)
    head_parts = head_parts.reshape(ctx_size, line, own_rows, -1)
    grad_w_query, grad_w_key, grad_w_value = join_heads(head_parts)
    spare = 3 * HEAD_DIM
    gain_grads = jnp.sum(head_parts[..., spare : spare + 2].astype(f32), (0, 1)).T
    return (
        result,
        grad_tokens,
        grad_w_query,
        grad_w_key,
        grad_w_value,
        grad_w_out,
        grad_w_gate,
        grad_w_up,
        grad_w_down,
        gain_grads[0],
        gain_grads[1],
    )


def layer_step(*arrays):
    heads_here = arrays[0].shape[-1] // lax.axis_size("fsdp") // HEAD_DIM
    if heads_here == lax.axis_size("ctx") == 8:
        return head_device(*arrays)
    return per_device(*arrays)


def solution(mesh):
    in_specs = (
        P("ctx", "fsdp", None),
        P(),
        P("fsdp", None),
        P("fsdp", None),
        P("fsdp", None),
        P("fsdp", None),
        P("fsdp", None),
        P("fsdp", None),
        P("fsdp", None),
        P("fsdp"),
        P("fsdp"),
        P("ctx", "fsdp", None),
    )
    out_specs = (
        P("ctx", "fsdp", None),
        P("ctx", "fsdp", None),
        P(("ctx", "fsdp"), None),
        P(("ctx", "fsdp"), None),
        P(("ctx", "fsdp"), None),
        P(("ctx", "fsdp"), None),
        P(("ctx", "fsdp"), None),
        P(("ctx", "fsdp"), None),
        P(("ctx", "fsdp"), None),
        P(("ctx", "fsdp")),
        P(("ctx", "fsdp")),
    )
    return jax.shard_map(
        layer_step, mesh=mesh, in_specs=in_specs, out_specs=out_specs, check_vma=False
    )
```

```python
import functools

import jax
import jax.numpy as jnp
from jax import lax
from jax.experimental import pallas as pl
from jax.experimental.pallas import tpu as pltpu
from jax.sharding import PartitionSpec as P

HEAD_DIM = 64


EPSILON = 1e-05
ROPE_BASE = 130000.0
MASKED_SCORE = -1e30


def rotate(values, places, direction):
    half_dim = values.shape[-1] // 2
    frequency = 1.0 / ROPE_BASE ** (
        jnp.arange(half_dim, dtype=jnp.float32) * (2.0 / values.shape[-1])
    )
    angles = places[..., None] * frequency
    cosine = jnp.cos(angles)[..., None, :]
    sine_part = direction * jnp.sin(angles)[..., None, :]
    leading = values[..., :half_dim]
    trailing = values[..., half_dim:]
    return jnp.concatenate(
        [leading * cosine - trailing * sine_part, trailing * cosine + leading * sine_part], -1
    )


def matmul(left, right):
    return jnp.dot(left, right, preferred_element_type=jnp.float32)


def contract(left, right):
    return lax.dot_general(
        left, right, (((1,), (1,)), ((), ())), preferred_element_type=jnp.float32
    )


def transpose_product(left, right):
    return lax.dot_general(
        left, right, (((0,), (0,)), ((), ())), preferred_element_type=jnp.float32
    )


def split_heads(values):
    return values.reshape(values.shape[:-1] + (-1, HEAD_DIM))


def keep_state(current):
    return current


def tile_scores(queries, key_rows, query_places, key_places, score_scale):
    scores = (
        jnp.einsum("qhd,khd->hqk", queries, key_rows, preferred_element_type=jnp.float32)
        * score_scale
    )
    allowed = (key_places[None, :] <= query_places[:, None])[None]
    return (jnp.where(allowed, scores, MASKED_SCORE), allowed)


def grow_state(current, queries, key_rows, value_rows, query_places, key_places, score_scale):
    run_peak, run_total, summed = current
    scores, allowed = tile_scores(queries, key_rows, query_places, key_places, score_scale)
    new_peak = jnp.maximum(run_peak, jnp.max(scores, -1))
    weights = jnp.where(allowed, jnp.exp(scores - new_peak[..., None]), 0.0)
    factor = jnp.exp(run_peak - new_peak)
    run_total = run_total * factor + jnp.sum(weights, -1)
    summed = summed * jnp.transpose(factor)[:, :, None] + jnp.einsum(
        "hqk,khd->qhd", weights.astype(jnp.bfloat16), value_rows, preferred_element_type=jnp.float32
    )
    return (new_peak, run_total, summed)


def backward_tile(
    queries,
    key_rows,
    value_rows,
    grad_out,
    log_total,
    row_delta,
    query_places,
    key_places,
    score_scale,
):
    scores, allowed = tile_scores(queries, key_rows, query_places, key_places, score_scale)
    probabilities = jnp.where(allowed, jnp.exp(scores - log_total[..., None]), 0.0)
    grad_probs = jnp.einsum(
        "qhd,khd->hqk", grad_out, value_rows, preferred_element_type=jnp.float32
    )
    grad_scores = (probabilities * (grad_probs - row_delta[..., None])).astype(jnp.bfloat16)
    return (probabilities, grad_scores)


def norm_back(grad_normed_in, normed_values, inverse_root, gain_vector):
    scaled = grad_normed_in * gain_vector
    return inverse_root * (
        scaled - normed_values * jnp.mean(scaled * normed_values, -1, keepdims=True)
    )


def per_device(
    tokens,
    block_order,
    w_query,
    w_key,
    w_value,
    w_out,
    w_gate,
    w_up,
    w_down,
    gain_attn,
    gain_mlp,
    cotangent,
):
    slot_count, share_rows, model_width = tokens.shape
    fsdp_size = lax.axis_size("fsdp")
    block_rows = share_rows * fsdp_size
    head_width = model_width // fsdp_size
    heads_here = head_width // HEAD_DIM
    row_count = slot_count * share_rows
    score_scale = HEAD_DIM ** (-0.5)
    own_slots = 2 * lax.axis_index("ctx") + jnp.arange(2, dtype=jnp.int32)
    own_blocks = block_order[own_slots]
    token_places = (
        (
            own_blocks[:, None] * block_rows
            + lax.axis_index("fsdp") * share_rows
            + jnp.arange(share_rows, dtype=jnp.int32)[None, :]
        )
        .astype(jnp.float32)
        .reshape(row_count)
    )
    head_places = (
        own_blocks[:, None] * block_rows + jnp.arange(block_rows, dtype=jnp.int32)[None, :]
    ).astype(jnp.float32)
    params = (w_query, w_key, w_value, w_out, w_gate, w_up, w_down, gain_attn, gain_mlp)
    weights_all = (
        lax.all_gather(params[0], "fsdp", axis=0, tiled=True),
        lax.all_gather(params[1], "fsdp", axis=0, tiled=True),
        lax.all_gather(params[2], "fsdp", axis=0, tiled=True),
        lax.all_gather(params[3], "fsdp", axis=0, tiled=True),
        lax.all_gather(params[4], "fsdp", axis=0, tiled=True),
        lax.all_gather(params[5], "fsdp", axis=0, tiled=True),
        lax.all_gather(params[6], "fsdp", axis=0, tiled=True),
        lax.all_gather(params[7], "fsdp", axis=0, tiled=True),
        lax.all_gather(params[8], "fsdp", axis=0, tiled=True),
    )
    stream = tokens.reshape(row_count, model_width).astype(jnp.float32)
    root_one = lax.rsqrt(jnp.mean(stream * stream, -1, keepdims=True) + EPSILON)
    norm_one = stream * root_one
    attn_input = (norm_one * weights_all[7].astype(jnp.float32)).astype(jnp.bfloat16)

    def project_turn(weight):
        linear = matmul(attn_input, weight).reshape(row_count, -1, HEAD_DIM)
        return (
            rotate(linear, token_places, 1.0)
            .astype(jnp.bfloat16)
            .reshape(slot_count, share_rows, model_width)
        )

    query_tok = project_turn(weights_all[0])
    key_tok = project_turn(weights_all[1])
    value_tok = (
        matmul(attn_input, weights_all[2])
        .astype(jnp.bfloat16)
        .reshape(slot_count, share_rows, model_width)
    )
    query_heads, key_heads, value_heads = (
        lax.all_to_all(query_tok, "fsdp", split_axis=2, concat_axis=1, tiled=True),
        lax.all_to_all(key_tok, "fsdp", split_axis=2, concat_axis=1, tiled=True),
        lax.all_to_all(value_tok, "fsdp", split_axis=2, concat_axis=1, tiled=True),
    )
    query_split = split_heads(query_heads)
    start_state = tuple(
        (
            (
                jnp.full((heads_here, block_rows), MASKED_SCORE, jnp.float32),
                jnp.zeros((heads_here, block_rows), jnp.float32),
                jnp.zeros((block_rows, heads_here, HEAD_DIM), jnp.float32),
            )
            for which_slot in range(2)
        )
    )
    carried = start_state
    key_part = lax.all_gather(key_heads, "ctx", axis=0, tiled=True)
    value_part = lax.all_gather(value_heads, "ctx", axis=0, tiled=True)

    def visit_slot(inner_state, element):
        key_one, value_one, offset = element
        key_block = block_order[offset]
        key_places = (key_block * block_rows + jnp.arange(block_rows, dtype=jnp.int32)).astype(
            jnp.float32
        )
        key_split = split_heads(key_one)
        value_split = split_heads(value_one)
        updated = []
        for which_slot in range(2):

            def grow_one(current, which_slot=which_slot):
                return grow_state(
                    current,
                    query_split[which_slot],
                    key_split,
                    value_split,
                    head_places[which_slot],
                    key_places,
                    score_scale,
                )

            updated.append(
                lax.cond(
                    key_block <= own_blocks[which_slot],
                    grow_one,
                    keep_state,
                    inner_state[which_slot],
                )
            )
        return (tuple(updated), None)

    offsets = jnp.arange(key_part.shape[0], dtype=jnp.int32)
    carried, unused = lax.scan(visit_slot, carried, (key_part, value_part, offsets))
    attended_parts = []
    log_parts = []
    for which_slot in range(2):
        run_peak, run_total, summed = carried[which_slot]
        log_parts.append(run_peak + jnp.log(run_total))
        attended_parts.append(summed / jnp.transpose(run_total)[:, :, None])
    attended = jnp.stack(attended_parts)
    log_total = jnp.stack(log_parts)
    mixed_send = attended.reshape(slot_count, block_rows, head_width).astype(jnp.bfloat16)
    mixed_tok = lax.all_to_all(mixed_send, "fsdp", split_axis=1, concat_axis=2, tiled=True)
    mixed_flat = mixed_tok.reshape(row_count, model_width)
    middle = stream + matmul(mixed_flat, weights_all[3])
    root_two = lax.rsqrt(jnp.mean(middle * middle, -1, keepdims=True) + EPSILON)
    norm_two = middle * root_two
    mlp_input = (norm_two * weights_all[8].astype(jnp.float32)).astype(jnp.bfloat16)
    gate_act = matmul(mlp_input, weights_all[4])
    upward = matmul(mlp_input, weights_all[5])
    gate_sigmoid = jax.nn.sigmoid(gate_act)
    gate_silu = gate_act * gate_sigmoid
    hidden = (gate_silu * upward).astype(jnp.bfloat16)
    output = middle + contract(hidden, weights_all[6])
    result = output.astype(jnp.bfloat16).reshape(slot_count, share_rows, model_width)
    upstream = cotangent.reshape(row_count, model_width)
    grad_hidden = matmul(upstream, weights_all[6])
    grad_gate = (
        grad_hidden * upward * gate_sigmoid * (1.0 + gate_act * (1.0 - gate_sigmoid))
    ).astype(jnp.bfloat16)
    grad_up = (grad_hidden * gate_silu).astype(jnp.bfloat16)
    grad_two = contract(grad_gate, weights_all[4]) + contract(grad_up, weights_all[5])
    gain_two_part = jnp.sum(grad_two * norm_two, 0)
    grad_middle = upstream.astype(jnp.float32) + norm_back(
        grad_two, norm_two, root_two, weights_all[8].astype(jnp.float32)
    )
    grad_branch = grad_middle.astype(jnp.bfloat16)
    grad_mixed = (
        contract(grad_branch, weights_all[3])
        .astype(jnp.bfloat16)
        .reshape(slot_count, share_rows, model_width)
    )
    grad_heads = lax.all_to_all(grad_mixed, "fsdp", split_axis=2, concat_axis=1, tiled=True)
    grad_split = split_heads(grad_heads)
    row_delta = jnp.transpose(jnp.sum(grad_split.astype(jnp.float32) * attended, -1), (0, 2, 1))
    gathered = (
        lax.all_gather(key_heads, "ctx", axis=0, tiled=True),
        lax.all_gather(value_heads, "ctx", axis=0, tiled=True),
    )
    key_all, value_all = gathered
    total_slots = key_all.shape[0]

    def query_visit(current, element):
        key_pair, value_pair, pair_index = element
        updated = list(current)
        for member in range(2):
            key_block = block_order[2 * pair_index + member]
            key_places = (key_block * block_rows + jnp.arange(block_rows, dtype=jnp.int32)).astype(
                jnp.float32
            )
            key_split = split_heads(key_pair[member])
            value_split = split_heads(value_pair[member])
            for which_slot in range(2):

                def take_query(
                    accum,
                    which_slot=which_slot,
                    key_split=key_split,
                    value_split=value_split,
                    key_places=key_places,
                ):
                    probabilities, grad_scores = backward_tile(
                        query_split[which_slot],
                        key_split,
                        value_split,
                        grad_split[which_slot],
                        log_total[which_slot],
                        row_delta[which_slot],
                        head_places[which_slot],
                        key_places,
                        score_scale,
                    )
                    return accum + score_scale * jnp.einsum(
                        "hqk,khd->qhd", grad_scores, key_split, preferred_element_type=jnp.float32
                    )

                updated[which_slot] = lax.cond(
                    key_block <= own_blocks[which_slot], take_query, keep_state, updated[which_slot]
                )
        return (tuple(updated), None)

    query_zero = jnp.zeros((block_rows, heads_here, HEAD_DIM), jnp.float32)
    pair_keys = key_all.reshape(total_slots // 2, 2, block_rows, head_width)
    pair_values = value_all.reshape(total_slots // 2, 2, block_rows, head_width)
    grad_query_parts, unused = lax.scan(
        query_visit,
        (query_zero, query_zero),
        (pair_keys, pair_values, jnp.arange(total_slots // 2, dtype=jnp.int32)),
    )
    key_part = key_all
    value_part = value_all

    def key_visit(unused_carry, element):
        key_one, value_one, offset = element
        key_block = block_order[offset]
        key_places = (key_block * block_rows + jnp.arange(block_rows, dtype=jnp.int32)).astype(
            jnp.float32
        )
        key_split = split_heads(key_one)
        value_split = split_heads(value_one)
        sums = (
            jnp.zeros((block_rows, heads_here, HEAD_DIM), jnp.float32),
            jnp.zeros((block_rows, heads_here, HEAD_DIM), jnp.float32),
        )
        for which_slot in range(2):

            def take_keys(current, which_slot=which_slot):
                probabilities, grad_scores = backward_tile(
                    query_split[which_slot],
                    key_split,
                    value_split,
                    grad_split[which_slot],
                    log_total[which_slot],
                    row_delta[which_slot],
                    head_places[which_slot],
                    key_places,
                    score_scale,
                )
                grad_key = current[0] + score_scale * jnp.einsum(
                    "hqk,qhd->khd",
                    grad_scores,
                    query_split[which_slot],
                    preferred_element_type=jnp.float32,
                )
                grad_value = current[1] + jnp.einsum(
                    "hqk,qhd->khd",
                    probabilities.astype(jnp.bfloat16),
                    grad_split[which_slot],
                    preferred_element_type=jnp.float32,
                )
                return (grad_key, grad_value)

            sums = lax.cond(key_block <= own_blocks[which_slot], take_keys, keep_state, sums)
        joined = jnp.concatenate(
            [sums[0].reshape(block_rows, head_width), sums[1].reshape(block_rows, head_width)], -1
        )
        return (unused_carry, joined)

    unused_final, terms = lax.scan(
        key_visit,
        jnp.zeros((), jnp.float32),
        (key_part, value_part, jnp.arange(slot_count * lax.axis_size("ctx"), dtype=jnp.int32)),
    )
    summed_kv = lax.psum_scatter(
        terms.astype(jnp.bfloat16), "ctx", scatter_dimension=0, tiled=True
    ).astype(jnp.float32)
    grad_keys = (
        rotate(split_heads(summed_kv[..., :head_width]), head_places, -1.0)
        .astype(jnp.bfloat16)
        .reshape(slot_count, block_rows, head_width)
    )
    grad_values = summed_kv[..., head_width:].astype(jnp.bfloat16)
    grad_queries = (
        rotate(jnp.stack(grad_query_parts), head_places, -1.0)
        .astype(jnp.bfloat16)
        .reshape(slot_count, block_rows, head_width)
    )
    grad_q_tok, grad_k_tok, grad_v_tok = (
        lax.all_to_all(grad_queries, "fsdp", split_axis=1, concat_axis=2, tiled=True),
        lax.all_to_all(grad_keys, "fsdp", split_axis=1, concat_axis=2, tiled=True),
        lax.all_to_all(grad_values, "fsdp", split_axis=1, concat_axis=2, tiled=True),
    )
    grad_q_lin = grad_q_tok.reshape(row_count, model_width)
    grad_k_lin = grad_k_tok.reshape(row_count, model_width)
    grad_v_lin = grad_v_tok.reshape(row_count, model_width)
    grad_one = (
        contract(grad_q_lin, weights_all[0])
        + contract(grad_k_lin, weights_all[1])
        + contract(grad_v_lin, weights_all[2])
    )
    gain_one_part = jnp.sum(grad_one * norm_one, 0)
    grad_input = grad_middle + norm_back(
        grad_one, norm_one, root_one, weights_all[7].astype(jnp.float32)
    )
    hidden_width = hidden.shape[1]
    gain_parts = jnp.stack([gain_one_part, gain_two_part], 1)
    wide_cols = (
        lax.all_to_all(grad_q_lin, "fsdp", split_axis=1, concat_axis=0, tiled=True),
        lax.all_to_all(grad_k_lin, "fsdp", split_axis=1, concat_axis=0, tiled=True),
        lax.all_to_all(grad_v_lin, "fsdp", split_axis=1, concat_axis=0, tiled=True),
        lax.all_to_all(grad_branch, "fsdp", split_axis=1, concat_axis=0, tiled=True),
        lax.all_to_all(grad_gate, "fsdp", split_axis=1, concat_axis=0, tiled=True),
        lax.all_to_all(grad_up, "fsdp", split_axis=1, concat_axis=0, tiled=True),
        lax.all_to_all(hidden, "fsdp", split_axis=1, concat_axis=0, tiled=True),
    )
    row_sets = (
        lax.all_gather(attn_input, "fsdp", axis=0, tiled=True),
        lax.all_gather(mixed_flat, "fsdp", axis=0, tiled=True),
        lax.all_gather(mlp_input, "fsdp", axis=0, tiled=True),
        lax.all_gather(upstream, "fsdp", axis=0, tiled=True),
    )
    group_rows = model_width // lax.axis_size("ctx")
    row_cuts = [values for values in row_sets]
    pieces = [
        transpose_product(row_cuts[0], wide_cols[0]),
        transpose_product(row_cuts[0], wide_cols[1]),
        transpose_product(row_cuts[0], wide_cols[2]),
        transpose_product(row_cuts[1], wide_cols[3]),
        transpose_product(row_cuts[2], wide_cols[4]),
        transpose_product(row_cuts[2], wide_cols[5]),
        transpose_product(row_cuts[3], wide_cols[6]),
        gain_parts,
        jnp.zeros((group_rows * lax.axis_size("ctx"), 126), jnp.float32),
    ]
    partial_sums = lax.psum_scatter(
        jnp.concatenate(pieces, 1).astype(jnp.bfloat16), "ctx", scatter_dimension=0, tiled=True
    ).astype(jnp.float32)
    owned = lax.all_to_all(
        partial_sums.astype(jnp.bfloat16), "fsdp", split_axis=0, concat_axis=1, tiled=True
    ).astype(partial_sums.dtype)
    span_width = partial_sums.shape[1]
    owned_rows = owned.shape[0]
    arranged = owned.reshape(owned_rows, fsdp_size, span_width)
    model_part = model_width // fsdp_size
    hidden_part = hidden_width // fsdp_size
    bounds = [
        0,
        model_part,
        2 * model_part,
        3 * model_part,
        4 * model_part,
        4 * model_part + hidden_part,
        4 * model_part + 2 * hidden_part,
        4 * model_part + 3 * hidden_part,
    ]

    def joined_cols(first_col, last_col):
        return arranged[:, :, first_col:last_col].reshape(owned_rows, -1)

    grad_w_query = joined_cols(bounds[0], bounds[1])
    grad_w_key = joined_cols(bounds[1], bounds[2])
    grad_w_value = joined_cols(bounds[2], bounds[3])
    grad_w_out = joined_cols(bounds[3], bounds[4])
    grad_w_gate = joined_cols(bounds[4], bounds[5])
    grad_w_up = joined_cols(bounds[5], bounds[6])
    grad_w_down = joined_cols(bounds[6], bounds[7])
    gain_totals = jnp.sum(arranged[:, :, bounds[7] : bounds[7] + 2], 1)
    grad_gain_attn = gain_totals[:, 0]
    grad_gain_mlp = gain_totals[:, 1]
    grad_tokens = grad_input.reshape(slot_count, share_rows, model_width)
    return (
        result,
        grad_tokens,
        grad_w_query,
        grad_w_key,
        grad_w_value,
        grad_w_out,
        grad_w_gate,
        grad_w_up,
        grad_w_down,
        grad_gain_attn,
        grad_gain_mlp,
    )


def dot_f32(a, b):
    return jnp.dot(a, b, preferred_element_type=jnp.float32)

def load_sequence(order_ref, rows_ref, block, stores):
    per_src = rows_ref.shape[2] // block
    def one(slot, carry):
        src = slot // per_src
        lane = pl.multiple_of((slot % per_src) * block, block)
        place = pl.multiple_of(order_ref[slot] * block, block)
        for at, store in stores:
            store(rows_ref[src, at:at + HEAD_DIM, pl.ds(lane, block)], place)
        return carry
    lax.fori_loop(0, rows_ref.shape[0] * per_src, one, 0)

def fwd_kernel(
    order_ref, qkv_ref, mixed_ref, out_ref, lse_ref, qt, kr, vt, peak, total, acc, *, block, tile, step
):
    seq = qt.shape[1]

    def put_q(x, place):
        qt[:, pl.ds(place, block)] = x * jnp.bfloat16(HEAD_DIM ** -0.5)

    def put_k(x, place):
        kr[pl.ds(place, block), :] = x.T

    def put_v(x, place):
        vt[:, pl.ds(place, block)] = x

    load_sequence(
        order_ref, qkv_ref, block, ((0, put_q), (HEAD_DIM, put_k), (2 * HEAD_DIM, put_v))
    )

    def one_tile(qi, unused):
        q0 = pl.multiple_of(qi * tile, tile)
        peak[...] = jnp.full_like(peak, MASKED_SCORE)
        total[...] = jnp.zeros_like(total)
        acc[...] = jnp.zeros_like(acc)

        def visit(k0, first, masked):
            queries = qt[:, pl.ds(pl.multiple_of(q0 + first, step), tile - first)]
            s = dot_f32(kr[pl.ds(k0, step), :], queries)
            if masked:
                keep = lax.broadcasted_iota(jnp.int32, s.shape, 0) <= lax.broadcasted_iota(
                    jnp.int32, s.shape, 1
                )
                s = jnp.where(keep, s, MASKED_SCORE)
            old = peak[:, first:]
            new = jnp.maximum(old, jnp.max(s, 0, keepdims=True))
            p = jnp.exp(s - new)
            alpha = jnp.exp(old - new)
            peak[:, first:] = new
            total[:, first:] = total[:, first:] * alpha + jnp.sum(p, 0, keepdims=True)
            acc[:, first:] = acc[:, first:] * alpha + dot_f32(
                vt[:, pl.ds(k0, step)], p.astype(jnp.bfloat16)
            )

        def below(j, carry):
            visit(pl.multiple_of(j * step, step), 0, False)
            return carry

        lax.fori_loop(0, qi * (tile // step), below, 0)
        for part in range(tile // step):
            visit(pl.multiple_of(q0 + part * step, step), part * step, True)
        out_ref[:, pl.ds(q0, tile)] = acc[...] / total[...]
        lse_ref[:, pl.ds(q0, tile)] = peak[...] + jnp.log(total[...])
        return unused

    lax.fori_loop(0, seq // tile, one_tile, 0)
    per_src = mixed_ref.shape[2] // block

    def send(slot, carry):
        place = pl.multiple_of(order_ref[slot] * block, block)
        lane = pl.multiple_of((slot % per_src) * block, block)
        mixed_ref[slot // per_src, :, pl.ds(lane, block)] = out_ref[:, pl.ds(place, block)].astype(
            jnp.bfloat16
        )
        return carry

    lax.fori_loop(0, mixed_ref.shape[0] * per_src, send, 0)


def attend(order, qkv, block, tile, step):
    groups, unused, width = qkv.shape
    seq = groups * width
    vm = pl.BlockSpec(memory_space=pltpu.VMEM)
    bf, f32 = jnp.bfloat16, jnp.float32
    return pl.pallas_call(
        functools.partial(fwd_kernel, block=block, tile=tile, step=step),
        out_shape=(
            jax.ShapeDtypeStruct((groups, HEAD_DIM, width), bf),
            jax.ShapeDtypeStruct((HEAD_DIM, seq), f32),
            jax.ShapeDtypeStruct((1, seq), f32),
        ),
        in_specs=[pl.BlockSpec(memory_space=pltpu.SMEM), vm],
        out_specs=(vm, vm, vm),
        scratch_shapes=[
            pltpu.VMEM((HEAD_DIM, seq), bf),
            pltpu.VMEM((seq, HEAD_DIM), bf),
            pltpu.VMEM((HEAD_DIM, seq), bf),
            pltpu.VMEM((1, tile), f32),
            pltpu.VMEM((1, tile), f32),
            pltpu.VMEM((HEAD_DIM, tile), f32),
        ],
        compiler_params=pltpu.CompilerParams(vmem_limit_bytes=48 << 20),
        cost_estimate=pl.CostEstimate(
            flops=int(4.0 * seq * seq * HEAD_DIM),
            bytes_accessed=8 * seq * HEAD_DIM,
            transcendentals=0,
        ),
        name="attend",
    )(order, qkv)


def bwd_kernel(order_ref, qkv_ref, go_ref, out_ref, lse_ref, cos_ref, sin_ref, grad_ref,
               qt, qr, kt, kr, vr, got, gor, delta, dqt, dkr, dvr, *, block, tile, step):
    seq = qt.shape[1]
    scale = jnp.bfloat16(HEAD_DIM ** -0.5)
    def put_q(x, place):
        x = x * scale
        qt[:, pl.ds(place, block)] = x
        qr[pl.ds(place, block), :] = x.T
    def put_k(x, place):
        kt[:, pl.ds(place, block)] = x * scale
        kr[pl.ds(place, block), :] = x.T
    def put_v(x, place):
        vr[pl.ds(place, block), :] = x.T
    def put_go(x, place):
        got[:, pl.ds(place, block)] = x
        gor[pl.ds(place, block), :] = x.T
        delta[:, pl.ds(place, block)] = jnp.sum(x.astype(jnp.float32) * out_ref[:, pl.ds(place, block)], 0, keepdims=True)
    load_sequence(order_ref, qkv_ref, block, ((0, put_q), (HEAD_DIM, put_k), (2 * HEAD_DIM, put_v)))
    load_sequence(order_ref, go_ref, block, ((0, put_go),))
    dqt[...] = jnp.zeros_like(dqt)
    tiles = seq // tile

    def key_tile(kj, unused):
        k0 = pl.multiple_of(kj * tile, tile)
        keys = kr[pl.ds(k0, tile), :]
        keys_t = kt[:, pl.ds(k0, tile)]
        vals = vr[pl.ds(k0, tile), :]
        dkr[...] = jnp.zeros_like(dkr)
        dvr[...] = jnp.zeros_like(dvr)

        def visit(q0, width, rows, masked):
            s = dot_f32(keys[:rows], qt[:, pl.ds(q0, width)])
            p = jnp.exp(s - lse_ref[:, pl.ds(q0, width)])
            if masked:
                keep = lax.broadcasted_iota(jnp.int32, s.shape, 0) <= lax.broadcasted_iota(
                    jnp.int32, s.shape, 1
                ) + (rows - width)
                p = jnp.where(keep, p, 0.0)
            dp = dot_f32(vals[:rows], got[:, pl.ds(q0, width)])
            ds = (p * (dp - delta[:, pl.ds(q0, width)])).astype(jnp.bfloat16)
            dvr[:rows] += dot_f32(p.astype(jnp.bfloat16), gor[pl.ds(q0, width), :])
            dkr[:rows] += dot_f32(ds, qr[pl.ds(q0, width), :])
            dqt[:, pl.ds(q0, width)] += dot_f32(keys_t[:, :rows], ds)

        for part in range(tile // step):
            first = pl.multiple_of(k0 + part * step, step)
            visit(first, step, (part + 1) * step, True)

        def later(j, carry):
            visit(pl.multiple_of(j * step, step), step, tile, False)
            return carry

        lax.fori_loop((kj + 1) * (tile // step), seq // step, later, 0)
        put_out(dkr[...].T, HEAD_DIM, k0, True)
        put_out(dvr[...].T, 2 * HEAD_DIM, k0, False)
        return unused

    half = HEAD_DIM // 2
    def put_out(x, at, place, turn):
        for part in range(tile // block):
            piece = x[:, part * block:(part + 1) * block]
            here = place + part * block
            if turn:
                lanes = pl.ds(pl.multiple_of(here, block), block)
                c, s = cos_ref[:, lanes], sin_ref[:, lanes]
                a, b = piece[:half], piece[half:]
                piece = jnp.concatenate([a * c + b * s, b * c - a * s], 0)
            slot = order_ref[seq // block + here // block]
            per_src = grad_ref.shape[2] // block
            lane = pl.multiple_of((slot % per_src) * block, block)
            grad_ref[slot // per_src, at:at + HEAD_DIM, pl.ds(lane, block)] = piece.astype(jnp.bfloat16)

    lax.fori_loop(0, tiles, key_tile, 0)
    def write_q(qi, c):
        q0 = pl.multiple_of(qi * tile, tile)
        put_out(dqt[:, pl.ds(q0, tile)], 0, q0, True)
        return c
    lax.fori_loop(0, tiles, write_q, 0)

def attend_back(order, qkv, go, out, lse, cos, sin, block, tile, step):
    groups, unused, width = qkv.shape
    seq = groups * width
    vm = pl.BlockSpec(memory_space=pltpu.VMEM)
    bf, f32 = jnp.bfloat16, jnp.float32
    wide = lambda t: pltpu.VMEM((HEAD_DIM, seq), t)
    tall = lambda t: pltpu.VMEM((seq, HEAD_DIM), t)
    return pl.pallas_call(
        functools.partial(bwd_kernel, block=block, tile=tile, step=step),
        out_shape=jax.ShapeDtypeStruct(qkv.shape, bf),
        in_specs=[pl.BlockSpec(memory_space=pltpu.SMEM)] + [vm] * 6,
        out_specs=vm,
        scratch_shapes=[wide(bf), tall(bf), wide(bf), tall(bf), tall(bf), wide(bf), tall(bf),
                        pltpu.VMEM((1, seq), f32), wide(f32),
                        pltpu.VMEM((tile, HEAD_DIM), f32), pltpu.VMEM((tile, HEAD_DIM), f32)],
        compiler_params=pltpu.CompilerParams(vmem_limit_bytes=48 << 20),
        cost_estimate=pl.CostEstimate(
            flops=int(6.4 * seq * seq * HEAD_DIM),
            bytes_accessed=16 * seq * HEAD_DIM,
            transcendentals=0,
        ),
        name="attend_back",
    )(order, qkv, go, out, lse, cos, sin)


def nt_dot(a, b):
    return lax.dot_general(a, b, (((1,), (1,)), ((), ())), preferred_element_type=jnp.float32)


def whole(space=pltpu.VMEM):
    return pl.BlockSpec(memory_space=space)


def spread(pieces, place_ref, rows_ref):
    hops = (len(pieces) - 1) // 2
    slots, share, unused = pieces[0].shape
    place = place_ref[0]

    def put(piece, position):
        for slot in range(slots):
            first = pl.multiple_of(slot * share * (hops + 1) + position * share, share)
            rows_ref[pl.ds(first, share), :] = piece[slot]

    put(pieces[0], place)
    for hop in range(1, hops + 1):

        @pl.when(place >= hop)
        def take_below(hop=hop):
            put(pieces[hop], place - hop)

        @pl.when(place + hop <= hops)
        def take_above(hop=hop):
            put(pieces[hops + hop], place + hop)


def deal(rows_ref, place_ref, own_ref, others):
    slots, share, unused = own_ref.shape
    line = len(others) + 1
    for step, target in enumerate([own_ref] + list(others)):
        position = lax.rem(place_ref[0] + step, line)
        for slot in range(slots):
            first = pl.multiple_of(slot * share * line + position * share, share)
            target[slot] = rows_ref[pl.ds(first, share), :].astype(target.dtype)


def dealt_shapes(slots, share, width, line):
    return [jax.ShapeDtypeStruct((slots, share, width), jnp.float32)] + [
        jax.ShapeDtypeStruct((slots, share, width), jnp.bfloat16) for unused in range(line - 1)
    ]


def work(flops, bytes_accessed=0, transcendentals=0):
    return pl.CostEstimate(
        flops=int(flops * 0.2), bytes_accessed=int(bytes_accessed * 0.2), transcendentals=0
    )


def vmem_limit(mebibytes):
    return pltpu.CompilerParams(vmem_limit_bytes=mebibytes << 20)


EXTRA_ROWS = 16
LANES = 128


def cut_columns(place, group, weights, rows, line, extra=None):
    count = len(weights)
    columns = weights[0].shape[1] // line
    cut_rows = count * rows + (EXTRA_ROWS if extra is not None else 0)
    extras = [] if extra is None else [extra]

    def kernel(place_ref, group_ref, *refs):
        outs = refs[count * line + len(extras) :]
        for step in range(line):
            for i in range(count):
                outs[step][i * rows : (i + 1) * rows] = refs[step * count + i][...]
            if extras:
                outs[step][count * rows :] = refs[count * line][...]

    def target(step):
        return lambda i, place, group: (group[0], lax.rem(place[0] + step, line))

    fixed = lambda shape: pl.BlockSpec(shape, lambda i, place, group: (0, 0))
    return pl.pallas_call(
        kernel,
        out_shape=[jax.ShapeDtypeStruct((cut_rows, columns), jnp.bfloat16)] * line,
        grid_spec=pltpu.PrefetchScalarGridSpec(
            num_scalar_prefetch=2,
            grid=(1,),
            in_specs=[
                pl.BlockSpec((rows, columns), target(step))
                for step in range(line)
                for unused in range(count)
            ]
            + [fixed((EXTRA_ROWS, columns)) for unused in extras],
            out_specs=[fixed((cut_rows, columns))] * line,
        ),
        compiler_params=vmem_limit(60),
        name="cut_columns",
    )(place, group, *(list(weights) * line), *extras)


def order_shares(place, shares, count, vectors=0):
    line = len(shares)
    share_rows, columns = shares[0].shape
    rows = (share_rows - (EXTRA_ROWS if vectors else 0)) // count

    def kernel(place_ref, *refs):
        for step in range(line):
            source = lax.rem(place_ref[0] + line - step, line)
            for i in range(count):
                refs[line][source, i] = refs[step][i * rows : (i + 1) * rows]
            if vectors:
                lanes = pl.ds(pl.multiple_of(source * columns, columns), columns)
                refs[line + 1][:, lanes] = refs[step][count * rows :].astype(jnp.float32)

    shapes = [jax.ShapeDtypeStruct((line, count, rows, columns), shares[0].dtype)]
    if vectors:
        shapes.append(jax.ShapeDtypeStruct((EXTRA_ROWS, line * columns), jnp.float32))
    outs = pl.pallas_call(
        kernel,
        out_shape=shapes,
        in_specs=[whole(pltpu.SMEM)] + [whole()] * line,
        out_specs=[whole()] * len(shapes),
        compiler_params=vmem_limit(40),
        name="order_shares",
    )(place, *shares)
    return (outs[0], outs[1][:vectors]) if vectors else outs[0]


def widen_columns(place, shares, count, rows):
    line = len(shares)
    share_rows, columns = shares[0].shape

    def kernel(place_ref, *refs):
        for step in range(line):

            @pl.when(pl.program_id(0) == step)
            def widen(step=step):
                for i in range(count):
                    refs[line + i][...] = refs[step][i * rows : (i + 1) * rows].astype(jnp.float32)

    return pl.pallas_call(
        kernel,
        out_shape=[jax.ShapeDtypeStruct((rows, line * columns), jnp.float32)] * count,
        grid_spec=pltpu.PrefetchScalarGridSpec(
            num_scalar_prefetch=1,
            grid=(line,),
            in_specs=[pl.BlockSpec((share_rows, columns), lambda j, place: (0, 0))] * line,
            out_specs=[
                pl.BlockSpec(
                    (rows, columns), lambda j, place: (0, lax.rem(place[0] + line - j, line))
                )
            ]
            * count,
        ),
        compiler_params=vmem_limit(40),
        name="widen_columns",
    )(place, *shares)


def project(place, pieces, gain, w_heads, cosine, sine):
    line, count, part, width = w_heads.shape
    slots, share, model_width = pieces[0].shape
    rows = slots * share * line
    tile = width // 2
    heads = tile // HEAD_DIM
    n_pieces = len(pieces)
    half = HEAD_DIM // 2

    def kernel(place_ref, *refs):
        piece_refs = refs[:n_pieces]
        gain_ref, w_ref, cos_ref, sin_ref, rows_ref, out_ref = refs[n_pieces:]

        @pl.when((pl.program_id(0) == 0) & (pl.program_id(1) == 0))
        def assemble():
            spread(piece_refs, place_ref, rows_ref)
            rows_ref[...] = (rows_ref[...].astype(jnp.float32) * gain_ref[...]).astype(jnp.bfloat16)

        weight = w_ref[...].reshape(line * part, tile)
        turned = dot_f32(rows_ref[...], weight).T
        c, s = cos_ref[0], sin_ref[0]
        for head in range(heads):
            a = turned[head * HEAD_DIM : head * HEAD_DIM + half]
            b = turned[head * HEAD_DIM + half : (head + 1) * HEAD_DIM]
            out_ref[head, 0, :half, :] = (a * c - b * s).astype(jnp.bfloat16)
            out_ref[head, 0, half:, :] = (b * c + a * s).astype(jnp.bfloat16)

    return pl.pallas_call(
        kernel,
        grid=(count, 2),
        out_shape=[
            jax.ShapeDtypeStruct((rows, model_width), jnp.bfloat16),
            jax.ShapeDtypeStruct((width // HEAD_DIM, count, HEAD_DIM, rows), jnp.bfloat16),
        ],
        in_specs=[whole(pltpu.SMEM)]
        + [whole()] * (n_pieces + 1)
        + [
            pl.BlockSpec((line, 1, part, tile), lambda m, h: (0, m, 0, h)),
            pl.BlockSpec((1, half, rows), lambda m, h: (m, 0, 0)),
            pl.BlockSpec((1, half, rows), lambda m, h: (m, 0, 0)),
        ],
        out_specs=[
            pl.BlockSpec((rows, model_width), lambda m, h: (0, 0)),
            pl.BlockSpec((heads, 1, HEAD_DIM, rows), lambda m, h: (h, m, 0, 0)),
        ],
        compiler_params=vmem_limit(48),
        cost_estimate=work(6 * rows * model_width * width, 8 * rows * model_width),
        name="project",
    )(place, *pieces, gain, w_heads, cosine, sine)


def mix_out(place, mixed, w_out, slots, line):
    heads, unused, rows = mixed.shape
    width, model_width = w_out.shape
    share = rows // slots // line

    def kernel(place_ref, mixed_ref, w_ref, own_ref, *rest):
        *others, total = rest
        left = mixed_ref[...].reshape(width, rows).T
        total[...] = dot_f32(left, w_ref[...])
        deal(total, place_ref, own_ref, others)

    return pl.pallas_call(
        kernel,
        out_shape=dealt_shapes(slots, share, model_width, line),
        in_specs=[whole(pltpu.SMEM), whole(), whole()],
        out_specs=[whole()] * line,
        scratch_shapes=[pltpu.VMEM((rows, model_width), jnp.float32)],
        compiler_params=vmem_limit(48),
        cost_estimate=work(2 * rows * model_width * width, 8 * rows * model_width),
        name="mix_out",
    )(place, mixed, w_out)


def mlp_forward(place, pieces, upstream_pieces, w_mlp, tile):
    line, count, part, width = w_mlp.shape
    slots, share, model_width = pieces[0].shape
    rows = slots * share * line
    n_pieces = len(pieces)
    bf, f32 = jnp.bfloat16, jnp.float32

    def kernel(place_ref, *refs):
        x_pieces, u_pieces = refs[:n_pieces], refs[n_pieces : 2 * n_pieces]
        w_ref, x_ref, u_ref, hidden_ref, gate_ref, up_ref, own_ref = refs[
            2 * n_pieces : 2 * n_pieces + 7
        ]
        *others, total = refs[2 * n_pieces + 7 :]
        step = pl.program_id(0)

        @pl.when(step == 0)
        def assemble():
            spread(x_pieces, place_ref, x_ref)
            spread(u_pieces, place_ref, u_ref)

        down = w_ref[:, 0].reshape(line * part, tile)
        gate = w_ref[:, 1].reshape(line * part, tile)
        up = w_ref[:, 2].reshape(line * part, tile)
        x = x_ref[...]
        grad_hidden = dot_f32(u_ref[...], down)
        gate_act = dot_f32(x, gate)
        upward = dot_f32(x, up)
        sigmoid = jax.nn.sigmoid(gate_act)
        silu = gate_act * sigmoid
        hidden_ref[...] = (silu * upward).astype(bf)
        grad_gate = (
            grad_hidden * upward * sigmoid * (1.0 + gate_act * (1.0 - sigmoid))
        ).astype(bf)
        grad_up = (grad_hidden * silu).astype(bf)
        gate_ref[...] = grad_gate
        up_ref[...] = grad_up
        part_two = nt_dot(grad_gate, gate) + nt_dot(grad_up, up)

        @pl.when(step == 0)
        def first():
            total[...] = part_two

        @pl.when(step > 0)
        def further():
            total[...] += part_two

        @pl.when(step == pl.num_programs(0) - 1)
        def last():
            deal(total, place_ref, own_ref, others)

    fixed = lambda shape: pl.BlockSpec(shape, lambda j: (0,) * len(shape))
    columns = pl.BlockSpec((rows, tile), lambda j: (0, j))
    dealt = dealt_shapes(slots, share, model_width, line)
    return pl.pallas_call(
        kernel,
        grid=(width // tile,),
        out_shape=[jax.ShapeDtypeStruct((rows, model_width), bf)] * 2
        + [jax.ShapeDtypeStruct((rows, width), bf)] * 3
        + dealt,
        in_specs=[whole(pltpu.SMEM)]
        + [whole()] * (2 * n_pieces)
        + [pl.BlockSpec((line, count, part, tile), lambda j: (0, 0, 0, j))],
        out_specs=[fixed((rows, model_width))] * 2
        + [columns] * 3
        + [fixed((slots, share, model_width))] * line,
        scratch_shapes=[pltpu.VMEM((rows, model_width), f32)],
        compiler_params=vmem_limit(60),
        cost_estimate=work(16 * rows * model_width * width, 14 * model_width * width),
        name="mlp_forward",
    )(place, *pieces, *upstream_pieces, w_mlp)


def gate_up_weights(x_rows, grad_gate, grad_up, groups, line, tile):
    rows, model_width = x_rows.shape
    width = grad_gate.shape[1]
    block = model_width // groups // line

    def kernel(x_ref, gate_ref, up_ref, out_ref):
        for i, ref in enumerate((gate_ref, up_ref)):
            grads = transpose_product(x_ref[...], ref[...]).astype(jnp.bfloat16)
            out_ref[:, :, i * block : (i + 1) * block] = grads.reshape(groups, line, block, tile)

    columns = pl.BlockSpec((rows, tile), lambda j: (0, j))
    return pl.pallas_call(
        kernel,
        grid=(width // tile,),
        out_shape=jax.ShapeDtypeStruct((groups, line, 2 * block, width), jnp.bfloat16),
        in_specs=[pl.BlockSpec((rows, model_width), lambda j: (0, 0)), columns, columns],
        out_specs=pl.BlockSpec((groups, line, 2 * block, tile), lambda j: (0, 0, 0, j)),
        compiler_params=vmem_limit(60),
        cost_estimate=work(4 * rows * model_width * width, 8 * model_width * width),
        name="gate_up_weights",
    )(x_rows, grad_gate, grad_up)


def down_weights(u_rows, hidden, groups, line, tile):
    rows, model_width = u_rows.shape
    width = hidden.shape[1]
    block = model_width // groups // line

    def kernel(u_ref, hidden_ref, out_ref):
        grads = transpose_product(u_ref[...], hidden_ref[...]).astype(jnp.bfloat16)
        out_ref[:, :line] = grads.reshape(groups, line, block, tile)

    return pl.pallas_call(
        kernel,
        grid=(width // tile,),
        out_shape=jax.ShapeDtypeStruct((groups, line + 1, block, width), jnp.bfloat16),
        in_specs=[
            pl.BlockSpec((rows, model_width), lambda j: (0, 0)),
            pl.BlockSpec((rows, tile), lambda j: (0, j)),
        ],
        out_specs=pl.BlockSpec((groups, line + 1, block, tile), lambda j: (0, 0, 0, j)),
        compiler_params=vmem_limit(60),
        cost_estimate=work(2 * rows * model_width * width, 4 * model_width * width),
        name="down_weights",
    )(u_rows, hidden)


def mlp_out(place, hidden, w_mlp, slots, tile):
    line, count, part, width = w_mlp.shape
    rows = hidden.shape[0]
    model_width = line * part
    share = rows // slots // line

    def kernel(place_ref, hidden_ref, w_ref, own_ref, *rest):
        *others, total = rest
        step = pl.program_id(0)
        part_out = nt_dot(hidden_ref[...], w_ref[...].reshape(line * part, tile))

        @pl.when(step == 0)
        def first():
            total[...] = part_out

        @pl.when(step > 0)
        def further():
            total[...] += part_out

        @pl.when(step == pl.num_programs(0) - 1)
        def last():
            deal(total, place_ref, own_ref, others)

    fixed = lambda shape: pl.BlockSpec(shape, lambda j: (0,) * len(shape))
    return pl.pallas_call(
        kernel,
        grid=(width // tile,),
        out_shape=dealt_shapes(slots, share, model_width, line),
        in_specs=[
            whole(pltpu.SMEM),
            pl.BlockSpec((rows, tile), lambda j: (0, j)),
            pl.BlockSpec((line, 1, part, tile), lambda j: (0, 0, 0, j)),
        ],
        out_specs=[fixed((slots, share, model_width))] * line,
        scratch_shapes=[pltpu.VMEM((rows, model_width), jnp.float32)],
        compiler_params=vmem_limit(60),
        cost_estimate=work(2 * rows * model_width * width, 2 * model_width * width),
        name="mlp_out",
    )(place, hidden, w_mlp)


def branch_back(place, pieces, w_out, heads):
    slots, share, model_width = pieces[0].shape
    line = (len(pieces) + 1) // 2
    rows = slots * share * line

    def kernel(place_ref, *refs):
        *piece_refs, w_ref, rows_ref, out_ref = refs
        spread(piece_refs, place_ref, rows_ref)
        turned = nt_dot(w_ref[...], rows_ref[...])
        out_ref[...] = turned.astype(jnp.bfloat16).reshape(out_ref.shape)

    return pl.pallas_call(
        kernel,
        out_shape=[
            jax.ShapeDtypeStruct((rows, model_width), jnp.bfloat16),
            jax.ShapeDtypeStruct((heads, HEAD_DIM, rows), jnp.bfloat16),
        ],
        in_specs=[whole(pltpu.SMEM)] + [whole()] * (len(pieces) + 1),
        out_specs=[whole(), whole()],
        compiler_params=vmem_limit(40),
        cost_estimate=work(2 * rows * model_width * heads * HEAD_DIM, 8 * rows * model_width),
        name="branch_back",
    )(place, *pieces, w_out)


def out_weight(grads, mixed, branch_rows, tile):
    groups, blocks, block, width = grads.shape
    heads, unused, rows = mixed.shape

    def kernel(grads_ref, mixed_ref, rows_ref, out_ref):
        left = mixed_ref[...].reshape(heads * HEAD_DIM, rows)
        product = dot_f32(left, rows_ref[...]).astype(jnp.bfloat16)
        out_ref[...] = product.reshape(groups, 1, block, tile)

    return pl.pallas_call(
        kernel,
        grid=(width // tile,),
        out_shape=jax.ShapeDtypeStruct(grads.shape, grads.dtype),
        in_specs=[
            pl.BlockSpec(memory_space=pl.ANY),
            pl.BlockSpec(mixed.shape, lambda j: (0, 0, 0)),
            pl.BlockSpec((rows, tile), lambda j: (0, j)),
        ],
        out_specs=pl.BlockSpec((groups, 1, block, tile), lambda j: (0, blocks - 1, 0, j)),
        input_output_aliases={0: 0},
        compiler_params=vmem_limit(60),
        cost_estimate=work(4 * rows * heads * HEAD_DIM * width, 8 * rows * width),
        name="out_weight",
    )(grads, mixed, branch_rows)


def head_weights(group, all_rows, corner, head_grads, w_head, gain, gain_two, owners):
    sources, features, rows = head_grads.shape
    model_width = all_rows[0].shape[1]
    block = model_width // owners
    lanes = 2 * LANES
    half = rows // 2
    f32 = jnp.float32

    def kernel(group_ref, *refs):
        x_refs, corner_refs = refs[: sources - 2], refs[sources - 2 : sources + 2]
        g_ref, w_ref, gain_ref, two_ref, out_ref, total = refs[sources + 2 :]
        step = pl.program_id(0)

        def product(bits, ref):
            return dot_f32(g_ref[lax.bitwise_xor(group_ref[0], bits)], ref[...])

        part = sum(product(bits, ref) for bits, ref in enumerate(x_refs))

        def with_corner(half_refs):
            return part + product(sources - 2, half_refs[0]) + product(sources - 1, half_refs[1])

        @pl.when(step == 0)
        def first():
            total[...] = with_corner(corner_refs[0::2])

        @pl.when(step == 1)
        def last():
            grads = (total[...] + with_corner(corner_refs[1::2])).T
            weighed = jnp.sum(grads * w_ref[...].astype(f32), 1, keepdims=True) / gain_ref[...].T
            spare = lanes - features
            at = lax.broadcasted_iota(jnp.int32, (model_width, spare), 1)
            tail = jnp.where(at == 0, weighed, jnp.where(at == 1, two_ref[...].T, 0.0))
            joined = jnp.concatenate([grads, tail], 1).astype(jnp.bfloat16)
            out_ref[...] = joined.reshape(owners, block, lanes)

    fixed = lambda shape: pl.BlockSpec(shape, lambda s: (0,) * len(shape))
    return pl.pallas_call(
        kernel,
        grid=(2,),
        out_shape=jax.ShapeDtypeStruct((owners, block, lanes), jnp.bfloat16),
        in_specs=[whole(pltpu.SMEM)]
        + [pl.BlockSpec((half, model_width), lambda s: (s, 0))] * (sources - 2)
        + [fixed((half, model_width))] * 4
        + [
            pl.BlockSpec((sources, features, half), lambda s: (0, 0, s)),
            fixed((model_width, features)),
            fixed((1, model_width)),
            fixed((1, model_width)),
        ],
        out_specs=fixed((owners, block, lanes)),
        scratch_shapes=[pltpu.VMEM((features, model_width), f32)],
        compiler_params=vmem_limit(60),
        cost_estimate=work(6 * sources * rows * features * model_width, 0),
        name="head_weights",
    )(group, *all_rows, *corner, head_grads, w_head, gain, gain_two)


def join_heads(parts):
    groups, line, rows, lanes = parts.shape
    width = groups * HEAD_DIM

    def kernel(parts_ref, *outs):
        for i, out in enumerate(outs):
            pick = slice(i * HEAD_DIM, (i + 1) * HEAD_DIM)
            heads = [parts_ref[c, 0][:, pick].astype(jnp.float32) for c in range(groups)]
            out[...] = jnp.concatenate(heads, 1)

    return pl.pallas_call(
        kernel,
        grid=(line,),
        out_shape=[jax.ShapeDtypeStruct((rows, line * width), jnp.float32)] * 3,
        in_specs=[pl.BlockSpec((groups, 1, rows, lanes), lambda f: (0, f, 0, 0))],
        out_specs=[pl.BlockSpec((rows, width), lambda f: (0, f))] * 3,
        compiler_params=vmem_limit(24),
        name="join_heads",
    )(parts)


def project_back(place, head_grads, w_heads, slots):
    line, count, part, width = w_heads.shape
    rows, model_width = head_grads.shape[-1], line * part
    heads = width // HEAD_DIM
    share = rows // slots // line

    def kernel(place_ref, g_ref, w_ref, own_ref, *rest):
        *others, total = rest
        m = pl.program_id(0)
        grads = g_ref[...].reshape(width, rows).T
        partial = nt_dot(grads, w_ref[...].reshape(line * part, width))

        @pl.when(m == 0)
        def first():
            total[...] = partial

        @pl.when(m > 0)
        def further():
            total[...] += partial

        @pl.when(m == count - 1)
        def last():
            deal(total, place_ref, own_ref, others)

    fixed = lambda shape: pl.BlockSpec(shape, lambda m: (0,) * len(shape))
    return pl.pallas_call(
        kernel,
        grid=(count,),
        out_shape=dealt_shapes(slots, share, model_width, line),
        in_specs=[
            whole(pltpu.SMEM),
            pl.BlockSpec((heads, 1, HEAD_DIM, rows), lambda m: (0, m, 0, 0)),
            pl.BlockSpec((line, 1, part, width), lambda m: (0, m, 0, 0)),
        ],
        out_specs=[fixed((slots, share, model_width))] * line,
        scratch_shapes=[pltpu.VMEM((rows, model_width), jnp.float32)],
        compiler_params=vmem_limit(48),
        cost_estimate=work(2 * count * rows * width * model_width, 8 * rows * model_width),
        name="project_back",
    )(place, head_grads, w_heads)


def line_steps(size, step):
    return [(i, i + step) for i in range(size) if 0 <= i + step < size]


def after(values, *earlier):
    return lax.optimization_barrier((values, earlier))[0]


def send_shares(share, axis, between=()):
    size = lax.axis_size(axis)
    ups, downs = [share], [share]
    for hop in range(1, size):
        up = lax.ppermute(ups[-1], axis, line_steps(size, 1)[hop - 1 :])
        down = lax.ppermute(downs[-1], axis, line_steps(size, -1)[: size - hop])
        if hop <= len(between):
            done = between[hop - 1]((ups[-1], downs[-1]))
            up, down = after((up, down), done)
        ups.append(up)
        downs.append(down)
    return ups + downs[1:]


def flip(values, bits):
    size = lax.axis_size("ctx")
    return lax.ppermute(values, "ctx", [(i, i ^ bits) for i in range(size)])


def send_dealt(others, axis):
    size = lax.axis_size(axis)
    return [
        lax.ppermute(other, axis, [(i, (i + step) % size) for i in range(size)])
        for step, other in enumerate(others, 1)
    ]


def scatter_line(others, axis, between=()):
    size = lax.axis_size(axis)
    up = down = None
    for hop in range(1, size):
        rising, falling = others[size - hop - 1], others[hop - 1]
        if hop > 1:
            rising = (rising.astype(jnp.float32) + up.astype(jnp.float32)).astype(rising.dtype)
            falling = (falling.astype(jnp.float32) + down.astype(jnp.float32)).astype(falling.dtype)
        up = lax.ppermute(rising, axis, line_steps(size, 1)[:hop])
        down = lax.ppermute(falling, axis, line_steps(size, -1)[size - 1 - hop :])
        if hop <= len(between):
            up, down = after((up, down), between[hop - 1]((rising, falling)))
    return [up, down]


def add_shares(own, received):
    return own + sum(share.astype(jnp.float32) for share in received)


def swap_dealt(shares):
    return [shares[0]] + send_dealt(shares[1:], "fsdp")


def deal_line(parts, place):
    line = parts.shape[0]
    return [
        lax.dynamic_index_in_dim(parts, lax.rem(place[0] + step, line), 0, keepdims=False)
        for step in range(line)
    ]


def swap_heads(parts):
    return lax.all_to_all(parts, "ctx", split_axis=0, concat_axis=0, tiled=True)


def sum_groups(parts):
    return lax.psum_scatter(parts, "ctx", scatter_dimension=0, tiled=True)[0]


def head_device(
    tokens,
    block_order,
    w_query,
    w_key,
    w_value,
    w_out,
    w_gate,
    w_up,
    w_down,
    gain_attn,
    gain_mlp,
    cotangent,
):
    slots, share_rows, model_width = tokens.shape
    ctx_size, line = lax.axis_size("ctx"), lax.axis_size("fsdp")
    block_rows = share_rows * line
    group_rows = slots * block_rows
    bf, f32 = jnp.bfloat16, jnp.float32
    place = lax.axis_index("fsdp").astype(jnp.int32).reshape(1)
    group = lax.axis_index("ctx").astype(jnp.int32).reshape(1)
    own_rows = w_query.shape[0] // ctx_size
    order = block_order.astype(jnp.int32)
    long_tile = (8 if ctx_size * slots % 8 == 0 else 2) * block_rows
    slot_of = jnp.sum(
        jnp.where(order[None, :] == jnp.arange(order.shape[0])[:, None], jnp.arange(order.shape[0], dtype=jnp.int32)[None, :], 0), 1
    ).astype(jnp.int32)

    stream = tokens.astype(f32)
    root_one = lax.rsqrt(jnp.mean(stream * stream, -1, keepdims=True) + EPSILON)
    norm_one = stream * root_one
    gain_rows = jnp.pad(jnp.stack([gain_attn, gain_mlp]), ((0, EXTRA_ROWS - 2), (0, 0)))
    head_cuts = swap_dealt(
        cut_columns(place, group, [w_query, w_key, w_value], own_rows, line, gain_rows)
    )
    own_heads, gains = order_shares(place, head_cuts, 3, 2)
    attn_gain, mlp_gain = gains[0], gains[1]
    w_heads = lax.all_gather(own_heads, "ctx", axis=2, tiled=True)

    attn_pieces = send_shares(after(norm_one.astype(bf), head_cuts), "fsdp")

    mlp_cuts = cut_columns(place, group, [w_down, w_gate, w_up], own_rows, line)
    w_heads = after(w_heads, mlp_cuts)
    mlp_cuts = swap_dealt(after(mlp_cuts, attn_pieces))

    w_head = lax.dynamic_slice_in_dim(w_heads, group[0] * HEAD_DIM, HEAD_DIM, 3)
    w_head = jnp.concatenate([w_head[:, i].reshape(model_width, HEAD_DIM) for i in range(3)], 1)

    half = HEAD_DIM // 2
    frequency = 1.0 / ROPE_BASE ** (jnp.arange(half, dtype=f32) * (2.0 / HEAD_DIM))
    places = jnp.arange(group_rows * ctx_size, dtype=jnp.int32).astype(f32)
    angles = frequency[:, None] * places[None, :]
    cosine, sine = jnp.cos(angles), jnp.sin(angles)

    def own_columns(table):
        return jnp.concatenate(
            [
                lax.dynamic_slice_in_dim(
                    table, order[slots * group[0] + i] * block_rows, block_rows, 1
                )
                for i in range(slots)
            ],
            1,
        )

    own_cosine, own_sine = own_columns(cosine), own_columns(sine)
    turn_cosine = jnp.stack([own_cosine, own_cosine, jnp.ones_like(own_cosine)])
    turn_sine = jnp.stack([own_sine, own_sine, jnp.zeros_like(own_sine)])

    attn_rows, heads_out = project(
        place, attn_pieces, attn_gain[None], w_heads, turn_cosine, turn_sine
    )
    heads_out = heads_out.reshape(ctx_size, 3 * HEAD_DIM, group_rows)
    head_rows = swap_heads(after(heads_out, mlp_cuts[1]))
    mixed_send, attended, log_total = attend(
        order, head_rows, block_rows, long_tile, 2 * block_rows
    )
    mixed = swap_heads(mixed_send)
    mlp_cuts = order_shares(place, after(mlp_cuts, mixed), 3)
    w_mlp = lax.all_gather(mlp_cuts, "ctx", axis=2, tiled=True)
    upstream_pieces = send_shares(after(cotangent, mlp_cuts), "fsdp")
    own, *others = mix_out(place, after(mixed, w_head, mlp_cuts), w_out, slots, line)
    middle = stream + add_shares(own, scatter_line(others, "fsdp"))

    root_two = lax.rsqrt(jnp.mean(middle * middle, -1, keepdims=True) + EPSILON)
    norm_two = middle * root_two
    mlp_input = (norm_two * mlp_gain).astype(bf)
    mlp_pieces = send_shares(mlp_input, "fsdp")

    all_rows = {0: attn_rows}
    start_rows = after(attn_rows, mlp_pieces, upstream_pieces)
    all_rows[2], all_rows[4] = flip(start_rows, 2), flip(start_rows, 4)
    mlp_rows, upstream_rows, hidden, grad_gate, grad_up, own, *others = mlp_forward(
        place, mlp_pieces, upstream_pieces, w_mlp, 512
    )
    results = {}

    def weigh_gate_up(sent):
        rows_here = after(mlp_rows, sent)
        results["gate_up"] = gate_up_weights(rows_here, grad_gate, grad_up, ctx_size, line, 512)
        return results["gate_up"], all_rows[2], all_rows[4]

    upper = attn_rows.shape[0] // 2

    def weigh_down(sent):
        results["down"] = down_weights(
            upstream_rows, after(hidden, sent), ctx_size, line, 512
        )
        results["gate_up_sums"] = sum_groups(after(results["gate_up"], sent))
        return results["down"]

    grad_two = add_shares(own, scatter_line(others, "fsdp", (weigh_gate_up, weigh_down)))
    gate_up_sums = results["gate_up_sums"]
    down_grads = results["down"]
    gain_two_part = jnp.sum(grad_two * norm_two, (0, 1))
    grad_middle = cotangent.astype(f32) + norm_back(grad_two, norm_two, root_two, mlp_gain)

    def weigh_out(sent):
        results["out"] = mlp_out(place, after(hidden, sent), w_mlp, slots, 512)
        return results["out"]

    def cut_corner(sent):
        by_x, by_y = after((all_rows[2], all_rows[4]), sent)
        results["corner"] = (by_x[:upper], by_y[upper:])
        return results["corner"]

    branch_pieces = send_shares(grad_middle.astype(bf), "fsdp", (weigh_out, cut_corner))
    corner = [flip(results["corner"][0], 4), flip(results["corner"][1], 2)]
    own_out, *others_out = results["out"]
    branch_rows, grad_mixed = branch_back(place, branch_pieces, w_out, ctx_size)

    out_received = send_dealt(after(others_out, branch_rows), "fsdp")
    for bits in (0, 2, 4):
        all_rows[bits + 1] = flip(after(all_rows[bits], branch_rows), 1)
    grad_heads = swap_heads(grad_mixed)
    down_grads = out_weight(down_grads, mixed, branch_rows, 512)
    head_grads = attend_back(
        jnp.concatenate([order, slot_of]),
        head_rows,
        after(
            grad_heads, down_grads, all_rows[1], all_rows[3], all_rows[5]
        ),
        attended,
        log_total,
        cosine,
        sine,
        block_rows,
        long_tile,
        2 * block_rows,
    )
    head_grads = after(head_grads, out_received, corner)
    corner = corner + [flip(part, 1) for part in after(corner, head_grads)]
    gate_up_dealt = deal_line(after(gate_up_sums, head_grads), place)
    gate_up_back = swap_dealt(gate_up_dealt)
    down_sums = sum_groups(after(down_grads, gate_up_sums, head_grads))
    lin_grads = swap_heads(after(head_grads, gate_up_dealt))
    head_parts = head_weights(
        group,
        [all_rows[bits] for bits in range(ctx_size - 2)],
        corner,
        after(head_grads, gate_up_dealt),
        w_head,
        attn_gain[None],
        gain_two_part[None],
        ctx_size * line,
    )
    lin_grads = after(lin_grads, head_parts, gate_up_back[1], gate_up_back[2])
    head_parts = lax.all_to_all(
        after(head_parts, lin_grads), ("ctx", "fsdp"), split_axis=0, concat_axis=0, tiled=True
    )
    lin_grads = lin_grads.reshape(ctx_size, 3, HEAD_DIM, group_rows)
    own, *others = project_back(place, lin_grads, w_heads, slots)

    def swap_down(sent):
        parts = deal_line(after(down_sums, sent)[:line], place)
        results["down_back"] = swap_dealt(parts)
        return results["down_back"][1]

    one_received = scatter_line(
        others, "fsdp", (lambda sent: (gate_up_back[3], head_parts), lambda sent: (), swap_down)
    )
    down_back = results["down_back"]
    grad_one = add_shares(own, one_received)
    result = (middle + add_shares(own_out, out_received)).astype(bf)
    grad_tokens = grad_middle + norm_back(grad_one, norm_one, root_one, attn_gain)
    owners = [(c * line + f, f * ctx_size + c) for c in range(ctx_size) for f in range(line)]
    grad_w_out = lax.ppermute(down_sums[line], ("ctx", "fsdp"), owners).astype(f32)
    grad_w_gate, grad_w_up = widen_columns(place, gate_up_back, 2, own_rows)
    (grad_w_down,) = widen_columns(place, after(down_back, grad_tokens), 1, own_rows)
    head_parts = head_parts.reshape(ctx_size, line, own_rows, -1)
    grad_w_query, grad_w_key, grad_w_value = join_heads(head_parts)
    spare = 3 * HEAD_DIM
    gain_grads = jnp.sum(head_parts[..., spare : spare + 2].astype(f32), (0, 1)).T
    return (
        result,
        grad_tokens,
        grad_w_query,
        grad_w_key,
        grad_w_value,
        grad_w_out,
        grad_w_gate,
        grad_w_up,
        grad_w_down,
        gain_grads[0],
        gain_grads[1],
    )


def layer_step(*arrays):
    heads_here = arrays[0].shape[-1] // lax.axis_size("fsdp") // HEAD_DIM
    if heads_here == lax.axis_size("ctx") == 8:
        return head_device(*arrays)
    return per_device(*arrays)


def solution(mesh):
    in_specs = (
        P("ctx", "fsdp", None),
        P(),
        P("fsdp", None),
        P("fsdp", None),
        P("fsdp", None),
        P("fsdp", None),
        P("fsdp", None),
        P("fsdp", None),
        P("fsdp", None),
        P("fsdp"),
        P("fsdp"),
        P("ctx", "fsdp", None),
    )
    out_specs = (
        P("ctx", "fsdp", None),
        P("ctx", "fsdp", None),
        P(("ctx", "fsdp"), None),
        P(("ctx", "fsdp"), None),
        P(("ctx", "fsdp"), None),
        P(("ctx", "fsdp"), None),
        P(("ctx", "fsdp"), None),
        P(("ctx", "fsdp"), None),
        P(("ctx", "fsdp"), None),
        P(("ctx", "fsdp")),
        P(("ctx", "fsdp")),
    )
    return jax.shard_map(
        layer_step, mesh=mesh, in_specs=in_specs, out_specs=out_specs, check_vma=False
    )
```

```python
import functools

import jax
import jax.numpy as jnp
from jax import lax
from jax.experimental import pallas as pl
from jax.experimental.pallas import tpu as pltpu
from jax.sharding import PartitionSpec as P

HEAD_DIM = 64


EPSILON = 1e-05
ROPE_BASE = 130000.0
MASKED_SCORE = -1e30


def rotate(values, places, direction):
    half_dim = values.shape[-1] // 2
    frequency = 1.0 / ROPE_BASE ** (
        jnp.arange(half_dim, dtype=jnp.float32) * (2.0 / values.shape[-1])
    )
    angles = places[..., None] * frequency
    cosine = jnp.cos(angles)[..., None, :]
    sine_part = direction * jnp.sin(angles)[..., None, :]
    leading = values[..., :half_dim]
    trailing = values[..., half_dim:]
    return jnp.concatenate(
        [leading * cosine - trailing * sine_part, trailing * cosine + leading * sine_part], -1
    )


def matmul(left, right):
    return jnp.dot(left, right, preferred_element_type=jnp.float32)


def contract(left, right):
    return lax.dot_general(
        left, right, (((1,), (1,)), ((), ())), preferred_element_type=jnp.float32
    )


def transpose_product(left, right):
    return lax.dot_general(
        left, right, (((0,), (0,)), ((), ())), preferred_element_type=jnp.float32
    )


def split_heads(values):
    return values.reshape(values.shape[:-1] + (-1, HEAD_DIM))


def keep_state(current):
    return current


def tile_scores(queries, key_rows, query_places, key_places, score_scale):
    scores = (
        jnp.einsum("qhd,khd->hqk", queries, key_rows, preferred_element_type=jnp.float32)
        * score_scale
    )
    allowed = (key_places[None, :] <= query_places[:, None])[None]
    return (jnp.where(allowed, scores, MASKED_SCORE), allowed)


def grow_state(current, queries, key_rows, value_rows, query_places, key_places, score_scale):
    run_peak, run_total, summed = current
    scores, allowed = tile_scores(queries, key_rows, query_places, key_places, score_scale)
    new_peak = jnp.maximum(run_peak, jnp.max(scores, -1))
    weights = jnp.where(allowed, jnp.exp(scores - new_peak[..., None]), 0.0)
    factor = jnp.exp(run_peak - new_peak)
    run_total = run_total * factor + jnp.sum(weights, -1)
    summed = summed * jnp.transpose(factor)[:, :, None] + jnp.einsum(
        "hqk,khd->qhd", weights.astype(jnp.bfloat16), value_rows, preferred_element_type=jnp.float32
    )
    return (new_peak, run_total, summed)


def backward_tile(
    queries,
    key_rows,
    value_rows,
    grad_out,
    log_total,
    row_delta,
    query_places,
    key_places,
    score_scale,
):
    scores, allowed = tile_scores(queries, key_rows, query_places, key_places, score_scale)
    probabilities = jnp.where(allowed, jnp.exp(scores - log_total[..., None]), 0.0)
    grad_probs = jnp.einsum(
        "qhd,khd->hqk", grad_out, value_rows, preferred_element_type=jnp.float32
    )
    grad_scores = (probabilities * (grad_probs - row_delta[..., None])).astype(jnp.bfloat16)
    return (probabilities, grad_scores)


def norm_back(grad_normed_in, normed_values, inverse_root, gain_vector):
    scaled = grad_normed_in * gain_vector
    return inverse_root * (
        scaled - normed_values * jnp.mean(scaled * normed_values, -1, keepdims=True)
    )


def per_device(
    tokens,
    block_order,
    w_query,
    w_key,
    w_value,
    w_out,
    w_gate,
    w_up,
    w_down,
    gain_attn,
    gain_mlp,
    cotangent,
):
    slot_count, share_rows, model_width = tokens.shape
    fsdp_size = lax.axis_size("fsdp")
    block_rows = share_rows * fsdp_size
    head_width = model_width // fsdp_size
    heads_here = head_width // HEAD_DIM
    row_count = slot_count * share_rows
    score_scale = HEAD_DIM ** (-0.5)
    own_slots = 2 * lax.axis_index("ctx") + jnp.arange(2, dtype=jnp.int32)
    own_blocks = block_order[own_slots]
    token_places = (
        (
            own_blocks[:, None] * block_rows
            + lax.axis_index("fsdp") * share_rows
            + jnp.arange(share_rows, dtype=jnp.int32)[None, :]
        )
        .astype(jnp.float32)
        .reshape(row_count)
    )
    head_places = (
        own_blocks[:, None] * block_rows + jnp.arange(block_rows, dtype=jnp.int32)[None, :]
    ).astype(jnp.float32)
    params = (w_query, w_key, w_value, w_out, w_gate, w_up, w_down, gain_attn, gain_mlp)
    weights_all = (
        lax.all_gather(params[0], "fsdp", axis=0, tiled=True),
        lax.all_gather(params[1], "fsdp", axis=0, tiled=True),
        lax.all_gather(params[2], "fsdp", axis=0, tiled=True),
        lax.all_gather(params[3], "fsdp", axis=0, tiled=True),
        lax.all_gather(params[4], "fsdp", axis=0, tiled=True),
        lax.all_gather(params[5], "fsdp", axis=0, tiled=True),
        lax.all_gather(params[6], "fsdp", axis=0, tiled=True),
        lax.all_gather(params[7], "fsdp", axis=0, tiled=True),
        lax.all_gather(params[8], "fsdp", axis=0, tiled=True),
    )
    stream = tokens.reshape(row_count, model_width).astype(jnp.float32)
    root_one = lax.rsqrt(jnp.mean(stream * stream, -1, keepdims=True) + EPSILON)
    norm_one = stream * root_one
    attn_input = (norm_one * weights_all[7].astype(jnp.float32)).astype(jnp.bfloat16)

    def project_turn(weight):
        linear = matmul(attn_input, weight).reshape(row_count, -1, HEAD_DIM)
        return (
            rotate(linear, token_places, 1.0)
            .astype(jnp.bfloat16)
            .reshape(slot_count, share_rows, model_width)
        )

    query_tok = project_turn(weights_all[0])
    key_tok = project_turn(weights_all[1])
    value_tok = (
        matmul(attn_input, weights_all[2])
        .astype(jnp.bfloat16)
        .reshape(slot_count, share_rows, model_width)
    )
    query_heads, key_heads, value_heads = (
        lax.all_to_all(query_tok, "fsdp", split_axis=2, concat_axis=1, tiled=True),
        lax.all_to_all(key_tok, "fsdp", split_axis=2, concat_axis=1, tiled=True),
        lax.all_to_all(value_tok, "fsdp", split_axis=2, concat_axis=1, tiled=True),
    )
    query_split = split_heads(query_heads)
    start_state = tuple(
        (
            (
                jnp.full((heads_here, block_rows), MASKED_SCORE, jnp.float32),
                jnp.zeros((heads_here, block_rows), jnp.float32),
                jnp.zeros((block_rows, heads_here, HEAD_DIM), jnp.float32),
            )
            for which_slot in range(2)
        )
    )
    carried = start_state
    key_part = lax.all_gather(key_heads, "ctx", axis=0, tiled=True)
    value_part = lax.all_gather(value_heads, "ctx", axis=0, tiled=True)

    def visit_slot(inner_state, element):
        key_one, value_one, offset = element
        key_block = block_order[offset]
        key_places = (key_block * block_rows + jnp.arange(block_rows, dtype=jnp.int32)).astype(
            jnp.float32
        )
        key_split = split_heads(key_one)
        value_split = split_heads(value_one)
        updated = []
        for which_slot in range(2):

            def grow_one(current, which_slot=which_slot):
                return grow_state(
                    current,
                    query_split[which_slot],
                    key_split,
                    value_split,
                    head_places[which_slot],
                    key_places,
                    score_scale,
                )

            updated.append(
                lax.cond(
                    key_block <= own_blocks[which_slot],
                    grow_one,
                    keep_state,
                    inner_state[which_slot],
                )
            )
        return (tuple(updated), None)

    offsets = jnp.arange(key_part.shape[0], dtype=jnp.int32)
    carried, unused = lax.scan(visit_slot, carried, (key_part, value_part, offsets))
    attended_parts = []
    log_parts = []
    for which_slot in range(2):
        run_peak, run_total, summed = carried[which_slot]
        log_parts.append(run_peak + jnp.log(run_total))
        attended_parts.append(summed / jnp.transpose(run_total)[:, :, None])
    attended = jnp.stack(attended_parts)
    log_total = jnp.stack(log_parts)
    mixed_send = attended.reshape(slot_count, block_rows, head_width).astype(jnp.bfloat16)
    mixed_tok = lax.all_to_all(mixed_send, "fsdp", split_axis=1, concat_axis=2, tiled=True)
    mixed_flat = mixed_tok.reshape(row_count, model_width)
    middle = stream + matmul(mixed_flat, weights_all[3])
    root_two = lax.rsqrt(jnp.mean(middle * middle, -1, keepdims=True) + EPSILON)
    norm_two = middle * root_two
    mlp_input = (norm_two * weights_all[8].astype(jnp.float32)).astype(jnp.bfloat16)
    gate_act = matmul(mlp_input, weights_all[4])
    upward = matmul(mlp_input, weights_all[5])
    gate_sigmoid = jax.nn.sigmoid(gate_act)
    gate_silu = gate_act * gate_sigmoid
    hidden = (gate_silu * upward).astype(jnp.bfloat16)
    output = middle + contract(hidden, weights_all[6])
    result = output.astype(jnp.bfloat16).reshape(slot_count, share_rows, model_width)
    upstream = cotangent.reshape(row_count, model_width)
    grad_hidden = matmul(upstream, weights_all[6])
    grad_gate = (
        grad_hidden * upward * gate_sigmoid * (1.0 + gate_act * (1.0 - gate_sigmoid))
    ).astype(jnp.bfloat16)
    grad_up = (grad_hidden * gate_silu).astype(jnp.bfloat16)
    grad_two = contract(grad_gate, weights_all[4]) + contract(grad_up, weights_all[5])
    gain_two_part = jnp.sum(grad_two * norm_two, 0)
    grad_middle = upstream.astype(jnp.float32) + norm_back(
        grad_two, norm_two, root_two, weights_all[8].astype(jnp.float32)
    )
    grad_branch = grad_middle.astype(jnp.bfloat16)
    grad_mixed = (
        contract(grad_branch, weights_all[3])
        .astype(jnp.bfloat16)
        .reshape(slot_count, share_rows, model_width)
    )
    grad_heads = lax.all_to_all(grad_mixed, "fsdp", split_axis=2, concat_axis=1, tiled=True)
    grad_split = split_heads(grad_heads)
    row_delta = jnp.transpose(jnp.sum(grad_split.astype(jnp.float32) * attended, -1), (0, 2, 1))
    gathered = (
        lax.all_gather(key_heads, "ctx", axis=0, tiled=True),
        lax.all_gather(value_heads, "ctx", axis=0, tiled=True),
    )
    key_all, value_all = gathered
    total_slots = key_all.shape[0]

    def query_visit(current, element):
        key_pair, value_pair, pair_index = element
        updated = list(current)
        for member in range(2):
            key_block = block_order[2 * pair_index + member]
            key_places = (key_block * block_rows + jnp.arange(block_rows, dtype=jnp.int32)).astype(
                jnp.float32
            )
            key_split = split_heads(key_pair[member])
            value_split = split_heads(value_pair[member])
            for which_slot in range(2):

                def take_query(
                    accum,
                    which_slot=which_slot,
                    key_split=key_split,
                    value_split=value_split,
                    key_places=key_places,
                ):
                    probabilities, grad_scores = backward_tile(
                        query_split[which_slot],
                        key_split,
                        value_split,
                        grad_split[which_slot],
                        log_total[which_slot],
                        row_delta[which_slot],
                        head_places[which_slot],
                        key_places,
                        score_scale,
                    )
                    return accum + score_scale * jnp.einsum(
                        "hqk,khd->qhd", grad_scores, key_split, preferred_element_type=jnp.float32
                    )

                updated[which_slot] = lax.cond(
                    key_block <= own_blocks[which_slot], take_query, keep_state, updated[which_slot]
                )
        return (tuple(updated), None)

    query_zero = jnp.zeros((block_rows, heads_here, HEAD_DIM), jnp.float32)
    pair_keys = key_all.reshape(total_slots // 2, 2, block_rows, head_width)
    pair_values = value_all.reshape(total_slots // 2, 2, block_rows, head_width)
    grad_query_parts, unused = lax.scan(
        query_visit,
        (query_zero, query_zero),
        (pair_keys, pair_values, jnp.arange(total_slots // 2, dtype=jnp.int32)),
    )
    key_part = key_all
    value_part = value_all

    def key_visit(unused_carry, element):
        key_one, value_one, offset = element
        key_block = block_order[offset]
        key_places = (key_block * block_rows + jnp.arange(block_rows, dtype=jnp.int32)).astype(
            jnp.float32
        )
        key_split = split_heads(key_one)
        value_split = split_heads(value_one)
        sums = (
            jnp.zeros((block_rows, heads_here, HEAD_DIM), jnp.float32),
            jnp.zeros((block_rows, heads_here, HEAD_DIM), jnp.float32),
        )
        for which_slot in range(2):

            def take_keys(current, which_slot=which_slot):
                probabilities, grad_scores = backward_tile(
                    query_split[which_slot],
                    key_split,
                    value_split,
                    grad_split[which_slot],
                    log_total[which_slot],
                    row_delta[which_slot],
                    head_places[which_slot],
                    key_places,
                    score_scale,
                )
                grad_key = current[0] + score_scale * jnp.einsum(
                    "hqk,qhd->khd",
                    grad_scores,
                    query_split[which_slot],
                    preferred_element_type=jnp.float32,
                )
                grad_value = current[1] + jnp.einsum(
                    "hqk,qhd->khd",
                    probabilities.astype(jnp.bfloat16),
                    grad_split[which_slot],
                    preferred_element_type=jnp.float32,
                )
                return (grad_key, grad_value)

            sums = lax.cond(key_block <= own_blocks[which_slot], take_keys, keep_state, sums)
        joined = jnp.concatenate(
            [sums[0].reshape(block_rows, head_width), sums[1].reshape(block_rows, head_width)], -1
        )
        return (unused_carry, joined)

    unused_final, terms = lax.scan(
        key_visit,
        jnp.zeros((), jnp.float32),
        (key_part, value_part, jnp.arange(slot_count * lax.axis_size("ctx"), dtype=jnp.int32)),
    )
    summed_kv = lax.psum_scatter(
        terms.astype(jnp.bfloat16), "ctx", scatter_dimension=0, tiled=True
    ).astype(jnp.float32)
    grad_keys = (
        rotate(split_heads(summed_kv[..., :head_width]), head_places, -1.0)
        .astype(jnp.bfloat16)
        .reshape(slot_count, block_rows, head_width)
    )
    grad_values = summed_kv[..., head_width:].astype(jnp.bfloat16)
    grad_queries = (
        rotate(jnp.stack(grad_query_parts), head_places, -1.0)
        .astype(jnp.bfloat16)
        .reshape(slot_count, block_rows, head_width)
    )
    grad_q_tok, grad_k_tok, grad_v_tok = (
        lax.all_to_all(grad_queries, "fsdp", split_axis=1, concat_axis=2, tiled=True),
        lax.all_to_all(grad_keys, "fsdp", split_axis=1, concat_axis=2, tiled=True),
        lax.all_to_all(grad_values, "fsdp", split_axis=1, concat_axis=2, tiled=True),
    )
    grad_q_lin = grad_q_tok.reshape(row_count, model_width)
    grad_k_lin = grad_k_tok.reshape(row_count, model_width)
    grad_v_lin = grad_v_tok.reshape(row_count, model_width)
    grad_one = (
        contract(grad_q_lin, weights_all[0])
        + contract(grad_k_lin, weights_all[1])
        + contract(grad_v_lin, weights_all[2])
    )
    gain_one_part = jnp.sum(grad_one * norm_one, 0)
    grad_input = grad_middle + norm_back(
        grad_one, norm_one, root_one, weights_all[7].astype(jnp.float32)
    )
    hidden_width = hidden.shape[1]
    gain_parts = jnp.stack([gain_one_part, gain_two_part], 1)
    wide_cols = (
        lax.all_to_all(grad_q_lin, "fsdp", split_axis=1, concat_axis=0, tiled=True),
        lax.all_to_all(grad_k_lin, "fsdp", split_axis=1, concat_axis=0, tiled=True),
        lax.all_to_all(grad_v_lin, "fsdp", split_axis=1, concat_axis=0, tiled=True),
        lax.all_to_all(grad_branch, "fsdp", split_axis=1, concat_axis=0, tiled=True),
        lax.all_to_all(grad_gate, "fsdp", split_axis=1, concat_axis=0, tiled=True),
        lax.all_to_all(grad_up, "fsdp", split_axis=1, concat_axis=0, tiled=True),
        lax.all_to_all(hidden, "fsdp", split_axis=1, concat_axis=0, tiled=True),
    )
    row_sets = (
        lax.all_gather(attn_input, "fsdp", axis=0, tiled=True),
        lax.all_gather(mixed_flat, "fsdp", axis=0, tiled=True),
        lax.all_gather(mlp_input, "fsdp", axis=0, tiled=True),
        lax.all_gather(upstream, "fsdp", axis=0, tiled=True),
    )
    group_rows = model_width // lax.axis_size("ctx")
    row_cuts = [values for values in row_sets]
    pieces = [
        transpose_product(row_cuts[0], wide_cols[0]),
        transpose_product(row_cuts[0], wide_cols[1]),
        transpose_product(row_cuts[0], wide_cols[2]),
        transpose_product(row_cuts[1], wide_cols[3]),
        transpose_product(row_cuts[2], wide_cols[4]),
        transpose_product(row_cuts[2], wide_cols[5]),
        transpose_product(row_cuts[3], wide_cols[6]),
        gain_parts,
        jnp.zeros((group_rows * lax.axis_size("ctx"), 126), jnp.float32),
    ]
    partial_sums = lax.psum_scatter(
        jnp.concatenate(pieces, 1).astype(jnp.bfloat16), "ctx", scatter_dimension=0, tiled=True
    ).astype(jnp.float32)
    owned = lax.all_to_all(
        partial_sums.astype(jnp.bfloat16), "fsdp", split_axis=0, concat_axis=1, tiled=True
    ).astype(partial_sums.dtype)
    span_width = partial_sums.shape[1]
    owned_rows = owned.shape[0]
    arranged = owned.reshape(owned_rows, fsdp_size, span_width)
    model_part = model_width // fsdp_size
    hidden_part = hidden_width // fsdp_size
    bounds = [
        0,
        model_part,
        2 * model_part,
        3 * model_part,
        4 * model_part,
        4 * model_part + hidden_part,
        4 * model_part + 2 * hidden_part,
        4 * model_part + 3 * hidden_part,
    ]

    def joined_cols(first_col, last_col):
        return arranged[:, :, first_col:last_col].reshape(owned_rows, -1)

    grad_w_query = joined_cols(bounds[0], bounds[1])
    grad_w_key = joined_cols(bounds[1], bounds[2])
    grad_w_value = joined_cols(bounds[2], bounds[3])
    grad_w_out = joined_cols(bounds[3], bounds[4])
    grad_w_gate = joined_cols(bounds[4], bounds[5])
    grad_w_up = joined_cols(bounds[5], bounds[6])
    grad_w_down = joined_cols(bounds[6], bounds[7])
    gain_totals = jnp.sum(arranged[:, :, bounds[7] : bounds[7] + 2], 1)
    grad_gain_attn = gain_totals[:, 0]
    grad_gain_mlp = gain_totals[:, 1]
    grad_tokens = grad_input.reshape(slot_count, share_rows, model_width)
    return (
        result,
        grad_tokens,
        grad_w_query,
        grad_w_key,
        grad_w_value,
        grad_w_out,
        grad_w_gate,
        grad_w_up,
        grad_w_down,
        grad_gain_attn,
        grad_gain_mlp,
    )


def dot_f32(a, b):
    return jnp.dot(a, b, preferred_element_type=jnp.float32)

def load_sequence(order_ref, rows_ref, block, stores):
    per_src = rows_ref.shape[2] // block
    def one(slot, carry):
        src = slot // per_src
        lane = pl.multiple_of((slot % per_src) * block, block)
        place = pl.multiple_of(order_ref[slot] * block, block)
        for at, store in stores:
            store(rows_ref[src, at:at + HEAD_DIM, pl.ds(lane, block)], place)
        return carry
    lax.fori_loop(0, rows_ref.shape[0] * per_src, one, 0)

def fwd_kernel(
    order_ref, qkv_ref, mixed_ref, out_ref, lse_ref, qt, kr, vt, peak, total, acc, *, block, tile, step
):
    seq = qt.shape[1]

    def put_q(x, place):
        qt[:, pl.ds(place, block)] = x * jnp.bfloat16(HEAD_DIM ** -0.5)

    def put_k(x, place):
        kr[pl.ds(place, block), :] = x.T

    def put_v(x, place):
        vt[:, pl.ds(place, block)] = x

    load_sequence(
        order_ref, qkv_ref, block, ((0, put_q), (HEAD_DIM, put_k), (2 * HEAD_DIM, put_v))
    )

    def one_tile(qi, unused):
        q0 = pl.multiple_of(qi * tile, tile)
        peak[...] = jnp.full_like(peak, MASKED_SCORE)
        total[...] = jnp.zeros_like(total)
        acc[...] = jnp.zeros_like(acc)

        def visit(k0, first, masked):
            queries = qt[:, pl.ds(pl.multiple_of(q0 + first, step), tile - first)]
            s = dot_f32(kr[pl.ds(k0, step), :], queries)
            if masked:
                keep = lax.broadcasted_iota(jnp.int32, s.shape, 0) <= lax.broadcasted_iota(
                    jnp.int32, s.shape, 1
                )
                s = jnp.where(keep, s, MASKED_SCORE)
            old = peak[:, first:]
            new = jnp.maximum(old, jnp.max(s, 0, keepdims=True))
            p = jnp.exp(s - new)
            alpha = jnp.exp(old - new)
            peak[:, first:] = new
            total[:, first:] = total[:, first:] * alpha + jnp.sum(p, 0, keepdims=True)
            acc[:, first:] = acc[:, first:] * alpha + dot_f32(
                vt[:, pl.ds(k0, step)], p.astype(jnp.bfloat16)
            )

        def below(j, carry):
            visit(pl.multiple_of(j * step, step), 0, False)
            return carry

        lax.fori_loop(0, qi * (tile // step), below, 0)
        for part in range(tile // step):
            visit(pl.multiple_of(q0 + part * step, step), part * step, True)
        out_ref[:, pl.ds(q0, tile)] = acc[...] / total[...]
        lse_ref[:, pl.ds(q0, tile)] = peak[...] + jnp.log(total[...])
        return unused

    lax.fori_loop(0, seq // tile, one_tile, 0)
    per_src = mixed_ref.shape[2] // block

    def send(slot, carry):
        place = pl.multiple_of(order_ref[slot] * block, block)
        lane = pl.multiple_of((slot % per_src) * block, block)
        mixed_ref[slot // per_src, :, pl.ds(lane, block)] = out_ref[:, pl.ds(place, block)].astype(
            jnp.bfloat16
        )
        return carry

    lax.fori_loop(0, mixed_ref.shape[0] * per_src, send, 0)


def attend(order, qkv, block, tile, step):
    groups, unused, width = qkv.shape
    seq = groups * width
    vm = pl.BlockSpec(memory_space=pltpu.VMEM)
    bf, f32 = jnp.bfloat16, jnp.float32
    return pl.pallas_call(
        functools.partial(fwd_kernel, block=block, tile=tile, step=step),
        out_shape=(
            jax.ShapeDtypeStruct((groups, HEAD_DIM, width), bf),
            jax.ShapeDtypeStruct((HEAD_DIM, seq), f32),
            jax.ShapeDtypeStruct((1, seq), f32),
        ),
        in_specs=[pl.BlockSpec(memory_space=pltpu.SMEM), vm],
        out_specs=(vm, vm, vm),
        scratch_shapes=[
            pltpu.VMEM((HEAD_DIM, seq), bf),
            pltpu.VMEM((seq, HEAD_DIM), bf),
            pltpu.VMEM((HEAD_DIM, seq), bf),
            pltpu.VMEM((1, tile), f32),
            pltpu.VMEM((1, tile), f32),
            pltpu.VMEM((HEAD_DIM, tile), f32),
        ],
        compiler_params=pltpu.CompilerParams(vmem_limit_bytes=48 << 20),
        cost_estimate=pl.CostEstimate(
            flops=int(4.0 * seq * seq * HEAD_DIM),
            bytes_accessed=8 * seq * HEAD_DIM,
            transcendentals=0,
        ),
        name="attend",
    )(order, qkv)


def bwd_kernel(order_ref, qkv_ref, go_ref, out_ref, lse_ref, cos_ref, sin_ref, grad_ref,
               qt, qr, kt, kr, vr, got, gor, delta, dqt, dkr, dvr, *, block, tile, step):
    seq = qt.shape[1]
    scale = jnp.bfloat16(HEAD_DIM ** -0.5)
    def put_q(x, place):
        x = x * scale
        qt[:, pl.ds(place, block)] = x
        qr[pl.ds(place, block), :] = x.T
    def put_k(x, place):
        kt[:, pl.ds(place, block)] = x * scale
        kr[pl.ds(place, block), :] = x.T
    def put_v(x, place):
        vr[pl.ds(place, block), :] = x.T
    def put_go(x, place):
        got[:, pl.ds(place, block)] = x
        gor[pl.ds(place, block), :] = x.T
        delta[:, pl.ds(place, block)] = jnp.sum(x.astype(jnp.float32) * out_ref[:, pl.ds(place, block)], 0, keepdims=True)
    load_sequence(order_ref, qkv_ref, block, ((0, put_q), (HEAD_DIM, put_k), (2 * HEAD_DIM, put_v)))
    load_sequence(order_ref, go_ref, block, ((0, put_go),))
    dqt[...] = jnp.zeros_like(dqt)
    tiles = seq // tile

    def key_tile(kj, unused):
        k0 = pl.multiple_of(kj * tile, tile)
        keys = kr[pl.ds(k0, tile), :]
        keys_t = kt[:, pl.ds(k0, tile)]
        vals = vr[pl.ds(k0, tile), :]
        dkr[...] = jnp.zeros_like(dkr)
        dvr[...] = jnp.zeros_like(dvr)

        def visit(q0, width, rows, masked):
            s = dot_f32(keys[:rows], qt[:, pl.ds(q0, width)])
            p = jnp.exp(s - lse_ref[:, pl.ds(q0, width)])
            if masked:
                keep = lax.broadcasted_iota(jnp.int32, s.shape, 0) <= lax.broadcasted_iota(
                    jnp.int32, s.shape, 1
                ) + (rows - width)
                p = jnp.where(keep, p, 0.0)
            dp = dot_f32(vals[:rows], got[:, pl.ds(q0, width)])
            ds = (p * (dp - delta[:, pl.ds(q0, width)])).astype(jnp.bfloat16)
            dvr[:rows] += dot_f32(p.astype(jnp.bfloat16), gor[pl.ds(q0, width), :])
            dkr[:rows] += dot_f32(ds, qr[pl.ds(q0, width), :])
            dqt[:, pl.ds(q0, width)] += dot_f32(keys_t[:, :rows], ds)

        for part in range(tile // step):
            first = pl.multiple_of(k0 + part * step, step)
            visit(first, step, (part + 1) * step, True)

        def later(j, carry):
            visit(pl.multiple_of(j * step, step), step, tile, False)
            return carry

        lax.fori_loop((kj + 1) * (tile // step), seq // step, later, 0)
        put_out(dkr[...].T, HEAD_DIM, k0, True)
        put_out(dvr[...].T, 2 * HEAD_DIM, k0, False)
        return unused

    half = HEAD_DIM // 2
    def put_out(x, at, place, turn):
        for part in range(tile // block):
            piece = x[:, part * block:(part + 1) * block]
            here = place + part * block
            if turn:
                lanes = pl.ds(pl.multiple_of(here, block), block)
                c, s = cos_ref[:, lanes], sin_ref[:, lanes]
                a, b = piece[:half], piece[half:]
                piece = jnp.concatenate([a * c + b * s, b * c - a * s], 0)
            slot = order_ref[seq // block + here // block]
            per_src = grad_ref.shape[2] // block
            lane = pl.multiple_of((slot % per_src) * block, block)
            grad_ref[slot // per_src, at:at + HEAD_DIM, pl.ds(lane, block)] = piece.astype(jnp.bfloat16)

    lax.fori_loop(0, tiles, key_tile, 0)
    def write_q(qi, c):
        q0 = pl.multiple_of(qi * tile, tile)
        put_out(dqt[:, pl.ds(q0, tile)], 0, q0, True)
        return c
    lax.fori_loop(0, tiles, write_q, 0)

def attend_back(order, qkv, go, out, lse, cos, sin, block, tile, step):
    groups, unused, width = qkv.shape
    seq = groups * width
    vm = pl.BlockSpec(memory_space=pltpu.VMEM)
    bf, f32 = jnp.bfloat16, jnp.float32
    wide = lambda t: pltpu.VMEM((HEAD_DIM, seq), t)
    tall = lambda t: pltpu.VMEM((seq, HEAD_DIM), t)
    return pl.pallas_call(
        functools.partial(bwd_kernel, block=block, tile=tile, step=step),
        out_shape=jax.ShapeDtypeStruct(qkv.shape, bf),
        in_specs=[pl.BlockSpec(memory_space=pltpu.SMEM)] + [vm] * 6,
        out_specs=vm,
        scratch_shapes=[wide(bf), tall(bf), wide(bf), tall(bf), tall(bf), wide(bf), tall(bf),
                        pltpu.VMEM((1, seq), f32), wide(f32),
                        pltpu.VMEM((tile, HEAD_DIM), f32), pltpu.VMEM((tile, HEAD_DIM), f32)],
        compiler_params=pltpu.CompilerParams(vmem_limit_bytes=48 << 20),
        cost_estimate=pl.CostEstimate(
            flops=int(6.4 * seq * seq * HEAD_DIM),
            bytes_accessed=16 * seq * HEAD_DIM,
            transcendentals=0,
        ),
        name="attend_back",
    )(order, qkv, go, out, lse, cos, sin)


def nt_dot(a, b):
    return lax.dot_general(a, b, (((1,), (1,)), ((), ())), preferred_element_type=jnp.float32)


def whole(space=pltpu.VMEM):
    return pl.BlockSpec(memory_space=space)


def spread(pieces, place_ref, rows_ref):
    hops = (len(pieces) - 1) // 2
    slots, share, unused = pieces[0].shape
    place = place_ref[0]

    def put(piece, position):
        for slot in range(slots):
            first = pl.multiple_of(slot * share * (hops + 1) + position * share, share)
            rows_ref[pl.ds(first, share), :] = piece[slot]

    put(pieces[0], place)
    for hop in range(1, hops + 1):

        @pl.when(place >= hop)
        def take_below(hop=hop):
            put(pieces[hop], place - hop)

        @pl.when(place + hop <= hops)
        def take_above(hop=hop):
            put(pieces[hops + hop], place + hop)


def deal(rows_ref, place_ref, own_ref, others):
    slots, share, unused = own_ref.shape
    line = len(others) + 1
    for step, target in enumerate([own_ref] + list(others)):
        position = lax.rem(place_ref[0] + step, line)
        for slot in range(slots):
            first = pl.multiple_of(slot * share * line + position * share, share)
            target[slot] = rows_ref[pl.ds(first, share), :].astype(target.dtype)


def dealt_shapes(slots, share, width, line):
    return [jax.ShapeDtypeStruct((slots, share, width), jnp.float32)] + [
        jax.ShapeDtypeStruct((slots, share, width), jnp.bfloat16) for unused in range(line - 1)
    ]


def work(flops, bytes_accessed=0, transcendentals=0):
    return pl.CostEstimate(
        flops=int(flops * 0.2), bytes_accessed=int(bytes_accessed * 0.2), transcendentals=0
    )


def vmem_limit(mebibytes):
    return pltpu.CompilerParams(vmem_limit_bytes=mebibytes << 20)


EXTRA_ROWS = 16
LANES = 128


def cut_columns(place, group, weights, rows, line, extra=None):
    count = len(weights)
    columns = weights[0].shape[1] // line
    cut_rows = count * rows + (EXTRA_ROWS if extra is not None else 0)
    extras = [] if extra is None else [extra]

    def kernel(place_ref, group_ref, *refs):
        outs = refs[count * line + len(extras) :]
        for step in range(line):
            for i in range(count):
                outs[step][i * rows : (i + 1) * rows] = refs[step * count + i][...]
            if extras:
                outs[step][count * rows :] = refs[count * line][...]

    def target(step):
        return lambda i, place, group: (group[0], lax.rem(place[0] + step, line))

    fixed = lambda shape: pl.BlockSpec(shape, lambda i, place, group: (0, 0))
    return pl.pallas_call(
        kernel,
        out_shape=[jax.ShapeDtypeStruct((cut_rows, columns), jnp.bfloat16)] * line,
        grid_spec=pltpu.PrefetchScalarGridSpec(
            num_scalar_prefetch=2,
            grid=(1,),
            in_specs=[
                pl.BlockSpec((rows, columns), target(step))
                for step in range(line)
                for unused in range(count)
            ]
            + [fixed((EXTRA_ROWS, columns)) for unused in extras],
            out_specs=[fixed((cut_rows, columns))] * line,
        ),
        compiler_params=vmem_limit(60),
        name="cut_columns",
    )(place, group, *(list(weights) * line), *extras)


def order_shares(place, shares, count, vectors=0):
    line = len(shares)
    share_rows, columns = shares[0].shape
    rows = (share_rows - (EXTRA_ROWS if vectors else 0)) // count

    def kernel(place_ref, *refs):
        for step in range(line):
            source = lax.rem(place_ref[0] + line - step, line)
            for i in range(count):
                refs[line][source, i] = refs[step][i * rows : (i + 1) * rows]
            if vectors:
                lanes = pl.ds(pl.multiple_of(source * columns, columns), columns)
                refs[line + 1][:, lanes] = refs[step][count * rows :].astype(jnp.float32)

    shapes = [jax.ShapeDtypeStruct((line, count, rows, columns), shares[0].dtype)]
    if vectors:
        shapes.append(jax.ShapeDtypeStruct((EXTRA_ROWS, line * columns), jnp.float32))
    outs = pl.pallas_call(
        kernel,
        out_shape=shapes,
        in_specs=[whole(pltpu.SMEM)] + [whole()] * line,
        out_specs=[whole()] * len(shapes),
        compiler_params=vmem_limit(40),
        name="order_shares",
    )(place, *shares)
    return (outs[0], outs[1][:vectors]) if vectors else outs[0]


def widen_columns(place, shares, count, rows):
    line = len(shares)
    share_rows, columns = shares[0].shape

    def kernel(place_ref, *refs):
        for step in range(line):

            @pl.when(pl.program_id(0) == step)
            def widen(step=step):
                for i in range(count):
                    refs[line + i][...] = refs[step][i * rows : (i + 1) * rows].astype(jnp.float32)

    return pl.pallas_call(
        kernel,
        out_shape=[jax.ShapeDtypeStruct((rows, line * columns), jnp.float32)] * count,
        grid_spec=pltpu.PrefetchScalarGridSpec(
            num_scalar_prefetch=1,
            grid=(line,),
            in_specs=[pl.BlockSpec((share_rows, columns), lambda j, place: (0, 0))] * line,
            out_specs=[
                pl.BlockSpec(
                    (rows, columns), lambda j, place: (0, lax.rem(place[0] + line - j, line))
                )
            ]
            * count,
        ),
        compiler_params=vmem_limit(40),
        name="widen_columns",
    )(place, *shares)


def project(place, pieces, gain, w_heads, cosine, sine):
    line, count, part, width = w_heads.shape
    slots, share, model_width = pieces[0].shape
    rows = slots * share * line
    tile = width // 2
    heads = tile // HEAD_DIM
    n_pieces = len(pieces)
    half = HEAD_DIM // 2

    def kernel(place_ref, *refs):
        piece_refs = refs[:n_pieces]
        gain_ref, w_ref, cos_ref, sin_ref, rows_ref, out_ref = refs[n_pieces:]

        @pl.when((pl.program_id(0) == 0) & (pl.program_id(1) == 0))
        def assemble():
            spread(piece_refs, place_ref, rows_ref)
            rows_ref[...] = (rows_ref[...].astype(jnp.float32) * gain_ref[...]).astype(jnp.bfloat16)

        weight = w_ref[...].reshape(line * part, tile)
        turned = dot_f32(rows_ref[...], weight).T
        c, s = cos_ref[0], sin_ref[0]
        for head in range(heads):
            a = turned[head * HEAD_DIM : head * HEAD_DIM + half]
            b = turned[head * HEAD_DIM + half : (head + 1) * HEAD_DIM]
            out_ref[head, 0, :half, :] = (a * c - b * s).astype(jnp.bfloat16)
            out_ref[head, 0, half:, :] = (b * c + a * s).astype(jnp.bfloat16)

    return pl.pallas_call(
        kernel,
        grid=(count, 2),
        out_shape=[
            jax.ShapeDtypeStruct((rows, model_width), jnp.bfloat16),
            jax.ShapeDtypeStruct((width // HEAD_DIM, count, HEAD_DIM, rows), jnp.bfloat16),
        ],
        in_specs=[whole(pltpu.SMEM)]
        + [whole()] * (n_pieces + 1)
        + [
            pl.BlockSpec((line, 1, part, tile), lambda m, h: (0, m, 0, h)),
            pl.BlockSpec((1, half, rows), lambda m, h: (m, 0, 0)),
            pl.BlockSpec((1, half, rows), lambda m, h: (m, 0, 0)),
        ],
        out_specs=[
            pl.BlockSpec((rows, model_width), lambda m, h: (0, 0)),
            pl.BlockSpec((heads, 1, HEAD_DIM, rows), lambda m, h: (h, m, 0, 0)),
        ],
        compiler_params=vmem_limit(48),
        cost_estimate=work(6 * rows * model_width * width, 8 * rows * model_width),
        name="project",
    )(place, *pieces, gain, w_heads, cosine, sine)


def mix_out(place, mixed, w_out, slots, line):
    heads, unused, rows = mixed.shape
    width, model_width = w_out.shape
    share = rows // slots // line

    def kernel(place_ref, mixed_ref, w_ref, own_ref, *rest):
        *others, total = rest
        left = mixed_ref[...].reshape(width, rows).T
        total[...] = dot_f32(left, w_ref[...])
        deal(total, place_ref, own_ref, others)

    return pl.pallas_call(
        kernel,
        out_shape=dealt_shapes(slots, share, model_width, line),
        in_specs=[whole(pltpu.SMEM), whole(), whole()],
        out_specs=[whole()] * line,
        scratch_shapes=[pltpu.VMEM((rows, model_width), jnp.float32)],
        compiler_params=vmem_limit(48),
        cost_estimate=work(2 * rows * model_width * width, 8 * rows * model_width),
        name="mix_out",
    )(place, mixed, w_out)


def mlp_forward(place, pieces, upstream_pieces, w_mlp, tile):
    line, count, part, width = w_mlp.shape
    slots, share, model_width = pieces[0].shape
    rows = slots * share * line
    n_pieces = len(pieces)
    bf, f32 = jnp.bfloat16, jnp.float32

    def kernel(place_ref, *refs):
        x_pieces, u_pieces = refs[:n_pieces], refs[n_pieces : 2 * n_pieces]
        w_ref, x_ref, u_ref, hidden_ref, gate_ref, up_ref, own_ref = refs[
            2 * n_pieces : 2 * n_pieces + 7
        ]
        *others, total = refs[2 * n_pieces + 7 :]
        step = pl.program_id(0)

        @pl.when(step == 0)
        def assemble():
            spread(x_pieces, place_ref, x_ref)
            spread(u_pieces, place_ref, u_ref)

        down = w_ref[:, 0].reshape(line * part, tile)
        gate = w_ref[:, 1].reshape(line * part, tile)
        up = w_ref[:, 2].reshape(line * part, tile)
        x = x_ref[...]
        grad_hidden = dot_f32(u_ref[...], down)
        gate_act = dot_f32(x, gate)
        upward = dot_f32(x, up)
        sigmoid = jax.nn.sigmoid(gate_act)
        silu = gate_act * sigmoid
        hidden_ref[...] = (silu * upward).astype(bf)
        grad_gate = (
            grad_hidden * upward * sigmoid * (1.0 + gate_act * (1.0 - sigmoid))
        ).astype(bf)
        grad_up = (grad_hidden * silu).astype(bf)
        gate_ref[...] = grad_gate
        up_ref[...] = grad_up
        part_two = nt_dot(grad_gate, gate) + nt_dot(grad_up, up)

        @pl.when(step == 0)
        def first():
            total[...] = part_two

        @pl.when(step > 0)
        def further():
            total[...] += part_two

        @pl.when(step == pl.num_programs(0) - 1)
        def last():
            deal(total, place_ref, own_ref, others)

    fixed = lambda shape: pl.BlockSpec(shape, lambda j: (0,) * len(shape))
    columns = pl.BlockSpec((rows, tile), lambda j: (0, j))
    dealt = dealt_shapes(slots, share, model_width, line)
    return pl.pallas_call(
        kernel,
        grid=(width // tile,),
        out_shape=[jax.ShapeDtypeStruct((rows, model_width), bf)] * 2
        + [jax.ShapeDtypeStruct((rows, width), bf)] * 3
        + dealt,
        in_specs=[whole(pltpu.SMEM)]
        + [whole()] * (2 * n_pieces)
        + [pl.BlockSpec((line, count, part, tile), lambda j: (0, 0, 0, j))],
        out_specs=[fixed((rows, model_width))] * 2
        + [columns] * 3
        + [fixed((slots, share, model_width))] * line,
        scratch_shapes=[pltpu.VMEM((rows, model_width), f32)],
        compiler_params=vmem_limit(60),
        cost_estimate=work(16 * rows * model_width * width, 14 * model_width * width),
        name="mlp_forward",
    )(place, *pieces, *upstream_pieces, w_mlp)


def gate_up_weights(x_rows, grad_gate, grad_up, groups, line, tile):
    rows, model_width = x_rows.shape
    width = grad_gate.shape[1]
    block = model_width // groups // line

    def kernel(x_ref, gate_ref, up_ref, out_ref):
        for i, ref in enumerate((gate_ref, up_ref)):
            grads = transpose_product(x_ref[...], ref[...]).astype(jnp.bfloat16)
            out_ref[:, :, i * block : (i + 1) * block] = grads.reshape(groups, line, block, tile)

    columns = pl.BlockSpec((rows, tile), lambda j: (0, j))
    return pl.pallas_call(
        kernel,
        grid=(width // tile,),
        out_shape=jax.ShapeDtypeStruct((groups, line, 2 * block, width), jnp.bfloat16),
        in_specs=[pl.BlockSpec((rows, model_width), lambda j: (0, 0)), columns, columns],
        out_specs=pl.BlockSpec((groups, line, 2 * block, tile), lambda j: (0, 0, 0, j)),
        compiler_params=vmem_limit(60),
        cost_estimate=work(4 * rows * model_width * width, 8 * model_width * width),
        name="gate_up_weights",
    )(x_rows, grad_gate, grad_up)


def down_weights(u_rows, hidden, groups, line, tile):
    rows, model_width = u_rows.shape
    width = hidden.shape[1]
    block = model_width // groups // line

    def kernel(u_ref, hidden_ref, out_ref):
        grads = transpose_product(u_ref[...], hidden_ref[...]).astype(jnp.bfloat16)
        out_ref[:, :line] = grads.reshape(groups, line, block, tile)

    return pl.pallas_call(
        kernel,
        grid=(width // tile,),
        out_shape=jax.ShapeDtypeStruct((groups, line + 1, block, width), jnp.bfloat16),
        in_specs=[
            pl.BlockSpec((rows, model_width), lambda j: (0, 0)),
            pl.BlockSpec((rows, tile), lambda j: (0, j)),
        ],
        out_specs=pl.BlockSpec((groups, line + 1, block, tile), lambda j: (0, 0, 0, j)),
        compiler_params=vmem_limit(60),
        cost_estimate=work(2 * rows * model_width * width, 4 * model_width * width),
        name="down_weights",
    )(u_rows, hidden)


def mlp_out(place, hidden, w_mlp, slots, tile):
    line, count, part, width = w_mlp.shape
    rows = hidden.shape[0]
    model_width = line * part
    share = rows // slots // line

    def kernel(place_ref, hidden_ref, w_ref, own_ref, *rest):
        *others, total = rest
        step = pl.program_id(0)
        part_out = nt_dot(hidden_ref[...], w_ref[...].reshape(line * part, tile))

        @pl.when(step == 0)
        def first():
            total[...] = part_out

        @pl.when(step > 0)
        def further():
            total[...] += part_out

        @pl.when(step == pl.num_programs(0) - 1)
        def last():
            deal(total, place_ref, own_ref, others)

    fixed = lambda shape: pl.BlockSpec(shape, lambda j: (0,) * len(shape))
    return pl.pallas_call(
        kernel,
        grid=(width // tile,),
        out_shape=dealt_shapes(slots, share, model_width, line),
        in_specs=[
            whole(pltpu.SMEM),
            pl.BlockSpec((rows, tile), lambda j: (0, j)),
            pl.BlockSpec((line, 1, part, tile), lambda j: (0, 0, 0, j)),
        ],
        out_specs=[fixed((slots, share, model_width))] * line,
        scratch_shapes=[pltpu.VMEM((rows, model_width), jnp.float32)],
        compiler_params=vmem_limit(60),
        cost_estimate=work(2 * rows * model_width * width, 2 * model_width * width),
        name="mlp_out",
    )(place, hidden, w_mlp)


def branch_back(place, pieces, w_out, heads):
    slots, share, model_width = pieces[0].shape
    line = (len(pieces) + 1) // 2
    rows = slots * share * line

    def kernel(place_ref, *refs):
        *piece_refs, w_ref, rows_ref, out_ref = refs
        spread(piece_refs, place_ref, rows_ref)
        turned = nt_dot(w_ref[...], rows_ref[...])
        out_ref[...] = turned.astype(jnp.bfloat16).reshape(out_ref.shape)

    return pl.pallas_call(
        kernel,
        out_shape=[
            jax.ShapeDtypeStruct((rows, model_width), jnp.bfloat16),
            jax.ShapeDtypeStruct((heads, HEAD_DIM, rows), jnp.bfloat16),
        ],
        in_specs=[whole(pltpu.SMEM)] + [whole()] * (len(pieces) + 1),
        out_specs=[whole(), whole()],
        compiler_params=vmem_limit(40),
        cost_estimate=work(2 * rows * model_width * heads * HEAD_DIM, 8 * rows * model_width),
        name="branch_back",
    )(place, *pieces, w_out)


def out_weight(grads, mixed, branch_rows, tile):
    groups, blocks, block, width = grads.shape
    heads, unused, rows = mixed.shape

    def kernel(grads_ref, mixed_ref, rows_ref, out_ref):
        left = mixed_ref[...].reshape(heads * HEAD_DIM, rows)
        product = dot_f32(left, rows_ref[...]).astype(jnp.bfloat16)
        out_ref[...] = product.reshape(groups, 1, block, tile)

    return pl.pallas_call(
        kernel,
        grid=(width // tile,),
        out_shape=jax.ShapeDtypeStruct(grads.shape, grads.dtype),
        in_specs=[
            pl.BlockSpec(memory_space=pl.ANY),
            pl.BlockSpec(mixed.shape, lambda j: (0, 0, 0)),
            pl.BlockSpec((rows, tile), lambda j: (0, j)),
        ],
        out_specs=pl.BlockSpec((groups, 1, block, tile), lambda j: (0, blocks - 1, 0, j)),
        input_output_aliases={0: 0},
        compiler_params=vmem_limit(60),
        cost_estimate=work(4 * rows * heads * HEAD_DIM * width, 8 * rows * width),
        name="out_weight",
    )(grads, mixed, branch_rows)


def head_weights(group, all_rows, corner, head_grads, w_head, gain, gain_two, owners):
    sources, features, rows = head_grads.shape
    model_width = all_rows[0].shape[1]
    block = model_width // owners
    lanes = 2 * LANES
    half = rows // 2
    f32 = jnp.float32

    def kernel(group_ref, *refs):
        x_refs, corner_refs = refs[: sources - 2], refs[sources - 2 : sources + 2]
        g_ref, w_ref, gain_ref, two_ref, out_ref, total = refs[sources + 2 :]
        step = pl.program_id(0)

        def product(bits, ref):
            return dot_f32(g_ref[lax.bitwise_xor(group_ref[0], bits)], ref[...])

        part = sum(product(bits, ref) for bits, ref in enumerate(x_refs))

        def with_corner(half_refs):
            return part + product(sources - 2, half_refs[0]) + product(sources - 1, half_refs[1])

        @pl.when(step == 0)
        def first():
            total[...] = with_corner(corner_refs[0::2])

        @pl.when(step == 1)
        def last():
            grads = (total[...] + with_corner(corner_refs[1::2])).T
            weighed = jnp.sum(grads * w_ref[...].astype(f32), 1, keepdims=True) / gain_ref[...].T
            spare = lanes - features
            at = lax.broadcasted_iota(jnp.int32, (model_width, spare), 1)
            tail = jnp.where(at == 0, weighed, jnp.where(at == 1, two_ref[...].T, 0.0))
            joined = jnp.concatenate([grads, tail], 1).astype(jnp.bfloat16)
            out_ref[...] = joined.reshape(owners, block, lanes)

    fixed = lambda shape: pl.BlockSpec(shape, lambda s: (0,) * len(shape))
    return pl.pallas_call(
        kernel,
        grid=(2,),
        out_shape=jax.ShapeDtypeStruct((owners, block, lanes), jnp.bfloat16),
        in_specs=[whole(pltpu.SMEM)]
        + [pl.BlockSpec((half, model_width), lambda s: (s, 0))] * (sources - 2)
        + [fixed((half, model_width))] * 4
        + [
            pl.BlockSpec((sources, features, half), lambda s: (0, 0, s)),
            fixed((model_width, features)),
            fixed((1, model_width)),
            fixed((1, model_width)),
        ],
        out_specs=fixed((owners, block, lanes)),
        scratch_shapes=[pltpu.VMEM((features, model_width), f32)],
        compiler_params=vmem_limit(60),
        cost_estimate=work(6 * sources * rows * features * model_width, 0),
        name="head_weights",
    )(group, *all_rows, *corner, head_grads, w_head, gain, gain_two)


def join_heads(parts):
    groups, line, rows, lanes = parts.shape
    width = groups * HEAD_DIM

    def kernel(parts_ref, *outs):
        for i, out in enumerate(outs):
            pick = slice(i * HEAD_DIM, (i + 1) * HEAD_DIM)
            heads = [parts_ref[c, 0][:, pick].astype(jnp.float32) for c in range(groups)]
            out[...] = jnp.concatenate(heads, 1)

    return pl.pallas_call(
        kernel,
        grid=(line,),
        out_shape=[jax.ShapeDtypeStruct((rows, line * width), jnp.float32)] * 3,
        in_specs=[pl.BlockSpec((groups, 1, rows, lanes), lambda f: (0, f, 0, 0))],
        out_specs=[pl.BlockSpec((rows, width), lambda f: (0, f))] * 3,
        compiler_params=vmem_limit(24),
        name="join_heads",
    )(parts)


def project_back(place, head_grads, w_heads, slots):
    line, count, part, width = w_heads.shape
    rows, model_width = head_grads.shape[-1], line * part
    heads = width // HEAD_DIM
    share = rows // slots // line

    def kernel(place_ref, g_ref, w_ref, own_ref, *rest):
        *others, total = rest
        m = pl.program_id(0)
        grads = g_ref[...].reshape(width, rows).T
        partial = nt_dot(grads, w_ref[...].reshape(line * part, width))

        @pl.when(m == 0)
        def first():
            total[...] = partial

        @pl.when(m > 0)
        def further():
            total[...] += partial

        @pl.when(m == count - 1)
        def last():
            deal(total, place_ref, own_ref, others)

    fixed = lambda shape: pl.BlockSpec(shape, lambda m: (0,) * len(shape))
    return pl.pallas_call(
        kernel,
        grid=(count,),
        out_shape=dealt_shapes(slots, share, model_width, line),
        in_specs=[
            whole(pltpu.SMEM),
            pl.BlockSpec((heads, 1, HEAD_DIM, rows), lambda m: (0, m, 0, 0)),
            pl.BlockSpec((line, 1, part, width), lambda m: (0, m, 0, 0)),
        ],
        out_specs=[fixed((slots, share, model_width))] * line,
        scratch_shapes=[pltpu.VMEM((rows, model_width), jnp.float32)],
        compiler_params=vmem_limit(48),
        cost_estimate=work(2 * count * rows * width * model_width, 8 * rows * model_width),
        name="project_back",
    )(place, head_grads, w_heads)


def line_steps(size, step):
    return [(i, i + step) for i in range(size) if 0 <= i + step < size]


def after(values, *earlier):
    return lax.optimization_barrier((values, earlier))[0]


def send_shares(share, axis, between=()):
    size = lax.axis_size(axis)
    ups, downs = [share], [share]
    for hop in range(1, size):
        up = lax.ppermute(ups[-1], axis, line_steps(size, 1)[hop - 1 :])
        down = lax.ppermute(downs[-1], axis, line_steps(size, -1)[: size - hop])
        if hop <= len(between):
            done = between[hop - 1]((ups[-1], downs[-1]))
            up, down = after((up, down), done)
        ups.append(up)
        downs.append(down)
    return ups + downs[1:]


def flip(values, bits):
    size = lax.axis_size("ctx")
    return lax.ppermute(values, "ctx", [(i, i ^ bits) for i in range(size)])


def send_dealt(others, axis):
    size = lax.axis_size(axis)
    return [
        lax.ppermute(other, axis, [(i, (i + step) % size) for i in range(size)])
        for step, other in enumerate(others, 1)
    ]


def scatter_line(others, axis, between=()):
    size = lax.axis_size(axis)
    up = down = None
    for hop in range(1, size):
        rising, falling = others[size - hop - 1], others[hop - 1]
        if hop > 1:
            rising = (rising.astype(jnp.float32) + up.astype(jnp.float32)).astype(rising.dtype)
            falling = (falling.astype(jnp.float32) + down.astype(jnp.float32)).astype(falling.dtype)
        up = lax.ppermute(rising, axis, line_steps(size, 1)[:hop])
        down = lax.ppermute(falling, axis, line_steps(size, -1)[size - 1 - hop :])
        if hop <= len(between):
            up, down = after((up, down), between[hop - 1]((rising, falling)))
    return [up, down]


def add_shares(own, received):
    return own + sum(share.astype(jnp.float32) for share in received)


def swap_dealt(shares):
    return [shares[0]] + send_dealt(shares[1:], "fsdp")


def deal_line(parts, place):
    line = parts.shape[0]
    return [
        lax.dynamic_index_in_dim(parts, lax.rem(place[0] + step, line), 0, keepdims=False)
        for step in range(line)
    ]


def swap_heads(parts):
    return lax.all_to_all(parts, "ctx", split_axis=0, concat_axis=0, tiled=True)


def sum_groups(parts):
    return lax.psum_scatter(parts, "ctx", scatter_dimension=0, tiled=True)[0]


def head_device(
    tokens,
    block_order,
    w_query,
    w_key,
    w_value,
    w_out,
    w_gate,
    w_up,
    w_down,
    gain_attn,
    gain_mlp,
    cotangent,
):
    slots, share_rows, model_width = tokens.shape
    ctx_size, line = lax.axis_size("ctx"), lax.axis_size("fsdp")
    block_rows = share_rows * line
    group_rows = slots * block_rows
    bf, f32 = jnp.bfloat16, jnp.float32
    place = lax.axis_index("fsdp").astype(jnp.int32).reshape(1)
    group = lax.axis_index("ctx").astype(jnp.int32).reshape(1)
    own_rows = w_query.shape[0] // ctx_size
    order = block_order.astype(jnp.int32)
    sequence = group_rows * ctx_size
    slot_of = jnp.sum(
        jnp.where(order[None, :] == jnp.arange(order.shape[0])[:, None], jnp.arange(order.shape[0], dtype=jnp.int32)[None, :], 0), 1
    ).astype(jnp.int32)

    stream = tokens.astype(f32)
    root_one = lax.rsqrt(jnp.mean(stream * stream, -1, keepdims=True) + EPSILON)
    norm_one = stream * root_one
    gain_rows = jnp.pad(jnp.stack([gain_attn, gain_mlp]), ((0, EXTRA_ROWS - 2), (0, 0)))
    head_cuts = swap_dealt(
        cut_columns(place, group, [w_query, w_key, w_value], own_rows, line, gain_rows)
    )
    own_heads, gains = order_shares(place, head_cuts, 3, 2)
    attn_gain, mlp_gain = gains[0], gains[1]
    w_heads = lax.all_gather(own_heads, "ctx", axis=2, tiled=True)

    attn_pieces = send_shares(after(norm_one.astype(bf), head_cuts), "fsdp")

    mlp_cuts = cut_columns(place, group, [w_down, w_gate, w_up], own_rows, line)
    w_heads = after(w_heads, mlp_cuts)
    mlp_cuts = swap_dealt(after(mlp_cuts, attn_pieces))

    w_head = lax.dynamic_slice_in_dim(w_heads, group[0] * HEAD_DIM, HEAD_DIM, 3)
    w_head = jnp.concatenate([w_head[:, i].reshape(model_width, HEAD_DIM) for i in range(3)], 1)

    half = HEAD_DIM // 2
    frequency = 1.0 / ROPE_BASE ** (jnp.arange(half, dtype=f32) * (2.0 / HEAD_DIM))
    places = jnp.arange(group_rows * ctx_size, dtype=jnp.int32).astype(f32)
    angles = frequency[:, None] * places[None, :]
    cosine, sine = jnp.cos(angles), jnp.sin(angles)

    def own_columns(table):
        return jnp.concatenate(
            [
                lax.dynamic_slice_in_dim(
                    table, order[slots * group[0] + i] * block_rows, block_rows, 1
                )
                for i in range(slots)
            ],
            1,
        )

    own_cosine, own_sine = own_columns(cosine), own_columns(sine)
    turn_cosine = jnp.stack([own_cosine, own_cosine, jnp.ones_like(own_cosine)])
    turn_sine = jnp.stack([own_sine, own_sine, jnp.zeros_like(own_sine)])

    attn_rows, heads_out = project(
        place, attn_pieces, attn_gain[None], w_heads, turn_cosine, turn_sine
    )
    heads_out = heads_out.reshape(ctx_size, 3 * HEAD_DIM, group_rows)
    head_rows = swap_heads(after(heads_out, mlp_cuts[1]))
    mixed_send, attended, log_total = attend(
        order, head_rows, block_rows, sequence, 2 * block_rows
    )
    mixed = swap_heads(mixed_send)
    mlp_cuts = order_shares(place, after(mlp_cuts, mixed), 3)
    w_mlp = lax.all_gather(mlp_cuts, "ctx", axis=2, tiled=True)
    upstream_pieces = send_shares(after(cotangent, mlp_cuts), "fsdp")
    own, *others = mix_out(place, after(mixed, w_head, mlp_cuts), w_out, slots, line)
    middle = stream + add_shares(own, scatter_line(others, "fsdp"))

    root_two = lax.rsqrt(jnp.mean(middle * middle, -1, keepdims=True) + EPSILON)
    norm_two = middle * root_two
    mlp_input = (norm_two * mlp_gain).astype(bf)
    mlp_pieces = send_shares(mlp_input, "fsdp")

    all_rows = {0: attn_rows}
    start_rows = after(attn_rows, mlp_pieces, upstream_pieces, w_mlp)
    all_rows[2], all_rows[4] = flip(start_rows, 2), flip(start_rows, 4)
    mlp_rows, upstream_rows, hidden, grad_gate, grad_up, own, *others = mlp_forward(
        place, mlp_pieces, upstream_pieces, w_mlp, 512
    )
    results = {}

    def weigh_gate_up(sent):
        rows_here = after(mlp_rows, sent)
        results["gate_up"] = gate_up_weights(rows_here, grad_gate, grad_up, ctx_size, line, 512)
        return results["gate_up"], all_rows[2], all_rows[4]

    upper = attn_rows.shape[0] // 2

    def weigh_down(sent):
        results["down"] = down_weights(
            upstream_rows, after(hidden, sent), ctx_size, line, 512
        )
        results["gate_up_sums"] = sum_groups(after(results["gate_up"], sent))
        return results["down"]

    grad_two = add_shares(own, scatter_line(others, "fsdp", (weigh_gate_up, weigh_down)))
    gate_up_sums = results["gate_up_sums"]
    down_grads = results["down"]
    gain_two_part = jnp.sum(grad_two * norm_two, (0, 1))
    grad_middle = cotangent.astype(f32) + norm_back(grad_two, norm_two, root_two, mlp_gain)

    def weigh_out(sent):
        results["out"] = mlp_out(place, after(hidden, sent), w_mlp, slots, 512)
        return results["out"]

    def cut_corner(sent):
        by_x, by_y = after((all_rows[2], all_rows[4]), sent)
        results["corner"] = (by_x[:upper], by_y[upper:])
        return results["corner"]

    branch_pieces = send_shares(grad_middle.astype(bf), "fsdp", (weigh_out, cut_corner))
    corner = [flip(results["corner"][0], 4), flip(results["corner"][1], 2)]
    own_out, *others_out = results["out"]
    branch_rows, grad_mixed = branch_back(place, branch_pieces, w_out, ctx_size)

    out_received = send_dealt(after(others_out, branch_rows), "fsdp")
    for bits in (0, 2, 4):
        all_rows[bits + 1] = flip(after(all_rows[bits], branch_rows), 1)
    grad_heads = swap_heads(grad_mixed)
    down_grads = out_weight(down_grads, mixed, branch_rows, 512)
    head_grads = attend_back(
        jnp.concatenate([order, slot_of]),
        head_rows,
        after(
            grad_heads, down_grads, all_rows[1], all_rows[3], all_rows[5]
        ),
        attended,
        log_total,
        cosine,
        sine,
        block_rows,
        sequence,
        block_rows,
    )
    head_grads = after(head_grads, out_received, corner)
    corner = corner + [flip(part, 1) for part in after(corner, head_grads)]
    gate_up_dealt = deal_line(after(gate_up_sums, head_grads), place)
    gate_up_back = swap_dealt(gate_up_dealt)
    down_sums = sum_groups(after(down_grads, gate_up_sums, head_grads))
    lin_grads = swap_heads(after(head_grads, gate_up_dealt))
    head_parts = head_weights(
        group,
        [all_rows[bits] for bits in range(ctx_size - 2)],
        corner,
        after(head_grads, gate_up_dealt),
        w_head,
        attn_gain[None],
        gain_two_part[None],
        ctx_size * line,
    )
    lin_grads = after(lin_grads, head_parts, gate_up_back[1], gate_up_back[2])
    head_parts = lax.all_to_all(
        after(head_parts, lin_grads), ("ctx", "fsdp"), split_axis=0, concat_axis=0, tiled=True
    )
    lin_grads = lin_grads.reshape(ctx_size, 3, HEAD_DIM, group_rows)
    own, *others = project_back(place, lin_grads, w_heads, slots)

    def swap_down(sent):
        parts = deal_line(after(down_sums, sent)[:line], place)
        results["down_back"] = swap_dealt(parts)
        return results["down_back"][1]

    one_received = scatter_line(
        others, "fsdp", (lambda sent: (gate_up_back[3], head_parts), lambda sent: (), swap_down)
    )
    down_back = results["down_back"]
    grad_one = add_shares(own, one_received)
    result = (middle + add_shares(own_out, out_received)).astype(bf)
    grad_tokens = grad_middle + norm_back(grad_one, norm_one, root_one, attn_gain)
    owners = [(c * line + f, f * ctx_size + c) for c in range(ctx_size) for f in range(line)]
    grad_w_out = lax.ppermute(down_sums[line], ("ctx", "fsdp"), owners).astype(f32)
    grad_w_gate, grad_w_up = widen_columns(place, gate_up_back, 2, own_rows)
    (grad_w_down,) = widen_columns(place, after(down_back, grad_tokens), 1, own_rows)
    head_parts = head_parts.reshape(ctx_size, line, own_rows, -1)
    grad_w_query, grad_w_key, grad_w_value = join_heads(head_parts)
    spare = 3 * HEAD_DIM
    gain_grads = jnp.sum(head_parts[..., spare : spare + 2].astype(f32), (0, 1)).T
    return (
        result,
        grad_tokens,
        grad_w_query,
        grad_w_key,
        grad_w_value,
        grad_w_out,
        grad_w_gate,
        grad_w_up,
        grad_w_down,
        gain_grads[0],
        gain_grads[1],
    )


def layer_step(*arrays):
    heads_here = arrays[0].shape[-1] // lax.axis_size("fsdp") // HEAD_DIM
    if heads_here == lax.axis_size("ctx") == 8:
        return head_device(*arrays)
    return per_device(*arrays)


def solution(mesh):
    in_specs = (
        P("ctx", "fsdp", None),
        P(),
        P("fsdp", None),
        P("fsdp", None),
        P("fsdp", None),
        P("fsdp", None),
        P("fsdp", None),
        P("fsdp", None),
        P("fsdp", None),
        P("fsdp"),
        P("fsdp"),
        P("ctx", "fsdp", None),
    )
    out_specs = (
        P("ctx", "fsdp", None),
        P("ctx", "fsdp", None),
        P(("ctx", "fsdp"), None),
        P(("ctx", "fsdp"), None),
        P(("ctx", "fsdp"), None),
        P(("ctx", "fsdp"), None),
        P(("ctx", "fsdp"), None),
        P(("ctx", "fsdp"), None),
        P(("ctx", "fsdp"), None),
        P(("ctx", "fsdp")),
        P(("ctx", "fsdp")),
    )
    return jax.shard_map(
        layer_step, mesh=mesh, in_specs=in_specs, out_specs=out_specs, check_vma=False
    )
```

```python
import functools

import jax
import jax.numpy as jnp
from jax import lax
from jax.experimental import pallas as pl
from jax.experimental.pallas import tpu as pltpu
from jax.sharding import PartitionSpec as P

HEAD_DIM = 64


EPSILON = 1e-05
ROPE_BASE = 130000.0
MASKED_SCORE = -1e30


def rotate(values, places, direction):
    half_dim = values.shape[-1] // 2
    frequency = 1.0 / ROPE_BASE ** (
        jnp.arange(half_dim, dtype=jnp.float32) * (2.0 / values.shape[-1])
    )
    angles = places[..., None] * frequency
    cosine = jnp.cos(angles)[..., None, :]
    sine_part = direction * jnp.sin(angles)[..., None, :]
    leading = values[..., :half_dim]
    trailing = values[..., half_dim:]
    return jnp.concatenate(
        [leading * cosine - trailing * sine_part, trailing * cosine + leading * sine_part], -1
    )


def matmul(left, right):
    return jnp.dot(left, right, preferred_element_type=jnp.float32)


def contract(left, right):
    return lax.dot_general(
        left, right, (((1,), (1,)), ((), ())), preferred_element_type=jnp.float32
    )


def transpose_product(left, right):
    return lax.dot_general(
        left, right, (((0,), (0,)), ((), ())), preferred_element_type=jnp.float32
    )


def split_heads(values):
    return values.reshape(values.shape[:-1] + (-1, HEAD_DIM))


def keep_state(current):
    return current


def tile_scores(queries, key_rows, query_places, key_places, score_scale):
    scores = (
        jnp.einsum("qhd,khd->hqk", queries, key_rows, preferred_element_type=jnp.float32)
        * score_scale
    )
    allowed = (key_places[None, :] <= query_places[:, None])[None]
    return (jnp.where(allowed, scores, MASKED_SCORE), allowed)


def grow_state(current, queries, key_rows, value_rows, query_places, key_places, score_scale):
    run_peak, run_total, summed = current
    scores, allowed = tile_scores(queries, key_rows, query_places, key_places, score_scale)
    new_peak = jnp.maximum(run_peak, jnp.max(scores, -1))
    weights = jnp.where(allowed, jnp.exp(scores - new_peak[..., None]), 0.0)
    factor = jnp.exp(run_peak - new_peak)
    run_total = run_total * factor + jnp.sum(weights, -1)
    summed = summed * jnp.transpose(factor)[:, :, None] + jnp.einsum(
        "hqk,khd->qhd", weights.astype(jnp.bfloat16), value_rows, preferred_element_type=jnp.float32
    )
    return (new_peak, run_total, summed)


def backward_tile(
    queries,
    key_rows,
    value_rows,
    grad_out,
    log_total,
    row_delta,
    query_places,
    key_places,
    score_scale,
):
    scores, allowed = tile_scores(queries, key_rows, query_places, key_places, score_scale)
    probabilities = jnp.where(allowed, jnp.exp(scores - log_total[..., None]), 0.0)
    grad_probs = jnp.einsum(
        "qhd,khd->hqk", grad_out, value_rows, preferred_element_type=jnp.float32
    )
    grad_scores = (probabilities * (grad_probs - row_delta[..., None])).astype(jnp.bfloat16)
    return (probabilities, grad_scores)


def norm_back(grad_normed_in, normed_values, inverse_root, gain_vector):
    scaled = grad_normed_in * gain_vector
    return inverse_root * (
        scaled - normed_values * jnp.mean(scaled * normed_values, -1, keepdims=True)
    )


def per_device(
    tokens,
    block_order,
    w_query,
    w_key,
    w_value,
    w_out,
    w_gate,
    w_up,
    w_down,
    gain_attn,
    gain_mlp,
    cotangent,
):
    slot_count, share_rows, model_width = tokens.shape
    fsdp_size = lax.axis_size("fsdp")
    block_rows = share_rows * fsdp_size
    head_width = model_width // fsdp_size
    heads_here = head_width // HEAD_DIM
    row_count = slot_count * share_rows
    score_scale = HEAD_DIM ** (-0.5)
    own_slots = 2 * lax.axis_index("ctx") + jnp.arange(2, dtype=jnp.int32)
    own_blocks = block_order[own_slots]
    token_places = (
        (
            own_blocks[:, None] * block_rows
            + lax.axis_index("fsdp") * share_rows
            + jnp.arange(share_rows, dtype=jnp.int32)[None, :]
        )
        .astype(jnp.float32)
        .reshape(row_count)
    )
    head_places = (
        own_blocks[:, None] * block_rows + jnp.arange(block_rows, dtype=jnp.int32)[None, :]
    ).astype(jnp.float32)
    params = (w_query, w_key, w_value, w_out, w_gate, w_up, w_down, gain_attn, gain_mlp)
    weights_all = (
        lax.all_gather(params[0], "fsdp", axis=0, tiled=True),
        lax.all_gather(params[1], "fsdp", axis=0, tiled=True),
        lax.all_gather(params[2], "fsdp", axis=0, tiled=True),
        lax.all_gather(params[3], "fsdp", axis=0, tiled=True),
        lax.all_gather(params[4], "fsdp", axis=0, tiled=True),
        lax.all_gather(params[5], "fsdp", axis=0, tiled=True),
        lax.all_gather(params[6], "fsdp", axis=0, tiled=True),
        lax.all_gather(params[7], "fsdp", axis=0, tiled=True),
        lax.all_gather(params[8], "fsdp", axis=0, tiled=True),
    )
    stream = tokens.reshape(row_count, model_width).astype(jnp.float32)
    root_one = lax.rsqrt(jnp.mean(stream * stream, -1, keepdims=True) + EPSILON)
    norm_one = stream * root_one
    attn_input = (norm_one * weights_all[7].astype(jnp.float32)).astype(jnp.bfloat16)

    def project_turn(weight):
        linear = matmul(attn_input, weight).reshape(row_count, -1, HEAD_DIM)
        return (
            rotate(linear, token_places, 1.0)
            .astype(jnp.bfloat16)
            .reshape(slot_count, share_rows, model_width)
        )

    query_tok = project_turn(weights_all[0])
    key_tok = project_turn(weights_all[1])
    value_tok = (
        matmul(attn_input, weights_all[2])
        .astype(jnp.bfloat16)
        .reshape(slot_count, share_rows, model_width)
    )
    query_heads, key_heads, value_heads = (
        lax.all_to_all(query_tok, "fsdp", split_axis=2, concat_axis=1, tiled=True),
        lax.all_to_all(key_tok, "fsdp", split_axis=2, concat_axis=1, tiled=True),
        lax.all_to_all(value_tok, "fsdp", split_axis=2, concat_axis=1, tiled=True),
    )
    query_split = split_heads(query_heads)
    start_state = tuple(
        (
            (
                jnp.full((heads_here, block_rows), MASKED_SCORE, jnp.float32),
                jnp.zeros((heads_here, block_rows), jnp.float32),
                jnp.zeros((block_rows, heads_here, HEAD_DIM), jnp.float32),
            )
            for which_slot in range(2)
        )
    )
    carried = start_state
    key_part = lax.all_gather(key_heads, "ctx", axis=0, tiled=True)
    value_part = lax.all_gather(value_heads, "ctx", axis=0, tiled=True)

    def visit_slot(inner_state, element):
        key_one, value_one, offset = element
        key_block = block_order[offset]
        key_places = (key_block * block_rows + jnp.arange(block_rows, dtype=jnp.int32)).astype(
            jnp.float32
        )
        key_split = split_heads(key_one)
        value_split = split_heads(value_one)
        updated = []
        for which_slot in range(2):

            def grow_one(current, which_slot=which_slot):
                return grow_state(
                    current,
                    query_split[which_slot],
                    key_split,
                    value_split,
                    head_places[which_slot],
                    key_places,
                    score_scale,
                )

            updated.append(
                lax.cond(
                    key_block <= own_blocks[which_slot],
                    grow_one,
                    keep_state,
                    inner_state[which_slot],
                )
            )
        return (tuple(updated), None)

    offsets = jnp.arange(key_part.shape[0], dtype=jnp.int32)
    carried, unused = lax.scan(visit_slot, carried, (key_part, value_part, offsets))
    attended_parts = []
    log_parts = []
    for which_slot in range(2):
        run_peak, run_total, summed = carried[which_slot]
        log_parts.append(run_peak + jnp.log(run_total))
        attended_parts.append(summed / jnp.transpose(run_total)[:, :, None])
    attended = jnp.stack(attended_parts)
    log_total = jnp.stack(log_parts)
    mixed_send = attended.reshape(slot_count, block_rows, head_width).astype(jnp.bfloat16)
    mixed_tok = lax.all_to_all(mixed_send, "fsdp", split_axis=1, concat_axis=2, tiled=True)
    mixed_flat = mixed_tok.reshape(row_count, model_width)
    middle = stream + matmul(mixed_flat, weights_all[3])
    root_two = lax.rsqrt(jnp.mean(middle * middle, -1, keepdims=True) + EPSILON)
    norm_two = middle * root_two
    mlp_input = (norm_two * weights_all[8].astype(jnp.float32)).astype(jnp.bfloat16)
    gate_act = matmul(mlp_input, weights_all[4])
    upward = matmul(mlp_input, weights_all[5])
    gate_sigmoid = jax.nn.sigmoid(gate_act)
    gate_silu = gate_act * gate_sigmoid
    hidden = (gate_silu * upward).astype(jnp.bfloat16)
    output = middle + contract(hidden, weights_all[6])
    result = output.astype(jnp.bfloat16).reshape(slot_count, share_rows, model_width)
    upstream = cotangent.reshape(row_count, model_width)
    grad_hidden = matmul(upstream, weights_all[6])
    grad_gate = (
        grad_hidden * upward * gate_sigmoid * (1.0 + gate_act * (1.0 - gate_sigmoid))
    ).astype(jnp.bfloat16)
    grad_up = (grad_hidden * gate_silu).astype(jnp.bfloat16)
    grad_two = contract(grad_gate, weights_all[4]) + contract(grad_up, weights_all[5])
    gain_two_part = jnp.sum(grad_two * norm_two, 0)
    grad_middle = upstream.astype(jnp.float32) + norm_back(
        grad_two, norm_two, root_two, weights_all[8].astype(jnp.float32)
    )
    grad_branch = grad_middle.astype(jnp.bfloat16)
    grad_mixed = (
        contract(grad_branch, weights_all[3])
        .astype(jnp.bfloat16)
        .reshape(slot_count, share_rows, model_width)
    )
    grad_heads = lax.all_to_all(grad_mixed, "fsdp", split_axis=2, concat_axis=1, tiled=True)
    grad_split = split_heads(grad_heads)
    row_delta = jnp.transpose(jnp.sum(grad_split.astype(jnp.float32) * attended, -1), (0, 2, 1))
    gathered = (
        lax.all_gather(key_heads, "ctx", axis=0, tiled=True),
        lax.all_gather(value_heads, "ctx", axis=0, tiled=True),
    )
    key_all, value_all = gathered
    total_slots = key_all.shape[0]

    def query_visit(current, element):
        key_pair, value_pair, pair_index = element
        updated = list(current)
        for member in range(2):
            key_block = block_order[2 * pair_index + member]
            key_places = (key_block * block_rows + jnp.arange(block_rows, dtype=jnp.int32)).astype(
                jnp.float32
            )
            key_split = split_heads(key_pair[member])
            value_split = split_heads(value_pair[member])
            for which_slot in range(2):

                def take_query(
                    accum,
                    which_slot=which_slot,
                    key_split=key_split,
                    value_split=value_split,
                    key_places=key_places,
                ):
                    probabilities, grad_scores = backward_tile(
                        query_split[which_slot],
                        key_split,
                        value_split,
                        grad_split[which_slot],
                        log_total[which_slot],
                        row_delta[which_slot],
                        head_places[which_slot],
                        key_places,
                        score_scale,
                    )
                    return accum + score_scale * jnp.einsum(
                        "hqk,khd->qhd", grad_scores, key_split, preferred_element_type=jnp.float32
                    )

                updated[which_slot] = lax.cond(
                    key_block <= own_blocks[which_slot], take_query, keep_state, updated[which_slot]
                )
        return (tuple(updated), None)

    query_zero = jnp.zeros((block_rows, heads_here, HEAD_DIM), jnp.float32)
    pair_keys = key_all.reshape(total_slots // 2, 2, block_rows, head_width)
    pair_values = value_all.reshape(total_slots // 2, 2, block_rows, head_width)
    grad_query_parts, unused = lax.scan(
        query_visit,
        (query_zero, query_zero),
        (pair_keys, pair_values, jnp.arange(total_slots // 2, dtype=jnp.int32)),
    )
    key_part = key_all
    value_part = value_all

    def key_visit(unused_carry, element):
        key_one, value_one, offset = element
        key_block = block_order[offset]
        key_places = (key_block * block_rows + jnp.arange(block_rows, dtype=jnp.int32)).astype(
            jnp.float32
        )
        key_split = split_heads(key_one)
        value_split = split_heads(value_one)
        sums = (
            jnp.zeros((block_rows, heads_here, HEAD_DIM), jnp.float32),
            jnp.zeros((block_rows, heads_here, HEAD_DIM), jnp.float32),
        )
        for which_slot in range(2):

            def take_keys(current, which_slot=which_slot):
                probabilities, grad_scores = backward_tile(
                    query_split[which_slot],
                    key_split,
                    value_split,
                    grad_split[which_slot],
                    log_total[which_slot],
                    row_delta[which_slot],
                    head_places[which_slot],
                    key_places,
                    score_scale,
                )
                grad_key = current[0] + score_scale * jnp.einsum(
                    "hqk,qhd->khd",
                    grad_scores,
                    query_split[which_slot],
                    preferred_element_type=jnp.float32,
                )
                grad_value = current[1] + jnp.einsum(
                    "hqk,qhd->khd",
                    probabilities.astype(jnp.bfloat16),
                    grad_split[which_slot],
                    preferred_element_type=jnp.float32,
                )
                return (grad_key, grad_value)

            sums = lax.cond(key_block <= own_blocks[which_slot], take_keys, keep_state, sums)
        joined = jnp.concatenate(
            [sums[0].reshape(block_rows, head_width), sums[1].reshape(block_rows, head_width)], -1
        )
        return (unused_carry, joined)

    unused_final, terms = lax.scan(
        key_visit,
        jnp.zeros((), jnp.float32),
        (key_part, value_part, jnp.arange(slot_count * lax.axis_size("ctx"), dtype=jnp.int32)),
    )
    summed_kv = lax.psum_scatter(
        terms.astype(jnp.bfloat16), "ctx", scatter_dimension=0, tiled=True
    ).astype(jnp.float32)
    grad_keys = (
        rotate(split_heads(summed_kv[..., :head_width]), head_places, -1.0)
        .astype(jnp.bfloat16)
        .reshape(slot_count, block_rows, head_width)
    )
    grad_values = summed_kv[..., head_width:].astype(jnp.bfloat16)
    grad_queries = (
        rotate(jnp.stack(grad_query_parts), head_places, -1.0)
        .astype(jnp.bfloat16)
        .reshape(slot_count, block_rows, head_width)
    )
    grad_q_tok, grad_k_tok, grad_v_tok = (
        lax.all_to_all(grad_queries, "fsdp", split_axis=1, concat_axis=2, tiled=True),
        lax.all_to_all(grad_keys, "fsdp", split_axis=1, concat_axis=2, tiled=True),
        lax.all_to_all(grad_values, "fsdp", split_axis=1, concat_axis=2, tiled=True),
    )
    grad_q_lin = grad_q_tok.reshape(row_count, model_width)
    grad_k_lin = grad_k_tok.reshape(row_count, model_width)
    grad_v_lin = grad_v_tok.reshape(row_count, model_width)
    grad_one = (
        contract(grad_q_lin, weights_all[0])
        + contract(grad_k_lin, weights_all[1])
        + contract(grad_v_lin, weights_all[2])
    )
    gain_one_part = jnp.sum(grad_one * norm_one, 0)
    grad_input = grad_middle + norm_back(
        grad_one, norm_one, root_one, weights_all[7].astype(jnp.float32)
    )
    hidden_width = hidden.shape[1]
    gain_parts = jnp.stack([gain_one_part, gain_two_part], 1)
    wide_cols = (
        lax.all_to_all(grad_q_lin, "fsdp", split_axis=1, concat_axis=0, tiled=True),
        lax.all_to_all(grad_k_lin, "fsdp", split_axis=1, concat_axis=0, tiled=True),
        lax.all_to_all(grad_v_lin, "fsdp", split_axis=1, concat_axis=0, tiled=True),
        lax.all_to_all(grad_branch, "fsdp", split_axis=1, concat_axis=0, tiled=True),
        lax.all_to_all(grad_gate, "fsdp", split_axis=1, concat_axis=0, tiled=True),
        lax.all_to_all(grad_up, "fsdp", split_axis=1, concat_axis=0, tiled=True),
        lax.all_to_all(hidden, "fsdp", split_axis=1, concat_axis=0, tiled=True),
    )
    row_sets = (
        lax.all_gather(attn_input, "fsdp", axis=0, tiled=True),
        lax.all_gather(mixed_flat, "fsdp", axis=0, tiled=True),
        lax.all_gather(mlp_input, "fsdp", axis=0, tiled=True),
        lax.all_gather(upstream, "fsdp", axis=0, tiled=True),
    )
    group_rows = model_width // lax.axis_size("ctx")
    row_cuts = [values for values in row_sets]
    pieces = [
        transpose_product(row_cuts[0], wide_cols[0]),
        transpose_product(row_cuts[0], wide_cols[1]),
        transpose_product(row_cuts[0], wide_cols[2]),
        transpose_product(row_cuts[1], wide_cols[3]),
        transpose_product(row_cuts[2], wide_cols[4]),
        transpose_product(row_cuts[2], wide_cols[5]),
        transpose_product(row_cuts[3], wide_cols[6]),
        gain_parts,
        jnp.zeros((group_rows * lax.axis_size("ctx"), 126), jnp.float32),
    ]
    partial_sums = lax.psum_scatter(
        jnp.concatenate(pieces, 1).astype(jnp.bfloat16), "ctx", scatter_dimension=0, tiled=True
    ).astype(jnp.float32)
    owned = lax.all_to_all(
        partial_sums.astype(jnp.bfloat16), "fsdp", split_axis=0, concat_axis=1, tiled=True
    ).astype(partial_sums.dtype)
    span_width = partial_sums.shape[1]
    owned_rows = owned.shape[0]
    arranged = owned.reshape(owned_rows, fsdp_size, span_width)
    model_part = model_width // fsdp_size
    hidden_part = hidden_width // fsdp_size
    bounds = [
        0,
        model_part,
        2 * model_part,
        3 * model_part,
        4 * model_part,
        4 * model_part + hidden_part,
        4 * model_part + 2 * hidden_part,
        4 * model_part + 3 * hidden_part,
    ]

    def joined_cols(first_col, last_col):
        return arranged[:, :, first_col:last_col].reshape(owned_rows, -1)

    grad_w_query = joined_cols(bounds[0], bounds[1])
    grad_w_key = joined_cols(bounds[1], bounds[2])
    grad_w_value = joined_cols(bounds[2], bounds[3])
    grad_w_out = joined_cols(bounds[3], bounds[4])
    grad_w_gate = joined_cols(bounds[4], bounds[5])
    grad_w_up = joined_cols(bounds[5], bounds[6])
    grad_w_down = joined_cols(bounds[6], bounds[7])
    gain_totals = jnp.sum(arranged[:, :, bounds[7] : bounds[7] + 2], 1)
    grad_gain_attn = gain_totals[:, 0]
    grad_gain_mlp = gain_totals[:, 1]
    grad_tokens = grad_input.reshape(slot_count, share_rows, model_width)
    return (
        result,
        grad_tokens,
        grad_w_query,
        grad_w_key,
        grad_w_value,
        grad_w_out,
        grad_w_gate,
        grad_w_up,
        grad_w_down,
        grad_gain_attn,
        grad_gain_mlp,
    )


def dot_f32(a, b):
    return jnp.dot(a, b, preferred_element_type=jnp.float32)

def load_sequence(order_ref, rows_ref, block, stores):
    per_src = rows_ref.shape[2] // block
    def one(slot, carry):
        src = slot // per_src
        lane = pl.multiple_of((slot % per_src) * block, block)
        place = pl.multiple_of(order_ref[slot] * block, block)
        for at, store in stores:
            store(rows_ref[src, at:at + HEAD_DIM, pl.ds(lane, block)], place)
        return carry
    lax.fori_loop(0, rows_ref.shape[0] * per_src, one, 0)

def fwd_kernel(
    order_ref, qkv_ref, mixed_ref, out_ref, lse_ref, qt, kr, vt, peak, total, acc, *, block, tile, step
):
    seq = qt.shape[1]

    def put_q(x, place):
        qt[:, pl.ds(place, block)] = x * jnp.bfloat16(HEAD_DIM ** -0.5)

    def put_k(x, place):
        kr[pl.ds(place, block), :] = x.T

    def put_v(x, place):
        vt[:, pl.ds(place, block)] = x

    load_sequence(
        order_ref, qkv_ref, block, ((0, put_q), (HEAD_DIM, put_k), (2 * HEAD_DIM, put_v))
    )

    def one_tile(qi, unused):
        q0 = pl.multiple_of(qi * tile, tile)
        peak[...] = jnp.full_like(peak, MASKED_SCORE)
        total[...] = jnp.zeros_like(total)
        acc[...] = jnp.zeros_like(acc)

        def visit(k0, first, masked):
            queries = qt[:, pl.ds(pl.multiple_of(q0 + first, step), tile - first)]
            s = dot_f32(kr[pl.ds(k0, step), :], queries)
            if masked:
                keep = lax.broadcasted_iota(jnp.int32, s.shape, 0) <= lax.broadcasted_iota(
                    jnp.int32, s.shape, 1
                )
                s = jnp.where(keep, s, MASKED_SCORE)
            old = peak[:, first:]
            new = jnp.maximum(old, jnp.max(s, 0, keepdims=True))
            p = jnp.exp(s - new)
            alpha = jnp.exp(old - new)
            peak[:, first:] = new
            total[:, first:] = total[:, first:] * alpha + jnp.sum(p, 0, keepdims=True)
            acc[:, first:] = acc[:, first:] * alpha + dot_f32(
                vt[:, pl.ds(k0, step)], p.astype(jnp.bfloat16)
            )

        def below(j, carry):
            visit(pl.multiple_of(j * step, step), 0, False)
            return carry

        lax.fori_loop(0, qi * (tile // step), below, 0)
        for part in range(tile // step):
            visit(pl.multiple_of(q0 + part * step, step), part * step, True)
        out_ref[:, pl.ds(q0, tile)] = acc[...] / total[...]
        lse_ref[:, pl.ds(q0, tile)] = peak[...] + jnp.log(total[...])
        return unused

    lax.fori_loop(0, seq // tile, one_tile, 0)
    per_src = mixed_ref.shape[2] // block

    def send(slot, carry):
        place = pl.multiple_of(order_ref[slot] * block, block)
        lane = pl.multiple_of((slot % per_src) * block, block)
        mixed_ref[slot // per_src, :, pl.ds(lane, block)] = out_ref[:, pl.ds(place, block)].astype(
            jnp.bfloat16
        )
        return carry

    lax.fori_loop(0, mixed_ref.shape[0] * per_src, send, 0)


def attend(order, qkv, block, tile, step):
    groups, unused, width = qkv.shape
    seq = groups * width
    vm = pl.BlockSpec(memory_space=pltpu.VMEM)
    bf, f32 = jnp.bfloat16, jnp.float32
    return pl.pallas_call(
        functools.partial(fwd_kernel, block=block, tile=tile, step=step),
        out_shape=(
            jax.ShapeDtypeStruct((groups, HEAD_DIM, width), bf),
            jax.ShapeDtypeStruct((HEAD_DIM, seq), f32),
            jax.ShapeDtypeStruct((1, seq), f32),
        ),
        in_specs=[pl.BlockSpec(memory_space=pltpu.SMEM), vm],
        out_specs=(vm, vm, vm),
        scratch_shapes=[
            pltpu.VMEM((HEAD_DIM, seq), bf),
            pltpu.VMEM((seq, HEAD_DIM), bf),
            pltpu.VMEM((HEAD_DIM, seq), bf),
            pltpu.VMEM((1, tile), f32),
            pltpu.VMEM((1, tile), f32),
            pltpu.VMEM((HEAD_DIM, tile), f32),
        ],
        compiler_params=pltpu.CompilerParams(vmem_limit_bytes=48 << 20),
        cost_estimate=pl.CostEstimate(
            flops=int(4.0 * seq * seq * HEAD_DIM),
            bytes_accessed=8 * seq * HEAD_DIM,
            transcendentals=0,
        ),
        name="attend",
    )(order, qkv)


def bwd_kernel(order_ref, qkv_ref, go_ref, out_ref, lse_ref, cos_ref, sin_ref, grad_ref,
               qt, qr, kt, kr, vr, got, gor, delta, dqt, dkr, dvr, *, block, tile, step):
    seq = qt.shape[1]
    scale = jnp.bfloat16(HEAD_DIM ** -0.5)
    def put_q(x, place):
        x = x * scale
        qt[:, pl.ds(place, block)] = x
        qr[pl.ds(place, block), :] = x.T
    def put_k(x, place):
        kt[:, pl.ds(place, block)] = x * scale
        kr[pl.ds(place, block), :] = x.T
    def put_v(x, place):
        vr[pl.ds(place, block), :] = x.T
    def put_go(x, place):
        got[:, pl.ds(place, block)] = x
        gor[pl.ds(place, block), :] = x.T
        delta[:, pl.ds(place, block)] = jnp.sum(x.astype(jnp.float32) * out_ref[:, pl.ds(place, block)], 0, keepdims=True)
    load_sequence(order_ref, qkv_ref, block, ((0, put_q), (HEAD_DIM, put_k), (2 * HEAD_DIM, put_v)))
    load_sequence(order_ref, go_ref, block, ((0, put_go),))
    dqt[...] = jnp.zeros_like(dqt)
    tiles = seq // tile

    def key_tile(kj, unused):
        k0 = pl.multiple_of(kj * tile, tile)
        keys = kr[pl.ds(k0, tile), :]
        keys_t = kt[:, pl.ds(k0, tile)]
        vals = vr[pl.ds(k0, tile), :]
        dkr[...] = jnp.zeros_like(dkr)
        dvr[...] = jnp.zeros_like(dvr)

        def visit(q0, width, rows, masked):
            s = dot_f32(keys[:rows], qt[:, pl.ds(q0, width)])
            p = jnp.exp(s - lse_ref[:, pl.ds(q0, width)])
            if masked:
                keep = lax.broadcasted_iota(jnp.int32, s.shape, 0) <= lax.broadcasted_iota(
                    jnp.int32, s.shape, 1
                ) + (rows - width)
                p = jnp.where(keep, p, 0.0)
            dp = dot_f32(vals[:rows], got[:, pl.ds(q0, width)])
            ds = (p * (dp - delta[:, pl.ds(q0, width)])).astype(jnp.bfloat16)
            dvr[:rows] += dot_f32(p.astype(jnp.bfloat16), gor[pl.ds(q0, width), :])
            dkr[:rows] += dot_f32(ds, qr[pl.ds(q0, width), :])
            dqt[:, pl.ds(q0, width)] += dot_f32(keys_t[:, :rows], ds)

        for part in range(tile // step):
            first = pl.multiple_of(k0 + part * step, step)
            visit(first, step, (part + 1) * step, True)

        def later(j, carry):
            visit(pl.multiple_of(j * step, step), step, tile, False)
            return carry

        lax.fori_loop((kj + 1) * (tile // step), seq // step, later, 0)
        put_out(dkr[...].T, HEAD_DIM, k0, True)
        put_out(dvr[...].T, 2 * HEAD_DIM, k0, False)
        return unused

    half = HEAD_DIM // 2
    def put_out(x, at, place, turn):
        for part in range(tile // block):
            piece = x[:, part * block:(part + 1) * block]
            here = place + part * block
            if turn:
                lanes = pl.ds(pl.multiple_of(here, block), block)
                c, s = cos_ref[:, lanes], sin_ref[:, lanes]
                a, b = piece[:half], piece[half:]
                piece = jnp.concatenate([a * c + b * s, b * c - a * s], 0)
            slot = order_ref[seq // block + here // block]
            per_src = grad_ref.shape[2] // block
            lane = pl.multiple_of((slot % per_src) * block, block)
            grad_ref[slot // per_src, at:at + HEAD_DIM, pl.ds(lane, block)] = piece.astype(jnp.bfloat16)

    lax.fori_loop(0, tiles, key_tile, 0)
    def write_q(qi, c):
        q0 = pl.multiple_of(qi * tile, tile)
        put_out(dqt[:, pl.ds(q0, tile)], 0, q0, True)
        return c
    lax.fori_loop(0, tiles, write_q, 0)

def attend_back(order, qkv, go, out, lse, cos, sin, block, tile, step):
    groups, unused, width = qkv.shape
    seq = groups * width
    vm = pl.BlockSpec(memory_space=pltpu.VMEM)
    bf, f32 = jnp.bfloat16, jnp.float32
    wide = lambda t: pltpu.VMEM((HEAD_DIM, seq), t)
    tall = lambda t: pltpu.VMEM((seq, HEAD_DIM), t)
    return pl.pallas_call(
        functools.partial(bwd_kernel, block=block, tile=tile, step=step),
        out_shape=jax.ShapeDtypeStruct(qkv.shape, bf),
        in_specs=[pl.BlockSpec(memory_space=pltpu.SMEM)] + [vm] * 6,
        out_specs=vm,
        scratch_shapes=[wide(bf), tall(bf), wide(bf), tall(bf), tall(bf), wide(bf), tall(bf),
                        pltpu.VMEM((1, seq), f32), wide(f32),
                        pltpu.VMEM((tile, HEAD_DIM), f32), pltpu.VMEM((tile, HEAD_DIM), f32)],
        compiler_params=pltpu.CompilerParams(vmem_limit_bytes=48 << 20),
        cost_estimate=pl.CostEstimate(
            flops=int(6.4 * seq * seq * HEAD_DIM),
            bytes_accessed=16 * seq * HEAD_DIM,
            transcendentals=0,
        ),
        name="attend_back",
    )(order, qkv, go, out, lse, cos, sin)


def nt_dot(a, b):
    return lax.dot_general(a, b, (((1,), (1,)), ((), ())), preferred_element_type=jnp.float32)


def whole(space=pltpu.VMEM):
    return pl.BlockSpec(memory_space=space)


def spread(pieces, place_ref, rows_ref):
    hops = (len(pieces) - 1) // 2
    slots, share, unused = pieces[0].shape
    place = place_ref[0]

    def put(piece, position):
        for slot in range(slots):
            first = pl.multiple_of(slot * share * (hops + 1) + position * share, share)
            rows_ref[pl.ds(first, share), :] = piece[slot]

    put(pieces[0], place)
    for hop in range(1, hops + 1):

        @pl.when(place >= hop)
        def take_below(hop=hop):
            put(pieces[hop], place - hop)

        @pl.when(place + hop <= hops)
        def take_above(hop=hop):
            put(pieces[hops + hop], place + hop)


def deal(rows_ref, place_ref, own_ref, others):
    slots, share, unused = own_ref.shape
    line = len(others) + 1
    for step, target in enumerate([own_ref] + list(others)):
        position = lax.rem(place_ref[0] + step, line)
        for slot in range(slots):
            first = pl.multiple_of(slot * share * line + position * share, share)
            target[slot] = rows_ref[pl.ds(first, share), :].astype(target.dtype)


def dealt_shapes(slots, share, width, line):
    return [jax.ShapeDtypeStruct((slots, share, width), jnp.float32)] + [
        jax.ShapeDtypeStruct((slots, share, width), jnp.bfloat16) for unused in range(line - 1)
    ]


def work(flops, bytes_accessed=0, transcendentals=0):
    return pl.CostEstimate(
        flops=int(flops * 0.2), bytes_accessed=int(bytes_accessed * 0.2), transcendentals=0
    )


def vmem_limit(mebibytes):
    return pltpu.CompilerParams(vmem_limit_bytes=mebibytes << 20)


EXTRA_ROWS = 16
LANES = 128


def cut_columns(place, group, weights, rows, line, extra=None):
    count = len(weights)
    columns = weights[0].shape[1] // line
    cut_rows = count * rows + (EXTRA_ROWS if extra is not None else 0)
    extras = [] if extra is None else [extra]

    def kernel(place_ref, group_ref, *refs):
        outs = refs[count * line + len(extras) :]
        for step in range(line):
            for i in range(count):
                outs[step][i * rows : (i + 1) * rows] = refs[step * count + i][...]
            if extras:
                outs[step][count * rows :] = refs[count * line][...]

    def target(step):
        return lambda i, place, group: (group[0], lax.rem(place[0] + step, line))

    fixed = lambda shape: pl.BlockSpec(shape, lambda i, place, group: (0, 0))
    return pl.pallas_call(
        kernel,
        out_shape=[jax.ShapeDtypeStruct((cut_rows, columns), jnp.bfloat16)] * line,
        grid_spec=pltpu.PrefetchScalarGridSpec(
            num_scalar_prefetch=2,
            grid=(1,),
            in_specs=[
                pl.BlockSpec((rows, columns), target(step))
                for step in range(line)
                for unused in range(count)
            ]
            + [fixed((EXTRA_ROWS, columns)) for unused in extras],
            out_specs=[fixed((cut_rows, columns))] * line,
        ),
        compiler_params=vmem_limit(60),
        name="cut_columns",
    )(place, group, *(list(weights) * line), *extras)


def order_shares(place, shares, count, vectors=0):
    line = len(shares)
    share_rows, columns = shares[0].shape
    rows = (share_rows - (EXTRA_ROWS if vectors else 0)) // count

    def kernel(place_ref, *refs):
        for step in range(line):
            source = lax.rem(place_ref[0] + line - step, line)
            for i in range(count):
                refs[line][source, i] = refs[step][i * rows : (i + 1) * rows]
            if vectors:
                lanes = pl.ds(pl.multiple_of(source * columns, columns), columns)
                refs[line + 1][:, lanes] = refs[step][count * rows :].astype(jnp.float32)

    shapes = [jax.ShapeDtypeStruct((line, count, rows, columns), shares[0].dtype)]
    if vectors:
        shapes.append(jax.ShapeDtypeStruct((EXTRA_ROWS, line * columns), jnp.float32))
    outs = pl.pallas_call(
        kernel,
        out_shape=shapes,
        in_specs=[whole(pltpu.SMEM)] + [whole()] * line,
        out_specs=[whole()] * len(shapes),
        compiler_params=vmem_limit(40),
        name="order_shares",
    )(place, *shares)
    return (outs[0], outs[1][:vectors]) if vectors else outs[0]


def widen_columns(place, shares, count, rows):
    line = len(shares)
    share_rows, columns = shares[0].shape

    def kernel(place_ref, *refs):
        for step in range(line):

            @pl.when(pl.program_id(0) == step)
            def widen(step=step):
                for i in range(count):
                    refs[line + i][...] = refs[step][i * rows : (i + 1) * rows].astype(jnp.float32)

    return pl.pallas_call(
        kernel,
        out_shape=[jax.ShapeDtypeStruct((rows, line * columns), jnp.float32)] * count,
        grid_spec=pltpu.PrefetchScalarGridSpec(
            num_scalar_prefetch=1,
            grid=(line,),
            in_specs=[pl.BlockSpec((share_rows, columns), lambda j, place: (0, 0))] * line,
            out_specs=[
                pl.BlockSpec(
                    (rows, columns), lambda j, place: (0, lax.rem(place[0] + line - j, line))
                )
            ]
            * count,
        ),
        compiler_params=vmem_limit(40),
        name="widen_columns",
    )(place, *shares)


def project(place, pieces, gain, w_heads, cosine, sine):
    line, count, part, width = w_heads.shape
    slots, share, model_width = pieces[0].shape
    rows = slots * share * line
    tile = width // 2
    heads = tile // HEAD_DIM
    n_pieces = len(pieces)
    half = HEAD_DIM // 2

    def kernel(place_ref, *refs):
        piece_refs = refs[:n_pieces]
        gain_ref, w_ref, cos_ref, sin_ref, rows_ref, out_ref = refs[n_pieces:]

        @pl.when((pl.program_id(0) == 0) & (pl.program_id(1) == 0))
        def assemble():
            spread(piece_refs, place_ref, rows_ref)
            rows_ref[...] = (rows_ref[...].astype(jnp.float32) * gain_ref[...]).astype(jnp.bfloat16)

        weight = w_ref[...].reshape(line * part, tile)
        turned = dot_f32(rows_ref[...], weight).T
        c, s = cos_ref[0], sin_ref[0]
        for head in range(heads):
            a = turned[head * HEAD_DIM : head * HEAD_DIM + half]
            b = turned[head * HEAD_DIM + half : (head + 1) * HEAD_DIM]
            out_ref[head, 0, :half, :] = (a * c - b * s).astype(jnp.bfloat16)
            out_ref[head, 0, half:, :] = (b * c + a * s).astype(jnp.bfloat16)

    return pl.pallas_call(
        kernel,
        grid=(count, 2),
        out_shape=[
            jax.ShapeDtypeStruct((rows, model_width), jnp.bfloat16),
            jax.ShapeDtypeStruct((width // HEAD_DIM, count, HEAD_DIM, rows), jnp.bfloat16),
        ],
        in_specs=[whole(pltpu.SMEM)]
        + [whole()] * (n_pieces + 1)
        + [
            pl.BlockSpec((line, 1, part, tile), lambda m, h: (0, m, 0, h)),
            pl.BlockSpec((1, half, rows), lambda m, h: (m, 0, 0)),
            pl.BlockSpec((1, half, rows), lambda m, h: (m, 0, 0)),
        ],
        out_specs=[
            pl.BlockSpec((rows, model_width), lambda m, h: (0, 0)),
            pl.BlockSpec((heads, 1, HEAD_DIM, rows), lambda m, h: (h, m, 0, 0)),
        ],
        compiler_params=vmem_limit(48),
        cost_estimate=work(6 * rows * model_width * width, 8 * rows * model_width),
        name="project",
    )(place, *pieces, gain, w_heads, cosine, sine)


def mix_out(place, mixed, w_out, slots, line):
    heads, unused, rows = mixed.shape
    width, model_width = w_out.shape
    share = rows // slots // line

    def kernel(place_ref, mixed_ref, w_ref, own_ref, *rest):
        *others, total = rest
        left = mixed_ref[...].reshape(width, rows).T
        total[...] = dot_f32(left, w_ref[...])
        deal(total, place_ref, own_ref, others)

    return pl.pallas_call(
        kernel,
        out_shape=dealt_shapes(slots, share, model_width, line),
        in_specs=[whole(pltpu.SMEM), whole(), whole()],
        out_specs=[whole()] * line,
        scratch_shapes=[pltpu.VMEM((rows, model_width), jnp.float32)],
        compiler_params=vmem_limit(48),
        cost_estimate=work(2 * rows * model_width * width, 8 * rows * model_width),
        name="mix_out",
    )(place, mixed, w_out)


def mlp_forward(place, pieces, upstream_pieces, w_mlp, tile):
    line, count, part, width = w_mlp.shape
    slots, share, model_width = pieces[0].shape
    rows = slots * share * line
    n_pieces = len(pieces)
    bf, f32 = jnp.bfloat16, jnp.float32

    def kernel(place_ref, *refs):
        x_pieces, u_pieces = refs[:n_pieces], refs[n_pieces : 2 * n_pieces]
        w_ref, x_ref, u_ref, hidden_ref, gate_ref, up_ref, own_ref = refs[
            2 * n_pieces : 2 * n_pieces + 7
        ]
        *others, total = refs[2 * n_pieces + 7 :]
        step = pl.program_id(0)

        @pl.when(step == 0)
        def assemble():
            spread(x_pieces, place_ref, x_ref)
            spread(u_pieces, place_ref, u_ref)

        down = w_ref[:, 0].reshape(line * part, tile)
        gate = w_ref[:, 1].reshape(line * part, tile)
        up = w_ref[:, 2].reshape(line * part, tile)
        x = x_ref[...]
        grad_hidden = dot_f32(u_ref[...], down)
        gate_act = dot_f32(x, gate)
        upward = dot_f32(x, up)
        sigmoid = jax.nn.sigmoid(gate_act)
        silu = gate_act * sigmoid
        hidden_ref[...] = (silu * upward).astype(bf)
        grad_gate = (
            grad_hidden * upward * sigmoid * (1.0 + gate_act * (1.0 - sigmoid))
        ).astype(bf)
        grad_up = (grad_hidden * silu).astype(bf)
        gate_ref[...] = grad_gate
        up_ref[...] = grad_up
        part_two = nt_dot(grad_gate, gate) + nt_dot(grad_up, up)

        @pl.when(step == 0)
        def first():
            total[...] = part_two

        @pl.when(step > 0)
        def further():
            total[...] += part_two

        @pl.when(step == pl.num_programs(0) - 1)
        def last():
            deal(total, place_ref, own_ref, others)

    fixed = lambda shape: pl.BlockSpec(shape, lambda j: (0,) * len(shape))
    columns = pl.BlockSpec((rows, tile), lambda j: (0, j))
    dealt = dealt_shapes(slots, share, model_width, line)
    return pl.pallas_call(
        kernel,
        grid=(width // tile,),
        out_shape=[jax.ShapeDtypeStruct((rows, model_width), bf)] * 2
        + [jax.ShapeDtypeStruct((rows, width), bf)] * 3
        + dealt,
        in_specs=[whole(pltpu.SMEM)]
        + [whole()] * (2 * n_pieces)
        + [pl.BlockSpec((line, count, part, tile), lambda j: (0, 0, 0, j))],
        out_specs=[fixed((rows, model_width))] * 2
        + [columns] * 3
        + [fixed((slots, share, model_width))] * line,
        scratch_shapes=[pltpu.VMEM((rows, model_width), f32)],
        compiler_params=vmem_limit(60),
        cost_estimate=work(16 * rows * model_width * width, 14 * model_width * width),
        name="mlp_forward",
    )(place, *pieces, *upstream_pieces, w_mlp)


def gate_up_weights(x_rows, grad_gate, grad_up, groups, line, tile):
    rows, model_width = x_rows.shape
    width = grad_gate.shape[1]
    block = model_width // groups // line

    def kernel(x_ref, gate_ref, up_ref, out_ref):
        for i, ref in enumerate((gate_ref, up_ref)):
            grads = transpose_product(x_ref[...], ref[...]).astype(jnp.bfloat16)
            out_ref[:, :, i * block : (i + 1) * block] = grads.reshape(groups, line, block, tile)

    columns = pl.BlockSpec((rows, tile), lambda j: (0, j))
    return pl.pallas_call(
        kernel,
        grid=(width // tile,),
        out_shape=jax.ShapeDtypeStruct((groups, line, 2 * block, width), jnp.bfloat16),
        in_specs=[pl.BlockSpec((rows, model_width), lambda j: (0, 0)), columns, columns],
        out_specs=pl.BlockSpec((groups, line, 2 * block, tile), lambda j: (0, 0, 0, j)),
        compiler_params=vmem_limit(60),
        cost_estimate=work(4 * rows * model_width * width, 8 * model_width * width),
        name="gate_up_weights",
    )(x_rows, grad_gate, grad_up)


def down_weights(u_rows, hidden, groups, line, tile):
    rows, model_width = u_rows.shape
    width = hidden.shape[1]
    block = model_width // groups // line

    def kernel(u_ref, hidden_ref, out_ref):
        grads = transpose_product(u_ref[...], hidden_ref[...]).astype(jnp.bfloat16)
        out_ref[:, :line] = grads.reshape(groups, line, block, tile)

    return pl.pallas_call(
        kernel,
        grid=(width // tile,),
        out_shape=jax.ShapeDtypeStruct((groups, line + 1, block, width), jnp.bfloat16),
        in_specs=[
            pl.BlockSpec((rows, model_width), lambda j: (0, 0)),
            pl.BlockSpec((rows, tile), lambda j: (0, j)),
        ],
        out_specs=pl.BlockSpec((groups, line + 1, block, tile), lambda j: (0, 0, 0, j)),
        compiler_params=vmem_limit(60),
        cost_estimate=work(2 * rows * model_width * width, 4 * model_width * width),
        name="down_weights",
    )(u_rows, hidden)


def mlp_out(place, hidden, w_mlp, slots, tile):
    line, count, part, width = w_mlp.shape
    rows = hidden.shape[0]
    model_width = line * part
    share = rows // slots // line

    def kernel(place_ref, hidden_ref, w_ref, own_ref, *rest):
        *others, total = rest
        step = pl.program_id(0)
        part_out = nt_dot(hidden_ref[...], w_ref[...].reshape(line * part, tile))

        @pl.when(step == 0)
        def first():
            total[...] = part_out

        @pl.when(step > 0)
        def further():
            total[...] += part_out

        @pl.when(step == pl.num_programs(0) - 1)
        def last():
            deal(total, place_ref, own_ref, others)

    fixed = lambda shape: pl.BlockSpec(shape, lambda j: (0,) * len(shape))
    return pl.pallas_call(
        kernel,
        grid=(width // tile,),
        out_shape=dealt_shapes(slots, share, model_width, line),
        in_specs=[
            whole(pltpu.SMEM),
            pl.BlockSpec((rows, tile), lambda j: (0, j)),
            pl.BlockSpec((line, 1, part, tile), lambda j: (0, 0, 0, j)),
        ],
        out_specs=[fixed((slots, share, model_width))] * line,
        scratch_shapes=[pltpu.VMEM((rows, model_width), jnp.float32)],
        compiler_params=vmem_limit(60),
        cost_estimate=work(2 * rows * model_width * width, 2 * model_width * width),
        name="mlp_out",
    )(place, hidden, w_mlp)


def branch_back(place, pieces, w_out, heads):
    slots, share, model_width = pieces[0].shape
    line = (len(pieces) + 1) // 2
    rows = slots * share * line

    def kernel(place_ref, *refs):
        *piece_refs, w_ref, rows_ref, out_ref = refs
        spread(piece_refs, place_ref, rows_ref)
        turned = nt_dot(w_ref[...], rows_ref[...])
        out_ref[...] = turned.astype(jnp.bfloat16).reshape(out_ref.shape)

    return pl.pallas_call(
        kernel,
        out_shape=[
            jax.ShapeDtypeStruct((rows, model_width), jnp.bfloat16),
            jax.ShapeDtypeStruct((heads, HEAD_DIM, rows), jnp.bfloat16),
        ],
        in_specs=[whole(pltpu.SMEM)] + [whole()] * (len(pieces) + 1),
        out_specs=[whole(), whole()],
        compiler_params=vmem_limit(40),
        cost_estimate=work(2 * rows * model_width * heads * HEAD_DIM, 8 * rows * model_width),
        name="branch_back",
    )(place, *pieces, w_out)


def out_weight(grads, mixed, branch_rows, tile):
    groups, blocks, block, width = grads.shape
    heads, unused, rows = mixed.shape

    def kernel(grads_ref, mixed_ref, rows_ref, out_ref):
        left = mixed_ref[...].reshape(heads * HEAD_DIM, rows)
        product = dot_f32(left, rows_ref[...]).astype(jnp.bfloat16)
        out_ref[...] = product.reshape(groups, 1, block, tile)

    return pl.pallas_call(
        kernel,
        grid=(width // tile,),
        out_shape=jax.ShapeDtypeStruct(grads.shape, grads.dtype),
        in_specs=[
            pl.BlockSpec(memory_space=pl.ANY),
            pl.BlockSpec(mixed.shape, lambda j: (0, 0, 0)),
            pl.BlockSpec((rows, tile), lambda j: (0, j)),
        ],
        out_specs=pl.BlockSpec((groups, 1, block, tile), lambda j: (0, blocks - 1, 0, j)),
        input_output_aliases={0: 0},
        compiler_params=vmem_limit(60),
        cost_estimate=work(4 * rows * heads * HEAD_DIM * width, 8 * rows * width),
        name="out_weight",
    )(grads, mixed, branch_rows)


def head_weights(group, all_rows, corner, head_grads, w_head, gain, gain_two, owners):
    sources, features, rows = head_grads.shape
    model_width = all_rows[0].shape[1]
    block = model_width // owners
    lanes = 2 * LANES
    half = rows // 2
    f32 = jnp.float32

    def kernel(group_ref, *refs):
        x_refs, corner_refs = refs[: sources - 2], refs[sources - 2 : sources + 2]
        g_ref, w_ref, gain_ref, two_ref, out_ref, total = refs[sources + 2 :]
        step = pl.program_id(0)

        def product(bits, ref):
            return dot_f32(g_ref[lax.bitwise_xor(group_ref[0], bits)], ref[...])

        part = sum(product(bits, ref) for bits, ref in enumerate(x_refs))

        def with_corner(half_refs):
            return part + product(sources - 2, half_refs[0]) + product(sources - 1, half_refs[1])

        @pl.when(step == 0)
        def first():
            total[...] = with_corner(corner_refs[0::2])

        @pl.when(step == 1)
        def last():
            grads = (total[...] + with_corner(corner_refs[1::2])).T
            weighed = jnp.sum(grads * w_ref[...].astype(f32), 1, keepdims=True) / gain_ref[...].T
            spare = lanes - features
            at = lax.broadcasted_iota(jnp.int32, (model_width, spare), 1)
            tail = jnp.where(at == 0, weighed, jnp.where(at == 1, two_ref[...].T, 0.0))
            joined = jnp.concatenate([grads, tail], 1).astype(jnp.bfloat16)
            out_ref[...] = joined.reshape(owners, block, lanes)

    fixed = lambda shape: pl.BlockSpec(shape, lambda s: (0,) * len(shape))
    return pl.pallas_call(
        kernel,
        grid=(2,),
        out_shape=jax.ShapeDtypeStruct((owners, block, lanes), jnp.bfloat16),
        in_specs=[whole(pltpu.SMEM)]
        + [pl.BlockSpec((half, model_width), lambda s: (s, 0))] * (sources - 2)
        + [fixed((half, model_width))] * 4
        + [
            pl.BlockSpec((sources, features, half), lambda s: (0, 0, s)),
            fixed((model_width, features)),
            fixed((1, model_width)),
            fixed((1, model_width)),
        ],
        out_specs=fixed((owners, block, lanes)),
        scratch_shapes=[pltpu.VMEM((features, model_width), f32)],
        compiler_params=vmem_limit(60),
        cost_estimate=work(6 * sources * rows * features * model_width, 0),
        name="head_weights",
    )(group, *all_rows, *corner, head_grads, w_head, gain, gain_two)


def join_heads(parts):
    groups, line, rows, lanes = parts.shape
    width = groups * HEAD_DIM

    def kernel(parts_ref, *outs):
        for i, out in enumerate(outs):
            pick = slice(i * HEAD_DIM, (i + 1) * HEAD_DIM)
            heads = [parts_ref[c, 0][:, pick].astype(jnp.float32) for c in range(groups)]
            out[...] = jnp.concatenate(heads, 1)

    return pl.pallas_call(
        kernel,
        grid=(line,),
        out_shape=[jax.ShapeDtypeStruct((rows, line * width), jnp.float32)] * 3,
        in_specs=[pl.BlockSpec((groups, 1, rows, lanes), lambda f: (0, f, 0, 0))],
        out_specs=[pl.BlockSpec((rows, width), lambda f: (0, f))] * 3,
        compiler_params=vmem_limit(24),
        name="join_heads",
    )(parts)


def project_back(place, head_grads, w_heads, slots):
    line, count, part, width = w_heads.shape
    rows, model_width = head_grads.shape[-1], line * part
    heads = width // HEAD_DIM
    share = rows // slots // line

    def kernel(place_ref, g_ref, w_ref, own_ref, *rest):
        *others, total = rest
        m = pl.program_id(0)
        grads = g_ref[...].reshape(width, rows).T
        partial = nt_dot(grads, w_ref[...].reshape(line * part, width))

        @pl.when(m == 0)
        def first():
            total[...] = partial

        @pl.when(m > 0)
        def further():
            total[...] += partial

        @pl.when(m == count - 1)
        def last():
            deal(total, place_ref, own_ref, others)

    fixed = lambda shape: pl.BlockSpec(shape, lambda m: (0,) * len(shape))
    return pl.pallas_call(
        kernel,
        grid=(count,),
        out_shape=dealt_shapes(slots, share, model_width, line),
        in_specs=[
            whole(pltpu.SMEM),
            pl.BlockSpec((heads, 1, HEAD_DIM, rows), lambda m: (0, m, 0, 0)),
            pl.BlockSpec((line, 1, part, width), lambda m: (0, m, 0, 0)),
        ],
        out_specs=[fixed((slots, share, model_width))] * line,
        scratch_shapes=[pltpu.VMEM((rows, model_width), jnp.float32)],
        compiler_params=vmem_limit(48),
        cost_estimate=work(2 * count * rows * width * model_width, 8 * rows * model_width),
        name="project_back",
    )(place, head_grads, w_heads)


def line_steps(size, step):
    return [(i, i + step) for i in range(size) if 0 <= i + step < size]


def after(values, *earlier):
    return lax.optimization_barrier((values, earlier))[0]


def send_shares(share, axis, between=()):
    size = lax.axis_size(axis)
    ups, downs = [share], [share]
    for hop in range(1, size):
        up = lax.ppermute(ups[-1], axis, line_steps(size, 1)[hop - 1 :])
        down = lax.ppermute(downs[-1], axis, line_steps(size, -1)[: size - hop])
        if hop <= len(between):
            done = between[hop - 1]((ups[-1], downs[-1]))
            up, down = after((up, down), done)
        ups.append(up)
        downs.append(down)
    return ups + downs[1:]


def flip(values, bits):
    size = lax.axis_size("ctx")
    return lax.ppermute(values, "ctx", [(i, i ^ bits) for i in range(size)])


def send_dealt(others, axis):
    size = lax.axis_size(axis)
    return [
        lax.ppermute(other, axis, [(i, (i + step) % size) for i in range(size)])
        for step, other in enumerate(others, 1)
    ]


def scatter_line(others, axis, between=()):
    size = lax.axis_size(axis)
    up = down = None
    for hop in range(1, size):
        rising, falling = others[size - hop - 1], others[hop - 1]
        if hop > 1:
            rising = (rising.astype(jnp.float32) + up.astype(jnp.float32)).astype(rising.dtype)
            falling = (falling.astype(jnp.float32) + down.astype(jnp.float32)).astype(falling.dtype)
        up = lax.ppermute(rising, axis, line_steps(size, 1)[:hop])
        down = lax.ppermute(falling, axis, line_steps(size, -1)[size - 1 - hop :])
        if hop <= len(between):
            up, down = after((up, down), between[hop - 1]((rising, falling)))
    return [up, down]


def add_shares(own, received):
    return own + sum(share.astype(jnp.float32) for share in received)


def swap_dealt(shares):
    return [shares[0]] + send_dealt(shares[1:], "fsdp")


def deal_line(parts, place):
    line = parts.shape[0]
    return [
        lax.dynamic_index_in_dim(parts, lax.rem(place[0] + step, line), 0, keepdims=False)
        for step in range(line)
    ]


def swap_heads(parts):
    return lax.all_to_all(parts, "ctx", split_axis=0, concat_axis=0, tiled=True)


def sum_groups(parts):
    return lax.psum_scatter(parts, "ctx", scatter_dimension=0, tiled=True)[0]


def head_device(
    tokens,
    block_order,
    w_query,
    w_key,
    w_value,
    w_out,
    w_gate,
    w_up,
    w_down,
    gain_attn,
    gain_mlp,
    cotangent,
):
    slots, share_rows, model_width = tokens.shape
    ctx_size, line = lax.axis_size("ctx"), lax.axis_size("fsdp")
    block_rows = share_rows * line
    group_rows = slots * block_rows
    bf, f32 = jnp.bfloat16, jnp.float32
    place = lax.axis_index("fsdp").astype(jnp.int32).reshape(1)
    group = lax.axis_index("ctx").astype(jnp.int32).reshape(1)
    own_rows = w_query.shape[0] // ctx_size
    order = block_order.astype(jnp.int32)
    sequence = group_rows * ctx_size
    slot_of = jnp.sum(
        jnp.where(order[None, :] == jnp.arange(order.shape[0])[:, None], jnp.arange(order.shape[0], dtype=jnp.int32)[None, :], 0), 1
    ).astype(jnp.int32)

    stream = tokens.astype(f32)
    root_one = lax.rsqrt(jnp.mean(stream * stream, -1, keepdims=True) + EPSILON)
    norm_one = stream * root_one
    gain_rows = jnp.pad(jnp.stack([gain_attn, gain_mlp]), ((0, EXTRA_ROWS - 2), (0, 0)))
    head_cuts = swap_dealt(
        cut_columns(place, group, [w_query, w_key, w_value], own_rows, line, gain_rows)
    )
    own_heads, gains = order_shares(place, head_cuts, 3, 2)
    attn_gain, mlp_gain = gains[0], gains[1]
    w_heads = lax.all_gather(own_heads, "ctx", axis=2, tiled=True)

    attn_pieces = send_shares(after(norm_one.astype(bf), head_cuts), "fsdp")

    mlp_cuts = cut_columns(place, group, [w_down, w_gate, w_up], own_rows, line)
    w_heads = after(w_heads, mlp_cuts)
    mlp_cuts = swap_dealt(after(mlp_cuts, attn_pieces))

    w_head = lax.dynamic_slice_in_dim(w_heads, group[0] * HEAD_DIM, HEAD_DIM, 3)
    w_head = jnp.concatenate([w_head[:, i].reshape(model_width, HEAD_DIM) for i in range(3)], 1)

    half = HEAD_DIM // 2
    frequency = 1.0 / ROPE_BASE ** (jnp.arange(half, dtype=f32) * (2.0 / HEAD_DIM))
    places = jnp.arange(group_rows * ctx_size, dtype=jnp.int32).astype(f32)
    angles = frequency[:, None] * places[None, :]
    cosine, sine = jnp.cos(angles), jnp.sin(angles)

    def own_columns(table):
        return jnp.concatenate(
            [
                lax.dynamic_slice_in_dim(
                    table, order[slots * group[0] + i] * block_rows, block_rows, 1
                )
                for i in range(slots)
            ],
            1,
        )

    own_cosine, own_sine = own_columns(cosine), own_columns(sine)
    turn_cosine = jnp.stack([own_cosine, own_cosine, jnp.ones_like(own_cosine)])
    turn_sine = jnp.stack([own_sine, own_sine, jnp.zeros_like(own_sine)])

    attn_rows, heads_out = project(
        place, attn_pieces, attn_gain[None], w_heads, turn_cosine, turn_sine
    )
    heads_out = heads_out.reshape(ctx_size, 3 * HEAD_DIM, group_rows)
    head_rows = swap_heads(after(heads_out, mlp_cuts[1]))
    mixed_send, attended, log_total = attend(
        order, head_rows, block_rows, sequence, 2 * block_rows
    )
    mixed = swap_heads(mixed_send)
    mlp_cuts = order_shares(place, after(mlp_cuts, mixed), 3)
    w_mlp = lax.all_gather(mlp_cuts, "ctx", axis=2, tiled=True)
    upstream_pieces = send_shares(after(cotangent, mlp_cuts), "fsdp")
    own, *others = mix_out(place, after(mixed, w_head, mlp_cuts), w_out, slots, line)
    middle = stream + add_shares(own, scatter_line(others, "fsdp"))

    root_two = lax.rsqrt(jnp.mean(middle * middle, -1, keepdims=True) + EPSILON)
    norm_two = middle * root_two
    mlp_input = (norm_two * mlp_gain).astype(bf)
    mlp_pieces = send_shares(mlp_input, "fsdp")

    all_rows = {0: attn_rows}
    start_rows = after(attn_rows, mlp_pieces, upstream_pieces, w_mlp)
    all_rows[2], all_rows[4] = flip(start_rows, 2), flip(start_rows, 4)
    mlp_rows, upstream_rows, hidden, grad_gate, grad_up, own, *others = mlp_forward(
        place, mlp_pieces, upstream_pieces, w_mlp, 512
    )
    results = {}

    def weigh_gate_up(sent):
        rows_here = after(mlp_rows, sent)
        results["gate_up"] = gate_up_weights(rows_here, grad_gate, grad_up, ctx_size, line, 512)
        return results["gate_up"], all_rows[2], all_rows[4]

    upper = attn_rows.shape[0] // 2

    def weigh_down(sent):
        results["down"] = down_weights(
            upstream_rows, after(hidden, sent), ctx_size, line, 512
        )
        results["gate_up_sums"] = sum_groups(after(results["gate_up"], sent))
        return results["down"]

    grad_two = add_shares(own, scatter_line(others, "fsdp", (weigh_gate_up, weigh_down)))
    gate_up_sums = results["gate_up_sums"]
    down_grads = results["down"]
    gain_two_part = jnp.sum(grad_two * norm_two, (0, 1))
    grad_middle = cotangent.astype(f32) + norm_back(grad_two, norm_two, root_two, mlp_gain)

    def weigh_out(sent):
        results["out"] = mlp_out(place, after(hidden, sent), w_mlp, slots, 512)
        return results["out"]

    def cut_corner(sent):
        by_x, by_y = after((all_rows[2], all_rows[4]), sent)
        results["corner"] = (by_x[:upper], by_y[upper:])
        return results["corner"]

    branch_pieces = send_shares(grad_middle.astype(bf), "fsdp", (weigh_out, cut_corner))
    corner = [flip(results["corner"][0], 4), flip(results["corner"][1], 2)]
    own_out, *others_out = results["out"]
    branch_rows, grad_mixed = branch_back(place, branch_pieces, w_out, ctx_size)

    out_received = send_dealt(after(others_out, branch_rows), "fsdp")
    for bits in (0, 2, 4):
        all_rows[bits + 1] = flip(after(all_rows[bits], branch_rows), 1)
    grad_heads = swap_heads(grad_mixed)
    head_grads = attend_back(
        jnp.concatenate([order, slot_of]),
        head_rows,
        after(
            grad_heads, all_rows[1], all_rows[3], all_rows[5]
        ),
        attended,
        log_total,
        cosine,
        sine,
        block_rows,
        sequence,
        block_rows,
    )
    head_grads = after(head_grads, out_received, corner)
    corner = corner + [flip(part, 1) for part in after(corner, head_grads)]
    gate_up_dealt = deal_line(after(gate_up_sums, head_grads), place)
    gate_up_back = swap_dealt(gate_up_dealt)
    lin_grads = swap_heads(after(head_grads, gate_up_dealt))
    head_parts = head_weights(
        group,
        [all_rows[bits] for bits in range(ctx_size - 2)],
        corner,
        after(head_grads, gate_up_dealt),
        w_head,
        attn_gain[None],
        gain_two_part[None],
        ctx_size * line,
    )
    down_grads = out_weight(down_grads, mixed, after(branch_rows, head_parts), 512)
    down_sums = sum_groups(after(down_grads, gate_up_sums))
    lin_grads = after(lin_grads, head_parts, gate_up_back[1], gate_up_back[2])
    head_parts = lax.all_to_all(
        after(head_parts, lin_grads), ("ctx", "fsdp"), split_axis=0, concat_axis=0, tiled=True
    )
    lin_grads = lin_grads.reshape(ctx_size, 3, HEAD_DIM, group_rows)
    own, *others = project_back(place, lin_grads, w_heads, slots)

    def swap_down(sent):
        parts = deal_line(after(down_sums, sent)[:line], place)
        results["down_back"] = swap_dealt(parts)
        return results["down_back"][1]

    one_received = scatter_line(
        others, "fsdp", (lambda sent: (gate_up_back[3], head_parts), lambda sent: (), swap_down)
    )
    down_back = results["down_back"]
    grad_one = add_shares(own, one_received)
    result = (middle + add_shares(own_out, out_received)).astype(bf)
    grad_tokens = grad_middle + norm_back(grad_one, norm_one, root_one, attn_gain)
    owners = [(c * line + f, f * ctx_size + c) for c in range(ctx_size) for f in range(line)]
    grad_w_out = lax.ppermute(down_sums[line], ("ctx", "fsdp"), owners).astype(f32)
    grad_w_gate, grad_w_up = widen_columns(place, gate_up_back, 2, own_rows)
    (grad_w_down,) = widen_columns(place, after(down_back, grad_tokens), 1, own_rows)
    head_parts = head_parts.reshape(ctx_size, line, own_rows, -1)
    grad_w_query, grad_w_key, grad_w_value = join_heads(head_parts)
    spare = 3 * HEAD_DIM
    gain_grads = jnp.sum(head_parts[..., spare : spare + 2].astype(f32), (0, 1)).T
    return (
        result,
        grad_tokens,
        grad_w_query,
        grad_w_key,
        grad_w_value,
        grad_w_out,
        grad_w_gate,
        grad_w_up,
        grad_w_down,
        gain_grads[0],
        gain_grads[1],
    )


def layer_step(*arrays):
    heads_here = arrays[0].shape[-1] // lax.axis_size("fsdp") // HEAD_DIM
    if heads_here == lax.axis_size("ctx") == 8:
        return head_device(*arrays)
    return per_device(*arrays)


def solution(mesh):
    in_specs = (
        P("ctx", "fsdp", None),
        P(),
        P("fsdp", None),
        P("fsdp", None),
        P("fsdp", None),
        P("fsdp", None),
        P("fsdp", None),
        P("fsdp", None),
        P("fsdp", None),
        P("fsdp"),
        P("fsdp"),
        P("ctx", "fsdp", None),
    )
    out_specs = (
        P("ctx", "fsdp", None),
        P("ctx", "fsdp", None),
        P(("ctx", "fsdp"), None),
        P(("ctx", "fsdp"), None),
        P(("ctx", "fsdp"), None),
        P(("ctx", "fsdp"), None),
        P(("ctx", "fsdp"), None),
        P(("ctx", "fsdp"), None),
        P(("ctx", "fsdp"), None),
        P(("ctx", "fsdp")),
        P(("ctx", "fsdp")),
    )
    return jax.shard_map(
        layer_step, mesh=mesh, in_specs=in_specs, out_specs=out_specs, check_vma=False
    )
```
